32 devices in a mesh: dp: 16 (over z, y, x), tensor: 2 (over core).
Axes of the slice: x: 2, y: 2, z: 4, core: 2. Of those that a mesh axis runs over, the one named last changes fastest.
Arguments:
- tokens: bfloat16 [8192, 768], P(('dp', 'tensor')), may hold values from -6 to 6
- query_weight: bfloat16 [768, 768], P('dp', 'tensor'), may hold values from -0.21875 to 0.21875
- key_weight: bfloat16 [768, 768], P('dp', 'tensor'), may hold values from -0.21875 to 0.21875
- value_weight: bfloat16 [768, 768], P('dp', 'tensor'), may hold values from -0.21875 to 0.21875
- output_weight: bfloat16 [768, 768], P('dp', 'tensor'), may hold values from -1.75 to 1.75
- inner_weight: bfloat16 [768, 3072], P('dp', 'tensor'), may hold values from -0.21875 to 0.21875
- outer_weight: bfloat16 [768, 3072], P('dp', 'tensor'), may hold values from -0.109375 to 0.109375
- attn_gain: float32 [768], replicated, may hold values from 0.5 to 1.5
- attn_shift: float32 [768], replicated, may hold values from -3 to 3
- ffn_gain: float32 [768], replicated, may hold values from 0.5 to 1.5
- ffn_shift: float32 [768], replicated, may hold values from -3 to 3
- teacher: bfloat16 [8192, 768], P(('dp', 'tensor')), may hold values from -6 to 6
- segments: int32 [2, 4096], replicated, may hold values from 0 to 4, as said below
- random_blocks: int32 [12, 64, 3], P('tensor'), may hold values from 0 to 63
- valid_tokens: int32 [8192], P(('dp', 'tensor')), may hold values from 0 to 1, as said below
Outputs:
- output: bfloat16 [8192, 768], P(('dp', 'tensor'))
- loss_value: float32 [], replicated
- grad_tokens: float32 [8192, 768], P(('dp', 'tensor'))
- grad_query: float32 [768, 768], P('dp', 'tensor')
- grad_key: float32 [768, 768], P('dp', 'tensor')
- grad_value: float32 [768, 768], P('dp', 'tensor')
- grad_output: float32 [768, 768], P('dp', 'tensor')
- grad_inner: float32 [768, 3072], P('dp', 'tensor')
- grad_outer: float32 [768, 3072], P('dp', 'tensor')
- grad_attn_gain: float32 [768], P(('dp', 'tensor'))
- grad_attn_shift: float32 [768], P(('dp', 'tensor'))
- grad_ffn_gain: float32 [768], P(('dp', 'tensor'))
- grad_ffn_shift: float32 [768], P(('dp', 'tensor'))
The draws below stay inside these ranges and needn't reach their ends.
Inputs may be any that keep to these rules, and one draw needn't show every extreme that they name: `segments`: each sequence holds five documents numbered 0 to 4 in order; document 2 covers at least positions 1843 to 2251. `valid_tokens`: the first token of every sequence is valid.
All inputs are finite; a program needn't handle non-finite values.
Results may differ from the reference program's by a relative error of at most 0.015.
Values may be sent and summed in bfloat16 or wider, within the bound.
No kernel may reach another device: no remote copies, remote signals or barrier semaphores. Data moves between devices by JAX's collectives and lax.ppermute only.
A program may use at most 192 MiB of HBM per device.

```python
import jax
import jax.numpy as jnp
from jax import lax

D = 768
HEADS = 12
FF = 3072
BLOCK = 64
RAND = 3
SEQ = 4096
NBLOCKS = 64
TOKENS = 8192


def draw_segments(key, part):
    key = jax.random.fold_in(key, 11)
    subkeys = jax.random.split(key, 4)
    cut_shape = (TOKENS // SEQ, 1)
    first_cut = jax.random.randint(subkeys[0], cut_shape, SEQ * 10 // 100, SEQ * 20 // 100 + 1)
    second_cut = jax.random.randint(subkeys[1], cut_shape, SEQ * 30 // 100, 9 * SEQ // 20 + 1)
    third_cut = jax.random.randint(subkeys[2], cut_shape, 11 * SEQ // 20, SEQ * 70 // 100 + 1)
    fourth_cut = jax.random.randint(subkeys[3], cut_shape, SEQ * 80 // 100, SEQ * 90 // 100 + 1)
    position = jnp.arange(SEQ, dtype=jnp.int32)[None, :]
    numbers = (position >= first_cut).astype(jnp.int32) + (position >= second_cut).astype(jnp.int32)
    numbers = numbers + (position >= third_cut).astype(jnp.int32) + (position >= fourth_cut).astype(jnp.int32)
    return numbers.astype(jnp.int32)


def draw_valid_tokens(key, part):
    key = jax.random.fold_in(key, 23)
    position = jnp.arange(TOKENS, dtype=jnp.int32)
    threshold = 300 + 600 * (position // SEQ) // (TOKENS // SEQ)
    rolled = jax.random.randint(key, (TOKENS,), 0, 1000)
    return ((rolled < threshold) | (position % SEQ == 0)).astype(jnp.int32)


def plant(array, key, least, top_value):
    longest = array.shape.index(max(array.shape))
    spots = []
    for shift in (0, 1):
        where = [jax.random.randint(jax.random.fold_in(key, axis), (), 0, length) for axis, length in enumerate(array.shape)]
        where[longest] = (where[longest] + shift) % array.shape[longest]
        spots.append(tuple(where))
    return array.at[spots[0]].set(least).at[spots[1]].set(top_value)


def block_scale(own_key, shape, shards, least, largest):
    def one(dim, parts):
        heights = jax.random.uniform(jax.random.fold_in(jax.random.fold_in(own_key, 6), dim), (parts,), jnp.float32, least / len(shards), largest / len(shards))
        return jnp.repeat(jnp.exp(heights), shape[dim] // parts).reshape((-1,) + (1,) * (len(shape) - dim - 1))

    gain = one(*shards[0])
    for cut in shards[1:]:
        gain = gain * one(*cut)
    return gain


def normal_values(key, shape, deviation, reach, cuts=(), kind=jnp.bfloat16):
    factor_of = block_scale(key, shape, cuts, -0.22, 0.18) if cuts else 1.0
    drawn = jax.random.normal(key, shape, jnp.float32) * deviation * factor_of
    return jnp.minimum(jnp.maximum(drawn, -reach), reach).astype(kind)


def setup_inputs(seed: int = 0) -> dict:
    streams_of = jax.random.split(jax.random.key(seed), 16)
    return {
        "tokens": normal_values(streams_of[0], (TOKENS, D), 1.0, 6.0, ((0, 32),)),
        "query_weight": normal_values(streams_of[1], (D, D), D ** -0.5, 0.21875, ((0, 16), (1, 2))),
        "key_weight": normal_values(streams_of[2], (D, D), D ** -0.5, 0.21875, ((0, 16), (1, 2))),
        "value_weight": normal_values(streams_of[3], (D, D), D ** -0.5, 0.21875, ((0, 16), (1, 2))),
        "output_weight": normal_values(streams_of[4], (D, D), (D // 64) ** -0.5, 1.75, ((0, 16), (1, 2))),
        "inner_weight": normal_values(streams_of[5], (D, FF), D ** -0.5, 0.21875, ((0, 16), (1, 2))),
        "outer_weight": normal_values(streams_of[6], (D, FF), FF ** -0.5, 0.109375, ((0, 16), (1, 2))),
        "attn_gain": jnp.clip(1.0 + 0.1 * jax.random.normal(streams_of[7], (D,), jnp.float32), 0.5, 1.5),
        "attn_shift": normal_values(streams_of[8], (D,), 0.5, 3.0, (), jnp.float32),
        "ffn_gain": jnp.clip(1.0 + 0.1 * jax.random.normal(streams_of[9], (D,), jnp.float32), 0.5, 1.5),
        "ffn_shift": normal_values(streams_of[10], (D,), 0.5, 3.0, (), jnp.float32),
        "teacher": normal_values(streams_of[11], (TOKENS, D), 1.0, 6.0, ((0, 32),)),
        "segments": draw_segments(jax.random.fold_in(streams_of[15], 71), 0),
        "random_blocks": plant(jax.random.randint(streams_of[13], (HEADS, NBLOCKS, RAND), 0, NBLOCKS), jax.random.fold_in(streams_of[13], 1), 0, NBLOCKS - 1).astype(jnp.int32),
        "valid_tokens": draw_valid_tokens(jax.random.fold_in(streams_of[15], 71), 0),
    }


@jax.custom_vjp
def low(v):
    return lax.optimization_barrier(v.astype(jnp.bfloat16)).astype(jnp.float32)

@jax.custom_vjp
def low_back(v):
    return v

def low_keep(v):
    return (low(v), None)

def low_pass(kept, grad):
    return (grad,)

def back_keep(v):
    return (v, None)

def back_low(kept, grad):
    return (low(grad),)
low.defvjp(low_keep, low_pass)
low_back.defvjp(back_keep, back_low)
epsilon = 1e-05
highest = lax.Precision.HIGHEST
masked_value = -1e+30

def product(left_side, right_side):
    return jnp.dot(left_side, right_side, precision=highest, preferred_element_type=jnp.float32)

def both_round(values):
    return low_back(low(values))

def layer_norm(values, gain_row, shift_row):
    centred = values - lax.optimization_barrier(jnp.mean(values, axis=-1, keepdims=True))
    spread = lax.optimization_barrier(jnp.mean(centred * centred, axis=-1, keepdims=True))
    return centred * lax.rsqrt(spread + epsilon) * gain_row + shift_row

def block_allowed(block_table):
    block_count = block_table.shape[1]
    block_ids = jnp.arange(block_count, dtype=jnp.int32)
    row_ids = block_ids[:, None]
    col_ids = block_ids[None, :]
    fixed_part = (jnp.abs(row_ids - col_ids) <= 1) | (col_ids == 0) | (col_ids == block_count - 1)
    fixed_part = fixed_part | (row_ids == 0) | (row_ids == block_count - 1)
    picked = jnp.any(block_table[:, :, :, None] == block_ids[None, None, None, :], axis=2)
    return fixed_part[None] | picked

def token_mask(allowed_rows, segment_rows, segment_all):
    head_count, query_blocks, key_blocks = allowed_rows.shape
    spread_out = jnp.broadcast_to(allowed_rows[:, :, None, :, None], (head_count, query_blocks, BLOCK, key_blocks, BLOCK))
    spread_out = spread_out.reshape(head_count, query_blocks * BLOCK, key_blocks * BLOCK)
    same_doc = segment_rows[:, None] == segment_all[None, :]
    return spread_out & same_doc[None]

def attend_tile(query_tile, key_heads, value_heads, allowed_tile, segment_tile, segment_all):
    head_count = key_heads.shape[0]
    tile_rows = query_tile.shape[0]
    query_heads = query_tile.reshape(tile_rows, head_count, -1).transpose(1, 0, 2)
    scores = jnp.einsum('hqd,hkd->hqk', query_heads, key_heads, precision=highest) * 0.125
    allowed_keys = token_mask(allowed_tile, segment_tile, segment_all)
    scores = low_back(jnp.where(allowed_keys, scores, masked_value))
    top_score = lax.optimization_barrier(jnp.max(scores, axis=-1, keepdims=True))
    raised = jnp.exp(scores - top_score)
    chances = raised / lax.optimization_barrier(jnp.sum(raised, axis=-1, keepdims=True))
    mixture = jnp.einsum('hqk,hkd->hqd', low(chances), value_heads, precision=highest)
    return mixture.transpose(1, 0, 2).reshape(tile_rows, -1)

def sequence_forward(params, sequence, segment_row, allowed):
    query_weight, key_weight, value_weight, output_weight, inner_weight, outer_weight, attn_gain, attn_shift, ffn_gain, ffn_shift = params
    length = sequence.shape[0]
    tile_rows = min(512, length)
    tile_count = length // tile_rows
    head_count = allowed.shape[0]
    queries = both_round(product(sequence, query_weight))
    keys_all = both_round(product(sequence, key_weight))
    values_all = both_round(product(sequence, value_weight))
    key_heads = keys_all.reshape(length, head_count, -1).transpose(1, 0, 2)
    value_heads = values_all.reshape(length, head_count, -1).transpose(1, 0, 2)
    query_tiles = queries.reshape(tile_count, tile_rows, -1)
    allowed_tiles = allowed.reshape(head_count, tile_count, tile_rows // BLOCK, -1).transpose(1, 0, 2, 3)
    segment_tiles = segment_row.reshape(tile_count, tile_rows)
    tile_step = jax.checkpoint(lambda pieces: attend_tile(pieces[0], key_heads, value_heads, pieces[1], pieces[2], segment_row))
    attended = lax.map(tile_step, (query_tiles, allowed_tiles, segment_tiles)).reshape(length, -1)
    attended = both_round(attended)
    branch = low_back(product(attended, output_weight.T))
    hidden = layer_norm(sequence + branch, attn_gain, attn_shift)
    upper_part = low_back(product(low(hidden), inner_weight))
    active = low(jax.nn.gelu(upper_part, approximate=False))
    feed = low_back(product(active, outer_weight.T))
    return layer_norm(hidden + feed, ffn_gain, ffn_shift)

def reference(tokens, query_weight, key_weight, value_weight, output_weight, inner_weight, outer_weight, attn_gain, attn_shift, ffn_gain, ffn_shift, teacher, segments, random_blocks, valid_tokens):
    params = tuple((item.astype(jnp.float32) for item in (query_weight, key_weight, value_weight, output_weight, inner_weight, outer_weight, attn_gain, attn_shift, ffn_gain, ffn_shift)))
    allowed = block_allowed(random_blocks)
    total_valid = jnp.sum(valid_tokens.astype(jnp.float32))
    seq_count = TOKENS // SEQ
    token_rows = tokens.astype(jnp.float32).reshape(seq_count, SEQ, D)
    teacher_rows = teacher.astype(jnp.float32).reshape(seq_count, SEQ, D)
    valid_rows = valid_tokens.astype(jnp.float32).reshape(seq_count, SEQ)
    pull_weight = TOKENS * 0.5 / total_valid

    def one_sequence(running, pieces):
        grad_sum, error_sum = running
        row_tokens, row_teacher, row_valid, row_segments = pieces

        def seq_forward(weights, inputs):
            outputs = sequence_forward(weights, inputs, row_segments, allowed)
            errors = (outputs - row_teacher) * row_valid[:, None]
            return (outputs, jnp.sum(errors * errors))
        (outputs, squared), pull = jax.vjp(seq_forward, params, row_tokens)
        weight_grads, token_grads = pull((jnp.zeros_like(outputs), pull_weight * jnp.ones_like(squared)))
        grad_sum = jax.tree.map(lambda total_part, new_part: total_part + new_part, grad_sum, weight_grads)
        return ((grad_sum, error_sum + squared), (outputs, token_grads))
    initial = (jax.tree.map(jnp.zeros_like, params), jnp.zeros((), jnp.float32))
    (grads, squared_total), (outputs, token_grads) = lax.scan(one_sequence, initial, (token_rows, teacher_rows, valid_rows, segments))
    loss_value = squared_total / (2.0 * D * total_valid)
    return (outputs.reshape(TOKENS, D).astype(jnp.bfloat16), loss_value, token_grads.reshape(TOKENS, D), grads[0], grads[1], grads[2], grads[3], grads[4], grads[5], grads[6], grads[7], grads[8], grads[9])
```

```python
import functools

import jax
import jax.numpy as jnp
from jax import lax
from jax.experimental import pallas as pl
from jax.experimental.pallas import tpu as pltpu
from jax.sharding import PartitionSpec as P

BLOCK = 64
HEAD = 64
PAIR = 2 * HEAD
SLOTS = 12
ROUTES = ((0, 1, 2), (1, 2, 0), (2, 0, 1))

epsilon = 1e-05
masked_value = -1e30
score_scale = 0.125


def swap_bit(block, bit):
    count = lax.axis_size("dp")
    return lax.ppermute(block, "dp", [(one, one ^ (1 << bit)) for one in range(count)])


def swap_core(block):
    return lax.ppermute(block, "tensor", [(0, 1), (1, 0)])


def dot_plain(left_side, right_side):
    return jnp.dot(left_side, right_side, preferred_element_type=jnp.float32)


def dot_cols(left_side, right_side):
    return lax.dot_general(
        left_side, right_side, (((1,), (1,)), ((), ())), preferred_element_type=jnp.float32
    )


def dot_rows(left_side, right_side):
    return lax.dot_general(
        left_side, right_side, (((0,), (0,)), ((), ())), preferred_element_type=jnp.float32
    )


def layer_norm(values, gain_row, shift_row):
    centred = values - jnp.mean(values, axis=-1, keepdims=True)
    spread = jnp.mean(centred * centred, axis=-1, keepdims=True)
    return centred * lax.rsqrt(spread + epsilon) * gain_row + shift_row


def exact_gelu(values):
    return jax.nn.gelu(values, approximate=False)


def grow(block, bits):
    held = block[None]
    for bit in bits:
        held = jnp.concatenate([held, swap_bit(held, bit)], 0)
    return held


def slot_masks(bits):
    return [
        sum(((slot >> at) & 1) << bit for at, bit in enumerate(bits))
        for slot in range(1 << len(bits))
    ]


def shrink(send, keep, bits):
    for at, bit in enumerate(bits):
        total = keep + swap_bit(send, bit).astype(jnp.float32)
        if at + 1 < len(bits):
            half = total.shape[0] // 2
            keep, send = total[:half], total[half:].astype(jnp.bfloat16)
        else:
            return total


def pick(table, index):
    spots = jnp.arange(table.shape[0], dtype=jnp.int32)
    chosen = (index[..., None] == spots).astype(jnp.float32)
    return lax.dot_general(
        chosen, table.astype(jnp.float32), (((chosen.ndim - 1,), (0,)), ((), ())),
        precision=lax.Precision.HIGHEST, preferred_element_type=jnp.float32,
    )


def attention_tables(random_blocks, segment_all, place, core, span, row_blocks):
    heads, blocks, draws = random_blocks.shape
    half = row_blocks // 2
    local = jnp.arange(row_blocks, dtype=jnp.int32)
    owner = jnp.where(local < half, core, 1 - core)
    absolute = place * row_blocks + owner * half + local % half
    edge = (absolute == 0) | (absolute == blocks - 1)
    chunks = -(-blocks // SLOTS)
    edge_local = jnp.argmax(edge).astype(jnp.int32)
    has_edge = jnp.any(edge)
    item_count = row_blocks + jnp.where(has_edge, chunks - 1, 0)
    extra = jnp.arange(1, chunks, dtype=jnp.int32)
    item_query = jnp.concatenate([local, jnp.full((chunks - 1,), 0, jnp.int32) + edge_local])
    here = absolute[:, None]
    common = jnp.concatenate(
        [here - 1, here, here + 1, jnp.zeros_like(here), jnp.full_like(here, blocks - 1)], 1
    )
    common_valid = jnp.concatenate(
        [here >= 1, here >= 0, here <= blocks - 2, here > 1, here < blocks - 2], 1
    )
    drawn = pick(
        random_blocks.transpose(1, 0, 2).reshape(blocks, heads * draws), absolute
    ).astype(jnp.int32).reshape(row_blocks, heads, draws)
    near = (jnp.abs(drawn - here[:, :, None]) <= 1) | (drawn == 0) | (drawn == blocks - 1)
    seen = jnp.stack(
        [
            functools.reduce(
                jnp.logical_or,
                [drawn[:, :, at] == drawn[:, :, before] for before in range(at)],
                jnp.zeros(drawn.shape[:2], bool),
            )
            for at in range(draws)
        ],
        -1,
    )
    drawn_valid = ~near & ~seen
    lists, valids = [], []
    pad = SLOTS - 5 - 2 * draws
    for pair in range(heads // 2):
        first, second = 2 * pair, 2 * pair + 1
        lists.append(
            jnp.concatenate(
                [common, drawn[:, first], drawn[:, second], jnp.zeros((row_blocks, pad), jnp.int32)], 1
            )
        )
        none = jnp.zeros((row_blocks, draws), bool)
        tail = jnp.zeros((row_blocks, pad), bool)
        valids.append(jnp.concatenate([common_valid, drawn_valid[:, first], none, tail], 1))
        valids.append(jnp.concatenate([common_valid, none, drawn_valid[:, second], tail], 1))
    lists = jnp.stack(lists, 1)
    valids = jnp.stack(valids, 1)
    sweep = jnp.arange(chunks, dtype=jnp.int32)[:, None] * SLOTS + jnp.arange(SLOTS, dtype=jnp.int32)
    first_list = jnp.where(edge[:, None, None], sweep[0], lists)
    first_valid = jnp.where(edge[:, None, None], sweep[0] < blocks, valids)
    rest_list = jnp.broadcast_to(sweep[1:, None, :], (chunks - 1, heads // 2, SLOTS))
    rest_valid = jnp.broadcast_to((sweep[1:] < blocks)[:, None, :], (chunks - 1, heads, SLOTS))
    item_blocks = jnp.clip(jnp.concatenate([first_list, rest_list], 0), 0, blocks - 1)
    item_valid = jnp.concatenate([first_valid, rest_valid], 0)
    per_half = span * half
    stored = (
        jnp.where((item_blocks % row_blocks) // half == core, 0, per_half)
        + ((item_blocks // row_blocks) ^ place) * half
        + item_blocks % half
    )
    segment_table = segment_all.reshape(blocks, BLOCK)
    picked = pick(segment_table, item_blocks)
    items = picked.shape[0]
    key_segments = jnp.where(
        item_valid.reshape(items, heads // 2, 2, SLOTS)[..., None], picked[:, :, None], -1.0
    ).reshape(items, heads, SLOTS * BLOCK)
    query_segments = pick(segment_table, absolute).reshape(row_blocks * BLOCK, 1)
    return (
        item_count.reshape(1).astype(jnp.int32),
        item_query.astype(jnp.int32),
        stored.reshape(-1).astype(jnp.int32),
        key_segments,
        query_segments,
    )


def two_heads(rows, low_lanes):
    rows = rows.astype(jnp.float32)
    zero = jnp.zeros_like(rows)
    return jnp.concatenate(
        [jnp.where(low_lanes, rows, zero), jnp.where(low_lanes, zero, rows)], 0
    )


def item_mask(key_segments_ref, query_segments_ref, item, rows, pair):
    query_side = query_segments_ref[rows, :]
    key_side = key_segments_ref[item]
    return jnp.concatenate(
        [query_side == key_side[2 * pair + part : 2 * pair + part + 1, :] for part in range(2)], 0
    )


def attend_kernel(
    count_ref, query_ref, blocks_ref, key_segments_ref, query_segments_ref, q_ref, kv_ref,
    mixed_ref, mass_ref, top_ref, total_ref, mixture_ref, *, pairs, row_blocks
):
    low_lanes = lax.broadcasted_iota(jnp.int32, (BLOCK, PAIR), 1) < HEAD

    def one_item(item, carry):
        query = query_ref[item]
        fresh = item < row_blocks
        rows = pl.ds(pl.multiple_of(query * BLOCK, BLOCK), BLOCK)
        for pair in range(pairs):
            both = two_heads(q_ref[rows, pair * PAIR : (pair + 1) * PAIR], low_lanes).astype(jnp.bfloat16)
            spots = [
                pl.ds(pl.multiple_of(blocks_ref[(item * pairs + pair) * SLOTS + slot] * BLOCK, BLOCK), BLOCK)
                for slot in range(SLOTS)
            ]
            start = pair * 2 * PAIR
            keys = jnp.concatenate([kv_ref[spot, start : start + PAIR] for spot in spots], 0)
            values = jnp.concatenate([kv_ref[spot, start + PAIR : start + 2 * PAIR] for spot in spots], 0)
            mask = item_mask(key_segments_ref, query_segments_ref, item, rows, pair)
            scores = jnp.where(mask, dot_cols(both, keys) * score_scale, masked_value)
            place = query * pairs + pair
            old_top = jnp.where(fresh, masked_value, top_ref[place])
            top = jnp.maximum(old_top, jnp.max(scores, axis=-1, keepdims=True))
            raised = jnp.exp(scores - top)
            shrunk = jnp.exp(old_top - top)
            total = jnp.where(fresh, 0.0, total_ref[place] * shrunk) + jnp.sum(raised, axis=-1, keepdims=True)
            mixture = jnp.where(fresh, 0.0, mixture_ref[place] * shrunk) + dot_plain(
                raised.astype(jnp.bfloat16), values
            )
            top_ref[place] = top
            total_ref[place] = total
            mixture_ref[place] = mixture
            normed = mixture / total
            mixed_ref[rows, pair * PAIR : (pair + 1) * PAIR] = jnp.where(
                low_lanes, normed[:BLOCK], normed[BLOCK:]
            )
            mass_ref[place] = jnp.broadcast_to(top + jnp.log(total), (2 * BLOCK, PAIR))
        return carry

    lax.fori_loop(0, count_ref[0], one_item, 0)


def attend_back_kernel(
    count_ref, query_ref, blocks_ref, key_segments_ref, query_segments_ref, q_ref, kv_ref,
    mixed_ref, mass_ref, grad_ref, query_grad_ref, kv_grad_ref, sum_ref, *, pairs, row_blocks
):
    low_lanes = lax.broadcasted_iota(jnp.int32, (BLOCK, PAIR), 1) < HEAD
    sum_ref[...] = jnp.zeros_like(sum_ref)

    def one_item(item, carry):
        query = query_ref[item]
        fresh = item < row_blocks
        rows = pl.ds(pl.multiple_of(query * BLOCK, BLOCK), BLOCK)
        for pair in range(pairs):
            lanes = slice(pair * PAIR, (pair + 1) * PAIR)
            both = two_heads(q_ref[rows, lanes], low_lanes).astype(jnp.bfloat16)
            grads = two_heads(grad_ref[rows, lanes], low_lanes)
            mixed = mixed_ref[rows, lanes]
            inner = jnp.sum(grads * jnp.concatenate([mixed, mixed], 0), axis=-1, keepdims=True)
            grads = grads.astype(jnp.bfloat16)
            spots = [
                pl.ds(pl.multiple_of(blocks_ref[(item * pairs + pair) * SLOTS + slot] * BLOCK, BLOCK), BLOCK)
                for slot in range(SLOTS)
            ]
            start = pair * 2 * PAIR
            kv = jnp.concatenate([kv_ref[spot, start : start + 2 * PAIR] for spot in spots], 0)
            blank = jnp.zeros_like(both)
            sides = jnp.concatenate(
                [jnp.concatenate([both, blank], 1), jnp.concatenate([blank, grads], 1)], 0
            )
            products = dot_cols(sides, kv)
            mask = item_mask(key_segments_ref, query_segments_ref, item, rows, pair)
            place = query * pairs + pair
            scores = jnp.where(mask, products[: 2 * BLOCK] * score_scale, masked_value)
            chances = jnp.exp(scores - mass_ref[place][:, :1])
            score_grads = (chances * (products[2 * BLOCK :] - inner)).astype(jnp.bfloat16)
            query_grad = dot_plain(score_grads, kv[:, :PAIR])
            query_grad = jnp.where(low_lanes, query_grad[:BLOCK], query_grad[BLOCK:])
            query_grad_ref[rows, lanes] = jnp.where(fresh, 0.0, query_grad_ref[rows, lanes]) + query_grad
            kv_grad = dot_rows(jnp.concatenate([score_grads, chances.astype(jnp.bfloat16)], 0), sides)
            for slot, spot in enumerate(spots):
                sum_ref[spot, start : start + 2 * PAIR] += kv_grad[slot * BLOCK : (slot + 1) * BLOCK]
        return carry

    lax.fori_loop(0, count_ref[0], one_item, 0)
    for pair in range(pairs):
        start = pair * 2 * PAIR
        kv_grad_ref[:, start : start + PAIR] = (sum_ref[:, start : start + PAIR] * score_scale).astype(jnp.bfloat16)
        kv_grad_ref[:, start + PAIR : start + 2 * PAIR] = sum_ref[:, start + PAIR : start + 2 * PAIR].astype(
            jnp.bfloat16
        )


def table_specs():
    return [pl.BlockSpec(memory_space=pltpu.SMEM)] * 3 + [pl.BlockSpec(memory_space=pltpu.VMEM)] * 2


def in_vmem(count):
    return [pl.BlockSpec(memory_space=pltpu.VMEM)] * count


def attend(tables, queries, kv):
    rows, width = queries.shape
    pairs, row_blocks = width // PAIR, rows // BLOCK
    places = pairs * row_blocks
    return pl.pallas_call(
        functools.partial(attend_kernel, pairs=pairs, row_blocks=row_blocks),
        out_shape=(
            jax.ShapeDtypeStruct((rows, width), jnp.float32),
            jax.ShapeDtypeStruct((places, 2 * BLOCK, PAIR), jnp.float32),
        ),
        in_specs=table_specs() + in_vmem(2),
        out_specs=tuple(in_vmem(2)),
        scratch_shapes=[
            pltpu.VMEM((places, 2 * BLOCK, 1), jnp.float32),
            pltpu.VMEM((places, 2 * BLOCK, 1), jnp.float32),
            pltpu.VMEM((places, 2 * BLOCK, PAIR), jnp.float32),
        ],
        compiler_params=pltpu.CompilerParams(vmem_limit_bytes=48 << 20),
        cost_estimate=pl.CostEstimate(flops=3 << 30, bytes_accessed=12 << 20, transcendentals=4 << 20),
    )(*tables, queries, kv)


def attend_back(tables, queries, kv, mixed, mass, grads):
    rows, width = queries.shape
    pairs, row_blocks = width // PAIR, rows // BLOCK
    return pl.pallas_call(
        functools.partial(attend_back_kernel, pairs=pairs, row_blocks=row_blocks),
        out_shape=(
            jax.ShapeDtypeStruct((rows, width), jnp.float32),
            jax.ShapeDtypeStruct(kv.shape, jnp.bfloat16),
        ),
        in_specs=table_specs() + in_vmem(5),
        out_specs=tuple(in_vmem(2)),
        scratch_shapes=[pltpu.VMEM(kv.shape, jnp.float32)],
        compiler_params=pltpu.CompilerParams(vmem_limit_bytes=48 << 20),
        cost_estimate=pl.CostEstimate(flops=6 << 30, bytes_accessed=20 << 20, transcendentals=4 << 20),
    )(*tables, queries, kv, mixed, mass, grads)


def natural_kernel(index_ref, held_ref, out_ref, *, rows):
    for block in range(held_ref.shape[0]):
        out_ref[block * rows : (block + 1) * rows, :] = held_ref[index_ref[block]]


def natural_rows(held, index):
    blocks, rows, columns = held.shape
    if rows % 16:
        return jnp.take(held, index, axis=0).reshape(blocks * rows, columns)
    return pl.pallas_call(
        functools.partial(natural_kernel, rows=rows),
        out_shape=jax.ShapeDtypeStruct((blocks * rows, columns), held.dtype),
        in_specs=[pl.BlockSpec(memory_space=pltpu.SMEM)] + in_vmem(1),
        out_specs=in_vmem(1)[0],
        compiler_params=pltpu.CompilerParams(vmem_limit_bytes=32 << 20),
    )(index, held)


def split_kernel(index_ref, grad_ref, keep_ref, send_ref, *, blocks, rows):
    half = blocks // 2
    for slot in range(blocks):
        start = pl.multiple_of(index_ref[slot] * rows, rows)
        piece = grad_ref[pl.ds(start, rows), :]
        if slot < half:
            keep_ref[slot] = piece
        else:
            send_ref[slot - half] = piece.astype(jnp.bfloat16)


def split_rows(grad, index):
    blocks = index.shape[0]
    rows, columns = grad.shape[0] // blocks, grad.shape[1]
    half = blocks // 2
    if rows % 16:
        placed = jnp.take(grad.reshape(blocks, rows, columns), index, axis=0)
        return placed[:half], placed[half:].astype(jnp.bfloat16)
    return pl.pallas_call(
        functools.partial(split_kernel, blocks=blocks, rows=rows),
        out_shape=(
            jax.ShapeDtypeStruct((half, rows, columns), jnp.float32),
            jax.ShapeDtypeStruct((half, rows, columns), jnp.bfloat16),
        ),
        in_specs=[pl.BlockSpec(memory_space=pltpu.SMEM)] + in_vmem(1),
        out_specs=tuple(in_vmem(2)),
        compiler_params=pltpu.CompilerParams(vmem_limit_bytes=48 << 20),
    )(index, grad)


def shards(
    tokens,
    query_weight,
    key_weight,
    value_weight,
    output_weight,
    inner_weight,
    outer_weight,
    attn_gain,
    attn_shift,
    ffn_gain,
    ffn_shift,
    teacher,
    segments,
    random_blocks,
    valid_tokens,
):
    devices = lax.axis_size("dp")
    dp_index = lax.axis_index("dp")
    core = lax.axis_index("tensor")
    rows, width = tokens.shape
    length = 2 * rows
    span = segments.shape[1] // length
    near_bits = span.bit_length() - 1
    far_bits = tuple(range(near_bits, devices.bit_length() - 1))
    routes = ROUTES if near_bits == 3 else (tuple(range(near_bits)),) * 3
    place = dp_index % span
    far_count = devices // span
    far_place = dp_index // span

    def gather_index(bits):
        masks = slot_masks(bits)
        slot_of = jnp.array([masks.index(mask) for mask in range(span)], jnp.int32)
        owners = jnp.arange(devices, dtype=jnp.int32)
        return slot_of[(owners % span) ^ place] * far_count + ((owners // span) ^ far_place)

    def scatter_index(bits):
        masks = jnp.array(slot_masks(bits[::-1]), jnp.int32)
        far = jnp.arange(far_count, dtype=jnp.int32)
        return ((far[None, :] ^ far_place) * span + (masks[:, None] ^ place)).reshape(-1)

    def gather_far(block):
        return grow(block, far_bits)

    def gather_near(held, bits):
        grown = grow(held, bits)
        return grown.reshape((devices,) + grown.shape[2:])

    pair_columns = []
    for pair in range(key_weight.shape[1] // PAIR):
        pair_columns += [
            key_weight[:, pair * PAIR : (pair + 1) * PAIR],
            value_weight[:, pair * PAIR : (pair + 1) * PAIR],
        ]
    first_weights = jnp.concatenate([query_weight] + pair_columns, 1)
    first_third = first_weights.shape[1] // 3
    token_third = width // 3
    local_count = jnp.sum(valid_tokens).astype(jnp.bfloat16)
    second_weights = jnp.concatenate(
        [output_weight, inner_weight, outer_weight,
         jnp.full((output_weight.shape[0], 3 * PAIR), local_count, jnp.bfloat16)], 1
    )
    second_third = second_weights.shape[1] // 3
    first_far = gather_far(first_weights)
    second_far = gather_far(second_weights)
    first_full, token_thirds = [], []
    for third, bits in enumerate(routes):
        token_held = grow(tokens[:, third * token_third : (third + 1) * token_third], bits)
        masks = slot_masks(bits)
        token_thirds.append(jnp.stack([token_held[masks.index(mask)] for mask in range(span)], 0))
        held = gather_near(first_far[..., third * first_third : (third + 1) * first_third], bits)
        first_full.append(natural_rows(held, gather_index(bits)))
    own_tokens = jnp.concatenate(token_thirds, -1).reshape(span * rows, width)
    other_tokens = swap_core(own_tokens)
    sequence = jnp.concatenate([own_tokens, other_tokens], 0)
    full_first = jnp.concatenate(first_full, 1)
    full_query, full_kv = full_first[:, : query_weight.shape[1]], full_first[:, query_weight.shape[1] :]

    second_far, sequence = lax.optimization_barrier((second_far, sequence))
    second_full = []
    for third, bits in enumerate(routes):
        held = gather_near(second_far[..., third * second_third : (third + 1) * second_third], bits)
        second_full.append(natural_rows(held, gather_index(bits)))
    full_second = jnp.concatenate(second_full, 1)
    ends = [output_weight.shape[1], output_weight.shape[1] + inner_weight.shape[1]]
    ends.append(ends[1] + outer_weight.shape[1])
    full_output = full_second[:, : ends[0]]
    full_inner = full_second[:, ends[0] : ends[1]]
    full_outer = full_second[:, ends[1] : ends[2]]
    counts = full_second[:: output_weight.shape[0], ends[2] : ends[2] + 1].astype(jnp.float32)
    half_count = jnp.sum(counts).reshape(1, 1)
    valid_total = (half_count + swap_core(half_count))[0, 0]

    segment_all = lax.dynamic_index_in_dim(segments, far_place, 0, keepdims=False)
    tables = attention_tables(random_blocks, segment_all, place, core, span, length // BLOCK)

    whole_tokens = jnp.concatenate([own_tokens[:rows], other_tokens[:rows]], 0)
    queries = dot_plain(whole_tokens, full_query).astype(jnp.bfloat16)
    kv = dot_plain(sequence, full_kv).astype(jnp.bfloat16)
    mixed, mass = attend(tables, queries, kv)
    attended = mixed.astype(jnp.bfloat16)

    def sum_halves(partial):
        return partial[:rows] + swap_core(partial[rows:].astype(jnp.bfloat16)).astype(jnp.float32)

    def both_halves(block):
        return jnp.concatenate([block, swap_core(block)], 0)

    first_sum = tokens.astype(jnp.float32) + sum_halves(dot_cols(attended, full_output))
    hidden, attn_norm_pull = jax.vjp(layer_norm, first_sum, attn_gain, attn_shift)
    whole_hidden = both_halves(hidden.astype(jnp.bfloat16))
    upper_part = dot_plain(whole_hidden, full_inner)
    active, gelu_pull = jax.vjp(exact_gelu, upper_part)
    active_low = active.astype(jnp.bfloat16)
    second_sum = hidden + sum_halves(dot_cols(active_low, full_outer))
    result, ffn_norm_pull = jax.vjp(layer_norm, second_sum, ffn_gain, ffn_shift)
    valid_float = valid_tokens.astype(jnp.float32)[:, None]
    errors = (result - teacher.astype(jnp.float32)) * valid_float
    error_part = jnp.sum(errors * errors)
    token_total = devices * lax.axis_size("tensor") * rows
    grad_second, grad_ffn_gain, grad_ffn_shift = ffn_norm_pull(errors * (token_total / valid_total))
    whole_grad_ffn = both_halves(grad_second.astype(jnp.bfloat16))
    grad_outer = dot_rows(whole_grad_ffn, active_low)
    grad_active = dot_plain(whole_grad_ffn, full_outer)
    grad_upper = gelu_pull(grad_active)[0].astype(jnp.bfloat16)
    grad_inner = dot_rows(whole_hidden, grad_upper)
    grad_hidden = grad_second + sum_halves(dot_cols(grad_upper, full_inner))
    grad_first, grad_attn_gain, grad_attn_shift = attn_norm_pull(grad_hidden)

    def scatter_rows(grad):
        third_width = grad.shape[1] // 3
        summed = []
        for third, bits in enumerate(routes):
            keep, send = split_rows(grad[:, third * third_width : (third + 1) * third_width], scatter_index(bits))
            summed.append(shrink(send, keep, bits + far_bits))
        return jnp.concatenate(summed, -1)[0]

    wide_sum = scatter_rows(jnp.concatenate([grad_outer, grad_inner], 1))
    part_outer, part_inner = wide_sum[:, : grad_outer.shape[1]], wide_sum[:, grad_outer.shape[1] :]

    small = jnp.stack(
        [grad_attn_gain, grad_attn_shift, grad_ffn_gain, grad_ffn_shift, jnp.broadcast_to(error_part, (width,))]
        + [jnp.zeros((width,), jnp.float32)] * 3
    )
    each = width // devices
    small = small.reshape(8, devices, each).transpose(1, 0, 2)
    small = jnp.take(small, scatter_index(tuple(range(near_bits))), axis=0)
    for bit in tuple(range(near_bits)) + far_bits:
        half = small.shape[0] // 2
        small = small[:half] + swap_bit(small[half:], bit)
    small = small[0]
    small = small + swap_core(small)

    whole_grad_attn = both_halves(grad_first.astype(jnp.bfloat16))
    grad_output = dot_rows(whole_grad_attn, attended)
    grad_attended = dot_plain(whole_grad_attn, full_output).astype(jnp.bfloat16)
    query_grad, kv_low = attend_back(tables, queries, kv, mixed, mass, grad_attended)
    query_low = (query_grad * score_scale).astype(jnp.bfloat16)
    grad_query = dot_rows(whole_tokens, query_low)
    grad_kv = dot_rows(sequence, kv_low)
    token_part = dot_cols(kv_low, full_kv)
    query_part = dot_cols(query_low, full_query)
    token_part = token_part.reshape(2, span, rows, width)
    token_part = token_part.at[:, 0].add(query_part.reshape(2, rows, width))
    token_sum = token_part[0].reshape(span * rows, width) + swap_core(
        token_part[1].reshape(span * rows, width).astype(jnp.bfloat16)
    ).astype(jnp.float32)
    token_sum = token_sum.reshape(span, rows, width)
    token_thirds = []
    for third, bits in enumerate(routes):
        masks = slot_masks(bits[::-1])
        piece = token_sum[..., third * token_third : (third + 1) * token_third]
        piece = jnp.stack([piece[mask] for mask in masks], 0)
        half = span // 2
        token_thirds.append(shrink(piece[half:].astype(jnp.bfloat16), piece[:half], bits))
    grad_tokens = grad_first + jnp.concatenate(token_thirds, -1)[0]

    narrow_sum = scatter_rows(jnp.concatenate([grad_query, grad_kv, grad_output], 1))
    head_width = query_weight.shape[1]
    part_query = narrow_sum[:, :head_width]
    kv_sum = narrow_sum[:, head_width : 3 * head_width]
    part_output = narrow_sum[:, 3 * head_width :]
    pairs = head_width // PAIR
    part_key = jnp.concatenate([kv_sum[:, 2 * pair * PAIR : (2 * pair + 1) * PAIR] for pair in range(pairs)], 1)
    part_value = jnp.concatenate(
        [kv_sum[:, (2 * pair + 1) * PAIR : (2 * pair + 2) * PAIR] for pair in range(pairs)], 1
    )
    loss_value = small[4, 0] / (2.0 * width * valid_total)
    mine = lax.dynamic_slice_in_dim(small, core * (each // 2), each // 2, 1)
    return (
        result.astype(jnp.bfloat16),
        loss_value,
        grad_tokens,
        part_query,
        part_key,
        part_value,
        part_output,
        part_inner,
        part_outer,
        mine[0],
        mine[1],
        mine[2],
        mine[3],
    )


def solution(mesh):
    both = P(("dp", "tensor"))
    rows_spec = P(("dp", "tensor"), None)
    weight_spec = P("dp", "tensor")
    in_specs = (rows_spec,) + (weight_spec,) * 6 + (P(),) * 4
    in_specs += (rows_spec, P(), P("tensor", None, None), both)
    out_specs = (rows_spec, P(), rows_spec) + (weight_spec,) * 6 + (both,) * 4
    return jax.shard_map(shards, mesh=mesh, in_specs=in_specs, out_specs=out_specs, check_vma=False)
```

```python
import functools

import jax
import jax.numpy as jnp
from jax import lax
from jax.experimental import pallas as pl
from jax.experimental.pallas import tpu as pltpu
from jax.sharding import PartitionSpec as P

BLOCK = 64
HEAD = 64
PAIR = 2 * HEAD
SLOTS = 6
ROUTES = ((0, 1, 2), (1, 2, 0), (2, 0, 1))

epsilon = 1e-05
masked_value = -1e30
score_scale = 0.125


def swap_mask(block, mask):
    count = lax.axis_size("dp")
    return lax.ppermute(block, "dp", [(one, one ^ mask) for one in range(count)])


def swap_core(block):
    return lax.ppermute(block, "tensor", [(0, 1), (1, 0)])


def dot_plain(left_side, right_side):
    return jnp.dot(left_side, right_side, preferred_element_type=jnp.float32)


def dot_cols(left_side, right_side):
    return lax.dot_general(
        left_side, right_side, (((1,), (1,)), ((), ())), preferred_element_type=jnp.float32
    )


def dot_rows(left_side, right_side):
    return lax.dot_general(
        left_side, right_side, (((0,), (0,)), ((), ())), preferred_element_type=jnp.float32
    )


def params(megabytes):
    return pltpu.CompilerParams(vmem_limit_bytes=int(megabytes) << 20)


def cost(flops=0, moved=0, transcendentals=0):
    return pl.CostEstimate(flops=int(flops), bytes_accessed=int(moved), transcendentals=int(transcendentals))


def in_vmem(count):
    return [pl.BlockSpec(memory_space=pltpu.VMEM)] * count


def in_smem(count):
    return [pl.BlockSpec(memory_space=pltpu.SMEM)] * count


def shaped(shape, dtype=jnp.float32):
    return jax.ShapeDtypeStruct(tuple(shape), dtype)


def local_call(kernel, outs, vmem_inputs, smem_inputs=(), scratch=(), flops=0, transcendentals=0, spare=3):
    moved = sum(one.size * one.dtype.itemsize for one in list(vmem_inputs) + list(outs))
    held = moved + sum(one.size * one.dtype.itemsize for one in (shaped(s.shape, s.dtype) for s in scratch))
    held = held // (1 << 20) + 1 + spare
    return pl.pallas_call(
        kernel,
        out_shape=tuple(outs),
        in_specs=in_smem(len(smem_inputs)) + in_vmem(len(vmem_inputs)),
        out_specs=tuple(in_vmem(len(outs))),
        scratch_shapes=list(scratch),
        compiler_params=params(held),
        cost_estimate=cost(flops, moved, transcendentals),
    )(*smem_inputs, *vmem_inputs)


def slot_masks(bits):
    return [
        sum(((slot >> at) & 1) << bit for at, bit in enumerate(bits))
        for slot in range(1 << len(bits))
    ]


def pack_kernel(*refs, sizes):
    count = sum(len(group) for group in sizes)
    at = 0
    for group, out_ref in zip(sizes, refs[count:]):
        start = 0
        for size in group:
            out_ref[start : start + size] = refs[at][...]
            start += size
            at += 1


def pack(groups):
    sizes = tuple(tuple(one.shape[0] for one in group) for group in groups)
    outs = [shaped((sum(size),) + group[0].shape[1:], group[0].dtype) for size, group in zip(sizes, groups)]
    return list(
        local_call(functools.partial(pack_kernel, sizes=sizes), outs, [one for group in groups for one in group])
    )


def fold_kernel(*refs, thirds, arrivals, last):
    for third in range(thirds):
        keep_ref = refs[third * (1 + arrivals)]
        came = refs[third * (1 + arrivals) + 1 : (third + 1) * (1 + arrivals)]
        outs = refs[thirds * (1 + arrivals) :]
        half = keep_ref.shape[0] // (1 if last else 2)

        def total(part):
            return sum([one[part].astype(jnp.float32) for one in came], keep_ref[part])

        if last:
            outs[third][...] = total(slice(0, half))
        else:
            outs[2 * third][...] = total(slice(0, half))
            outs[2 * third + 1][...] = total(slice(half, 2 * half)).astype(jnp.bfloat16)


def fold(keeps, arrivals, last=False):
    outs = []
    for keep in keeps:
        if last:
            outs.append(shaped(keep.shape))
        else:
            half = (keep.shape[0] // 2,) + keep.shape[1:]
            outs += [shaped(half), shaped(half, jnp.bfloat16)]
    operands = []
    for keep, came in zip(keeps, arrivals):
        operands += [keep] + list(came)
    kernel = functools.partial(fold_kernel, thirds=len(keeps), arrivals=len(arrivals[0]), last=last)
    outs = local_call(kernel, outs, operands)
    if last:
        return list(outs)
    return list(outs[::2]), list(outs[1::2])


def pick(chosen, table):
    return lax.dot_general(
        chosen.astype(jnp.bfloat16), table.astype(jnp.bfloat16), (((chosen.ndim - 1,), (0,)), ((), ())),
        preferred_element_type=jnp.float32,
    )


def attention_tables(random_blocks, segment_all, place, core, span, row_blocks):
    heads, blocks, draws = random_blocks.shape
    half, pairs = row_blocks // 2, heads // 2
    local = jnp.arange(row_blocks, dtype=jnp.int32)
    owner = jnp.where(local < half, core, 1 - core)
    absolute = place * row_blocks + owner * half + local % half
    every = jnp.arange(blocks, dtype=jnp.int32)
    mine = absolute[:, None] == every
    edge = (every == 0) | (every == blocks - 1)
    fixed = (jnp.abs(absolute[:, None] - every) <= 1) | edge | edge[absolute][:, None]
    segment_table = segment_all.reshape(blocks, BLOCK).astype(jnp.float32)
    low, high = jnp.min(segment_table, 1), jnp.max(segment_table, 1)
    reach = (jnp.max(jnp.where(mine, low, -1.0), 1)[:, None] <= high) & (
        low <= jnp.max(jnp.where(mine, high, -1.0), 1)[:, None]
    )
    drawn = pick(mine, random_blocks.transpose(1, 0, 2).reshape(blocks, heads * draws))
    drawn = drawn.reshape(row_blocks, heads, draws, 1) == every.astype(jnp.float32)
    allowed = (jnp.any(drawn, 2) | fixed[:, None]) & reach[:, None]
    allowed = allowed.reshape(row_blocks, pairs, 2, blocks)
    listed = jnp.any(allowed, 2)
    rank = pick(listed, every[:, None] < every[None, :])
    count = jnp.max(jnp.sum(listed.astype(jnp.int32), -1), -1)
    chunks = -(-count // SLOTS)
    ends = jnp.sum(jnp.where(local[:, None] >= local[None, :], chunks[None, :], 0), 1)
    most = (row_blocks - 1) * -(-min(blocks, 5 + 2 * draws) // SLOTS) + -(-blocks // SLOTS)
    if span == 1:
        most += -(-blocks // SLOTS)
    items = jnp.arange(most, dtype=jnp.int32)
    item_query = jnp.minimum(jnp.sum((items[:, None] >= ends[None, :]).astype(jnp.int32), 1), row_blocks - 1)
    item_is = item_query[:, None] == local
    first = jnp.sum(jnp.where(item_is, (ends - chunks)[None, :], 0), 1)
    spots = ((items - first) * SLOTS)[:, None] + jnp.arange(SLOTS, dtype=jnp.int32)
    stored = (
        jnp.where((every % row_blocks) // half == core, 0, span * half)
        + ((every // row_blocks) ^ place) * half + every % half
    )
    rows = jnp.concatenate([jnp.where(listed, rank, -1.0)[:, :, None], allowed.astype(jnp.float32)], 2)
    rows = pick(item_is, rows.reshape(row_blocks, -1)).reshape(most, pairs, 3, blocks)
    here = rows[:, :, 0, None, :] == spots[:, None, :, None].astype(jnp.float32)
    code = rows[:, :, 1, None, :] * 256.0 + rows[:, :, 2, None, :] * 512.0 + stored.astype(jnp.float32)
    codes = jnp.sum(jnp.where(here, code, 0.0), -1).astype(jnp.int32)
    order = jnp.arange(2 * span * half, dtype=jnp.int32)
    order_block = (
        ((order % (span * half)) // half) ^ place
    ) * row_blocks + jnp.where(order < span * half, core, 1 - core) * half + order % half
    key_side = pick(order_block[:, None] == every, segment_table).reshape(-1, 1)
    query_side = pick(mine, segment_table)
    query_side = jnp.concatenate([query_side, query_side], 1)
    return (
        ends[-1:].astype(jnp.int32),
        item_query.astype(jnp.int32),
        (items == first).astype(jnp.int32),
        codes.reshape(-1),
        query_side,
        jnp.broadcast_to(key_side, (key_side.shape[0], PAIR)),
    )


def two_heads(rows, low_lanes):
    rows = rows.astype(jnp.float32)
    zero = jnp.zeros_like(rows)
    return jnp.concatenate(
        [jnp.where(low_lanes, rows, zero), jnp.where(low_lanes, zero, rows)], 0
    )


def item_blocks(codes_ref, first, side, key_side_ref):
    low_row = lax.broadcasted_iota(jnp.int32, (1, PAIR), 1) < HEAD
    spots, masks = [], []
    for slot in range(SLOTS):
        code = codes_ref[first + slot]
        spot = pl.ds(pl.multiple_of((code & 255) * BLOCK, BLOCK), BLOCK)
        flags = jnp.where(low_row, code & 256, code & 512)
        spots.append(spot)
        masks.append(key_side_ref[spot, :] == jnp.where(flags != 0, side, -1.0))
    return spots, jnp.concatenate(masks, 0)


def attend_kernel(
    count_ref, query_ref, fresh_ref, codes_ref, query_side_ref, key_side_ref,
    own_query_ref, own_kv_ref, other_ref, query_weight_ref, kv_weight_ref,
    mixed_ref, mass_ref, q_ref, kv_ref, state_ref, mixture_ref, *, pairs
):
    half_rows, half_kv = own_query_ref.shape[0], own_kv_ref.shape[0]
    q_ref[:half_rows, :] = own_query_ref[...]
    q_ref[half_rows:, :] = dot_plain(other_ref[:half_rows, :], query_weight_ref[...]).astype(jnp.bfloat16)
    kv_ref[:half_kv, :] = own_kv_ref[...]
    step = 512
    for start in range(0, half_kv, step):
        kv_ref[half_kv + start : half_kv + start + step, :] = dot_plain(
            other_ref[start : start + step, :], kv_weight_ref[...]
        ).astype(jnp.bfloat16)
    low_lanes = lax.broadcasted_iota(jnp.int32, (BLOCK, PAIR), 1) < HEAD

    def one_item(item, carry):
        query = query_ref[item]
        fresh = fresh_ref[item] == 1
        side = query_side_ref[pl.ds(query, 1), :]
        rows = pl.ds(pl.multiple_of(query * BLOCK, BLOCK), BLOCK)
        held = []
        for pair in range(pairs):
            both = two_heads(q_ref[rows, pair * PAIR : (pair + 1) * PAIR], low_lanes).astype(jnp.bfloat16)
            spots, mask = item_blocks(codes_ref, (item * pairs + pair) * SLOTS, side, key_side_ref)
            start = pair * 2 * PAIR
            keys = jnp.concatenate([kv_ref[spot, start : start + PAIR] for spot in spots], 0)
            values = jnp.concatenate([kv_ref[spot, start + PAIR : start + 2 * PAIR] for spot in spots], 0)
            held.append((jnp.where(mask, dot_cols(keys, both) * score_scale, masked_value), values))
        done = []
        for pair in range(pairs):
            scores, values = held[pair]
            place = query * pairs + pair
            state = state_ref[place]
            old_top = jnp.where(fresh, masked_value, state[0:1, :])
            top = jnp.maximum(old_top, jnp.max(scores, axis=0, keepdims=True))
            raised = jnp.exp(scores - top)
            shrunk = jnp.exp(old_top - top)
            total = jnp.where(fresh, 0.0, state[1:2, :] * shrunk) + jnp.sum(raised, axis=0, keepdims=True)
            mixture = jnp.where(fresh, 0.0, mixture_ref[place] * shrunk) + dot_rows(
                values, raised.astype(jnp.bfloat16)
            )
            done.append((top, total, mixture))
        for pair in range(pairs):
            top, total, mixture = done[pair]
            place = query * pairs + pair
            state_ref[place, 0:1, :] = top
            state_ref[place, 1:2, :] = total
            mixture_ref[place] = mixture
            normed = (mixture / total).T
            mixed_ref[rows, pair * PAIR : (pair + 1) * PAIR] = jnp.where(
                low_lanes, normed[:BLOCK], normed[BLOCK:]
            )
            mass_ref[place] = jnp.broadcast_to(top + jnp.log(total), (8, PAIR))
        return carry

    lax.fori_loop(0, count_ref[0], one_item, 0)


def attend(tables, own_query, own_kv, other, query_weight, kv_weight):
    rows, width = 2 * own_query.shape[0], own_query.shape[1]
    pairs, row_blocks = width // PAIR, rows // BLOCK
    places = pairs * row_blocks
    return local_call(
        functools.partial(attend_kernel, pairs=pairs),
        [
            shaped((rows, width)),
            shaped((places, 8, PAIR)),
            shaped((rows, width), jnp.bfloat16),
            shaped((2 * own_kv.shape[0], own_kv.shape[1]), jnp.bfloat16),
        ],
        list(tables[4:]) + [own_query, own_kv, other, query_weight, kv_weight],
        tables[:4],
        [
            pltpu.VMEM((places, 8, PAIR), jnp.float32),
            pltpu.VMEM((places, PAIR, PAIR), jnp.float32),
        ],
        flops=8e9, transcendentals=4e6, spare=10,
    )


def attend_back_kernel(
    count_ref, query_ref, fresh_ref, codes_ref, query_side_ref, key_side_ref, q_ref, kv_ref,
    mixed_ref, mass_ref, own_grad_ref, other_grad_ref, weight_ref,
    query_grad_ref, kv_grad_ref, sum_ref, grad_ref, query_sum_ref, *, pairs
):
    half_rows = own_grad_ref.shape[0]
    grad_ref[:half_rows, :] = dot_plain(own_grad_ref[...], weight_ref[...]).astype(jnp.bfloat16)
    grad_ref[half_rows:, :] = dot_plain(other_grad_ref[...], weight_ref[...]).astype(jnp.bfloat16)
    low_lanes = lax.broadcasted_iota(jnp.int32, (BLOCK, PAIR), 1) < HEAD
    sum_ref[...] = jnp.zeros_like(sum_ref)

    def one_item(item, carry):
        query = query_ref[item]
        fresh = fresh_ref[item] == 1
        side = query_side_ref[pl.ds(query, 1), :]
        rows = pl.ds(pl.multiple_of(query * BLOCK, BLOCK), BLOCK)
        held = []
        for pair in range(pairs):
            lanes = slice(pair * PAIR, (pair + 1) * PAIR)
            both = two_heads(q_ref[rows, lanes], low_lanes).astype(jnp.bfloat16)
            grads = grad_ref[rows, lanes].astype(jnp.float32)
            turned = (grads * mixed_ref[rows, lanes]).T
            inner = jnp.concatenate(
                [jnp.sum(turned[:HEAD], axis=0, keepdims=True), jnp.sum(turned[HEAD:], axis=0, keepdims=True)], 1
            )
            grads = two_heads(grads, low_lanes).astype(jnp.bfloat16)
            spots, mask = item_blocks(codes_ref, (item * pairs + pair) * SLOTS, side, key_side_ref)
            start = pair * 2 * PAIR
            kv = jnp.concatenate([kv_ref[spot, start : start + 2 * PAIR] for spot in spots], 0)
            blank = jnp.zeros_like(both)
            sides = jnp.concatenate(
                [jnp.concatenate([both, blank], 1), jnp.concatenate([blank, grads], 1)], 0
            )
            held.append((dot_cols(kv, sides), inner, sides, kv, spots, mask))
        done = []
        for pair in range(pairs):
            products, inner, sides, kv, spots, mask = held[pair]
            place = query * pairs + pair
            scores = jnp.where(mask, products[:, :PAIR] * score_scale, masked_value)
            chances = jnp.exp(scores - mass_ref[place, 0:1, :])
            score_grads = (chances * (products[:, PAIR:] - inner)).astype(jnp.bfloat16)
            query_grad = dot_rows(score_grads, kv[:, :PAIR])
            kv_grad = dot_plain(jnp.concatenate([score_grads, chances.astype(jnp.bfloat16)], 1), sides)
            done.append((query_grad, kv_grad))
        for pair in range(pairs):
            lanes = slice(pair * PAIR, (pair + 1) * PAIR)
            start = pair * 2 * PAIR
            query_grad, kv_grad = done[pair]
            spots = held[pair][4]
            query_grad = jnp.where(low_lanes, query_grad[:BLOCK], query_grad[BLOCK:])
            query_sum_ref[rows, lanes] = jnp.where(fresh, 0.0, query_sum_ref[rows, lanes]) + query_grad
            for slot, spot in enumerate(spots):
                sum_ref[spot, start : start + 2 * PAIR] += kv_grad[slot * BLOCK : (slot + 1) * BLOCK]
        return carry

    lax.fori_loop(0, count_ref[0], one_item, 0)
    query_grad_ref[...] = (query_sum_ref[...] * score_scale).astype(jnp.bfloat16)
    for pair in range(pairs):
        start = pair * 2 * PAIR
        kv_grad_ref[:, start : start + PAIR] = (sum_ref[:, start : start + PAIR] * score_scale).astype(jnp.bfloat16)
        kv_grad_ref[:, start + PAIR : start + 2 * PAIR] = sum_ref[:, start + PAIR : start + 2 * PAIR].astype(
            jnp.bfloat16
        )


def attend_back(tables, queries, kv, mixed, mass, own_grad, other_grad, weight):
    rows, width = queries.shape
    pairs = width // PAIR
    return local_call(
        functools.partial(attend_back_kernel, pairs=pairs),
        [shaped((rows, width), jnp.bfloat16), shaped(kv.shape, jnp.bfloat16)],
        list(tables[4:]) + [queries, kv, mixed, mass, own_grad, other_grad, weight],
        tables[:4],
        [
            pltpu.VMEM(kv.shape, jnp.float32),
            pltpu.VMEM((rows, width), jnp.bfloat16),
            pltpu.VMEM((rows, width), jnp.float32),
        ],
        flops=10e9, transcendentals=4e6, spare=10,
    )


def fold_block(block, rows):
    return jnp.concatenate(
        [block[:, : 2 * PAIR], jnp.concatenate([block[:rows, 2 * PAIR :], block[rows:, 2 * PAIR :]], 1)], 0
    )


def unfold_block(block, rows):
    tail = block[2 * rows :]
    return jnp.concatenate(
        [block[: 2 * rows], jnp.concatenate([tail[:, :PAIR], tail[:, PAIR:]], 0)], 1
    )


def first_pack_kernel(tokens_ref, *refs):
    came, weights_ref, outs = refs[:3], refs[3], refs[4:]
    rows, columns = came[0].shape
    half = weights_ref.shape[0] // 2
    third = weights_ref.shape[1] // 3
    for at in range(3):
        outs[at][:rows, :] = tokens_ref[:, at * columns : (at + 1) * columns]
        outs[at][rows : 2 * rows, :] = came[at][...]
        outs[at][2 * rows :, :] = fold_block(weights_ref[:, at * third : (at + 1) * third], half)


def second_pack_kernel(*refs, rows):
    for at in range(3):
        sent_ref, came_ref, out_ref = refs[2 * at], refs[2 * at + 1], refs[6 + at]
        tail = sent_ref.shape[0] - rows
        out_ref[:rows, :] = sent_ref[:rows, :]
        out_ref[rows : 2 * rows, :] = came_ref[:rows, :]
        out_ref[2 * rows : 2 * rows + tail, :] = sent_ref[rows:, :]
        out_ref[2 * rows + tail :, :] = came_ref[rows:, :]


def third_pack_kernel(*refs, masks, rows):
    out_ref = refs[6]
    columns = refs[0].shape[1]
    for at in range(3):
        tokens = len(masks[2 * at]) * rows
        for side in range(2):
            piece = refs[2 * at + side]
            for slot, mask in enumerate(masks[2 * at + side]):
                out_ref[mask * rows : (mask + 1) * rows, at * columns : (at + 1) * columns] = piece[
                    slot * rows : (slot + 1) * rows, :
                ]
            tail = piece.shape[0] - tokens
            refs[7 + at][side * tail : (side + 1) * tail, :] = piece[tokens:, :]


def first_weights_kernel(owner_ref, *refs, masks, rows):
    pieces, query_ref, kv_ref = refs[:6], refs[6], refs[7]
    for at, group in enumerate(masks):
        third = at // 2
        for slot, mask in enumerate(group):
            base = slot * 3 * rows
            for far in range(2):
                start = pl.multiple_of(owner_ref[mask * 2 + far] * rows, rows)
                wide = pieces[at][base + far * rows : base + (far + 1) * rows, :]
                tail = pieces[at][base + 2 * rows : base + 3 * rows, far * PAIR : (far + 1) * PAIR]
                lines = pl.ds(start, rows)
                if third == 0:
                    query_ref[lines, : 2 * PAIR] = wide
                    query_ref[lines, 2 * PAIR :] = tail
                else:
                    shift = (third - 1) * PAIR
                    kv_ref[lines, shift : shift + PAIR] = wide[:, :PAIR]
                    kv_ref[lines, 2 * PAIR + shift : 3 * PAIR + shift] = wide[:, PAIR:]
                    kv_ref[lines, 4 * PAIR + shift : 5 * PAIR + shift] = tail


def first_weights(owner, pieces, masks, rows):
    blocks = owner.shape[0]
    features = blocks * rows
    outs = [shaped((features, 3 * PAIR), jnp.bfloat16), shaped((features, 6 * PAIR), jnp.bfloat16)]
    far_count = blocks // 8
    if rows % 16 == 0 and far_count == 2:
        return local_call(
            functools.partial(first_weights_kernel, masks=masks, rows=rows), outs, pieces, [owner]
        )
    slot_rows = far_count * rows
    thirds = []
    for third in range(3):
        made = jnp.zeros((features, 3 * PAIR), jnp.bfloat16)
        for at in (2 * third, 2 * third + 1):
            for slot, mask in enumerate(masks[at]):
                packed = pieces[at][slot * 3 * slot_rows // 2 : (slot + 1) * 3 * slot_rows // 2]
                lines = owner.reshape(8, far_count)[mask][:, None] * rows + jnp.arange(rows, dtype=jnp.int32)
                made = made.at[lines.reshape(-1)].set(unfold_block(packed, slot_rows // 2))
        thirds.append(made)
    mixed = [
        thirds[1 + which][:, pair * PAIR : (pair + 1) * PAIR] for pair in range(3) for which in range(2)
    ]
    return thirds[0], jnp.concatenate(mixed, 1)


def place_weights_kernel(owner_ref, *refs, plan, far_count, rows):
    pieces, outs = refs[: len(plan)], refs[len(plan) :]
    for piece, (masks, targets) in zip(pieces, plan):
        for slot, mask in enumerate(masks):
            for far in range(far_count):
                start = pl.multiple_of(owner_ref[mask * far_count + far] * rows, rows)
                for first, last, out, column in targets:
                    outs[out][pl.ds(start, rows), column : column + last - first] = piece[
                        slot * far_count + far, :, first:last
                    ]


def place_weights(owner, pieces, plan, widths):
    rows = pieces[0].shape[1]
    blocks = owner.shape[0]
    far_count = blocks // 8
    outs = [shaped((blocks * rows, width), jnp.bfloat16) for width in widths]
    if rows % 16 == 0:
        kernel = functools.partial(place_weights_kernel, plan=plan, far_count=far_count, rows=rows)
        return local_call(kernel, outs, pieces, [owner])
    made = [jnp.zeros(out.shape, out.dtype) for out in outs]
    for piece, (masks, targets) in zip(pieces, plan):
        spots = owner.reshape(8, far_count)[jnp.array(masks)].reshape(-1)
        lines = (spots[:, None] * rows + jnp.arange(rows, dtype=jnp.int32)).reshape(-1)
        flat = piece.reshape(-1, piece.shape[2])
        for first, last, out, column in targets:
            made[out] = made[out].at[lines, column : column + last - first].set(flat[:, first:last])
    return made


def placed_blocks(grad, owner, masks):
    blocks = owner.shape[0]
    rows = grad.shape[0] // blocks
    spots = owner.reshape(8, -1)[jnp.array(masks)].reshape(-1)
    return jnp.take(grad.reshape(blocks, rows, grad.shape[1]), spots, axis=0)


def token_kernel(x_ref, query_weight_ref, kv_weight_ref, query_ref, kv_ref):
    @pl.when(pl.program_id(0) == 0)
    def _():
        rows = query_ref.shape[0]
        query_ref[...] = dot_plain(x_ref[:rows, :], query_weight_ref[...]).astype(jnp.bfloat16)

    kv_ref[...] = dot_plain(x_ref[...], kv_weight_ref[...]).astype(jnp.bfloat16)


def project_tokens(x, query_weight, kv_weight, rows):
    step = 512
    whole = lambda at: (0, 0)
    part = lambda at: (at, 0)
    return pl.pallas_call(
        token_kernel,
        grid=(x.shape[0] // step,),
        out_shape=(
            shaped((rows, query_weight.shape[1]), jnp.bfloat16),
            shaped((x.shape[0], kv_weight.shape[1]), jnp.bfloat16),
        ),
        in_specs=[
            pl.BlockSpec((step, x.shape[1]), part),
            pl.BlockSpec(query_weight.shape, whole),
            pl.BlockSpec(kv_weight.shape, whole),
        ],
        out_specs=(
            pl.BlockSpec((rows, query_weight.shape[1]), whole),
            pl.BlockSpec((step, kv_weight.shape[1]), part),
        ),
        compiler_params=params(16),
        cost_estimate=cost(2 * x.size * kv_weight.shape[1], 8 * x.size),
    )(x, query_weight, kv_weight)


def project_kernel(mixed_ref, weight_ref, own_ref, other_ref, low_ref):
    low = mixed_ref[...].astype(jnp.bfloat16)
    low_ref[...] = low
    total = dot_cols(low, weight_ref[...])
    half = own_ref.shape[0]
    own_ref[...] = total[:half]
    other_ref[...] = total[half:].astype(jnp.bfloat16)


def normed_rows(values):
    centred = values - jnp.mean(values, axis=-1, keepdims=True)
    spread = jnp.mean(centred * centred, axis=-1, keepdims=True)
    scale = lax.rsqrt(spread + epsilon)
    return centred * scale, scale


def norm_back(grads, normed, scale, gain):
    inner = grads * gain
    middle = jnp.mean(inner, axis=-1, keepdims=True)
    slant = jnp.mean(inner * normed, axis=-1, keepdims=True)
    return scale * (inner - middle - normed * slant)


def first_norm_kernel(tokens_ref, own_ref, came_ref, gain_ref, shift_ref, sum_ref, hidden_ref, low_ref):
    total = tokens_ref[...].astype(jnp.float32) + (own_ref[...] + came_ref[...].astype(jnp.float32))
    sum_ref[...] = total
    normed, _ = normed_rows(total)
    hidden = normed * gain_ref[...] + shift_ref[...]
    hidden_ref[...] = hidden
    low_ref[...] = hidden.astype(jnp.bfloat16)


def feed_kernel(own_hidden_ref, other_hidden_ref, inner_ref, outer_ref, own_ref, other_ref, active_ref, slope_ref, total_ref):
    hidden = jnp.concatenate([own_hidden_ref[...], other_hidden_ref[...]], 0)
    step = 256
    for start in range(0, inner_ref.shape[1], step):
        columns = slice(start, start + step)
        upper = dot_plain(hidden, inner_ref[:, columns])
        chance = 0.5 * (1.0 + lax.erf(upper * (0.5**0.5)))
        active = (upper * chance).astype(jnp.bfloat16)
        active_ref[:, columns] = active
        slope_ref[:, columns] = chance + upper * (jnp.exp(-0.5 * upper * upper) * 0.3989422804014327)
        part = dot_cols(active, outer_ref[:, columns])
        if start:
            total_ref[...] += part
        else:
            total_ref[...] = part
    half = own_ref.shape[0]
    own_ref[...] = total_ref[:half, :]
    other_ref[...] = total_ref[half:, :].astype(jnp.bfloat16)


def second_norm_kernel(
    factor_ref, hidden_ref, own_ref, came_ref, gain_ref, shift_ref, teacher_ref, valid_ref,
    result_ref, grad_ref, low_ref, stats_ref
):
    total = hidden_ref[...] + (own_ref[...] + came_ref[...].astype(jnp.float32))
    normed, scale = normed_rows(total)
    gain = gain_ref[...]
    result = normed * gain + shift_ref[...]
    result_ref[...] = result.astype(jnp.bfloat16)
    errors = (result - teacher_ref[...].astype(jnp.float32)) * valid_ref[...]
    grads = errors * factor_ref[0]
    grad = norm_back(grads, normed, scale, gain)
    grad_ref[...] = grad
    low_ref[...] = grad.astype(jnp.bfloat16)
    stats_ref[...] = jnp.zeros_like(stats_ref)
    stats_ref[0:1, :] = jnp.sum(grads * normed, axis=0, keepdims=True)
    stats_ref[1:2, :] = jnp.sum(grads, axis=0, keepdims=True)
    stats_ref[2:3, :] = jnp.sum(errors * errors, axis=0, keepdims=True)


def feed_back_kernel(own_grad_ref, other_grad_ref, slope_ref, inner_ref, outer_ref, upper_ref, own_ref, other_ref, total_ref):
    grads = jnp.concatenate([own_grad_ref[...], other_grad_ref[...]], 0)
    step = 256
    for start in range(0, inner_ref.shape[1], step):
        columns = slice(start, start + step)
        upper = (dot_plain(grads, outer_ref[:, columns]) * slope_ref[:, columns]).astype(jnp.bfloat16)
        upper_ref[:, columns] = upper
        part = dot_cols(upper, inner_ref[:, columns])
        if start:
            total_ref[...] += part
        else:
            total_ref[...] = part
    half = own_ref.shape[0]
    own_ref[...] = total_ref[:half, :]
    other_ref[...] = total_ref[half:, :].astype(jnp.bfloat16)


def first_back_kernel(grad_ref, own_ref, came_ref, sum_ref, gain_ref, out_ref, low_ref, stats_ref):
    grads = grad_ref[...] + (own_ref[...] + came_ref[...].astype(jnp.float32))
    normed, scale = normed_rows(sum_ref[...])
    grad = norm_back(grads, normed, scale, gain_ref[...])
    out_ref[...] = grad
    low_ref[...] = grad.astype(jnp.bfloat16)
    stats_ref[...] = jnp.zeros_like(stats_ref)
    stats_ref[0:1, :] = jnp.sum(grads * normed, axis=0, keepdims=True)
    stats_ref[1:2, :] = jnp.sum(grads, axis=0, keepdims=True)


def write_blocks(owner_ref, made_ref, column, width, out_ref, out_column, masks, far_count, rows):
    for slot, mask in enumerate(masks):
        for far in range(far_count):
            start = pl.multiple_of(owner_ref[mask * far_count + far] * rows, rows)
            out_ref[slot * far_count + far, :, out_column : out_column + width] = made_ref[
                pl.ds(start, rows), column : column + width
            ].astype(out_ref.dtype)


def wide_kernel(
    owner_ref, own_grad_ref, other_grad_ref, active_ref, own_hidden_ref, other_hidden_ref, upper_ref, *refs,
    groups, far_count, rows, step
):
    outs, made_ref = refs[:-1], refs[-1]
    grads = jnp.concatenate([own_grad_ref[...], other_grad_ref[...]], 0)
    hidden = jnp.concatenate([own_hidden_ref[...], other_hidden_ref[...]], 0)
    width = active_ref.shape[1]
    third_width = 2 * width // 3
    for start in range(0, 2 * width, step):
        if start < width:
            made_ref[...] = dot_rows(grads, active_ref[:, start : start + step])
        else:
            made_ref[...] = dot_rows(hidden, upper_ref[:, start - width : start - width + step])
        third = start // third_width
        for at, masks in enumerate(groups[third]):
            write_blocks(
                owner_ref, made_ref, 0, step, outs[third * len(groups[third]) + at], start % third_width,
                masks, far_count, rows
            )


def wide_gradients(owner, own_grad, other_grad, active, own_hidden, other_hidden, upper, groups):
    blocks = owner.shape[0]
    far_count, rows = blocks // 8, own_grad.shape[1] // blocks
    width = active.shape[1]
    third_width = 2 * width // 3
    if rows % 16:
        made = jnp.concatenate(
            [
                dot_rows(jnp.concatenate([own_grad, other_grad], 0), active),
                dot_rows(jnp.concatenate([own_hidden, other_hidden], 0), upper),
            ],
            1,
        )
        outs = []
        for third, group in enumerate(groups):
            columns = made[:, third * third_width : (third + 1) * third_width]
            for at, masks in enumerate(group):
                outs.append(placed_blocks(columns, owner, masks).astype(jnp.bfloat16 if at else jnp.float32))
        return outs
    step = 512
    outs = []
    for group in groups:
        for at, masks in enumerate(group):
            outs.append(
                shaped((len(masks) * far_count, rows, third_width), jnp.bfloat16 if at else jnp.float32)
            )
    kernel = functools.partial(wide_kernel, groups=groups, far_count=far_count, rows=rows, step=step)
    return local_call(
        kernel, outs, [own_grad, other_grad, active, own_hidden, other_hidden, upper], [owner],
        [pltpu.VMEM((own_grad.shape[1], step), jnp.float32)],
        flops=8 * own_grad.size * width, spare=8,
    )


def narrow_kernel(
    own_ref, other_ref, kv_grad_ref, query_grad_ref, own_grad_ref, other_grad_ref, low_ref, made_ref
):
    half, near = own_ref.shape[0], own_grad_ref.shape[0]
    width = query_grad_ref.shape[1]
    made_ref[:, :width] = dot_rows(own_ref[:near, :], query_grad_ref[:near, :]) + dot_rows(
        other_ref[:near, :], query_grad_ref[near:, :]
    )
    made_ref[:, width : 2 * width] = dot_rows(own_grad_ref[...], low_ref[:near, :]) + dot_rows(
        other_grad_ref[...], low_ref[near:, :]
    )
    made_ref[:, 2 * width :] = dot_rows(own_ref[...], kv_grad_ref[:half, :])
    made_ref[:, 2 * width :] += dot_rows(other_ref[...], kv_grad_ref[half:, :])


def narrow_gradients(own, other, kv_grad, query_grad, own_grad, other_grad, low):
    width = query_grad.shape[1]
    return local_call(
        narrow_kernel, [shaped((own.shape[1], 4 * width))],
        [own, other, kv_grad, query_grad, own_grad, other_grad, low],
        flops=4 * own.size * 2 * width + 8 * own_grad.size * width, spare=10,
    )[0]


def token_other_kernel(kv_grad_ref, query_grad_ref, kv_weight_ref, query_weight_ref, out_ref):
    near, half = query_grad_ref.shape[0] // 2, kv_grad_ref.shape[0] // 2
    for start in range(0, half, near):
        total = dot_cols(kv_grad_ref[half + start : half + start + near, :], kv_weight_ref[...])
        if start == 0:
            total += dot_cols(query_grad_ref[near:, :], query_weight_ref[...])
        out_ref[start : start + near, :] = total.astype(jnp.bfloat16)


def token_other(kv_grad, query_grad, kv_weight, query_weight):
    return local_call(
        token_other_kernel, [shaped((kv_grad.shape[0] // 2, kv_weight.shape[0]), jnp.bfloat16)],
        [kv_grad, query_grad, kv_weight, query_weight],
        flops=kv_grad.size * kv_weight.shape[0], spare=6,
    )[0]


def token_own_kernel(
    owner_ref, kv_grad_ref, query_grad_ref, kv_weight_ref, query_weight_ref, came_ref, made_ref, *outs,
    masks, rows, placed
):
    near = query_grad_ref.shape[0] // 2
    half, columns = outs[0].shape[0], outs[0].shape[2]
    slot_rows = made_ref.shape[1] if placed else made_ref.shape[0] // (2 * half)
    for mask in range(2 * half):
        lines = slice(mask * near, (mask + 1) * near)
        total = dot_cols(kv_grad_ref[lines, :], kv_weight_ref[...]) + came_ref[lines, :].astype(jnp.float32)
        if mask == 0:
            total += dot_cols(query_grad_ref[:near, :], query_weight_ref[...])
        for third, order in enumerate(masks):
            slot = order.index(mask)
            out_ref = outs[2 * third + slot // half]
            at = slot % half
            out_ref[at, :near, :] = total[:, third * columns : (third + 1) * columns].astype(out_ref.dtype)
            for side in range(2):
                base = near + side * slot_rows
                part = slice((2 * third + side) * columns, (2 * third + side + 1) * columns)
                if placed:
                    out_ref[at, base : base + slot_rows, :] = made_ref[mask, :, part].astype(out_ref.dtype)
                    continue
                for far in range(slot_rows // rows):
                    start = pl.multiple_of(owner_ref[mask * (slot_rows // rows) + far] * rows, rows)
                    out_ref[at, base + far * rows : base + (far + 1) * rows, :] = made_ref[
                        pl.ds(start, rows), part
                    ].astype(out_ref.dtype)


def token_own(owner, kv_grad, query_grad, kv_weight, query_weight, came, made, masks):
    near = query_grad.shape[0] // 2
    half = came.shape[0] // near // 2
    blocks, features = owner.shape[0], made.shape[0]
    rows, slot_rows = features // blocks, features // (2 * half)
    columns = kv_weight.shape[0] // 3
    placed = rows % 16 != 0
    if placed:
        made = placed_blocks(made, owner, tuple(range(2 * half))).reshape(2 * half, slot_rows, made.shape[1])
    outs = []
    for _ in masks:
        shape = (half, near + 2 * slot_rows, columns)
        outs += [shaped(shape), shaped(shape, jnp.bfloat16)]
    outs = local_call(
        functools.partial(token_own_kernel, masks=masks, rows=rows, placed=placed), outs,
        [kv_grad, query_grad, kv_weight, query_weight, came, made], [owner],
        flops=2 * came.shape[0] * kv_weight.size, spare=6,
    )
    return list(outs[::2]), list(outs[1::2])


def last_kernel(grad_ref, *refs):
    token_ref, made_ref = refs[-2:]
    near, columns = grad_ref.shape[0], refs[0].shape[2]
    slot_rows = made_ref.shape[0]
    for third in range(3):
        total = refs[2 * third][0] + refs[2 * third + 1][0].astype(jnp.float32)
        part = slice(third * columns, (third + 1) * columns)
        token_ref[:, part] = grad_ref[:, part] + total[:near]
        for side in range(2):
            at = (2 * third + side) * columns
            made_ref[:, at : at + columns] = total[near + side * slot_rows : near + (side + 1) * slot_rows]


def wide_end_kernel(*refs):
    out_ref = refs[-1]
    columns = refs[0].shape[2]
    for third in range(3):
        out_ref[:, third * columns : (third + 1) * columns] = refs[2 * third][0] + refs[2 * third + 1][0].astype(
            jnp.float32
        )


def tie(first, second):
    leaves, tree = jax.tree.flatten(second)
    tied = lax.optimization_barrier(tuple(leaves) + (first,))
    return jax.tree.unflatten(tree, tied[:-1])


def shards(
    tokens,
    query_weight,
    key_weight,
    value_weight,
    output_weight,
    inner_weight,
    outer_weight,
    attn_gain,
    attn_shift,
    ffn_gain,
    ffn_shift,
    teacher,
    segments,
    random_blocks,
    valid_tokens,
):
    devices = lax.axis_size("dp")
    dp_index = lax.axis_index("dp")
    core = lax.axis_index("tensor")
    rows, width = tokens.shape
    length = 2 * rows
    span = segments.shape[1] // length
    near_bits = span.bit_length() - 1
    far_bits = tuple(range(near_bits, devices.bit_length() - 1))
    place, far_place = dp_index % span, dp_index // span
    far_count = devices // span
    each = width // devices
    slot_rows = far_count * each
    head_width = query_weight.shape[1]
    wide = inner_weight.shape[1]
    masks = jnp.arange(span, dtype=jnp.int32)
    fars = jnp.arange(far_count, dtype=jnp.int32)
    owner = ((fars[None, :] ^ far_place) * span + (masks[:, None] ^ place)).reshape(-1)

    def far_gather(block):
        held = block[None]
        for bit in far_bits:
            held = jnp.concatenate([held, swap_mask(held, 1 << bit)], 0)
        return held.reshape(slot_rows, block.shape[1])

    def step(held, at):
        return [swap_mask(one, 1 << bits[at]) for one, bits in zip(held, ROUTES)]

    def both(held, came):
        return [one for pair in zip(held, came) for one in pair]

    def message(lines):
        return [shaped((lines, third), jnp.bfloat16)] * 3

    third = width // 3
    packed = 3 * slot_rows // 2
    first_held = far_gather(jnp.concatenate([query_weight, key_weight, value_weight], 1))
    came = step([tokens[:, at * third : (at + 1) * third] for at in range(3)], 0)
    held = local_call(first_pack_kernel, message(2 * rows + packed), [tokens] + came + [first_held])
    came = step(held, 1)
    count_block = jnp.full((each, PAIR), jnp.sum(valid_tokens).astype(jnp.bfloat16), jnp.bfloat16)
    second_held = far_gather(jnp.concatenate([inner_weight, outer_weight, output_weight, count_block], 1))
    held = local_call(
        functools.partial(second_pack_kernel, rows=2 * rows), message(4 * rows + 2 * packed), both(held, came)
    )
    came = step(held, 2)
    sent_masks = [tuple(slot_masks(bits[:2])) for bits in ROUTES]
    came_masks = [tuple(mask ^ (1 << bits[2]) for mask in sent) for sent, bits in zip(sent_masks, ROUTES)]
    own, *held = local_call(
        functools.partial(third_pack_kernel, masks=tuple(both(sent_masks, came_masks)), rows=rows),
        [shaped((span * rows, width), jnp.bfloat16)] + message(4 * packed), both(held, came),
    )
    came = step(held, 0)
    other = swap_core(own)

    cut = 3 * wide // 4
    spans = (((0, cut),), ((wide, wide + cut),), ((cut, wide), (wide + cut, second_held.shape[1])))
    second_held = tie(held[0], second_held)
    seconds = [
        jnp.concatenate([second_held[:, first:last] for first, last in group], 1)[None] for group in spans
    ]
    arrived = step(seconds, 0)

    weight_masks = [tuple(slot_masks((bits[1], bits[2]))) for bits in ROUTES]
    late_masks = [tuple(mask ^ (1 << bits[0]) for mask in sent) for sent, bits in zip(weight_masks, ROUTES)]
    full_query, full_kv = first_weights(
        owner, both(held, came), tuple(both(weight_masks, late_masks)), each
    )
    seconds = pack([[one, late] for one, late in zip(tie(full_kv, seconds), arrived)])
    arrived = step(seconds, 1)

    segment_all = lax.dynamic_index_in_dim(segments, far_place, 0, keepdims=False)
    tables = attention_tables(random_blocks, segment_all, place, core, span, length // BLOCK)
    own_query, own_kv = project_tokens(own, full_query, full_kv, rows)
    seconds = pack([[one, late] for one, late in zip(tie(own_kv, seconds), arrived)])
    arrived = step(seconds, 2)
    mixed, mass, queries, kv = attend(
        tables, own_query, tie(seconds[0], own_kv), other, full_query, full_kv
    )

    seconds, arrived = tie(mixed, (seconds, arrived))
    targets = (
        ((0, cut, 0, 0),),
        ((0, cut, 1, 0),),
        (
            (0, wide - cut, 0, cut),
            (wide - cut, 2 * (wide - cut), 1, cut),
            (2 * (wide - cut), 2 * (wide - cut) + head_width, 2, 0),
            (2 * (wide - cut) + head_width, 2 * (wide - cut) + head_width + PAIR, 3, 0),
        ),
    )
    plan = [
        (group, targets[at // 2]) for at, group in enumerate(both(sent_masks, came_masks))
    ]
    pieces = [one.reshape(-1, each, one.shape[2]) for one in both(seconds, arrived)]
    full_inner, full_outer, full_output, counts = place_weights(
        owner, pieces, tuple(plan), (wide, wide, head_width, PAIR)
    )
    half_count = jnp.sum(counts[::each, :1].astype(jnp.float32)).reshape(1, 1)
    valid_total = (half_count + swap_core(half_count))[0, 0]

    half_shape, low_shape = shaped((rows, width)), shaped((rows, width), jnp.bfloat16)
    gain_one, shift_one, gain_two, shift_two = (
        one.reshape(1, width) for one in (attn_gain, attn_shift, ffn_gain, ffn_shift)
    )
    part_own, part_other, attended = local_call(
        project_kernel, [half_shape, low_shape, shaped(mixed.shape, jnp.bfloat16)], [mixed, full_output],
        flops=2 * mixed.size * width,
    )
    first_sum, hidden, hidden_own = local_call(
        first_norm_kernel, [half_shape, half_shape, low_shape],
        [tokens, part_own, swap_core(part_other), gain_one, shift_one],
    )
    hidden_other = swap_core(hidden_own)
    part_own, part_other, active, slope = local_call(
        feed_kernel,
        [half_shape, low_shape, shaped((length, wide), jnp.bfloat16), shaped((length, wide))],
        [hidden_own, hidden_other, full_inner, full_outer],
        scratch=[pltpu.VMEM((length, width), jnp.float32)],
        flops=4 * length * width * wide, transcendentals=2 * length * wide, spare=6,
    )
    token_total = devices * lax.axis_size("tensor") * rows
    result, grad_second, grad_ffn_own, stats_two = local_call(
        second_norm_kernel, [low_shape, half_shape, low_shape, shaped((8, width))],
        [hidden, part_own, swap_core(part_other), gain_two, shift_two, teacher,
         valid_tokens.astype(jnp.float32)[:, None]],
        [(token_total / valid_total).reshape(1)],
    )
    grad_ffn_other = swap_core(grad_ffn_own)
    upper_grad, part_own, part_other = local_call(
        feed_back_kernel, [shaped((length, wide), jnp.bfloat16), half_shape, low_shape],
        [grad_ffn_own, grad_ffn_other, slope, full_inner, full_outer],
        scratch=[pltpu.VMEM((length, width), jnp.float32)],
        flops=4 * length * width * wide, spare=6,
    )
    part_came = swap_core(part_other)
    scatter_masks = tuple(tuple(slot_masks(bits[::-1])) for bits in ROUTES)
    groups = tuple((one[: span // 2], one[span // 2 :]) for one in scatter_masks)
    outs = wide_gradients(
        owner, grad_ffn_own, grad_ffn_other, active, hidden_own, hidden_other, upper_grad, groups
    )
    outs = [one.reshape(span // 2, slot_rows, one.shape[2]) for one in outs]
    wide_keep, wide_came = outs[::2], step(outs[1::2], 0)
    part_came = tie(outs[0], part_came)
    grad_first, grad_attn_own, stats_one = local_call(
        first_back_kernel, [half_shape, low_shape, shaped((8, width))],
        [grad_second, part_own, part_came, first_sum, gain_one],
    )
    grad_attn_other = swap_core(grad_attn_own)
    query_grad, kv_grad = attend_back(
        tables, queries, kv, mixed, mass, grad_attn_own, grad_attn_other, full_output
    )

    def folded(keep, came):
        return fold(keep, [[one] for one in came])

    wide_keep, wide_send = folded(wide_keep, tie(query_grad, wide_came))
    wide_came = step(wide_send, 1)
    token_sent = token_other(tie(wide_keep[0], kv_grad), query_grad, full_kv, full_query)
    token_came = swap_core(token_sent)
    made = narrow_gradients(
        own, other, tie(token_sent, kv_grad), query_grad, grad_attn_own, grad_attn_other, attended
    )
    wide_keep, wide_send = folded(wide_keep, tie(made, wide_came))
    wide_came = step(wide_send, 2)
    keep, send = token_own(
        owner, kv_grad, query_grad, full_kv, full_query, tie(wide_keep[0], token_came), made, scatter_masks
    )
    came = step(send, 0)
    wide_sum = local_call(
        wide_end_kernel, [shaped((slot_rows, 2 * wide))], both(wide_keep, tie(keep[0], wide_came))
    )[0]

    def far_scatter(total):
        total = total.reshape(far_count, each, total.shape[1])
        for bit in far_bits[::-1]:
            half = total.shape[0] // 2
            total = total[:half] + swap_mask(total[half:].astype(jnp.bfloat16), 1 << bit).astype(jnp.float32)
        return total[0]

    wide_sum = far_scatter(wide_sum)
    part_outer, part_inner = wide_sum[:, :wide], wide_sum[:, wide:]
    keep, send = folded(keep, came)
    came = step(send, 1)
    keep, send = folded(keep, came)
    came = step(send, 2)
    grad_tokens, narrow_sum = local_call(
        last_kernel, [half_shape, shaped((slot_rows, 4 * head_width))], [grad_first] + both(keep, came)
    )
    narrow_sum = far_scatter(narrow_sum)

    small = jnp.concatenate(
        [
            stats_one[:2], stats_two[:2],
            jnp.broadcast_to(jnp.sum(stats_two[2]), (1, width)), jnp.zeros((3, width), jnp.float32),
        ]
    )
    small = small.reshape(8, devices, each).transpose(1, 0, 2)
    small = jnp.take(small, owner, axis=0)
    for bit in tuple(range(near_bits))[::-1] + far_bits[::-1]:
        half = small.shape[0] // 2
        small = small[:half] + swap_mask(small[half:], 1 << bit)
    small = small[0]
    small = small + swap_core(small)
    loss_value = small[4, 0] / (2.0 * width * valid_total)
    mine = lax.dynamic_slice_in_dim(small, core * (each // 2), each // 2, 1)

    part_query, part_output = narrow_sum[:, :head_width], narrow_sum[:, head_width : 2 * head_width]
    kv_sum = narrow_sum[:, 2 * head_width :]
    pairs = head_width // PAIR
    part_key = jnp.concatenate([kv_sum[:, 2 * pair * PAIR : (2 * pair + 1) * PAIR] for pair in range(pairs)], 1)
    part_value = jnp.concatenate(
        [kv_sum[:, (2 * pair + 1) * PAIR : (2 * pair + 2) * PAIR] for pair in range(pairs)], 1
    )
    return (
        result,
        loss_value,
        grad_tokens,
        part_query,
        part_key,
        part_value,
        part_output,
        part_inner,
        part_outer,
        mine[0],
        mine[1],
        mine[2],
        mine[3],
    )


def solution(mesh):
    both = P(("dp", "tensor"))
    rows_spec = P(("dp", "tensor"), None)
    weight_spec = P("dp", "tensor")
    in_specs = (rows_spec,) + (weight_spec,) * 6 + (P(),) * 4
    in_specs += (rows_spec, P(), P("tensor", None, None), both)
    out_specs = (rows_spec, P(), rows_spec) + (weight_spec,) * 6 + (both,) * 4
    return jax.shard_map(shards, mesh=mesh, in_specs=in_specs, out_specs=out_specs, check_vma=False)
```

```python
import functools

import jax
import jax.numpy as jnp
from jax import lax
from jax.experimental import pallas as pl
from jax.experimental.pallas import tpu as pltpu
from jax.sharding import PartitionSpec as P

BLOCK = 64
HEAD = 64
PAIR = 2 * HEAD
SLOTS = 6
ROUTES = ((0, 1, 2), (1, 2, 0), (2, 0, 1))

epsilon = 1e-05
masked_value = -1e30
score_scale = 0.125


def swap_mask(block, mask):
    count = lax.axis_size("dp")
    return lax.ppermute(block, "dp", [(one, one ^ mask) for one in range(count)])


def swap_core(block):
    return lax.ppermute(block, "tensor", [(0, 1), (1, 0)])


def dot_plain(left_side, right_side):
    return jnp.dot(left_side, right_side, preferred_element_type=jnp.float32)


def dot_cols(left_side, right_side):
    return lax.dot_general(
        left_side, right_side, (((1,), (1,)), ((), ())), preferred_element_type=jnp.float32
    )


def dot_rows(left_side, right_side):
    return lax.dot_general(
        left_side, right_side, (((0,), (0,)), ((), ())), preferred_element_type=jnp.float32
    )


def params(megabytes):
    return pltpu.CompilerParams(vmem_limit_bytes=int(megabytes) << 20)


def cost(flops=0, moved=0, transcendentals=0):
    return pl.CostEstimate(flops=int(flops), bytes_accessed=int(moved), transcendentals=int(transcendentals))


def in_vmem(count):
    return [pl.BlockSpec(memory_space=pltpu.VMEM)] * count


def in_smem(count):
    return [pl.BlockSpec(memory_space=pltpu.SMEM)] * count


def shaped(shape, dtype=jnp.float32):
    return jax.ShapeDtypeStruct(tuple(shape), dtype)


def local_call(kernel, outs, vmem_inputs, smem_inputs=(), scratch=(), flops=0, transcendentals=0, spare=8):
    moved = sum(one.size * one.dtype.itemsize for one in list(vmem_inputs) + list(outs))
    held = sum(one.size * one.dtype.itemsize for one in (shaped(s.shape, s.dtype) for s in scratch))
    held = held // (1 << 20) + 1 + spare
    return pl.pallas_call(
        kernel,
        out_shape=tuple(pltpu.VMEM(one.shape, one.dtype) for one in outs),
        in_specs=in_smem(len(smem_inputs)) + in_vmem(len(vmem_inputs)),
        out_specs=tuple(in_vmem(len(outs))),
        scratch_shapes=list(scratch),
        compiler_params=params(held),
        cost_estimate=cost(flops, moved, transcendentals),
    )(*smem_inputs, *[pltpu.with_memory_space_constraint(one, pltpu.VMEM) for one in vmem_inputs])


def slot_masks(bits):
    return [
        sum(((slot >> at) & 1) << bit for at, bit in enumerate(bits))
        for slot in range(1 << len(bits))
    ]


def in_pieces(values):
    high = values.astype(jnp.bfloat16).astype(jnp.float32)
    middle = (values - high).astype(jnp.bfloat16).astype(jnp.float32)
    return high + pltpu.roll(middle, 8, 1) + pltpu.roll(values - high - middle, 16, 1)


def from_pieces(pieces):
    lanes = pieces.shape[1]
    total = pieces + pltpu.roll(pieces, lanes - 8, 1) + pltpu.roll(pieces, lanes - 16, 1)
    return jnp.where(lax.broadcasted_iota(jnp.int32, pieces.shape, 1) % PAIR < 8, total, 0.0)


def fold_kernel(*refs, thirds, arrivals, plain):
    outs = refs[thirds * (1 + arrivals) :]
    for third in range(thirds):
        keep_ref = refs[third * (1 + arrivals)]
        came = refs[third * (1 + arrivals) + 1 : (third + 1) * (1 + arrivals)]
        half, lines = keep_ref.shape[0] // 2, keep_ref.shape[1]
        most = lines if plain is None else min(plain, lines)
        for side in range(2):
            part = slice(side * half, (side + 1) * half)
            total = sum([one[part, :most].astype(jnp.float32) for one in came], keep_ref[part, :most])
            out_ref = outs[2 * third + side]
            out_ref[:, :most] = total.astype(out_ref.dtype)
            if most == lines:
                continue
            for at in range(half):
                total = keep_ref[side * half + at, most:]
                for one in came:
                    total += from_pieces(one[side * half + at, most:].astype(jnp.float32))
                out_ref[at, most:] = (in_pieces(total) if side else total).astype(out_ref.dtype)


def fold(keeps, arrivals, plain=None):
    outs = []
    for keep in keeps:
        half = (keep.shape[0] // 2,) + keep.shape[1:]
        outs += [shaped(half), shaped(half, jnp.bfloat16)]
    operands = []
    for keep, came in zip(keeps, arrivals):
        operands += [keep] + list(came)
    kernel = functools.partial(fold_kernel, thirds=len(keeps), arrivals=len(arrivals[0]), plain=plain)
    outs = local_call(kernel, outs, operands)
    return list(outs[::2]), list(outs[1::2])


def pick(chosen, table):
    return lax.dot_general(
        chosen.astype(jnp.bfloat16), table.astype(jnp.bfloat16), (((chosen.ndim - 1,), (0,)), ((), ())),
        preferred_element_type=jnp.float32,
    )


def attention_tables(random_blocks, segment_all, place, core, span, row_blocks):
    heads, blocks, draws = random_blocks.shape
    half, pairs = row_blocks // 2, heads // 2
    local = jnp.arange(row_blocks, dtype=jnp.int32)
    owner = jnp.where(local < half, core, 1 - core)
    absolute = place * row_blocks + owner * half + local % half
    every = jnp.arange(blocks, dtype=jnp.int32)
    mine = absolute[:, None] == every
    edge = (every == 0) | (every == blocks - 1)
    fixed = (jnp.abs(absolute[:, None] - every) <= 1) | edge | edge[absolute][:, None]
    segment_table = segment_all.reshape(blocks, BLOCK).astype(jnp.float32)
    low, high = jnp.min(segment_table, 1), jnp.max(segment_table, 1)
    reach = (jnp.max(jnp.where(mine, low, -1.0), 1)[:, None] <= high) & (
        low <= jnp.max(jnp.where(mine, high, -1.0), 1)[:, None]
    )
    drawn = pick(mine, random_blocks.transpose(1, 0, 2).reshape(blocks, heads * draws))
    drawn = drawn.reshape(row_blocks, heads, draws, 1) == every.astype(jnp.float32)
    allowed = (jnp.any(drawn, 2) | fixed[:, None]) & reach[:, None]
    allowed = allowed.reshape(row_blocks, pairs, 2, blocks)
    listed = jnp.any(allowed, 2)
    rank = pick(listed, every[:, None] < every[None, :])
    count = jnp.max(jnp.sum(listed.astype(jnp.int32), -1), -1)
    chunks = -(-count // SLOTS)
    ends = jnp.sum(jnp.where(local[:, None] >= local[None, :], chunks[None, :], 0), 1)
    most = (row_blocks - 1) * -(-min(blocks, 5 + 2 * draws) // SLOTS) + -(-blocks // SLOTS)
    if span == 1:
        most += -(-blocks // SLOTS)
    items = jnp.arange(most, dtype=jnp.int32)
    item_query = jnp.minimum(jnp.sum((items[:, None] >= ends[None, :]).astype(jnp.int32), 1), row_blocks - 1)
    item_is = item_query[:, None] == local
    first = jnp.sum(jnp.where(item_is, (ends - chunks)[None, :], 0), 1)
    spots = ((items - first) * SLOTS)[:, None] + jnp.arange(SLOTS, dtype=jnp.int32)
    stored = (
        jnp.where((every % row_blocks) // half == core, 0, span * half)
        + ((every // row_blocks) ^ place) * half + every % half
    )
    rows = jnp.concatenate([jnp.where(listed, rank, -1.0)[:, :, None], allowed.astype(jnp.float32)], 2)
    rows = pick(item_is, rows.reshape(row_blocks, -1)).reshape(most, pairs, 3, blocks)
    here = rows[:, :, 0, None, :] == spots[:, None, :, None].astype(jnp.float32)
    code = rows[:, :, 1, None, :] * 256.0 + rows[:, :, 2, None, :] * 512.0 + stored.astype(jnp.float32)
    codes = jnp.sum(jnp.where(here, code, 0.0), -1).astype(jnp.int32)
    order = jnp.arange(2 * span * half, dtype=jnp.int32)
    order_block = (
        ((order % (span * half)) // half) ^ place
    ) * row_blocks + jnp.where(order < span * half, core, 1 - core) * half + order % half
    key_side = pick(order_block[:, None] == every, segment_table).reshape(-1, 1)
    query_side = pick(mine, segment_table)
    query_side = jnp.concatenate([query_side, query_side], 1)
    return (
        ends[-1:].astype(jnp.int32),
        item_query.astype(jnp.int32),
        (items == first).astype(jnp.int32),
        codes.reshape(-1),
        query_side,
        jnp.broadcast_to(key_side, (key_side.shape[0], PAIR)),
    )


def two_heads(rows, low_lanes):
    rows = rows.astype(jnp.float32)
    zero = jnp.zeros_like(rows)
    return jnp.concatenate(
        [jnp.where(low_lanes, rows, zero), jnp.where(low_lanes, zero, rows)], 0
    )


def item_blocks(codes_ref, first, side, key_side_ref):
    low_row = lax.broadcasted_iota(jnp.int32, (1, PAIR), 1) < HEAD
    spots, masks = [], []
    for slot in range(SLOTS):
        code = codes_ref[first + slot]
        spot = pl.ds(pl.multiple_of((code & 255) * BLOCK, BLOCK), BLOCK)
        flags = jnp.where(low_row, code & 256, code & 512)
        spots.append(spot)
        masks.append(key_side_ref[spot, :] == jnp.where(flags != 0, side, -1.0))
    return spots, jnp.concatenate(masks, 0)


def attend_kernel(
    count_ref, query_ref, fresh_ref, codes_ref, query_side_ref, key_side_ref,
    own_query_ref, own_kv_ref, other_ref, query_weight_ref, kv_weight_ref,
    mixed_ref, mass_ref, q_ref, kv_ref, state_ref, mixture_ref, *, pairs
):
    half_rows, half_kv = own_query_ref.shape[0], own_kv_ref.shape[0]
    q_ref[:half_rows, :] = own_query_ref[...]
    q_ref[half_rows:, :] = dot_plain(other_ref[:half_rows, :], query_weight_ref[...]).astype(jnp.bfloat16)
    kv_ref[:half_kv, :] = own_kv_ref[...]
    step = 512
    for start in range(0, half_kv, step):
        kv_ref[half_kv + start : half_kv + start + step, :] = dot_plain(
            other_ref[start : start + step, :], kv_weight_ref[...]
        ).astype(jnp.bfloat16)
    low_lanes = lax.broadcasted_iota(jnp.int32, (BLOCK, PAIR), 1) < HEAD

    def one_item(item, carry):
        query = query_ref[item]
        fresh = fresh_ref[item] == 1
        side = query_side_ref[pl.ds(query, 1), :]
        rows = pl.ds(pl.multiple_of(query * BLOCK, BLOCK), BLOCK)
        held = []
        for pair in range(pairs):
            both = two_heads(q_ref[rows, pair * PAIR : (pair + 1) * PAIR], low_lanes).astype(jnp.bfloat16)
            spots, mask = item_blocks(codes_ref, (item * pairs + pair) * SLOTS, side, key_side_ref)
            start = pair * 2 * PAIR
            keys = jnp.concatenate([kv_ref[spot, start : start + PAIR] for spot in spots], 0)
            values = jnp.concatenate([kv_ref[spot, start + PAIR : start + 2 * PAIR] for spot in spots], 0)
            held.append((jnp.where(mask, dot_cols(keys, both) * score_scale, masked_value), values))
        done = []
        for pair in range(pairs):
            scores, values = held[pair]
            place = query * pairs + pair
            state = state_ref[place]
            old_top = jnp.where(fresh, masked_value, state[0:1, :])
            top = jnp.maximum(old_top, jnp.max(scores, axis=0, keepdims=True))
            raised = jnp.exp(scores - top)
            shrunk = jnp.exp(old_top - top)
            total = jnp.where(fresh, 0.0, state[1:2, :] * shrunk) + jnp.sum(raised, axis=0, keepdims=True)
            mixture = jnp.where(fresh, 0.0, mixture_ref[place] * shrunk) + dot_rows(
                values, raised.astype(jnp.bfloat16)
            )
            done.append((top, total, mixture))
        for pair in range(pairs):
            top, total, mixture = done[pair]
            place = query * pairs + pair
            state_ref[place, 0:1, :] = top
            state_ref[place, 1:2, :] = total
            mixture_ref[place] = mixture
            normed = (mixture / total).T
            mixed_ref[rows, pair * PAIR : (pair + 1) * PAIR] = jnp.where(
                low_lanes, normed[:BLOCK], normed[BLOCK:]
            )
            mass_ref[place] = jnp.broadcast_to(top + jnp.log(total), (8, PAIR))
        return carry

    lax.fori_loop(0, count_ref[0], one_item, 0)


def attend(tables, own_query, own_kv, other, query_weight, kv_weight):
    rows, width = 2 * own_query.shape[0], own_query.shape[1]
    pairs, row_blocks = width // PAIR, rows // BLOCK
    places = pairs * row_blocks
    return local_call(
        functools.partial(attend_kernel, pairs=pairs),
        [
            shaped((rows, width)),
            shaped((places, 8, PAIR)),
            shaped((rows, width), jnp.bfloat16),
            shaped((2 * own_kv.shape[0], own_kv.shape[1]), jnp.bfloat16),
        ],
        list(tables[4:]) + [own_query, own_kv, other, query_weight, kv_weight],
        tables[:4],
        [
            pltpu.VMEM((places, 8, PAIR), jnp.float32),
            pltpu.VMEM((places, PAIR, PAIR), jnp.float32),
        ],
        flops=8e9, transcendentals=4e6, spare=12,
    )


def attend_back_kernel(
    count_ref, query_ref, fresh_ref, codes_ref, query_side_ref, key_side_ref, q_ref, kv_ref,
    mixed_ref, mass_ref, own_grad_ref, other_grad_ref, weight_ref,
    query_grad_ref, kv_grad_ref, sum_ref, grad_ref, query_sum_ref, *, pairs
):
    half_rows = own_grad_ref.shape[0]
    grad_ref[:half_rows, :] = dot_plain(own_grad_ref[...], weight_ref[...]).astype(jnp.bfloat16)
    grad_ref[half_rows:, :] = dot_plain(other_grad_ref[...], weight_ref[...]).astype(jnp.bfloat16)
    low_lanes = lax.broadcasted_iota(jnp.int32, (BLOCK, PAIR), 1) < HEAD
    sum_ref[...] = jnp.zeros_like(sum_ref)

    def one_item(item, carry):
        query = query_ref[item]
        fresh = fresh_ref[item] == 1
        side = query_side_ref[pl.ds(query, 1), :]
        rows = pl.ds(pl.multiple_of(query * BLOCK, BLOCK), BLOCK)
        held = []
        for pair in range(pairs):
            lanes = slice(pair * PAIR, (pair + 1) * PAIR)
            both = two_heads(q_ref[rows, lanes], low_lanes).astype(jnp.bfloat16)
            grads = grad_ref[rows, lanes].astype(jnp.float32)
            turned = (grads * mixed_ref[rows, lanes]).T
            inner = jnp.concatenate(
                [jnp.sum(turned[:HEAD], axis=0, keepdims=True), jnp.sum(turned[HEAD:], axis=0, keepdims=True)], 1
            )
            grads = two_heads(grads, low_lanes).astype(jnp.bfloat16)
            spots, mask = item_blocks(codes_ref, (item * pairs + pair) * SLOTS, side, key_side_ref)
            start = pair * 2 * PAIR
            kv = jnp.concatenate([kv_ref[spot, start : start + 2 * PAIR] for spot in spots], 0)
            blank = jnp.zeros_like(both)
            sides = jnp.concatenate(
                [jnp.concatenate([both, blank], 1), jnp.concatenate([blank, grads], 1)], 0
            )
            held.append((dot_cols(kv, sides), inner, sides, kv, spots, mask))
        done = []
        for pair in range(pairs):
            products, inner, sides, kv, spots, mask = held[pair]
            place = query * pairs + pair
            scores = jnp.where(mask, products[:, :PAIR] * score_scale, masked_value)
            chances = jnp.exp(scores - mass_ref[place, 0:1, :])
            score_grads = (chances * (products[:, PAIR:] - inner)).astype(jnp.bfloat16)
            query_grad = dot_rows(score_grads, kv[:, :PAIR])
            kv_grad = dot_plain(jnp.concatenate([score_grads, chances.astype(jnp.bfloat16)], 1), sides)
            done.append((query_grad, kv_grad))
        for pair in range(pairs):
            lanes = slice(pair * PAIR, (pair + 1) * PAIR)
            start = pair * 2 * PAIR
            query_grad, kv_grad = done[pair]
            spots = held[pair][4]
            query_grad = jnp.where(low_lanes, query_grad[:BLOCK], query_grad[BLOCK:])
            query_sum_ref[rows, lanes] = jnp.where(fresh, 0.0, query_sum_ref[rows, lanes]) + query_grad
            for slot, spot in enumerate(spots):
                sum_ref[spot, start : start + 2 * PAIR] += kv_grad[slot * BLOCK : (slot + 1) * BLOCK]
        return carry

    lax.fori_loop(0, count_ref[0], one_item, 0)
    query_grad_ref[...] = (query_sum_ref[...] * score_scale).astype(jnp.bfloat16)
    for pair in range(pairs):
        start = pair * 2 * PAIR
        kv_grad_ref[:, start : start + PAIR] = (sum_ref[:, start : start + PAIR] * score_scale).astype(jnp.bfloat16)
        kv_grad_ref[:, start + PAIR : start + 2 * PAIR] = sum_ref[:, start + PAIR : start + 2 * PAIR].astype(
            jnp.bfloat16
        )


def attend_back(tables, queries, kv, mixed, mass, own_grad, other_grad, weight):
    rows, width = queries.shape
    pairs = width // PAIR
    return local_call(
        functools.partial(attend_back_kernel, pairs=pairs),
        [shaped((rows, width), jnp.bfloat16), shaped(kv.shape, jnp.bfloat16)],
        list(tables[4:]) + [queries, kv, mixed, mass, own_grad, other_grad, weight],
        tables[:4],
        [
            pltpu.VMEM(kv.shape, jnp.float32),
            pltpu.VMEM((rows, width), jnp.bfloat16),
            pltpu.VMEM((rows, width), jnp.float32),
        ],
        flops=10e9, transcendentals=4e6, spare=12,
    )


LANES = 2 * PAIR


def packed_rows(slot_rows, columns):
    return columns // LANES * slot_rows + (slot_rows // 2 if columns % LANES else 0)


def put_packed(out_ref, base, source_ref, first, columns, slot_rows):
    for chunk in range(columns // LANES):
        at = first + chunk * LANES
        out_ref[base : base + slot_rows, :] = source_ref[:, at : at + LANES]
        base += slot_rows
    if columns % LANES:
        half, at = slot_rows // 2, first + columns - PAIR
        out_ref[base : base + half, :PAIR] = source_ref[:half, at : at + PAIR]
        out_ref[base : base + half, PAIR:] = source_ref[half:, at : at + PAIR]


def unpacked(packed, slot_rows):
    full = packed.shape[0] // slot_rows
    parts = [packed[at * slot_rows : (at + 1) * slot_rows] for at in range(full)]
    tail = packed[full * slot_rows :]
    if tail.shape[0]:
        parts.append(jnp.concatenate([tail[:, :PAIR], tail[:, PAIR:]], 0))
    return jnp.concatenate(parts, 1)


def start_kernel(
    tokens_ref, query_ref, key_ref, value_ref, inner_ref, outer_ref, output_ref, valid_ref,
    first_ref, second_ref, *thirds, cut
):
    columns = thirds[0].shape[1]
    for at in range(3):
        thirds[at][...] = tokens_ref[:, at * columns : (at + 1) * columns]
    width, wide = query_ref.shape[1], inner_ref.shape[1]
    for at, one in enumerate((query_ref, key_ref, value_ref)):
        first_ref[:, at * width : (at + 1) * width] = one[...]
    second_ref[:, :cut] = inner_ref[:, :cut]
    second_ref[:, cut : 2 * cut] = outer_ref[:, :cut]
    at = 2 * cut
    for one, first in ((inner_ref, cut), (outer_ref, cut), (output_ref, 0)):
        size = one.shape[1] - first
        second_ref[:, at : at + size] = one[:, first:]
        at += size
    count = jnp.sum(valid_ref[...].astype(jnp.float32), axis=1, keepdims=True)
    second_ref[:, at:] = jnp.broadcast_to(count, (second_ref.shape[0], PAIR)).astype(jnp.bfloat16)


def first_pack_kernel(*refs, slot_rows):
    sent, came, weights_ref, outs = refs[:3], refs[3:6], refs[6], refs[7:]
    rows = sent[0].shape[0]
    third = weights_ref.shape[1] // 3
    for at in range(3):
        outs[at][:rows, :] = sent[at][...]
        outs[at][rows : 2 * rows, :] = came[at][...]
        put_packed(outs[at], 2 * rows, weights_ref, at * third, third, slot_rows)


def second_pack_kernel(*refs, rows, slot_rows, cuts):
    second_ref, outs = refs[6], refs[7:]
    for at in range(3):
        sent_ref, came_ref, out_ref = refs[2 * at], refs[2 * at + 1], outs[at]
        tail = sent_ref.shape[0] - rows
        out_ref[:rows, :] = sent_ref[:rows, :]
        out_ref[rows : 2 * rows, :] = came_ref[:rows, :]
        out_ref[2 * rows : 2 * rows + tail, :] = sent_ref[rows:, :]
        out_ref[2 * rows + tail : 2 * (rows + tail), :] = came_ref[rows:, :]
        put_packed(out_ref, 2 * (rows + tail), second_ref, cuts[at], cuts[at + 1] - cuts[at], slot_rows)


def third_pack_kernel(*refs, masks, rows, tail):
    out_ref = refs[6]
    columns = refs[0].shape[1]
    for at in range(3):
        tokens = len(masks[2 * at]) * rows
        for side in range(2):
            piece, target = refs[2 * at + side], refs[7 + at]
            for slot, mask in enumerate(masks[2 * at + side]):
                out_ref[mask * rows : (mask + 1) * rows, at * columns : (at + 1) * columns] = piece[
                    slot * rows : (slot + 1) * rows, :
                ]
            target[side * tail : (side + 1) * tail, :] = piece[tokens : tokens + tail, :]
            rest = piece.shape[0] - tokens - tail
            base = 2 * tail + side * rest
            target[base : base + rest, :] = piece[tokens + tail :, :]


def fourth_pack_kernel(*refs, skip):
    for at in range(3):
        rest = refs[2 * at].shape[0] - skip
        for side in range(2):
            refs[6 + at][side * rest : (side + 1) * rest, :] = refs[2 * at + side][skip:, :]


def place_packed_kernel(owner_ref, *refs, plan, slot_rows, rows):
    pieces, outs = refs[: len(plan)], refs[len(plan) :]
    for piece, (masks, units) in zip(pieces, plan):
        size = packed_rows(slot_rows, len(units) * PAIR)
        for slot, mask in enumerate(masks):
            for far in range(2):
                lines = pl.ds(pl.multiple_of(owner_ref[mask * 2 + far] * rows, rows), rows)
                unit = 0
                while unit < len(units):
                    out, column = units[unit]
                    base = slot * size + unit // 2 * slot_rows
                    if unit + 1 == len(units) and unit % 2 == 0:
                        outs[out][lines, column : column + PAIR] = piece[
                            base : base + rows, far * PAIR : (far + 1) * PAIR
                        ]
                        unit += 1
                        continue
                    base += far * rows
                    if unit % 2 == 0 and units[unit + 1] == (out, column + PAIR):
                        outs[out][lines, column : column + LANES] = piece[base : base + rows, :]
                        unit += 2
                        continue
                    side = unit % 2 * PAIR
                    outs[out][lines, column : column + PAIR] = piece[base : base + rows, side : side + PAIR]
                    unit += 1


def place_packed(owner, pieces, plan, widths, rows):
    blocks = owner.shape[0]
    far_count = blocks // 8
    slot_rows = far_count * rows
    outs = [shaped((blocks * rows, width), jnp.bfloat16) for width in widths]
    if rows % 16 == 0 and far_count == 2:
        kernel = functools.partial(place_packed_kernel, plan=plan, slot_rows=slot_rows, rows=rows)
        return local_call(kernel, outs, pieces, [owner], spare=12)
    made = [jnp.zeros(out.shape, out.dtype) for out in outs]
    for piece, (masks, units) in zip(pieces, plan):
        size = packed_rows(slot_rows, len(units) * PAIR)
        for slot, mask in enumerate(masks):
            block = unpacked(piece[slot * size : (slot + 1) * size], slot_rows)
            lines = owner.reshape(8, far_count)[mask][:, None] * rows + jnp.arange(rows, dtype=jnp.int32)
            for unit, (out, column) in enumerate(units):
                made[out] = made[out].at[lines.reshape(-1), column : column + PAIR].set(
                    block[:, unit * PAIR : (unit + 1) * PAIR]
                )
    return made


def units_of(targets):
    return tuple((out, column + at) for out, column, size in targets for at in range(0, size, PAIR))


def placed_blocks(grad, owner, masks):
    blocks = owner.shape[0]
    rows = grad.shape[0] // blocks
    spots = owner.reshape(8, -1)[jnp.array(masks)].reshape(-1)
    return jnp.take(grad.reshape(blocks, rows, grad.shape[1]), spots, axis=0)


def token_kernel(x_ref, query_weight_ref, kv_weight_ref, query_ref, kv_ref):
    rows = query_ref.shape[0]
    query_ref[...] = dot_plain(x_ref[:rows, :], query_weight_ref[...]).astype(jnp.bfloat16)
    step = 512
    for start in range(0, kv_ref.shape[0], step):
        kv_ref[start : start + step, :] = dot_plain(x_ref[start : start + step, :], kv_weight_ref[...]).astype(
            jnp.bfloat16
        )


def project_kernel(mixed_ref, weight_ref, counts_ref, own_ref, other_ref, low_ref, count_ref, *, each):
    count = jnp.sum(counts_ref[...].astype(jnp.float32), axis=0, keepdims=True) / each
    count_ref[...] = jnp.broadcast_to(count, count_ref.shape)
    low = mixed_ref[...].astype(jnp.bfloat16)
    low_ref[...] = low
    total = dot_cols(low, weight_ref[...])
    half = own_ref.shape[0]
    own_ref[...] = total[:half]
    other_ref[...] = total[half:].astype(jnp.bfloat16)


def normed_rows(values):
    centred = values - jnp.mean(values, axis=-1, keepdims=True)
    spread = jnp.mean(centred * centred, axis=-1, keepdims=True)
    scale = lax.rsqrt(spread + epsilon)
    return centred * scale, scale


def norm_back(grads, normed, scale, gain):
    inner = grads * gain
    middle = jnp.mean(inner, axis=-1, keepdims=True)
    slant = jnp.mean(inner * normed, axis=-1, keepdims=True)
    return scale * (inner - middle - normed * slant)


def first_norm_kernel(tokens_ref, own_ref, came_ref, gain_ref, shift_ref, sum_ref, hidden_ref, low_ref):
    total = tokens_ref[...].astype(jnp.float32) + (own_ref[...] + came_ref[...].astype(jnp.float32))
    sum_ref[...] = total
    normed, _ = normed_rows(total)
    hidden = normed * gain_ref[...] + shift_ref[...]
    hidden_ref[...] = hidden
    low_ref[...] = hidden.astype(jnp.bfloat16)


def feed_kernel(own_hidden_ref, other_hidden_ref, inner_ref, outer_ref, own_ref, other_ref, active_ref, slope_ref, total_ref):
    hidden = jnp.concatenate([own_hidden_ref[...], other_hidden_ref[...]], 0)
    step = 256
    for start in range(0, inner_ref.shape[1], step):
        columns = slice(start, start + step)
        upper = dot_plain(hidden, inner_ref[:, columns])
        chance = 0.5 * (1.0 + lax.erf(upper * (0.5**0.5)))
        active = (upper * chance).astype(jnp.bfloat16)
        active_ref[:, columns] = active
        slope_ref[:, columns] = chance + upper * (jnp.exp(-0.5 * upper * upper) * 0.3989422804014327)
        part = dot_cols(active, outer_ref[:, columns])
        if start:
            total_ref[...] += part
        else:
            total_ref[...] = part
    half = own_ref.shape[0]
    own_ref[...] = total_ref[:half, :]
    other_ref[...] = total_ref[half:, :].astype(jnp.bfloat16)


def second_norm_kernel(
    hidden_ref, own_ref, came_ref, gain_ref, shift_ref, teacher_ref, valid_ref, count_own_ref, count_came_ref,
    result_ref, grad_ref, low_ref, stats_ref, *, token_total
):
    valid = jnp.broadcast_to(valid_ref[...].astype(jnp.float32), (PAIR, valid_ref.shape[1])).T[:, :1]
    factor = token_total / (count_own_ref[0:1, 0:1] + count_came_ref[0:1, 0:1])
    total = hidden_ref[...] + (own_ref[...] + came_ref[...].astype(jnp.float32))
    normed, scale = normed_rows(total)
    gain = gain_ref[...]
    result = normed * gain + shift_ref[...]
    result_ref[...] = result.astype(jnp.bfloat16)
    errors = (result - teacher_ref[...].astype(jnp.float32)) * valid
    grads = errors * factor
    grad = norm_back(grads, normed, scale, gain)
    grad_ref[...] = grad
    low_ref[...] = grad.astype(jnp.bfloat16)
    stats_ref[...] = jnp.zeros_like(stats_ref)
    stats_ref[0:1, :] = jnp.sum(grads * normed, axis=0, keepdims=True)
    stats_ref[1:2, :] = jnp.sum(grads, axis=0, keepdims=True)
    squares = jnp.sum(jnp.sum(errors * errors, axis=0, keepdims=True), axis=1, keepdims=True)
    stats_ref[2:3, :] = jnp.broadcast_to(squares, (1, stats_ref.shape[1]))


def feed_back_kernel(own_grad_ref, other_grad_ref, slope_ref, inner_ref, outer_ref, upper_ref, own_ref, other_ref, total_ref):
    grads = jnp.concatenate([own_grad_ref[...], other_grad_ref[...]], 0)
    step = 256
    for start in range(0, inner_ref.shape[1], step):
        columns = slice(start, start + step)
        upper = (dot_plain(grads, outer_ref[:, columns]) * slope_ref[:, columns]).astype(jnp.bfloat16)
        upper_ref[:, columns] = upper
        part = dot_cols(upper, inner_ref[:, columns])
        if start:
            total_ref[...] += part
        else:
            total_ref[...] = part
    half = own_ref.shape[0]
    own_ref[...] = total_ref[:half, :]
    other_ref[...] = total_ref[half:, :].astype(jnp.bfloat16)


def first_back_kernel(grad_ref, own_ref, came_ref, sum_ref, gain_ref, out_ref, low_ref, stats_ref):
    grads = grad_ref[...] + (own_ref[...] + came_ref[...].astype(jnp.float32))
    normed, scale = normed_rows(sum_ref[...])
    grad = norm_back(grads, normed, scale, gain_ref[...])
    out_ref[...] = grad
    low_ref[...] = grad.astype(jnp.bfloat16)
    stats_ref[...] = jnp.zeros_like(stats_ref)
    stats_ref[0:1, :] = jnp.sum(grads * normed, axis=0, keepdims=True)
    stats_ref[1:2, :] = jnp.sum(grads, axis=0, keepdims=True)


def write_blocks(owner_ref, made_ref, column, width, out_ref, out_column, masks, far_count, rows):
    for slot, mask in enumerate(masks):
        for far in range(far_count):
            start = pl.multiple_of(owner_ref[mask * far_count + far] * rows, rows)
            out_ref[slot * far_count + far, :, out_column : out_column + width] = made_ref[
                pl.ds(start, rows), column : column + width
            ].astype(out_ref.dtype)


def wide_kernel(
    owner_ref, own_grad_ref, other_grad_ref, active_ref, own_hidden_ref, other_hidden_ref, upper_ref, *refs,
    groups, far_count, rows, step
):
    outs, made_ref = refs[:-1], refs[-1]
    grads = jnp.concatenate([own_grad_ref[...], other_grad_ref[...]], 0)
    hidden = jnp.concatenate([own_hidden_ref[...], other_hidden_ref[...]], 0)
    width = active_ref.shape[1]
    third_width = 2 * width // 3
    for start in range(0, 2 * width, step):
        if start < width:
            made_ref[...] = dot_rows(grads, active_ref[:, start : start + step])
        else:
            made_ref[...] = dot_rows(hidden, upper_ref[:, start - width : start - width + step])
        third = start // third_width
        for at, masks in enumerate(groups[third]):
            write_blocks(
                owner_ref, made_ref, 0, step, outs[third * len(groups[third]) + at], start % third_width,
                masks, far_count, rows
            )


def wide_gradients(owner, own_grad, other_grad, active, own_hidden, other_hidden, upper, groups):
    blocks = owner.shape[0]
    far_count, rows = blocks // 8, own_grad.shape[1] // blocks
    width = active.shape[1]
    third_width = 2 * width // 3
    if rows % 16:
        made = jnp.concatenate(
            [
                dot_rows(jnp.concatenate([own_grad, other_grad], 0), active),
                dot_rows(jnp.concatenate([own_hidden, other_hidden], 0), upper),
            ],
            1,
        )
        outs = []
        for third, group in enumerate(groups):
            columns = made[:, third * third_width : (third + 1) * third_width]
            for at, masks in enumerate(group):
                outs.append(placed_blocks(columns, owner, masks).astype(jnp.bfloat16 if at else jnp.float32))
        return outs
    step = 512
    outs = []
    for group in groups:
        for at, masks in enumerate(group):
            outs.append(
                shaped((len(masks) * far_count, rows, third_width), jnp.bfloat16 if at else jnp.float32)
            )
    kernel = functools.partial(wide_kernel, groups=groups, far_count=far_count, rows=rows, step=step)
    return local_call(
        kernel, outs, [own_grad, other_grad, active, own_hidden, other_hidden, upper], [owner],
        [pltpu.VMEM((own_grad.shape[1], step), jnp.float32)],
        flops=8 * own_grad.size * width, spare=12,
    )


def narrow_kernel(
    own_ref, other_ref, kv_grad_ref, query_grad_ref, own_grad_ref, other_grad_ref, low_ref, made_ref
):
    half, near = own_ref.shape[0], own_grad_ref.shape[0]
    width = query_grad_ref.shape[1]
    made_ref[:, :width] = dot_rows(own_ref[:near, :], query_grad_ref[:near, :]) + dot_rows(
        other_ref[:near, :], query_grad_ref[near:, :]
    )
    made_ref[:, width : 2 * width] = dot_rows(own_grad_ref[...], low_ref[:near, :]) + dot_rows(
        other_grad_ref[...], low_ref[near:, :]
    )
    made_ref[:, 2 * width :] = dot_rows(own_ref[...], kv_grad_ref[:half, :])
    made_ref[:, 2 * width :] += dot_rows(other_ref[...], kv_grad_ref[half:, :])


def narrow_gradients(own, other, kv_grad, query_grad, own_grad, other_grad, low):
    width = query_grad.shape[1]
    return local_call(
        narrow_kernel, [shaped((own.shape[1], 4 * width))],
        [own, other, kv_grad, query_grad, own_grad, other_grad, low],
        flops=4 * own.size * 2 * width + 8 * own_grad.size * width, spare=12,
    )[0]


def token_other_kernel(kv_grad_ref, query_grad_ref, kv_weight_ref, query_weight_ref, out_ref):
    near, half = query_grad_ref.shape[0] // 2, kv_grad_ref.shape[0] // 2
    for start in range(0, half, near):
        total = dot_cols(kv_grad_ref[half + start : half + start + near, :], kv_weight_ref[...])
        if start == 0:
            total += dot_cols(query_grad_ref[near:, :], query_weight_ref[...])
        out_ref[start : start + near, :] = total.astype(jnp.bfloat16)


def token_other(kv_grad, query_grad, kv_weight, query_weight):
    return local_call(
        token_other_kernel, [shaped((kv_grad.shape[0] // 2, kv_weight.shape[0]), jnp.bfloat16)],
        [kv_grad, query_grad, kv_weight, query_weight],
        flops=kv_grad.size * kv_weight.shape[0], spare=12,
    )[0]


def small_kernel(own_one_ref, came_one_ref, own_two_ref, came_two_ref, out_ref):
    one = own_one_ref[...] + came_one_ref[...]
    two = own_two_ref[...] + came_two_ref[...]
    lines = jnp.concatenate([one[:2], two[:3], jnp.zeros((PAIR - 5, one.shape[1]), jnp.float32)], 0)
    out_ref[...] = lines.T


def token_own_kernel(
    owner_ref, kv_grad_ref, query_grad_ref, kv_weight_ref, query_weight_ref, came_ref, made_ref, small_ref, *outs,
    masks, rows, placed
):
    near = query_grad_ref.shape[0] // 2
    half, columns = outs[0].shape[0], outs[0].shape[2]
    slot_rows = made_ref.shape[1] if placed else made_ref.shape[0] // (2 * half)
    for mask in range(2 * half):
        lines = slice(mask * near, (mask + 1) * near)
        total = dot_cols(kv_grad_ref[lines, :], kv_weight_ref[...]) + came_ref[lines, :].astype(jnp.float32)
        if mask == 0:
            total += dot_cols(query_grad_ref[:near, :], query_weight_ref[...])
        for third, order in enumerate(masks):
            slot = order.index(mask)
            out_ref = outs[2 * third + slot // half]
            at = slot % half
            out_ref[at, :near, :] = total[:, third * columns : (third + 1) * columns].astype(out_ref.dtype)
            for side in range(2):
                base = near + side * slot_rows
                part = slice((2 * third + side) * columns, (2 * third + side + 1) * columns)
                if placed:
                    out_ref[at, base : base + slot_rows, :] = made_ref[mask, :, part].astype(out_ref.dtype)
                    continue
                for far in range(slot_rows // rows):
                    start = pl.multiple_of(owner_ref[mask * (slot_rows // rows) + far] * rows, rows)
                    out_ref[at, base + far * rows : base + (far + 1) * rows, :] = made_ref[
                        pl.ds(start, rows), part
                    ].astype(out_ref.dtype)
            if third == 0:
                if placed:
                    small = small_ref[mask]
                else:
                    far_count = slot_rows // rows
                    small = jnp.concatenate(
                        [
                            small_ref[pl.ds(pl.multiple_of(owner_ref[mask * far_count + far] * rows, rows), rows), :]
                            for far in range(far_count)
                        ],
                        0,
                    )
                small = jnp.concatenate([small[: slot_rows // 2], small[slot_rows // 2 :]], 1)
                if slot >= half:
                    small = in_pieces(small)
                out_ref[at, near + 2 * slot_rows :, :] = small.astype(out_ref.dtype)


def token_own(owner, kv_grad, query_grad, kv_weight, query_weight, came, made, small, masks):
    near = query_grad.shape[0] // 2
    half = came.shape[0] // near // 2
    blocks, features = owner.shape[0], made.shape[0]
    rows, slot_rows = features // blocks, features // (2 * half)
    columns = kv_weight.shape[0] // 3
    placed = rows % 16 != 0
    if placed:
        made, small = (
            placed_blocks(one, owner, tuple(range(2 * half))).reshape(2 * half, slot_rows, one.shape[1])
            for one in (made, small)
        )
    outs = []
    for third in range(len(masks)):
        shape = (half, near + 2 * slot_rows + (slot_rows // 2 if third == 0 else 0), columns)
        outs += [shaped(shape), shaped(shape, jnp.bfloat16)]
    outs = local_call(
        functools.partial(token_own_kernel, masks=masks, rows=rows, placed=placed), outs,
        [kv_grad, query_grad, kv_weight, query_weight, came, made, small], [owner],
        flops=2 * came.shape[0] * kv_weight.size, spare=12,
    )
    return list(outs[::2]), list(outs[1::2])


def last_kernel(grad_ref, *refs):
    token_ref, made_ref, small_ref = refs[-3:]
    near, columns = grad_ref.shape[0], refs[0].shape[2]
    slot_rows = made_ref.shape[0]
    for third in range(3):
        plain = near + 2 * slot_rows
        total = refs[2 * third][0, :plain] + refs[2 * third + 1][0, :plain].astype(jnp.float32)
        if third == 0:
            small = refs[0][0, plain:] + from_pieces(refs[1][0, plain:].astype(jnp.float32))
            small_ref[: slot_rows // 2, :] = small[:, :PAIR]
            small_ref[slot_rows // 2 :, :] = small[:, PAIR:]
        part = slice(third * columns, (third + 1) * columns)
        token_ref[:, part] = grad_ref[:, part] + total[:near]
        for side in range(2):
            at = (2 * third + side) * columns
            made_ref[:, at : at + columns] = total[near + side * slot_rows : near + (side + 1) * slot_rows]


def wide_end_kernel(*refs):
    out_ref = refs[-1]
    columns = refs[0].shape[2]
    for third in range(3):
        out_ref[:, third * columns : (third + 1) * columns] = refs[2 * third][0] + refs[2 * third + 1][0].astype(
            jnp.float32
        )


def tie(first, second):
    leaves, tree = jax.tree.flatten(second)
    tied = lax.optimization_barrier(tuple(leaves) + (first,))
    return jax.tree.unflatten(tree, tied[:-1])


def shards(
    tokens,
    query_weight,
    key_weight,
    value_weight,
    output_weight,
    inner_weight,
    outer_weight,
    attn_gain,
    attn_shift,
    ffn_gain,
    ffn_shift,
    teacher,
    segments,
    random_blocks,
    valid_tokens,
):
    devices = lax.axis_size("dp")
    dp_index = lax.axis_index("dp")
    core = lax.axis_index("tensor")
    rows, width = tokens.shape
    length = 2 * rows
    span = segments.shape[1] // length
    near_bits = span.bit_length() - 1
    far_bits = tuple(range(near_bits, devices.bit_length() - 1))
    place, far_place = dp_index % span, dp_index // span
    far_count = devices // span
    each = width // devices
    slot_rows = far_count * each
    head_width = query_weight.shape[1]
    wide = inner_weight.shape[1]
    masks = jnp.arange(span, dtype=jnp.int32)
    fars = jnp.arange(far_count, dtype=jnp.int32)
    owner = ((fars[None, :] ^ far_place) * span + (masks[:, None] ^ place)).reshape(-1)

    def far_gather(block):
        held = block[None]
        for bit in far_bits:
            held = jnp.concatenate([held, swap_mask(held, 1 << bit)], 0)
        return held.reshape(slot_rows, block.shape[1])

    def step(held, at):
        return [swap_mask(one, 1 << bits[at]) for one, bits in zip(held, ROUTES)]

    def both(held, came):
        return [one for pair in zip(held, came) for one in pair]

    def messages(lines):
        return [shaped((one, third), jnp.bfloat16) for one in lines]

    third = width // 3
    cut = 3 * wide // 4
    tail = packed_rows(slot_rows, head_width)
    rest = (cut, cut, 2 * (wide - cut) + head_width + PAIR)
    cuts = (0, cut, 2 * cut, 2 * cut + rest[2])
    sizes = [packed_rows(slot_rows, one) for one in rest]
    valid_row = valid_tokens.reshape(1, rows)
    first, second, *held = local_call(
        functools.partial(start_kernel, cut=cut),
        [shaped((each, 3 * head_width), jnp.bfloat16), shaped((each, cuts[3]), jnp.bfloat16)]
        + [shaped((rows, third), jnp.bfloat16)] * 3,
        [tokens, query_weight, key_weight, value_weight, inner_weight, outer_weight, output_weight, valid_row],
    )
    came = step(held, 0)
    first_held, second_held = far_gather(first), far_gather(second)
    held = local_call(
        functools.partial(first_pack_kernel, slot_rows=slot_rows), messages([2 * rows + tail] * 3),
        held + came + [first_held],
    )
    came = step(held, 1)
    held = local_call(
        functools.partial(second_pack_kernel, rows=2 * rows, slot_rows=slot_rows, cuts=cuts),
        messages([4 * rows + 2 * tail + size for size in sizes]), both(held, came) + [second_held],
    )
    came = step(held, 2)
    segment_all = lax.dynamic_index_in_dim(segments, far_place, 0, keepdims=False)
    tables = attention_tables(random_blocks, segment_all, place, core, span, length // BLOCK)
    tables, owner, came = lax.optimization_barrier((tables, owner, came))
    sent_masks = [tuple(slot_masks(bits[:2])) for bits in ROUTES]
    came_masks = [tuple(mask ^ (1 << bits[2]) for mask in sent) for sent, bits in zip(sent_masks, ROUTES)]
    own, *held = local_call(
        functools.partial(third_pack_kernel, masks=tuple(both(sent_masks, came_masks)), rows=rows, tail=2 * tail),
        [shaped((span * rows, width), jnp.bfloat16)] + messages([4 * tail + 2 * size for size in sizes]),
        both(held, came),
    )
    came = step(held, 0)
    other = swap_core(own)
    late = local_call(
        functools.partial(fourth_pack_kernel, skip=4 * tail), messages([4 * size for size in sizes]),
        both(held, came),
    )
    late_came = step(late, 1)

    held, came = tie(late[0], (held, came))
    plan = []
    for bits, units in zip(
        ROUTES,
        [((0, 0, head_width),)]
        + [tuple((1, 2 * at + shift, PAIR) for at in range(0, head_width, PAIR)) for shift in (0, PAIR)],
    ):
        sent = tuple(slot_masks((bits[1], bits[2])))
        plan += [(sent, units_of(units)), (tuple(mask ^ (1 << bits[0]) for mask in sent), units_of(units))]
    full_query, full_kv = place_packed(
        owner, both(held, came), tuple(plan), (head_width, 2 * head_width), each
    )
    own_query, own_kv = local_call(
        token_kernel, [shaped((rows, head_width), jnp.bfloat16), shaped((span * rows, 2 * head_width), jnp.bfloat16)],
        [own, full_query, full_kv], flops=4 * own.size * head_width, spare=12,
    )
    mixed, mass, queries, kv = attend(tables, own_query, own_kv, other, full_query, full_kv)

    late, late_came = tie(mixed, (late, late_came))
    plan = []
    for bits, units in zip(
        ROUTES,
        (
            ((0, 0, cut),),
            ((1, 0, cut),),
            ((0, cut, wide - cut), (1, cut, wide - cut), (2, 0, head_width), (3, 0, PAIR)),
        ),
    ):
        sent = tuple(slot_masks((bits[2], bits[0])))
        plan += [(sent, units_of(units)), (tuple(mask ^ (1 << bits[1]) for mask in sent), units_of(units))]
    full_inner, full_outer, full_output, counts = place_packed(
        owner, both(late, late_came), tuple(plan), (wide, wide, head_width, PAIR), each
    )

    half_shape, low_shape = shaped((rows, width)), shaped((rows, width), jnp.bfloat16)
    gain_one, shift_one, gain_two, shift_two = (
        one.reshape(1, width) for one in (attn_gain, attn_shift, ffn_gain, ffn_shift)
    )
    count_shape = shaped((8, PAIR))
    part_own, part_other, attended, count_own = local_call(
        functools.partial(project_kernel, each=each),
        [half_shape, low_shape, shaped(mixed.shape, jnp.bfloat16), count_shape], [mixed, full_output, counts],
        flops=2 * mixed.size * width,
    )
    count_came = swap_core(count_own)
    first_sum, hidden, hidden_own = local_call(
        first_norm_kernel, [half_shape, half_shape, low_shape],
        [tokens, part_own, swap_core(part_other), gain_one, shift_one],
    )
    hidden_other = swap_core(hidden_own)
    part_own, part_other, active, slope = local_call(
        feed_kernel,
        [half_shape, low_shape, shaped((length, wide), jnp.bfloat16), shaped((length, wide))],
        [hidden_own, hidden_other, full_inner, full_outer],
        scratch=[pltpu.VMEM((length, width), jnp.float32)],
        flops=4 * length * width * wide, transcendentals=2 * length * wide, spare=12,
    )
    token_total = devices * lax.axis_size("tensor") * rows
    result, grad_second, grad_ffn_own, stats_two = local_call(
        functools.partial(second_norm_kernel, token_total=token_total),
        [low_shape, half_shape, low_shape, shaped((8, width))],
        [hidden, part_own, swap_core(part_other), gain_two, shift_two, teacher, valid_row, count_own, count_came],
    )
    grad_ffn_other = swap_core(grad_ffn_own)
    upper_grad, part_own, part_other = local_call(
        feed_back_kernel, [shaped((length, wide), jnp.bfloat16), half_shape, low_shape],
        [grad_ffn_own, grad_ffn_other, slope, full_inner, full_outer],
        scratch=[pltpu.VMEM((length, width), jnp.float32)],
        flops=4 * length * width * wide, spare=12,
    )
    part_came = swap_core(part_other)
    scatter_masks = tuple(tuple(slot_masks(bits[::-1])) for bits in ROUTES)
    groups = tuple((one[: span // 2], one[span // 2 :]) for one in scatter_masks)
    outs = wide_gradients(
        owner, grad_ffn_own, grad_ffn_other, active, hidden_own, hidden_other, upper_grad, groups
    )
    outs = [one.reshape(span // 2, slot_rows, one.shape[2]) for one in outs]
    wide_keep, wide_came = outs[::2], step(outs[1::2], 0)
    part_came = tie(outs[0], part_came)
    grad_first, grad_attn_own, stats_one = local_call(
        first_back_kernel, [half_shape, low_shape, shaped((8, width))],
        [grad_second, part_own, part_came, first_sum, gain_one],
    )
    grad_attn_other = swap_core(grad_attn_own)
    stats_one_came, stats_two_came = swap_core(stats_one), swap_core(stats_two)
    query_grad, kv_grad = attend_back(
        tables, queries, kv, mixed, mass, grad_attn_own, grad_attn_other, full_output
    )

    def folded(keep, came):
        return fold(keep, [[one] for one in came])

    wide_keep, wide_send = folded(wide_keep, tie(query_grad, wide_came))
    wide_came = step(wide_send, 1)
    token_sent = token_other(tie(wide_keep[0], kv_grad), query_grad, full_kv, full_query)
    token_came = swap_core(token_sent)
    made = narrow_gradients(
        own, other, tie(token_sent, kv_grad), query_grad, grad_attn_own, grad_attn_other, attended
    )
    small = local_call(
        small_kernel, [shaped((width, PAIR))], [stats_one, stats_one_came, tie(made, stats_two), stats_two_came]
    )[0]
    wide_keep, wide_send = folded(wide_keep, tie(small, wide_came))
    wide_came = step(wide_send, 2)
    keep, send = token_own(
        owner, kv_grad, query_grad, full_kv, full_query, tie(wide_keep[0], token_came), made, small,
        scatter_masks
    )
    came = step(send, 0)
    wide_sum = local_call(
        wide_end_kernel, [shaped((slot_rows, 2 * wide))], both(wide_keep, tie(keep[0], wide_came))
    )[0]

    def far_scatter(total, dtype=jnp.bfloat16):
        total = total.reshape(far_count, each, total.shape[1])
        for bit in far_bits[::-1]:
            half = total.shape[0] // 2
            total = total[:half] + swap_mask(total[half:].astype(dtype), 1 << bit).astype(jnp.float32)
        return total[0]

    wide_sum = far_scatter(wide_sum)
    part_outer, part_inner = wide_sum[:, :wide], wide_sum[:, wide:]
    plain = rows + 2 * slot_rows
    keep, send = fold(keep, [[one] for one in came], plain)
    came = step(send, 1)
    keep, send = fold(keep, [[one] for one in came], plain)
    came = step(send, 2)
    grad_tokens, narrow_sum, small = local_call(
        last_kernel, [half_shape, shaped((slot_rows, 4 * head_width)), shaped((slot_rows, PAIR))],
        [grad_first] + both(keep, came),
    )
    narrow_sum, small = far_scatter(narrow_sum), far_scatter(small, jnp.float32)

    loss_value = small[0, 4] / (2.0 * width * (count_own[0, 0] + count_came[0, 0]))
    half = each // 2
    mine = jnp.where(core == 0, small[:half], small[half:])
    part_query, part_output = narrow_sum[:, :head_width], narrow_sum[:, head_width : 2 * head_width]
    kv_sum = narrow_sum[:, 2 * head_width :]
    pairs = head_width // PAIR
    part_key = jnp.concatenate([kv_sum[:, 2 * pair * PAIR : (2 * pair + 1) * PAIR] for pair in range(pairs)], 1)
    part_value = jnp.concatenate(
        [kv_sum[:, (2 * pair + 1) * PAIR : (2 * pair + 2) * PAIR] for pair in range(pairs)], 1
    )
    return (
        result,
        loss_value,
        grad_tokens,
        part_query,
        part_key,
        part_value,
        part_output,
        part_inner,
        part_outer,
        mine[:, 0],
        mine[:, 1],
        mine[:, 2],
        mine[:, 3],
    )


def solution(mesh):
    both = P(("dp", "tensor"))
    rows_spec = P(("dp", "tensor"), None)
    weight_spec = P("dp", "tensor")
    in_specs = (rows_spec,) + (weight_spec,) * 6 + (P(),) * 4
    in_specs += (rows_spec, P(), P("tensor", None, None), both)
    out_specs = (rows_spec, P(), rows_spec) + (weight_spec,) * 6 + (both,) * 4
    return jax.shard_map(shards, mesh=mesh, in_specs=in_specs, out_specs=out_specs, check_vma=False)
```

```python
import functools

import jax
import jax.numpy as jnp
from jax import lax
from jax.experimental import pallas as pl
from jax.experimental.pallas import tpu as pltpu
from jax.sharding import PartitionSpec as P

BLOCK = 64
HEAD = 64
PAIR = 2 * HEAD
SLOTS = 6
ROUTES = ((0, 1, 2), (1, 2, 0), (2, 0, 1))

epsilon = 1e-05
masked_value = -1e30
score_scale = 0.125


def swap_mask(block, mask):
    count = lax.axis_size("dp")
    return lax.ppermute(block, "dp", [(one, one ^ mask) for one in range(count)])


def swap_core(block):
    return lax.ppermute(block, "tensor", [(0, 1), (1, 0)])


def dot_plain(left_side, right_side):
    return jnp.dot(left_side, right_side, preferred_element_type=jnp.float32)


def dot_cols(left_side, right_side):
    return lax.dot_general(
        left_side, right_side, (((1,), (1,)), ((), ())), preferred_element_type=jnp.float32
    )


def dot_rows(left_side, right_side):
    return lax.dot_general(
        left_side, right_side, (((0,), (0,)), ((), ())), preferred_element_type=jnp.float32
    )


def params(megabytes):
    return pltpu.CompilerParams(vmem_limit_bytes=int(megabytes) << 20)


def cost(flops=0, moved=0, transcendentals=0):
    return pl.CostEstimate(flops=int(flops), bytes_accessed=int(moved), transcendentals=int(transcendentals))


def in_vmem(count):
    return [pl.BlockSpec(memory_space=pltpu.VMEM)] * count


def in_smem(count):
    return [pl.BlockSpec(memory_space=pltpu.SMEM)] * count


def shaped(shape, dtype=jnp.float32):
    return jax.ShapeDtypeStruct(tuple(shape), dtype)


def local_call(kernel, outs, vmem_inputs, smem_inputs=(), scratch=(), flops=0, transcendentals=0, spare=8, free=0):
    moved = sum(one.size * one.dtype.itemsize for one in list(vmem_inputs) + list(outs))
    held = sum(one.size * one.dtype.itemsize for one in (shaped(s.shape, s.dtype) for s in scratch))
    held = held // (1 << 20) + 1 + spare
    return pl.pallas_call(
        kernel,
        out_shape=tuple(
            one if len(outs) - at <= free else pltpu.VMEM(one.shape, one.dtype) for at, one in enumerate(outs)
        ),
        in_specs=in_smem(len(smem_inputs)) + in_vmem(len(vmem_inputs)),
        out_specs=tuple(in_vmem(len(outs))),
        scratch_shapes=list(scratch),
        compiler_params=params(held),
        cost_estimate=pl.CostEstimate(flops=1000, bytes_accessed=1000, transcendentals=0),
    )(*smem_inputs, *[pltpu.with_memory_space_constraint(one, pltpu.VMEM) for one in vmem_inputs])


def slot_masks(bits):
    return [
        sum(((slot >> at) & 1) << bit for at, bit in enumerate(bits))
        for slot in range(1 << len(bits))
    ]


def in_pieces(values):
    high = values.astype(jnp.bfloat16).astype(jnp.float32)
    middle = (values - high).astype(jnp.bfloat16).astype(jnp.float32)
    return high + pltpu.roll(middle, 8, 1) + pltpu.roll(values - high - middle, 16, 1)


def from_pieces(pieces):
    lanes = pieces.shape[1]
    total = pieces + pltpu.roll(pieces, lanes - 8, 1) + pltpu.roll(pieces, lanes - 16, 1)
    return jnp.where(lax.broadcasted_iota(jnp.int32, pieces.shape, 1) % PAIR < 8, total, 0.0)


def fold_kernel(*refs, thirds, arrivals, plain):
    outs = refs[thirds * (1 + arrivals) :]
    for third in range(thirds):
        keep_ref = refs[third * (1 + arrivals)]
        came = refs[third * (1 + arrivals) + 1 : (third + 1) * (1 + arrivals)]
        half, lines = keep_ref.shape[0] // 2, keep_ref.shape[1]
        most = lines if plain is None else min(plain, lines)
        for side in range(2):
            part = slice(side * half, (side + 1) * half)
            total = sum([one[part, :most].astype(jnp.float32) for one in came], keep_ref[part, :most])
            out_ref = outs[2 * third + side]
            out_ref[:, :most] = total.astype(out_ref.dtype)
            if most == lines:
                continue
            for at in range(half):
                total = keep_ref[side * half + at, most:]
                for one in came:
                    total += from_pieces(one[side * half + at, most:].astype(jnp.float32))
                out_ref[at, most:] = (in_pieces(total) if side else total).astype(out_ref.dtype)


def fold(keeps, arrivals, plain=None):
    outs = []
    for keep in keeps:
        half = (keep.shape[0] // 2,) + keep.shape[1:]
        outs += [shaped(half), shaped(half, jnp.bfloat16)]
    operands = []
    for keep, came in zip(keeps, arrivals):
        operands += [keep] + list(came)
    kernel = functools.partial(fold_kernel, thirds=len(keeps), arrivals=len(arrivals[0]), plain=plain)
    outs = local_call(kernel, outs, operands)
    return list(outs[::2]), list(outs[1::2])


def pick(chosen, table):
    return lax.dot_general(
        chosen.astype(jnp.bfloat16), table.astype(jnp.bfloat16), (((chosen.ndim - 1,), (0,)), ((), ())),
        preferred_element_type=jnp.float32,
    )


def attention_tables(random_blocks, segment_all, place, core, span, row_blocks):
    heads, blocks, draws = random_blocks.shape
    half, pairs = row_blocks // 2, heads // 2
    local = jnp.arange(row_blocks, dtype=jnp.int32)
    owner = jnp.where(local < half, core, 1 - core)
    absolute = place * row_blocks + owner * half + local % half
    every = jnp.arange(blocks, dtype=jnp.int32)
    mine = absolute[:, None] == every
    edge = (every == 0) | (every == blocks - 1)
    fixed = (jnp.abs(absolute[:, None] - every) <= 1) | edge | edge[absolute][:, None]
    segment_table = segment_all.reshape(blocks, BLOCK).astype(jnp.float32)
    low, high = jnp.min(segment_table, 1), jnp.max(segment_table, 1)
    reach = (jnp.max(jnp.where(mine, low, -1.0), 1)[:, None] <= high) & (
        low <= jnp.max(jnp.where(mine, high, -1.0), 1)[:, None]
    )
    drawn = pick(mine, random_blocks.transpose(1, 0, 2).reshape(blocks, heads * draws))
    drawn = drawn.reshape(row_blocks, heads, draws, 1) == every.astype(jnp.float32)
    allowed = (jnp.any(drawn, 2) | fixed[:, None]) & reach[:, None]
    allowed = allowed.reshape(row_blocks, pairs, 2, blocks)
    listed = jnp.any(allowed, 2)
    rank = pick(listed, every[:, None] < every[None, :])
    count = jnp.max(jnp.sum(listed.astype(jnp.int32), -1), -1)
    chunks = -(-count // SLOTS)
    ends = jnp.sum(jnp.where(local[:, None] >= local[None, :], chunks[None, :], 0), 1)
    most = (row_blocks - 1) * -(-min(blocks, 5 + 2 * draws) // SLOTS) + -(-blocks // SLOTS)
    if span == 1:
        most += -(-blocks // SLOTS)
    items = jnp.arange(most, dtype=jnp.int32)
    item_query = jnp.minimum(jnp.sum((items[:, None] >= ends[None, :]).astype(jnp.int32), 1), row_blocks - 1)
    item_is = item_query[:, None] == local
    first = jnp.sum(jnp.where(item_is, (ends - chunks)[None, :], 0), 1)
    spots = ((items - first) * SLOTS)[:, None] + jnp.arange(SLOTS, dtype=jnp.int32)
    stored = (
        jnp.where((every % row_blocks) // half == core, 0, span * half)
        + ((every // row_blocks) ^ place) * half + every % half
    )
    rows = jnp.concatenate([jnp.where(listed, rank, -1.0)[:, :, None], allowed.astype(jnp.float32)], 2)
    rows = pick(item_is, rows.reshape(row_blocks, -1)).reshape(most, pairs, 3, blocks)
    here = rows[:, :, 0, None, :] == spots[:, None, :, None].astype(jnp.float32)
    code = rows[:, :, 1, None, :] * 256.0 + rows[:, :, 2, None, :] * 512.0 + stored.astype(jnp.float32)
    codes = jnp.sum(jnp.where(here, code, 0.0), -1).astype(jnp.int32)
    order = jnp.arange(2 * span * half, dtype=jnp.int32)
    order_block = (
        ((order % (span * half)) // half) ^ place
    ) * row_blocks + jnp.where(order < span * half, core, 1 - core) * half + order % half
    key_side = pick(order_block[:, None] == every, segment_table).reshape(-1, 1)
    query_side = pick(mine, segment_table)
    query_side = jnp.concatenate([query_side, query_side], 1)
    numbers = [ends[-1:], item_query, (items == first), codes.reshape(-1)]
    return (
        jnp.concatenate([one.astype(jnp.int32) for one in numbers]),
        query_side,
        jnp.broadcast_to(key_side, (key_side.shape[0], PAIR)),
    )


def two_heads(rows, low_lanes):
    rows = rows.astype(jnp.float32)
    zero = jnp.zeros_like(rows)
    return jnp.concatenate(
        [jnp.where(low_lanes, rows, zero), jnp.where(low_lanes, zero, rows)], 0
    )


def item_blocks(numbers_ref, first, side, key_side_ref):
    low_row = lax.broadcasted_iota(jnp.int32, (1, PAIR), 1) < HEAD
    spots, masks = [], []
    for slot in range(SLOTS):
        code = numbers_ref[first + slot]
        spot = pl.ds(pl.multiple_of((code & 255) * BLOCK, BLOCK), BLOCK)
        flags = jnp.where(low_row, code & 256, code & 512)
        spots.append(spot)
        masks.append(key_side_ref[spot, :] == jnp.where(flags != 0, side, -1.0))
    return spots, jnp.concatenate(masks, 0)


def attend_kernel(
    numbers_ref, query_side_ref, key_side_ref,
    own_query_ref, own_kv_ref, other_ref, query_weight_ref, kv_weight_ref,
    mixed_ref, mass_ref, q_ref, kv_ref, state_ref, mixture_ref, *, pairs
):
    half_rows, half_kv = own_query_ref.shape[0], own_kv_ref.shape[0]
    q_ref[:half_rows, :] = own_query_ref[...]
    q_ref[half_rows:, :] = dot_plain(other_ref[:half_rows, :], query_weight_ref[...]).astype(jnp.bfloat16)
    kv_ref[:half_kv, :] = own_kv_ref[...]
    step = 512
    for start in range(0, half_kv, step):
        kv_ref[half_kv + start : half_kv + start + step, :] = dot_plain(
            other_ref[start : start + step, :], kv_weight_ref[...]
        ).astype(jnp.bfloat16)
    low_lanes = lax.broadcasted_iota(jnp.int32, (BLOCK, PAIR), 1) < HEAD
    most = (numbers_ref.shape[0] - 1) // (2 + pairs * SLOTS)

    def one_item(item, carry):
        query = numbers_ref[1 + item]
        fresh = numbers_ref[1 + most + item] == 1
        side = query_side_ref[pl.ds(query, 1), :]
        rows = pl.ds(pl.multiple_of(query * BLOCK, BLOCK), BLOCK)
        held = []
        for pair in range(pairs):
            both = two_heads(q_ref[rows, pair * PAIR : (pair + 1) * PAIR], low_lanes).astype(jnp.bfloat16)
            spots, mask = item_blocks(
                numbers_ref, 1 + 2 * most + (item * pairs + pair) * SLOTS, side, key_side_ref
            )
            start = pair * 2 * PAIR
            keys = jnp.concatenate([kv_ref[spot, start : start + PAIR] for spot in spots], 0)
            values = jnp.concatenate([kv_ref[spot, start + PAIR : start + 2 * PAIR] for spot in spots], 0)
            held.append((jnp.where(mask, dot_cols(keys, both) * score_scale, masked_value), values))
        done = []
        for pair in range(pairs):
            scores, values = held[pair]
            place = query * pairs + pair
            state = state_ref[place]
            old_top = jnp.where(fresh, masked_value, state[0:1, :])
            top = jnp.maximum(old_top, jnp.max(scores, axis=0, keepdims=True))
            raised = jnp.exp(scores - top)
            shrunk = jnp.exp(old_top - top)
            total = jnp.where(fresh, 0.0, state[1:2, :] * shrunk) + jnp.sum(raised, axis=0, keepdims=True)
            mixture = jnp.where(fresh, 0.0, mixture_ref[place] * shrunk) + dot_rows(
                values, raised.astype(jnp.bfloat16)
            )
            done.append((top, total, mixture))
        for pair in range(pairs):
            top, total, mixture = done[pair]
            place = query * pairs + pair
            state_ref[place, 0:1, :] = top
            state_ref[place, 1:2, :] = total
            mixture_ref[place] = mixture
            normed = (mixture / total).T
            mixed_ref[rows, pair * PAIR : (pair + 1) * PAIR] = jnp.where(
                low_lanes, normed[:BLOCK], normed[BLOCK:]
            )
            mass_ref[place] = jnp.broadcast_to(top + jnp.log(total), (8, PAIR))
        return carry

    lax.fori_loop(0, numbers_ref[0], one_item, 0)


def attend(tables, own_query, own_kv, other, query_weight, kv_weight):
    rows, width = 2 * own_query.shape[0], own_query.shape[1]
    pairs, row_blocks = width // PAIR, rows // BLOCK
    places = pairs * row_blocks
    return local_call(
        functools.partial(attend_kernel, pairs=pairs),
        [
            shaped((rows, width)),
            shaped((places, 8, PAIR)),
            shaped((rows, width), jnp.bfloat16),
            shaped((2 * own_kv.shape[0], own_kv.shape[1]), jnp.bfloat16),
        ],
        list(tables[1:]) + [own_query, own_kv, other, query_weight, kv_weight],
        tables[:1],
        [
            pltpu.VMEM((places, 8, PAIR), jnp.float32),
            pltpu.VMEM((places, PAIR, PAIR), jnp.float32),
        ],
        flops=8e9, transcendentals=4e6, spare=12,
    )


def attend_back_kernel(
    numbers_ref, query_side_ref, key_side_ref, q_ref, kv_ref,
    mixed_ref, mass_ref, own_grad_ref, other_grad_ref, weight_ref,
    query_grad_ref, kv_grad_ref, sum_ref, grad_ref, query_sum_ref, *, pairs
):
    half_rows = own_grad_ref.shape[0]
    grad_ref[:half_rows, :] = dot_plain(own_grad_ref[...], weight_ref[...]).astype(jnp.bfloat16)
    grad_ref[half_rows:, :] = dot_plain(other_grad_ref[...], weight_ref[...]).astype(jnp.bfloat16)
    low_lanes = lax.broadcasted_iota(jnp.int32, (BLOCK, PAIR), 1) < HEAD
    most = (numbers_ref.shape[0] - 1) // (2 + pairs * SLOTS)
    sum_ref[...] = jnp.zeros_like(sum_ref)

    def one_item(item, carry):
        query = numbers_ref[1 + item]
        fresh = numbers_ref[1 + most + item] == 1
        side = query_side_ref[pl.ds(query, 1), :]
        rows = pl.ds(pl.multiple_of(query * BLOCK, BLOCK), BLOCK)
        held = []
        for pair in range(pairs):
            lanes = slice(pair * PAIR, (pair + 1) * PAIR)
            both = two_heads(q_ref[rows, lanes], low_lanes).astype(jnp.bfloat16)
            grads = grad_ref[rows, lanes].astype(jnp.float32)
            turned = (grads * mixed_ref[rows, lanes]).T
            inner = jnp.concatenate(
                [jnp.sum(turned[:HEAD], axis=0, keepdims=True), jnp.sum(turned[HEAD:], axis=0, keepdims=True)], 1
            )
            grads = two_heads(grads, low_lanes).astype(jnp.bfloat16)
            spots, mask = item_blocks(
                numbers_ref, 1 + 2 * most + (item * pairs + pair) * SLOTS, side, key_side_ref
            )
            start = pair * 2 * PAIR
            kv = jnp.concatenate([kv_ref[spot, start : start + 2 * PAIR] for spot in spots], 0)
            blank = jnp.zeros_like(both)
            sides = jnp.concatenate(
                [jnp.concatenate([both, blank], 1), jnp.concatenate([blank, grads], 1)], 0
            )
            held.append((dot_cols(kv, sides), inner, sides, kv, spots, mask))
        done = []
        for pair in range(pairs):
            products, inner, sides, kv, spots, mask = held[pair]
            place = query * pairs + pair
            scores = jnp.where(mask, products[:, :PAIR] * score_scale, masked_value)
            chances = jnp.exp(scores - mass_ref[place, 0:1, :])
            score_grads = (chances * (products[:, PAIR:] - inner)).astype(jnp.bfloat16)
            query_grad = dot_rows(score_grads, kv[:, :PAIR])
            kv_grad = dot_plain(jnp.concatenate([score_grads, chances.astype(jnp.bfloat16)], 1), sides)
            done.append((query_grad, kv_grad))
        for pair in range(pairs):
            lanes = slice(pair * PAIR, (pair + 1) * PAIR)
            start = pair * 2 * PAIR
            query_grad, kv_grad = done[pair]
            spots = held[pair][4]
            query_grad = jnp.where(low_lanes, query_grad[:BLOCK], query_grad[BLOCK:])
            query_sum_ref[rows, lanes] = jnp.where(fresh, 0.0, query_sum_ref[rows, lanes]) + query_grad
            for slot, spot in enumerate(spots):
                sum_ref[spot, start : start + 2 * PAIR] += kv_grad[slot * BLOCK : (slot + 1) * BLOCK]
        return carry

    lax.fori_loop(0, numbers_ref[0], one_item, 0)
    query_grad_ref[...] = (query_sum_ref[...] * score_scale).astype(jnp.bfloat16)
    for pair in range(pairs):
        start = pair * 2 * PAIR
        kv_grad_ref[:, start : start + PAIR] = (sum_ref[:, start : start + PAIR] * score_scale).astype(jnp.bfloat16)
        kv_grad_ref[:, start + PAIR : start + 2 * PAIR] = sum_ref[:, start + PAIR : start + 2 * PAIR].astype(
            jnp.bfloat16
        )


def attend_back(tables, queries, kv, mixed, mass, own_grad, other_grad, weight):
    rows, width = queries.shape
    pairs = width // PAIR
    return local_call(
        functools.partial(attend_back_kernel, pairs=pairs),
        [shaped((rows, width), jnp.bfloat16), shaped(kv.shape, jnp.bfloat16)],
        list(tables[1:]) + [queries, kv, mixed, mass, own_grad, other_grad, weight],
        tables[:1],
        [
            pltpu.VMEM(kv.shape, jnp.float32),
            pltpu.VMEM((rows, width), jnp.bfloat16),
            pltpu.VMEM((rows, width), jnp.float32),
        ],
        flops=10e9, transcendentals=4e6, spare=12,
    )


LANES = 2 * PAIR


def packed_rows(slot_rows, columns):
    return columns // LANES * slot_rows + (slot_rows // 2 if columns % LANES else 0)


def put_packed(out_ref, base, source_ref, first, columns, slot_rows):
    for chunk in range(columns // LANES):
        at = first + chunk * LANES
        out_ref[base : base + slot_rows, :] = source_ref[:, at : at + LANES]
        base += slot_rows
    if columns % LANES:
        half, at = slot_rows // 2, first + columns - PAIR
        out_ref[base : base + half, :PAIR] = source_ref[:half, at : at + PAIR]
        out_ref[base : base + half, PAIR:] = source_ref[half:, at : at + PAIR]


def unpacked(packed, slot_rows):
    full = packed.shape[0] // slot_rows
    parts = [packed[at * slot_rows : (at + 1) * slot_rows] for at in range(full)]
    tail = packed[full * slot_rows :]
    if tail.shape[0]:
        parts.append(jnp.concatenate([tail[:, :PAIR], tail[:, PAIR:]], 0))
    return jnp.concatenate(parts, 1)


def fetched(far, near, arrived):
    copies = [
        pltpu.make_async_copy(far_ref, near_ref, arrived.at[at])
        for at, (far_ref, near_ref) in enumerate(zip(far, near))
    ]
    for copy in copies:
        copy.start()
    for copy in copies:
        copy.wait()


def weight_start_kernel(*refs, cut):
    near = refs[9:-1]
    fetched(refs[:7], near, refs[-1])
    query_ref, key_ref, value_ref, inner_ref, outer_ref, output_ref, valid_ref = near
    first_ref, second_ref = refs[7:9]
    width = query_ref.shape[1]
    for at, one in enumerate((query_ref, key_ref, value_ref)):
        first_ref[:, at * width : (at + 1) * width] = one[...]
    second_ref[:, :cut] = inner_ref[:, :cut]
    second_ref[:, cut : 2 * cut] = outer_ref[:, :cut]
    at = 2 * cut
    for one, first in ((inner_ref, cut), (outer_ref, cut), (output_ref, 0)):
        size = one.shape[1] - first
        second_ref[:, at : at + size] = one[:, first:]
        at += size
    count = jnp.sum(valid_ref[...].astype(jnp.float32), axis=1, keepdims=True)
    second_ref[:, at:] = jnp.broadcast_to(count, (second_ref.shape[0], PAIR)).astype(jnp.bfloat16)


def token_start_kernel(tokens_ref, *refs):
    near_ref, arrived = refs[3:]
    fetched([tokens_ref], [near_ref], arrived)
    columns = refs[0].shape[1]
    for at in range(3):
        refs[at][...] = near_ref[:, at * columns : (at + 1) * columns]


def fetching_call(kernel, outs, sources):
    return pl.pallas_call(
        kernel,
        out_shape=[pltpu.VMEM(one.shape, one.dtype) for one in outs],
        in_specs=[pl.BlockSpec(memory_space=pltpu.HBM)] * len(sources),
        out_specs=in_vmem(len(outs)),
        scratch_shapes=[pltpu.VMEM(one.shape, one.dtype) for one in sources]
        + [pltpu.SemaphoreType.DMA((len(sources),))],
        compiler_params=params(8),
    )(*[pltpu.with_memory_space_constraint(one, pltpu.HBM) for one in sources])


def first_pack_kernel(*refs, slot_rows):
    sent, came, weights_ref, outs = refs[:3], refs[3:6], refs[6], refs[7:]
    rows = sent[0].shape[0]
    third = weights_ref.shape[1] // 3
    for at in range(3):
        outs[at][:rows, :] = sent[at][...]
        outs[at][rows : 2 * rows, :] = came[at][...]
        put_packed(outs[at], 2 * rows, weights_ref, at * third, third, slot_rows)


def second_pack_kernel(*refs, rows, slot_rows, cuts):
    second_ref, outs = refs[6], refs[7:]
    for at in range(3):
        sent_ref, came_ref, out_ref = refs[2 * at], refs[2 * at + 1], outs[at]
        tail = sent_ref.shape[0] - rows
        out_ref[:rows, :] = sent_ref[:rows, :]
        out_ref[rows : 2 * rows, :] = came_ref[:rows, :]
        out_ref[2 * rows : 2 * rows + tail, :] = sent_ref[rows:, :]
        out_ref[2 * rows + tail : 2 * (rows + tail), :] = came_ref[rows:, :]
        put_packed(out_ref, 2 * (rows + tail), second_ref, cuts[at], cuts[at + 1] - cuts[at], slot_rows)


def third_pack_kernel(*refs, masks, rows, tail):
    out_ref = refs[6]
    columns = refs[0].shape[1]
    for at in range(3):
        tokens = len(masks[2 * at]) * rows
        for side in range(2):
            piece, target = refs[2 * at + side], refs[7 + at]
            for slot, mask in enumerate(masks[2 * at + side]):
                out_ref[mask * rows : (mask + 1) * rows, at * columns : (at + 1) * columns] = piece[
                    slot * rows : (slot + 1) * rows, :
                ]
            target[side * tail : (side + 1) * tail, :] = piece[tokens : tokens + tail, :]
            rest = piece.shape[0] - tokens - tail
            base = 2 * tail + side * rest
            target[base : base + rest, :] = piece[tokens + tail :, :]


def fourth_pack_kernel(*refs, skip):
    for at in range(3):
        rest = refs[2 * at].shape[0] - skip
        for side in range(2):
            refs[6 + at][side * rest : (side + 1) * rest, :] = refs[2 * at + side][skip:, :]


def place_packed_kernel(owner_ref, *refs, plan, slot_rows, rows):
    pieces, outs = refs[: len(plan)], refs[len(plan) :]
    for piece, (masks, units) in zip(pieces, plan):
        size = packed_rows(slot_rows, len(units) * PAIR)
        for slot, mask in enumerate(masks):
            for far in range(2):
                lines = pl.ds(pl.multiple_of(owner_ref[mask * 2 + far] * rows, rows), rows)
                unit = 0
                while unit < len(units):
                    out, column = units[unit]
                    base = slot * size + unit // 2 * slot_rows
                    if unit + 1 == len(units) and unit % 2 == 0:
                        outs[out][lines, column : column + PAIR] = piece[
                            base : base + rows, far * PAIR : (far + 1) * PAIR
                        ]
                        unit += 1
                        continue
                    base += far * rows
                    if unit % 2 == 0 and units[unit + 1] == (out, column + PAIR):
                        outs[out][lines, column : column + LANES] = piece[base : base + rows, :]
                        unit += 2
                        continue
                    side = unit % 2 * PAIR
                    outs[out][lines, column : column + PAIR] = piece[base : base + rows, side : side + PAIR]
                    unit += 1


def place_packed(owner, pieces, plan, widths, rows):
    blocks = owner.shape[0]
    far_count = blocks // 8
    slot_rows = far_count * rows
    outs = [shaped((blocks * rows, width), jnp.bfloat16) for width in widths]
    if rows % 16 == 0 and far_count == 2:
        kernel = functools.partial(place_packed_kernel, plan=plan, slot_rows=slot_rows, rows=rows)
        return local_call(kernel, outs, pieces, [owner], spare=12)
    made = [jnp.zeros(out.shape, out.dtype) for out in outs]
    for piece, (masks, units) in zip(pieces, plan):
        size = packed_rows(slot_rows, len(units) * PAIR)
        for slot, mask in enumerate(masks):
            block = unpacked(piece[slot * size : (slot + 1) * size], slot_rows)
            lines = owner.reshape(8, far_count)[mask][:, None] * rows + jnp.arange(rows, dtype=jnp.int32)
            for unit, (out, column) in enumerate(units):
                made[out] = made[out].at[lines.reshape(-1), column : column + PAIR].set(
                    block[:, unit * PAIR : (unit + 1) * PAIR]
                )
    return made


def units_of(targets):
    return tuple((out, column + at) for out, column, size in targets for at in range(0, size, PAIR))


def placed_blocks(grad, owner, masks):
    blocks = owner.shape[0]
    rows = grad.shape[0] // blocks
    spots = owner.reshape(8, -1)[jnp.array(masks)].reshape(-1)
    return jnp.take(grad.reshape(blocks, rows, grad.shape[1]), spots, axis=0)


def token_kernel(x_ref, query_weight_ref, kv_weight_ref, query_ref, kv_ref):
    rows = query_ref.shape[0]
    query_ref[...] = dot_plain(x_ref[:rows, :], query_weight_ref[...]).astype(jnp.bfloat16)
    step = 512
    for start in range(0, kv_ref.shape[0], step):
        kv_ref[start : start + step, :] = dot_plain(x_ref[start : start + step, :], kv_weight_ref[...]).astype(
            jnp.bfloat16
        )


def project_kernel(mixed_ref, weight_ref, counts_ref, own_ref, other_ref, low_ref, count_ref, *, each):
    count = jnp.sum(counts_ref[...].astype(jnp.float32), axis=0, keepdims=True) / each
    count_ref[...] = jnp.broadcast_to(count, count_ref.shape)
    low = mixed_ref[...].astype(jnp.bfloat16)
    low_ref[...] = low
    total = dot_cols(low, weight_ref[...])
    half = own_ref.shape[0]
    own_ref[...] = total[:half]
    other_ref[...] = total[half:].astype(jnp.bfloat16)


def normed_rows(values):
    centred = values - jnp.mean(values, axis=-1, keepdims=True)
    spread = jnp.mean(centred * centred, axis=-1, keepdims=True)
    scale = lax.rsqrt(spread + epsilon)
    return centred * scale, scale


def norm_back(grads, normed, scale, gain):
    inner = grads * gain
    middle = jnp.mean(inner, axis=-1, keepdims=True)
    slant = jnp.mean(inner * normed, axis=-1, keepdims=True)
    return scale * (inner - middle - normed * slant)


def first_norm_kernel(tokens_ref, own_ref, came_ref, gain_ref, shift_ref, sum_ref, hidden_ref, low_ref):
    total = tokens_ref[...].astype(jnp.float32) + (own_ref[...] + came_ref[...].astype(jnp.float32))
    sum_ref[...] = total
    normed, _ = normed_rows(total)
    hidden = normed * gain_ref[...] + shift_ref[...]
    hidden_ref[...] = hidden
    low_ref[...] = hidden.astype(jnp.bfloat16)


def feed_kernel(own_hidden_ref, other_hidden_ref, inner_ref, outer_ref, own_ref, other_ref, active_ref, slope_ref, total_ref):
    hidden = jnp.concatenate([own_hidden_ref[...], other_hidden_ref[...]], 0)
    step = 256
    for start in range(0, inner_ref.shape[1], step):
        columns = slice(start, start + step)
        upper = dot_plain(hidden, inner_ref[:, columns])
        chance = 0.5 * (1.0 + lax.erf(upper * (0.5**0.5)))
        active = (upper * chance).astype(jnp.bfloat16)
        active_ref[:, columns] = active
        slope_ref[:, columns] = chance + upper * (jnp.exp(-0.5 * upper * upper) * 0.3989422804014327)
        part = dot_cols(active, outer_ref[:, columns])
        if start:
            total_ref[...] += part
        else:
            total_ref[...] = part
    half = own_ref.shape[0]
    own_ref[...] = total_ref[:half, :]
    other_ref[...] = total_ref[half:, :].astype(jnp.bfloat16)


def second_norm_kernel(
    hidden_ref, own_ref, came_ref, gain_ref, shift_ref, teacher_ref, valid_ref, count_own_ref, count_came_ref,
    grad_ref, low_ref, stats_ref, result_ref, *, token_total
):
    valid = jnp.broadcast_to(valid_ref[...].astype(jnp.float32), (PAIR, valid_ref.shape[1])).T[:, :1]
    factor = token_total / (count_own_ref[0:1, 0:1] + count_came_ref[0:1, 0:1])
    total = hidden_ref[...] + (own_ref[...] + came_ref[...].astype(jnp.float32))
    normed, scale = normed_rows(total)
    gain = gain_ref[...]
    result = normed * gain + shift_ref[...]
    result_ref[...] = result.astype(jnp.bfloat16)
    errors = (result - teacher_ref[...].astype(jnp.float32)) * valid
    grads = errors * factor
    grad = norm_back(grads, normed, scale, gain)
    grad_ref[...] = grad
    low_ref[...] = grad.astype(jnp.bfloat16)
    stats_ref[...] = jnp.zeros_like(stats_ref)
    stats_ref[2:3, :] = jnp.sum(grads * normed, axis=0, keepdims=True)
    stats_ref[3:4, :] = jnp.sum(grads, axis=0, keepdims=True)
    squares = jnp.sum(jnp.sum(errors * errors, axis=0, keepdims=True), axis=1, keepdims=True)
    stats_ref[4:5, :] = jnp.broadcast_to(squares, (1, stats_ref.shape[1]))


def feed_back_kernel(own_grad_ref, other_grad_ref, slope_ref, inner_ref, outer_ref, upper_ref, own_ref, other_ref, total_ref):
    grads = jnp.concatenate([own_grad_ref[...], other_grad_ref[...]], 0)
    step = 256
    for start in range(0, inner_ref.shape[1], step):
        columns = slice(start, start + step)
        upper = (dot_plain(grads, outer_ref[:, columns]) * slope_ref[:, columns]).astype(jnp.bfloat16)
        upper_ref[:, columns] = upper
        part = dot_cols(upper, inner_ref[:, columns])
        if start:
            total_ref[...] += part
        else:
            total_ref[...] = part
    half = own_ref.shape[0]
    own_ref[...] = total_ref[:half, :]
    other_ref[...] = total_ref[half:, :].astype(jnp.bfloat16)


def first_back_kernel(
    grad_ref, own_ref, came_ref, sum_ref, gain_ref, other_stats_ref, out_ref, low_ref, stats_ref
):
    grads = grad_ref[...] + (own_ref[...] + came_ref[...].astype(jnp.float32))
    normed, scale = normed_rows(sum_ref[...])
    grad = norm_back(grads, normed, scale, gain_ref[...])
    out_ref[...] = grad
    low_ref[...] = grad.astype(jnp.bfloat16)
    stats_ref[...] = other_stats_ref[...]
    stats_ref[0:1, :] = jnp.sum(grads * normed, axis=0, keepdims=True)
    stats_ref[1:2, :] = jnp.sum(grads, axis=0, keepdims=True)


def write_blocks(owner_ref, made_ref, column, width, out_ref, out_column, masks, far_count, rows):
    for slot, mask in enumerate(masks):
        for far in range(far_count):
            start = pl.multiple_of(owner_ref[mask * far_count + far] * rows, rows)
            out_ref[slot * far_count + far, :, out_column : out_column + width] = made_ref[
                pl.ds(start, rows), column : column + width
            ].astype(out_ref.dtype)


def wide_kernel(
    owner_ref, own_grad_ref, other_grad_ref, active_ref, own_hidden_ref, other_hidden_ref, upper_ref, *refs,
    groups, far_count, rows, step
):
    outs, made_ref = refs[:-1], refs[-1]
    grads = jnp.concatenate([own_grad_ref[...], other_grad_ref[...]], 0)
    hidden = jnp.concatenate([own_hidden_ref[...], other_hidden_ref[...]], 0)
    width = active_ref.shape[1]
    third_width = 2 * width // 3
    for start in range(0, 2 * width, step):
        if start < width:
            made_ref[...] = dot_rows(grads, active_ref[:, start : start + step])
        else:
            made_ref[...] = dot_rows(hidden, upper_ref[:, start - width : start - width + step])
        third = start // third_width
        for at, masks in enumerate(groups[third]):
            write_blocks(
                owner_ref, made_ref, 0, step, outs[third * len(groups[third]) + at], start % third_width,
                masks, far_count, rows
            )


def wide_gradients(owner, own_grad, other_grad, active, own_hidden, other_hidden, upper, groups):
    blocks = owner.shape[0]
    far_count, rows = blocks // 8, own_grad.shape[1] // blocks
    width = active.shape[1]
    third_width = 2 * width // 3
    if rows % 16:
        made = jnp.concatenate(
            [
                dot_rows(jnp.concatenate([own_grad, other_grad], 0), active),
                dot_rows(jnp.concatenate([own_hidden, other_hidden], 0), upper),
            ],
            1,
        )
        outs = []
        for third, group in enumerate(groups):
            columns = made[:, third * third_width : (third + 1) * third_width]
            for at, masks in enumerate(group):
                outs.append(placed_blocks(columns, owner, masks).astype(jnp.bfloat16 if at else jnp.float32))
        return outs
    step = 512
    outs = []
    for group in groups:
        for at, masks in enumerate(group):
            outs.append(
                shaped((len(masks) * far_count, rows, third_width), jnp.bfloat16 if at else jnp.float32)
            )
    kernel = functools.partial(wide_kernel, groups=groups, far_count=far_count, rows=rows, step=step)
    return local_call(
        kernel, outs, [own_grad, other_grad, active, own_hidden, other_hidden, upper], [owner],
        [pltpu.VMEM((own_grad.shape[1], step), jnp.float32)],
        flops=8 * own_grad.size * width, spare=12,
    )


def narrow_kernel(
    own_ref, other_ref, kv_grad_ref, query_grad_ref, own_grad_ref, other_grad_ref, low_ref, made_ref
):
    half, near = own_ref.shape[0], own_grad_ref.shape[0]
    width = query_grad_ref.shape[1]
    made_ref[:, :width] = dot_rows(own_ref[:near, :], query_grad_ref[:near, :]) + dot_rows(
        other_ref[:near, :], query_grad_ref[near:, :]
    )
    made_ref[:, width : 2 * width] = dot_rows(own_grad_ref[...], low_ref[:near, :]) + dot_rows(
        other_grad_ref[...], low_ref[near:, :]
    )
    made_ref[:, 2 * width :] = dot_rows(own_ref[...], kv_grad_ref[:half, :])
    made_ref[:, 2 * width :] += dot_rows(other_ref[...], kv_grad_ref[half:, :])


def narrow_gradients(own, other, kv_grad, query_grad, own_grad, other_grad, low):
    width = query_grad.shape[1]
    return local_call(
        narrow_kernel, [shaped((own.shape[1], 4 * width))],
        [own, other, kv_grad, query_grad, own_grad, other_grad, low],
        flops=4 * own.size * 2 * width + 8 * own_grad.size * width, spare=12,
    )[0]


def token_other_kernel(kv_grad_ref, query_grad_ref, kv_weight_ref, query_weight_ref, out_ref):
    near, half = query_grad_ref.shape[0] // 2, kv_grad_ref.shape[0] // 2
    for start in range(0, half, near):
        total = dot_cols(kv_grad_ref[half + start : half + start + near, :], kv_weight_ref[...])
        if start == 0:
            total += dot_cols(query_grad_ref[near:, :], query_weight_ref[...])
        out_ref[start : start + near, :] = total.astype(jnp.bfloat16)


def token_other(kv_grad, query_grad, kv_weight, query_weight):
    return local_call(
        token_other_kernel, [shaped((kv_grad.shape[0] // 2, kv_weight.shape[0]), jnp.bfloat16)],
        [kv_grad, query_grad, kv_weight, query_weight],
        flops=kv_grad.size * kv_weight.shape[0], spare=12,
    )[0]


def small_kernel(own_ref, came_ref, out_ref):
    lines = own_ref[...] + came_ref[...]
    out_ref[...] = jnp.concatenate([lines, jnp.zeros((PAIR - lines.shape[0], lines.shape[1]), jnp.float32)], 0).T


def token_own_kernel(
    owner_ref, kv_grad_ref, query_grad_ref, kv_weight_ref, query_weight_ref, came_ref, made_ref, small_ref, *outs,
    masks, rows, placed
):
    near = query_grad_ref.shape[0] // 2
    half, columns = outs[0].shape[0], outs[0].shape[2]
    slot_rows = made_ref.shape[1] if placed else made_ref.shape[0] // (2 * half)
    for mask in range(2 * half):
        lines = slice(mask * near, (mask + 1) * near)
        total = dot_cols(kv_grad_ref[lines, :], kv_weight_ref[...]) + came_ref[lines, :].astype(jnp.float32)
        if mask == 0:
            total += dot_cols(query_grad_ref[:near, :], query_weight_ref[...])
        for third, order in enumerate(masks):
            slot = order.index(mask)
            out_ref = outs[2 * third + slot // half]
            at = slot % half
            out_ref[at, :near, :] = total[:, third * columns : (third + 1) * columns].astype(out_ref.dtype)
            for side in range(2):
                base = near + side * slot_rows
                part = slice((2 * third + side) * columns, (2 * third + side + 1) * columns)
                if placed:
                    out_ref[at, base : base + slot_rows, :] = made_ref[mask, :, part].astype(out_ref.dtype)
                    continue
                for far in range(slot_rows // rows):
                    start = pl.multiple_of(owner_ref[mask * (slot_rows // rows) + far] * rows, rows)
                    out_ref[at, base + far * rows : base + (far + 1) * rows, :] = made_ref[
                        pl.ds(start, rows), part
                    ].astype(out_ref.dtype)
            if third == 0:
                if placed:
                    small = small_ref[mask]
                else:
                    far_count = slot_rows // rows
                    small = jnp.concatenate(
                        [
                            small_ref[pl.ds(pl.multiple_of(owner_ref[mask * far_count + far] * rows, rows), rows), :]
                            for far in range(far_count)
                        ],
                        0,
                    )
                small = jnp.concatenate([small[: slot_rows // 2], small[slot_rows // 2 :]], 1)
                if slot >= half:
                    small = in_pieces(small)
                out_ref[at, near + 2 * slot_rows :, :] = small.astype(out_ref.dtype)


def token_own(owner, kv_grad, query_grad, kv_weight, query_weight, came, made, small, masks):
    near = query_grad.shape[0] // 2
    half = came.shape[0] // near // 2
    blocks, features = owner.shape[0], made.shape[0]
    rows, slot_rows = features // blocks, features // (2 * half)
    columns = kv_weight.shape[0] // 3
    placed = rows % 16 != 0
    if placed:
        made, small = (
            placed_blocks(one, owner, tuple(range(2 * half))).reshape(2 * half, slot_rows, one.shape[1])
            for one in (made, small)
        )
    outs = []
    for third in range(len(masks)):
        shape = (half, near + 2 * slot_rows + (slot_rows // 2 if third == 0 else 0), columns)
        outs += [shaped(shape), shaped(shape, jnp.bfloat16)]
    outs = local_call(
        functools.partial(token_own_kernel, masks=masks, rows=rows, placed=placed), outs,
        [kv_grad, query_grad, kv_weight, query_weight, came, made, small], [owner],
        flops=2 * came.shape[0] * kv_weight.size, spare=12,
    )
    return list(outs[::2]), list(outs[1::2])


def last_kernel(grad_ref, *refs):
    token_ref, made_ref = refs[-1], refs[6]
    near, columns = grad_ref.shape[0], refs[0].shape[2]
    slot_rows = made_ref.shape[0]
    width = 6 * columns
    for third in range(3):
        plain = near + 2 * slot_rows
        total = refs[2 * third][0, :plain] + refs[2 * third + 1][0, :plain].astype(jnp.float32)
        if third == 0:
            small = refs[0][0, plain:] + from_pieces(refs[1][0, plain:].astype(jnp.float32))
            made_ref[: slot_rows // 2, width:] = small[:, :PAIR]
            made_ref[slot_rows // 2 :, width:] = small[:, PAIR:]
        part = slice(third * columns, (third + 1) * columns)
        token_ref[:, part] = grad_ref[:, part] + total[:near]
        for side in range(2):
            at = (2 * third + side) * columns
            made_ref[:, at : at + columns] = total[near + side * slot_rows : near + (side + 1) * slot_rows]
    if len(refs) > 8:
        send_ref = refs[7]
        half = slot_rows // 2
        send_ref[:, :width] = made_ref[half:, :width].astype(jnp.bfloat16)
        send_ref[:, width:] = in_pieces(made_ref[half:, width:]).astype(jnp.bfloat16)


def end_kernel(made_ref, came_ref, query_ref, key_ref, value_ref, output_ref, small_ref):
    rows, width = query_ref.shape
    total = made_ref[:rows, : 4 * width] + came_ref[:, : 4 * width].astype(jnp.float32)
    query_ref[...] = total[:, :width]
    output_ref[...] = total[:, width : 2 * width]
    for at in range(0, width, PAIR):
        first = 2 * width + 2 * at
        key_ref[:, at : at + PAIR] = total[:, first : first + PAIR]
        value_ref[:, at : at + PAIR] = total[:, first + PAIR : first + 2 * PAIR]
    small_ref[...] = made_ref[:rows, 4 * width :] + from_pieces(came_ref[:, 4 * width :].astype(jnp.float32))


def wide_end_kernel(*refs):
    out_ref = refs[6]
    columns = refs[0].shape[2]
    for third in range(3):
        out_ref[:, third * columns : (third + 1) * columns] = refs[2 * third][0] + refs[2 * third + 1][0].astype(
            jnp.float32
        )
    if len(refs) > 7:
        refs[7][...] = out_ref[out_ref.shape[0] // 2 :, :].astype(jnp.bfloat16)


def wide_out_kernel(made_ref, came_ref, outer_ref, inner_ref):
    rows, width = outer_ref.shape
    outer_ref[...] = made_ref[:rows, :width] + came_ref[:, :width].astype(jnp.float32)
    inner_ref[...] = made_ref[:rows, width:] + came_ref[:, width:].astype(jnp.float32)


def tie(first, second):
    leaves, tree = jax.tree.flatten(second)
    tied = lax.optimization_barrier(tuple(leaves) + (first,))
    return jax.tree.unflatten(tree, tied[:-1])


def shards(
    tokens,
    query_weight,
    key_weight,
    value_weight,
    output_weight,
    inner_weight,
    outer_weight,
    attn_gain,
    attn_shift,
    ffn_gain,
    ffn_shift,
    teacher,
    segments,
    random_blocks,
    valid_tokens,
):
    devices = lax.axis_size("dp")
    dp_index = lax.axis_index("dp")
    core = lax.axis_index("tensor")
    rows, width = tokens.shape
    length = 2 * rows
    span = segments.shape[1] // length
    near_bits = span.bit_length() - 1
    far_bits = tuple(range(near_bits, devices.bit_length() - 1))
    place, far_place = dp_index % span, dp_index // span
    far_count = devices // span
    each = width // devices
    slot_rows = far_count * each
    head_width = query_weight.shape[1]
    wide = inner_weight.shape[1]
    masks = jnp.arange(span, dtype=jnp.int32)
    fars = jnp.arange(far_count, dtype=jnp.int32)
    owner = ((fars[None, :] ^ far_place) * span + (masks[:, None] ^ place)).reshape(-1)

    def far_gather(block):
        held = block[None]
        for bit in far_bits:
            held = jnp.concatenate([held, swap_mask(held, 1 << bit)], 0)
        return held.reshape(slot_rows, block.shape[1])

    def step(held, at):
        return [swap_mask(one, 1 << bits[at]) for one, bits in zip(held, ROUTES)]

    def both(held, came):
        return [one for pair in zip(held, came) for one in pair]

    def messages(lines):
        return [shaped((one, third), jnp.bfloat16) for one in lines]

    third = width // 3
    cut = 3 * wide // 4
    tail = packed_rows(slot_rows, head_width)
    rest = (cut, cut, 2 * (wide - cut) + head_width + PAIR)
    cuts = (0, cut, 2 * cut, 2 * cut + rest[2])
    sizes = [packed_rows(slot_rows, one) for one in rest]
    valid_row = valid_tokens.reshape(1, rows)
    first, second = fetching_call(
        functools.partial(weight_start_kernel, cut=cut),
        [shaped((each, 3 * head_width), jnp.bfloat16), shaped((each, cuts[3]), jnp.bfloat16)],
        [query_weight, key_weight, value_weight, inner_weight, outer_weight, output_weight, valid_row],
    )
    held = list(
        fetching_call(token_start_kernel, [shaped((rows, third), jnp.bfloat16)] * 3, [tie(first, tokens)])
    )
    came = step(held, 0)
    first_held, second_held = far_gather(first), far_gather(second)
    held = local_call(
        functools.partial(first_pack_kernel, slot_rows=slot_rows), messages([2 * rows + tail] * 3),
        held + came + [first_held],
    )
    came = step(held, 1)
    held = local_call(
        functools.partial(second_pack_kernel, rows=2 * rows, slot_rows=slot_rows, cuts=cuts),
        messages([4 * rows + 2 * tail + size for size in sizes]), both(held, came) + [second_held],
    )
    came = step(held, 2)
    segment_all = lax.dynamic_index_in_dim(segments, far_place, 0, keepdims=False)
    tables = attention_tables(random_blocks, segment_all, place, core, span, length // BLOCK)
    tables, owner, came = lax.optimization_barrier((tables, owner, came))
    sent_masks = [tuple(slot_masks(bits[:2])) for bits in ROUTES]
    came_masks = [tuple(mask ^ (1 << bits[2]) for mask in sent) for sent, bits in zip(sent_masks, ROUTES)]
    own, *held = local_call(
        functools.partial(third_pack_kernel, masks=tuple(both(sent_masks, came_masks)), rows=rows, tail=2 * tail),
        [shaped((span * rows, width), jnp.bfloat16)] + messages([4 * tail + 2 * size for size in sizes]),
        both(held, came),
    )
    came = step(held, 0)
    other = swap_core(own)
    late = local_call(
        functools.partial(fourth_pack_kernel, skip=4 * tail), messages([4 * size for size in sizes]),
        both(held, came),
    )
    late_came = step(late, 1)

    held, came = tie(late[0], (held, came))
    plan = []
    for bits, units in zip(
        ROUTES,
        [((0, 0, head_width),)]
        + [tuple((1, 2 * at + shift, PAIR) for at in range(0, head_width, PAIR)) for shift in (0, PAIR)],
    ):
        sent = tuple(slot_masks((bits[1], bits[2])))
        plan += [(sent, units_of(units)), (tuple(mask ^ (1 << bits[0]) for mask in sent), units_of(units))]
    full_query, full_kv = place_packed(
        owner, both(held, came), tuple(plan), (head_width, 2 * head_width), each
    )
    own_query, own_kv = local_call(
        token_kernel, [shaped((rows, head_width), jnp.bfloat16), shaped((span * rows, 2 * head_width), jnp.bfloat16)],
        [own, full_query, full_kv], flops=4 * own.size * head_width, spare=12,
    )
    mixed, mass, queries, kv = attend(tables, own_query, own_kv, other, full_query, full_kv)

    late, late_came = tie(mixed, (late, late_came))
    plan = []
    for bits, units in zip(
        ROUTES,
        (
            ((0, 0, cut),),
            ((1, 0, cut),),
            ((0, cut, wide - cut), (1, cut, wide - cut), (2, 0, head_width), (3, 0, PAIR)),
        ),
    ):
        sent = tuple(slot_masks((bits[2], bits[0])))
        plan += [(sent, units_of(units)), (tuple(mask ^ (1 << bits[1]) for mask in sent), units_of(units))]
    full_inner, full_outer, full_output, counts = place_packed(
        owner, both(late, late_came), tuple(plan), (wide, wide, head_width, PAIR), each
    )

    half_shape, low_shape = shaped((rows, width)), shaped((rows, width), jnp.bfloat16)
    gain_one, shift_one, gain_two, shift_two = (
        one.reshape(1, width) for one in (attn_gain, attn_shift, ffn_gain, ffn_shift)
    )
    count_shape = shaped((8, PAIR))
    part_own, part_other, attended, count_own = local_call(
        functools.partial(project_kernel, each=each),
        [half_shape, low_shape, shaped(mixed.shape, jnp.bfloat16), count_shape], [mixed, full_output, counts],
        flops=2 * mixed.size * width,
    )
    count_came = swap_core(count_own)
    first_sum, hidden, hidden_own = local_call(
        first_norm_kernel, [half_shape, half_shape, low_shape],
        [tokens, part_own, swap_core(part_other), gain_one, shift_one],
    )
    hidden_other = swap_core(hidden_own)
    part_own, part_other, active, slope = local_call(
        feed_kernel,
        [half_shape, low_shape, shaped((length, wide), jnp.bfloat16), shaped((length, wide))],
        [hidden_own, hidden_other, full_inner, full_outer],
        scratch=[pltpu.VMEM((length, width), jnp.float32)],
        flops=4 * length * width * wide, transcendentals=2 * length * wide, spare=12,
    )
    token_total = devices * lax.axis_size("tensor") * rows
    grad_second, grad_ffn_own, stats_two, result = local_call(
        functools.partial(second_norm_kernel, token_total=token_total),
        [half_shape, low_shape, shaped((8, width)), low_shape],
        [hidden, part_own, swap_core(part_other), gain_two, shift_two, teacher, valid_row, count_own, count_came],
        free=1,
    )
    grad_ffn_other = swap_core(grad_ffn_own)
    upper_grad, part_own, part_other = local_call(
        feed_back_kernel, [shaped((length, wide), jnp.bfloat16), half_shape, low_shape],
        [grad_ffn_own, grad_ffn_other, slope, full_inner, full_outer],
        scratch=[pltpu.VMEM((length, width), jnp.float32)],
        flops=4 * length * width * wide, spare=12,
    )
    part_came = swap_core(part_other)
    scatter_masks = tuple(tuple(slot_masks(bits[::-1])) for bits in ROUTES)
    groups = tuple((one[: span // 2], one[span // 2 :]) for one in scatter_masks)
    outs = wide_gradients(
        owner, grad_ffn_own, grad_ffn_other, active, hidden_own, hidden_other, upper_grad, groups
    )
    outs = [one.reshape(span // 2, slot_rows, one.shape[2]) for one in outs]
    wide_keep, wide_came = outs[::2], step(outs[1::2], 0)
    part_came = tie(outs[0], part_came)
    grad_first, grad_attn_own, stats_one = local_call(
        first_back_kernel, [half_shape, low_shape, shaped((8, width))],
        [grad_second, part_own, part_came, first_sum, gain_one, stats_two],
    )
    grad_attn_other = swap_core(grad_attn_own)
    stats_came = swap_core(stats_one)
    query_grad, kv_grad = attend_back(
        tables, queries, kv, mixed, mass, grad_attn_own, grad_attn_other, full_output
    )

    def folded(keep, came):
        return fold(keep, [[one] for one in came])

    small = local_call(small_kernel, [shaped((width, PAIR))], [stats_one, tie(query_grad, stats_came)])[0]
    wide_keep, wide_send = folded(wide_keep, tie(small, wide_came))
    wide_came = step(wide_send, 1)
    token_sent = token_other(tie(wide_keep[0], kv_grad), query_grad, full_kv, full_query)
    token_came = swap_core(token_sent)
    made = narrow_gradients(
        own, other, tie(token_sent, kv_grad), query_grad, grad_attn_own, grad_attn_other, attended
    )
    wide_keep, wide_send = folded(wide_keep, tie(made, wide_came))
    wide_came = step(wide_send, 2)
    keep, send = token_own(
        owner, kv_grad, query_grad, full_kv, full_query, tie(wide_keep[0], token_came), made, small, scatter_masks
    )
    came = step(send, 0)
    far_send = [shaped((each, 2 * wide), jnp.bfloat16)] if far_count == 2 else []
    wide_sum, *wide_send = local_call(
        wide_end_kernel, [shaped((slot_rows, 2 * wide))] + far_send, both(wide_keep, tie(keep[0], wide_came))
    )
    plain = rows + 2 * slot_rows
    keep, send = fold(keep, [[one] for one in tie(wide_sum, came)], plain)
    came = step(send, 1)

    def far_scatter(total, after=None, dtype=jnp.bfloat16):
        total = total.reshape(far_count, each, total.shape[1])
        for bit in far_bits[::-1]:
            half = total.shape[0] // 2
            came = swap_mask(total[half:].astype(dtype), 1 << bit)
            if after is not None:
                came, total = tie(after, (came, total))
            total = total[:half] + came.astype(jnp.float32)
        return total[0]

    keep, send = fold(keep, [[one] for one in came], plain)
    came = step(send, 2)
    made_shape = shaped((slot_rows, 4 * head_width + PAIR))
    send_shape = [shaped((each, 4 * head_width + PAIR), jnp.bfloat16)] if far_count == 2 else []
    *made, grad_tokens = local_call(
        last_kernel, [made_shape] + send_shape + [half_shape], [grad_first] + both(keep, came), free=1
    )
    made, send = made[0], made[1:]
    if far_count == 2:
        weight_shape = shaped((each, head_width))
        part_query, part_key, part_value, part_output, small = local_call(
            end_kernel, [weight_shape] * 4 + [shaped((each, PAIR))], [made, swap_mask(send[0], 1 << far_bits[0])],
            free=5,
        )
    else:
        narrow_sum = far_scatter(made[:, : 4 * head_width])
        small = far_scatter(made[:, 4 * head_width :], None, jnp.float32)
        part_query, part_output = narrow_sum[:, :head_width], narrow_sum[:, head_width : 2 * head_width]
        kv_sum = narrow_sum[:, 2 * head_width :].reshape(each, head_width // PAIR, 2, PAIR)
        part_key, part_value = (kv_sum[:, :, one].reshape(each, head_width) for one in range(2))
    if far_count == 2:
        wide_came = swap_mask(wide_send[0], 1 << far_bits[0])
        part_outer, part_inner = local_call(
            wide_out_kernel, [shaped((each, wide))] * 2, [wide_sum, tie(grad_tokens, wide_came)], free=2
        )
    else:
        wide_sum = far_scatter(wide_sum, grad_tokens)
        part_outer, part_inner = wide_sum[:, :wide], wide_sum[:, wide:]
    loss_value = small[0, 4] / (2.0 * width * (count_own[0, 0] + count_came[0, 0]))
    half = each // 2
    mine = jnp.where(core == 0, small[:half], small[half:])
    return (
        result,
        loss_value,
        grad_tokens,
        part_query,
        part_key,
        part_value,
        part_output,
        part_inner,
        part_outer,
        mine[:, 0],
        mine[:, 1],
        mine[:, 2],
        mine[:, 3],
    )


def solution(mesh):
    both = P(("dp", "tensor"))
    rows_spec = P(("dp", "tensor"), None)
    weight_spec = P("dp", "tensor")
    in_specs = (rows_spec,) + (weight_spec,) * 6 + (P(),) * 4
    in_specs += (rows_spec, P(), P("tensor", None, None), both)
    out_specs = (rows_spec, P(), rows_spec) + (weight_spec,) * 6 + (both,) * 4
    return jax.shard_map(shards, mesh=mesh, in_specs=in_specs, out_specs=out_specs, check_vma=False)
```

```python
import functools

import jax
import jax.numpy as jnp
from jax import lax
from jax.experimental import pallas as pl
from jax.experimental.pallas import tpu as pltpu
from jax.sharding import PartitionSpec as P

BLOCK = 64
HEAD = 64
PAIR = 2 * HEAD
SLOTS = 6
ROUTES = ((0, 1, 2), (1, 2, 0), (2, 0, 1))

epsilon = 1e-05
masked_value = -1e30
score_scale = 0.125


def swap_mask(block, mask):
    count = lax.axis_size("dp")
    return lax.ppermute(block, "dp", [(one, one ^ mask) for one in range(count)])


def swap_core(block):
    return lax.ppermute(block, "tensor", [(0, 1), (1, 0)])


def dot_plain(left_side, right_side):
    return jnp.dot(left_side, right_side, preferred_element_type=jnp.float32)


def dot_cols(left_side, right_side):
    return lax.dot_general(
        left_side, right_side, (((1,), (1,)), ((), ())), preferred_element_type=jnp.float32
    )


def dot_rows(left_side, right_side):
    return lax.dot_general(
        left_side, right_side, (((0,), (0,)), ((), ())), preferred_element_type=jnp.float32
    )


def params(megabytes):
    return pltpu.CompilerParams(vmem_limit_bytes=int(megabytes) << 20)


def cost(flops=0, moved=0, transcendentals=0):
    return pl.CostEstimate(flops=int(flops), bytes_accessed=int(moved), transcendentals=int(transcendentals))


def in_vmem(count):
    return [pl.BlockSpec(memory_space=pltpu.VMEM)] * count


def in_smem(count):
    return [pl.BlockSpec(memory_space=pltpu.SMEM)] * count


def shaped(shape, dtype=jnp.float32):
    return jax.ShapeDtypeStruct(tuple(shape), dtype)


def local_call(kernel, outs, vmem_inputs, smem_inputs=(), scratch=(), flops=0, transcendentals=0, spare=8, free=0):
    moved = sum(one.size * one.dtype.itemsize for one in list(vmem_inputs) + list(outs))
    held = sum(one.size * one.dtype.itemsize for one in (shaped(s.shape, s.dtype) for s in scratch))
    held = held // (1 << 20) + 1 + spare
    return pl.pallas_call(
        kernel,
        out_shape=tuple(
            one if len(outs) - at <= free else pltpu.VMEM(one.shape, one.dtype) for at, one in enumerate(outs)
        ),
        in_specs=in_smem(len(smem_inputs)) + in_vmem(len(vmem_inputs)),
        out_specs=tuple(in_vmem(len(outs))),
        scratch_shapes=list(scratch),
        compiler_params=params(held),
        cost_estimate=pl.CostEstimate(flops=1000, bytes_accessed=1000, transcendentals=0),
    )(*smem_inputs, *[pltpu.with_memory_space_constraint(one, pltpu.VMEM) for one in vmem_inputs])


def slot_masks(bits):
    return [
        sum(((slot >> at) & 1) << bit for at, bit in enumerate(bits))
        for slot in range(1 << len(bits))
    ]


def in_pieces(values):
    high = values.astype(jnp.bfloat16).astype(jnp.float32)
    middle = (values - high).astype(jnp.bfloat16).astype(jnp.float32)
    return high + pltpu.roll(middle, 8, 1) + pltpu.roll(values - high - middle, 16, 1)


def from_pieces(pieces):
    lanes = pieces.shape[1]
    total = pieces + pltpu.roll(pieces, lanes - 8, 1) + pltpu.roll(pieces, lanes - 16, 1)
    return jnp.where(lax.broadcasted_iota(jnp.int32, pieces.shape, 1) % PAIR < 8, total, 0.0)


def fold_kernel(*refs, thirds, arrivals, plain):
    outs = refs[thirds * (1 + arrivals) :]
    for third in range(thirds):
        keep_ref = refs[third * (1 + arrivals)]
        came = refs[third * (1 + arrivals) + 1 : (third + 1) * (1 + arrivals)]
        half, lines = keep_ref.shape[0] // 2, keep_ref.shape[1]
        most = lines if plain is None else min(plain, lines)
        for side in range(2):
            part = slice(side * half, (side + 1) * half)
            total = sum([one[part, :most].astype(jnp.float32) for one in came], keep_ref[part, :most])
            out_ref = outs[2 * third + side]
            out_ref[:, :most] = total.astype(out_ref.dtype)
            if most == lines:
                continue
            for at in range(half):
                total = keep_ref[side * half + at, most:]
                for one in came:
                    total += from_pieces(one[side * half + at, most:].astype(jnp.float32))
                out_ref[at, most:] = (in_pieces(total) if side else total).astype(out_ref.dtype)


def fold(keeps, arrivals, plain=None):
    outs = []
    for keep in keeps:
        half = (keep.shape[0] // 2,) + keep.shape[1:]
        outs += [shaped(half), shaped(half, jnp.bfloat16)]
    operands = []
    for keep, came in zip(keeps, arrivals):
        operands += [keep] + list(came)
    kernel = functools.partial(fold_kernel, thirds=len(keeps), arrivals=len(arrivals[0]), plain=plain)
    outs = local_call(kernel, outs, operands)
    return list(outs[::2]), list(outs[1::2])


def pick(chosen, table):
    return lax.dot_general(
        chosen.astype(jnp.bfloat16), table.astype(jnp.bfloat16), (((chosen.ndim - 1,), (0,)), ((), ())),
        preferred_element_type=jnp.float32,
    )


def attention_tables(random_blocks, segment_all, place, core, span, row_blocks):
    heads, blocks, draws = random_blocks.shape
    half, pairs = row_blocks // 2, heads // 2
    local = jnp.arange(row_blocks, dtype=jnp.int32)
    owner = jnp.where(local < half, core, 1 - core)
    absolute = place * row_blocks + owner * half + local % half
    every = jnp.arange(blocks, dtype=jnp.int32)
    mine = absolute[:, None] == every
    edge = (every == 0) | (every == blocks - 1)
    fixed = (jnp.abs(absolute[:, None] - every) <= 1) | edge | edge[absolute][:, None]
    segment_table = segment_all.reshape(blocks, BLOCK).astype(jnp.float32)
    low, high = jnp.min(segment_table, 1), jnp.max(segment_table, 1)
    reach = (jnp.max(jnp.where(mine, low, -1.0), 1)[:, None] <= high) & (
        low <= jnp.max(jnp.where(mine, high, -1.0), 1)[:, None]
    )
    drawn = pick(mine, random_blocks.transpose(1, 0, 2).reshape(blocks, heads * draws))
    drawn = drawn.reshape(row_blocks, heads, draws, 1) == every.astype(jnp.float32)
    allowed = (jnp.any(drawn, 2) | fixed[:, None]) & reach[:, None]
    allowed = allowed.reshape(row_blocks, pairs, 2, blocks)
    listed = jnp.any(allowed, 2)
    rank = pick(listed, every[:, None] < every[None, :])
    count = jnp.max(jnp.sum(listed.astype(jnp.int32), -1), -1)
    chunks = -(-count // SLOTS)
    ends = jnp.sum(jnp.where(local[:, None] >= local[None, :], chunks[None, :], 0), 1)
    most = (row_blocks - 1) * -(-min(blocks, 5 + 2 * draws) // SLOTS) + -(-blocks // SLOTS)
    if span == 1:
        most += -(-blocks // SLOTS)
    items = jnp.arange(most, dtype=jnp.int32)
    item_query = jnp.minimum(jnp.sum((items[:, None] >= ends[None, :]).astype(jnp.int32), 1), row_blocks - 1)
    item_is = item_query[:, None] == local
    first = jnp.sum(jnp.where(item_is, (ends - chunks)[None, :], 0), 1)
    spots = ((items - first) * SLOTS)[:, None] + jnp.arange(SLOTS, dtype=jnp.int32)
    stored = (
        jnp.where((every % row_blocks) // half == core, 0, span * half)
        + ((every // row_blocks) ^ place) * half + every % half
    )
    rows = jnp.concatenate([jnp.where(listed, rank, -1.0)[:, :, None], allowed.astype(jnp.float32)], 2)
    rows = pick(item_is, rows.reshape(row_blocks, -1)).reshape(most, pairs, 3, blocks)
    here = rows[:, :, 0, None, :] == spots[:, None, :, None].astype(jnp.float32)
    code = rows[:, :, 1, None, :] * 256.0 + rows[:, :, 2, None, :] * 512.0 + stored.astype(jnp.float32)
    codes = jnp.sum(jnp.where(here, code, 0.0), -1).astype(jnp.int32)
    order = jnp.arange(2 * span * half, dtype=jnp.int32)
    order_block = (
        ((order % (span * half)) // half) ^ place
    ) * row_blocks + jnp.where(order < span * half, core, 1 - core) * half + order % half
    key_side = pick(order_block[:, None] == every, segment_table).reshape(-1, 1)
    query_side = pick(mine, segment_table)
    query_side = jnp.concatenate([query_side, query_side], 1)
    numbers = [ends[-1:], item_query, (items == first), codes.reshape(-1)]
    return (
        jnp.concatenate([one.astype(jnp.int32) for one in numbers]),
        query_side,
        jnp.broadcast_to(key_side, (key_side.shape[0], PAIR)),
    )


def two_heads(rows, low_lanes):
    rows = rows.astype(jnp.float32)
    zero = jnp.zeros_like(rows)
    return jnp.concatenate(
        [jnp.where(low_lanes, rows, zero), jnp.where(low_lanes, zero, rows)], 0
    )


def item_blocks(numbers_ref, first, side, key_side_ref):
    low_row = lax.broadcasted_iota(jnp.int32, (1, PAIR), 1) < HEAD
    spots, masks = [], []
    for slot in range(SLOTS):
        code = numbers_ref[first + slot]
        spot = pl.ds(pl.multiple_of((code & 255) * BLOCK, BLOCK), BLOCK)
        flags = jnp.where(low_row, code & 256, code & 512)
        spots.append(spot)
        masks.append(key_side_ref[spot, :] == jnp.where(flags != 0, side, -1.0))
    return spots, jnp.concatenate(masks, 0)


def attend_kernel(
    numbers_ref, query_side_ref, key_side_ref,
    own_query_ref, own_kv_ref, other_ref, query_weight_ref, kv_weight_ref,
    mixed_ref, mass_ref, q_ref, kv_ref, state_ref, mixture_ref, *, pairs
):
    half_rows, half_kv = own_query_ref.shape[0], own_kv_ref.shape[0]
    q_ref[:half_rows, :] = own_query_ref[...]
    q_ref[half_rows:, :] = dot_plain(other_ref[:half_rows, :], query_weight_ref[...]).astype(jnp.bfloat16)
    kv_ref[:half_kv, :] = own_kv_ref[...]
    step = 512
    for start in range(0, half_kv, step):
        kv_ref[half_kv + start : half_kv + start + step, :] = dot_plain(
            other_ref[start : start + step, :], kv_weight_ref[...]
        ).astype(jnp.bfloat16)
    low_lanes = lax.broadcasted_iota(jnp.int32, (BLOCK, PAIR), 1) < HEAD
    most = (numbers_ref.shape[0] - 1) // (2 + pairs * SLOTS)

    def one_item(item, carry):
        query = numbers_ref[1 + item]
        fresh = numbers_ref[1 + most + item] == 1
        side = query_side_ref[pl.ds(query, 1), :]
        rows = pl.ds(pl.multiple_of(query * BLOCK, BLOCK), BLOCK)
        held = []
        for pair in range(pairs):
            both = two_heads(q_ref[rows, pair * PAIR : (pair + 1) * PAIR], low_lanes).astype(jnp.bfloat16)
            spots, mask = item_blocks(
                numbers_ref, 1 + 2 * most + (item * pairs + pair) * SLOTS, side, key_side_ref
            )
            start = pair * 2 * PAIR
            keys = jnp.concatenate([kv_ref[spot, start : start + PAIR] for spot in spots], 0)
            values = jnp.concatenate([kv_ref[spot, start + PAIR : start + 2 * PAIR] for spot in spots], 0)
            held.append((jnp.where(mask, dot_cols(keys, both) * score_scale, masked_value), values))
        done = []
        for pair in range(pairs):
            scores, values = held[pair]
            place = query * pairs + pair
            state = state_ref[place]
            old_top = jnp.where(fresh, masked_value, state[0:1, :])
            top = jnp.maximum(old_top, jnp.max(scores, axis=0, keepdims=True))
            raised = jnp.exp(scores - top)
            shrunk = jnp.exp(old_top - top)
            total = jnp.where(fresh, 0.0, state[1:2, :] * shrunk) + jnp.sum(raised, axis=0, keepdims=True)
            mixture = jnp.where(fresh, 0.0, mixture_ref[place] * shrunk) + dot_rows(
                values, raised.astype(jnp.bfloat16)
            )
            done.append((top, total, mixture))
        for pair in range(pairs):
            top, total, mixture = done[pair]
            place = query * pairs + pair
            state_ref[place, 0:1, :] = top
            state_ref[place, 1:2, :] = total
            mixture_ref[place] = mixture
            normed = (mixture / total).T
            mixed_ref[rows, pair * PAIR : (pair + 1) * PAIR] = jnp.where(
                low_lanes, normed[:BLOCK], normed[BLOCK:]
            )
            mass_ref[place] = jnp.broadcast_to(top + jnp.log(total), (8, PAIR))
        return carry

    lax.fori_loop(0, numbers_ref[0], one_item, 0)


def attend(tables, own_query, own_kv, other, query_weight, kv_weight):
    rows, width = 2 * own_query.shape[0], own_query.shape[1]
    pairs, row_blocks = width // PAIR, rows // BLOCK
    places = pairs * row_blocks
    return local_call(
        functools.partial(attend_kernel, pairs=pairs),
        [
            shaped((rows, width)),
            shaped((places, 8, PAIR)),
            shaped((rows, width), jnp.bfloat16),
            shaped((2 * own_kv.shape[0], own_kv.shape[1]), jnp.bfloat16),
        ],
        list(tables[1:]) + [own_query, own_kv, other, query_weight, kv_weight],
        tables[:1],
        [
            pltpu.VMEM((places, 8, PAIR), jnp.float32),
            pltpu.VMEM((places, PAIR, PAIR), jnp.float32),
        ],
        flops=8e9, transcendentals=4e6, spare=12,
    )


def attend_back_kernel(
    numbers_ref, query_side_ref, key_side_ref, q_ref, kv_ref,
    mixed_ref, mass_ref, own_grad_ref, other_grad_ref, weight_ref,
    query_grad_ref, kv_grad_ref, sum_ref, grad_ref, query_sum_ref, *, pairs
):
    half_rows = own_grad_ref.shape[0]
    grad_ref[:half_rows, :] = dot_plain(own_grad_ref[...], weight_ref[...]).astype(jnp.bfloat16)
    grad_ref[half_rows:, :] = dot_plain(other_grad_ref[...], weight_ref[...]).astype(jnp.bfloat16)
    low_lanes = lax.broadcasted_iota(jnp.int32, (BLOCK, PAIR), 1) < HEAD
    most = (numbers_ref.shape[0] - 1) // (2 + pairs * SLOTS)
    sum_ref[...] = jnp.zeros_like(sum_ref)

    def one_item(item, carry):
        query = numbers_ref[1 + item]
        fresh = numbers_ref[1 + most + item] == 1
        side = query_side_ref[pl.ds(query, 1), :]
        rows = pl.ds(pl.multiple_of(query * BLOCK, BLOCK), BLOCK)
        held = []
        for pair in range(pairs):
            lanes = slice(pair * PAIR, (pair + 1) * PAIR)
            both = two_heads(q_ref[rows, lanes], low_lanes).astype(jnp.bfloat16)
            grads = grad_ref[rows, lanes].astype(jnp.float32)
            turned = (grads * mixed_ref[rows, lanes]).T
            inner = jnp.concatenate(
                [jnp.sum(turned[:HEAD], axis=0, keepdims=True), jnp.sum(turned[HEAD:], axis=0, keepdims=True)], 1
            )
            grads = two_heads(grads, low_lanes).astype(jnp.bfloat16)
            spots, mask = item_blocks(
                numbers_ref, 1 + 2 * most + (item * pairs + pair) * SLOTS, side, key_side_ref
            )
            start = pair * 2 * PAIR
            kv = jnp.concatenate([kv_ref[spot, start : start + 2 * PAIR] for spot in spots], 0)
            blank = jnp.zeros_like(both)
            sides = jnp.concatenate(
                [jnp.concatenate([both, blank], 1), jnp.concatenate([blank, grads], 1)], 0
            )
            held.append((dot_cols(kv, sides), inner, sides, kv, spots, mask))
        done = []
        for pair in range(pairs):
            products, inner, sides, kv, spots, mask = held[pair]
            place = query * pairs + pair
            scores = jnp.where(mask, products[:, :PAIR] * score_scale, masked_value)
            chances = jnp.exp(scores - mass_ref[place, 0:1, :])
            score_grads = (chances * (products[:, PAIR:] - inner)).astype(jnp.bfloat16)
            query_grad = dot_rows(score_grads, kv[:, :PAIR])
            kv_grad = dot_plain(jnp.concatenate([score_grads, chances.astype(jnp.bfloat16)], 1), sides)
            done.append((query_grad, kv_grad))
        for pair in range(pairs):
            lanes = slice(pair * PAIR, (pair + 1) * PAIR)
            start = pair * 2 * PAIR
            query_grad, kv_grad = done[pair]
            spots = held[pair][4]
            query_grad = jnp.where(low_lanes, query_grad[:BLOCK], query_grad[BLOCK:])
            query_sum_ref[rows, lanes] = jnp.where(fresh, 0.0, query_sum_ref[rows, lanes]) + query_grad
            for slot, spot in enumerate(spots):
                sum_ref[spot, start : start + 2 * PAIR] += kv_grad[slot * BLOCK : (slot + 1) * BLOCK]
        return carry

    lax.fori_loop(0, numbers_ref[0], one_item, 0)
    query_grad_ref[...] = (query_sum_ref[...] * score_scale).astype(jnp.bfloat16)
    for pair in range(pairs):
        start = pair * 2 * PAIR
        kv_grad_ref[:, start : start + PAIR] = (sum_ref[:, start : start + PAIR] * score_scale).astype(jnp.bfloat16)
        kv_grad_ref[:, start + PAIR : start + 2 * PAIR] = sum_ref[:, start + PAIR : start + 2 * PAIR].astype(
            jnp.bfloat16
        )


def attend_back(tables, queries, kv, mixed, mass, own_grad, other_grad, weight):
    rows, width = queries.shape
    pairs = width // PAIR
    return local_call(
        functools.partial(attend_back_kernel, pairs=pairs),
        [shaped((rows, width), jnp.bfloat16), shaped(kv.shape, jnp.bfloat16)],
        list(tables[1:]) + [queries, kv, mixed, mass, own_grad, other_grad, weight],
        tables[:1],
        [
            pltpu.VMEM(kv.shape, jnp.float32),
            pltpu.VMEM((rows, width), jnp.bfloat16),
            pltpu.VMEM((rows, width), jnp.float32),
        ],
        flops=10e9, transcendentals=4e6, spare=12,
    )


LANES = 2 * PAIR


def packed_rows(slot_rows, columns):
    return columns // LANES * slot_rows + (slot_rows // 2 if columns % LANES else 0)


def put_packed(out_ref, base, source_ref, first, columns, slot_rows):
    for chunk in range(columns // LANES):
        at = first + chunk * LANES
        out_ref[base : base + slot_rows, :] = source_ref[:, at : at + LANES]
        base += slot_rows
    if columns % LANES:
        half, at = slot_rows // 2, first + columns - PAIR
        out_ref[base : base + half, :PAIR] = source_ref[:half, at : at + PAIR]
        out_ref[base : base + half, PAIR:] = source_ref[half:, at : at + PAIR]


def unpacked(packed, slot_rows):
    full = packed.shape[0] // slot_rows
    parts = [packed[at * slot_rows : (at + 1) * slot_rows] for at in range(full)]
    tail = packed[full * slot_rows :]
    if tail.shape[0]:
        parts.append(jnp.concatenate([tail[:, :PAIR], tail[:, PAIR:]], 0))
    return jnp.concatenate(parts, 1)


def fetched(far, near, arrived):
    copies = [
        pltpu.make_async_copy(far_ref, near_ref, arrived.at[at])
        for at, (far_ref, near_ref) in enumerate(zip(far, near))
    ]
    for copy in copies:
        copy.start()
    for copy in copies:
        copy.wait()


def weight_start_kernel(*refs):
    near = refs[9:-1]
    fetched(refs[:7], near, refs[-1])
    first_ref, second_ref = refs[7:9]
    for out_ref, sources in ((first_ref, near[:4]), (second_ref, near[4:6])):
        at = 0
        for one in sources:
            out_ref[:, at : at + one.shape[1]] = one[...]
            at += one.shape[1]
    count = jnp.sum(near[6][...].astype(jnp.float32), axis=1, keepdims=True)
    second_ref[:, at:] = jnp.broadcast_to(count, (second_ref.shape[0], PAIR)).astype(jnp.bfloat16)


def token_start_kernel(tokens_ref, *refs):
    near_ref, arrived = refs[3:]
    fetched([tokens_ref], [near_ref], arrived)
    columns = refs[0].shape[1]
    for at in range(3):
        refs[at][...] = near_ref[:, at * columns : (at + 1) * columns]


def fetching_call(kernel, outs, sources):
    return pl.pallas_call(
        kernel,
        out_shape=[pltpu.VMEM(one.shape, one.dtype) for one in outs],
        in_specs=[pl.BlockSpec(memory_space=pltpu.HBM)] * len(sources),
        out_specs=in_vmem(len(outs)),
        scratch_shapes=[pltpu.VMEM(one.shape, one.dtype) for one in sources]
        + [pltpu.SemaphoreType.DMA((len(sources),))],
        compiler_params=params(8),
    )(*[pltpu.with_memory_space_constraint(one, pltpu.HBM) for one in sources])


def first_pack_kernel(*refs, slot_rows):
    sent, came, weights_ref, outs = refs[:3], refs[3:6], refs[6], refs[7:]
    rows = sent[0].shape[0]
    third = weights_ref.shape[1] // 3
    for at in range(3):
        outs[at][:rows, :] = sent[at][...]
        outs[at][rows : 2 * rows, :] = came[at][...]
        put_packed(outs[at], 2 * rows, weights_ref, at * third, third, slot_rows)


def second_pack_kernel(*refs, rows, slot_rows, cuts):
    second_ref, outs = refs[6], refs[7:]
    for at in range(3):
        sent_ref, came_ref, out_ref = refs[2 * at], refs[2 * at + 1], outs[at]
        tail = sent_ref.shape[0] - rows
        out_ref[:rows, :] = sent_ref[:rows, :]
        out_ref[rows : 2 * rows, :] = came_ref[:rows, :]
        out_ref[2 * rows : 2 * rows + tail, :] = sent_ref[rows:, :]
        out_ref[2 * rows + tail : 2 * (rows + tail), :] = came_ref[rows:, :]
        put_packed(out_ref, 2 * (rows + tail), second_ref, cuts[at], cuts[at + 1] - cuts[at], slot_rows)


def third_pack_kernel(*refs, masks, rows, tail):
    out_ref = refs[6]
    columns = refs[0].shape[1]
    for at in range(3):
        tokens = len(masks[2 * at]) * rows
        for side in range(2):
            piece, target = refs[2 * at + side], refs[7 + at]
            for slot, mask in enumerate(masks[2 * at + side]):
                out_ref[mask * rows : (mask + 1) * rows, at * columns : (at + 1) * columns] = piece[
                    slot * rows : (slot + 1) * rows, :
                ]
            target[side * tail : (side + 1) * tail, :] = piece[tokens : tokens + tail, :]
            rest = piece.shape[0] - tokens - tail
            base = 2 * tail + side * rest
            target[base : base + rest, :] = piece[tokens + tail :, :]


def fourth_pack_kernel(*refs, skip):
    for at in range(3):
        rest = refs[2 * at].shape[0] - skip
        for side in range(2):
            refs[6 + at][side * rest : (side + 1) * rest, :] = refs[2 * at + side][skip:, :]


def place_packed_kernel(owner_ref, *refs, plan, slot_rows, rows):
    pieces, outs = refs[: len(plan)], refs[len(plan) :]
    for piece, (masks, units) in zip(pieces, plan):
        size = packed_rows(slot_rows, len(units) * PAIR)
        for slot, mask in enumerate(masks):
            for far in range(2):
                lines = pl.ds(pl.multiple_of(owner_ref[mask * 2 + far] * rows, rows), rows)
                unit = 0
                while unit < len(units):
                    out, column = units[unit]
                    base = slot * size + unit // 2 * slot_rows
                    if unit + 1 == len(units) and unit % 2 == 0:
                        outs[out][lines, column : column + PAIR] = piece[
                            base : base + rows, far * PAIR : (far + 1) * PAIR
                        ]
                        unit += 1
                        continue
                    base += far * rows
                    if unit % 2 == 0 and units[unit + 1] == (out, column + PAIR):
                        outs[out][lines, column : column + LANES] = piece[base : base + rows, :]
                        unit += 2
                        continue
                    side = unit % 2 * PAIR
                    outs[out][lines, column : column + PAIR] = piece[base : base + rows, side : side + PAIR]
                    unit += 1


def place_packed(owner, pieces, plan, widths, rows):
    blocks = owner.shape[0]
    far_count = blocks // 8
    slot_rows = far_count * rows
    outs = [shaped((blocks * rows, width), jnp.bfloat16) for width in widths]
    if rows % 16 == 0 and far_count == 2:
        kernel = functools.partial(place_packed_kernel, plan=plan, slot_rows=slot_rows, rows=rows)
        return local_call(kernel, outs, pieces, [owner], spare=12)
    made = [jnp.zeros(out.shape, out.dtype) for out in outs]
    for piece, (masks, units) in zip(pieces, plan):
        size = packed_rows(slot_rows, len(units) * PAIR)
        for slot, mask in enumerate(masks):
            block = unpacked(piece[slot * size : (slot + 1) * size], slot_rows)
            lines = owner.reshape(8, far_count)[mask][:, None] * rows + jnp.arange(rows, dtype=jnp.int32)
            for unit, (out, column) in enumerate(units):
                made[out] = made[out].at[lines.reshape(-1), column : column + PAIR].set(
                    block[:, unit * PAIR : (unit + 1) * PAIR]
                )
    return made


def units_of(targets):
    return tuple((out, column + at) for out, column, size in targets for at in range(0, size, PAIR))


def placed_blocks(grad, owner, masks):
    blocks = owner.shape[0]
    rows = grad.shape[0] // blocks
    spots = owner.reshape(8, -1)[jnp.array(masks)].reshape(-1)
    return jnp.take(grad.reshape(blocks, rows, grad.shape[1]), spots, axis=0)


def token_kernel(x_ref, query_weight_ref, kv_weight_ref, query_ref, kv_ref):
    rows = query_ref.shape[0]
    query_ref[...] = dot_plain(x_ref[:rows, :], query_weight_ref[...]).astype(jnp.bfloat16)
    step = 512
    for start in range(0, kv_ref.shape[0], step):
        kv_ref[start : start + step, :] = dot_plain(x_ref[start : start + step, :], kv_weight_ref[...]).astype(
            jnp.bfloat16
        )


def project_kernel(mixed_ref, weight_ref, own_ref, other_ref, low_ref):
    low = mixed_ref[...].astype(jnp.bfloat16)
    low_ref[...] = low
    total = dot_cols(low, weight_ref[...])
    half = own_ref.shape[0]
    own_ref[...] = total[:half]
    other_ref[...] = total[half:].astype(jnp.bfloat16)


def normed_rows(values):
    centred = values - jnp.mean(values, axis=-1, keepdims=True)
    spread = jnp.mean(centred * centred, axis=-1, keepdims=True)
    scale = lax.rsqrt(spread + epsilon)
    return centred * scale, scale


def norm_back(grads, normed, scale, gain):
    inner = grads * gain
    middle = jnp.mean(inner, axis=-1, keepdims=True)
    slant = jnp.mean(inner * normed, axis=-1, keepdims=True)
    return scale * (inner - middle - normed * slant)


def first_norm_kernel(tokens_ref, own_ref, came_ref, gain_ref, shift_ref, sum_ref, hidden_ref, low_ref):
    total = tokens_ref[...].astype(jnp.float32) + (own_ref[...] + came_ref[...].astype(jnp.float32))
    sum_ref[...] = total
    normed, _ = normed_rows(total)
    hidden = normed * gain_ref[...] + shift_ref[...]
    hidden_ref[...] = hidden
    low_ref[...] = hidden.astype(jnp.bfloat16)


def feed_kernel(
    own_hidden_ref, other_hidden_ref, inner_ref, outer_ref, counts_ref,
    own_ref, other_ref, active_ref, slope_ref, count_ref, total_ref, *, each
):
    count = jnp.sum(counts_ref[...].astype(jnp.float32), axis=0, keepdims=True) / each
    count_ref[...] = jnp.broadcast_to(count, count_ref.shape)
    hidden = jnp.concatenate([own_hidden_ref[...], other_hidden_ref[...]], 0)
    step = 256
    for start in range(0, inner_ref.shape[1], step):
        columns = slice(start, start + step)
        upper = dot_plain(hidden, inner_ref[:, columns])
        chance = 0.5 * (1.0 + lax.erf(upper * (0.5**0.5)))
        active = (upper * chance).astype(jnp.bfloat16)
        active_ref[:, columns] = active
        slope_ref[:, columns] = chance + upper * (jnp.exp(-0.5 * upper * upper) * 0.3989422804014327)
        part = dot_cols(active, outer_ref[:, columns])
        if start:
            total_ref[...] += part
        else:
            total_ref[...] = part
    half = own_ref.shape[0]
    own_ref[...] = total_ref[:half, :]
    other_ref[...] = total_ref[half:, :].astype(jnp.bfloat16)


def second_norm_kernel(
    hidden_ref, own_ref, came_ref, gain_ref, shift_ref, teacher_ref, valid_ref, count_own_ref, count_came_ref,
    grad_ref, low_ref, stats_ref, result_ref, *, token_total
):
    valid = jnp.broadcast_to(valid_ref[...].astype(jnp.float32), (PAIR, valid_ref.shape[1])).T[:, :1]
    factor = token_total / (count_own_ref[0:1, 0:1] + count_came_ref[0:1, 0:1])
    total = hidden_ref[...] + (own_ref[...] + came_ref[...].astype(jnp.float32))
    normed, scale = normed_rows(total)
    gain = gain_ref[...]
    result = normed * gain + shift_ref[...]
    result_ref[...] = result.astype(jnp.bfloat16)
    errors = (result - teacher_ref[...].astype(jnp.float32)) * valid
    grads = errors * factor
    grad = norm_back(grads, normed, scale, gain)
    grad_ref[...] = grad
    low_ref[...] = grad.astype(jnp.bfloat16)
    stats_ref[...] = jnp.zeros_like(stats_ref)
    stats_ref[2:3, :] = jnp.sum(grads * normed, axis=0, keepdims=True)
    stats_ref[3:4, :] = jnp.sum(grads, axis=0, keepdims=True)
    squares = jnp.sum(jnp.sum(errors * errors, axis=0, keepdims=True), axis=1, keepdims=True)
    stats_ref[4:5, :] = jnp.broadcast_to(squares, (1, stats_ref.shape[1]))


def feed_back_kernel(own_grad_ref, other_grad_ref, slope_ref, inner_ref, outer_ref, upper_ref, own_ref, other_ref, total_ref):
    grads = jnp.concatenate([own_grad_ref[...], other_grad_ref[...]], 0)
    step = 256
    for start in range(0, inner_ref.shape[1], step):
        columns = slice(start, start + step)
        upper = (dot_plain(grads, outer_ref[:, columns]) * slope_ref[:, columns]).astype(jnp.bfloat16)
        upper_ref[:, columns] = upper
        part = dot_cols(upper, inner_ref[:, columns])
        if start:
            total_ref[...] += part
        else:
            total_ref[...] = part
    half = own_ref.shape[0]
    own_ref[...] = total_ref[:half, :]
    other_ref[...] = total_ref[half:, :].astype(jnp.bfloat16)


def first_back_kernel(
    grad_ref, own_ref, came_ref, sum_ref, gain_ref, other_stats_ref, out_ref, low_ref, stats_ref
):
    grads = grad_ref[...] + (own_ref[...] + came_ref[...].astype(jnp.float32))
    normed, scale = normed_rows(sum_ref[...])
    grad = norm_back(grads, normed, scale, gain_ref[...])
    out_ref[...] = grad
    low_ref[...] = grad.astype(jnp.bfloat16)
    stats_ref[...] = other_stats_ref[...]
    stats_ref[0:1, :] = jnp.sum(grads * normed, axis=0, keepdims=True)
    stats_ref[1:2, :] = jnp.sum(grads, axis=0, keepdims=True)


def write_blocks(owner_ref, made_ref, column, width, out_ref, out_column, masks, far_count, rows):
    for slot, mask in enumerate(masks):
        for far in range(far_count):
            start = pl.multiple_of(owner_ref[mask * far_count + far] * rows, rows)
            out_ref[slot * far_count + far, :, out_column : out_column + width] = made_ref[
                pl.ds(start, rows), column : column + width
            ].astype(out_ref.dtype)


def wide_kernel(
    owner_ref, own_grad_ref, other_grad_ref, active_ref, own_hidden_ref, other_hidden_ref, upper_ref, *refs,
    groups, far_count, rows, step
):
    outs, made_ref = refs[:-1], refs[-1]
    grads = jnp.concatenate([own_grad_ref[...], other_grad_ref[...]], 0)
    hidden = jnp.concatenate([own_hidden_ref[...], other_hidden_ref[...]], 0)
    width = active_ref.shape[1]
    third_width = 2 * width // 3
    for start in range(0, 2 * width, step):
        if start < width:
            made_ref[...] = dot_rows(grads, active_ref[:, start : start + step])
        else:
            made_ref[...] = dot_rows(hidden, upper_ref[:, start - width : start - width + step])
        third = start // third_width
        for at, masks in enumerate(groups[third]):
            write_blocks(
                owner_ref, made_ref, 0, step, outs[third * len(groups[third]) + at], start % third_width,
                masks, far_count, rows
            )


def wide_gradients(owner, own_grad, other_grad, active, own_hidden, other_hidden, upper, groups):
    blocks = owner.shape[0]
    far_count, rows = blocks // 8, own_grad.shape[1] // blocks
    width = active.shape[1]
    third_width = 2 * width // 3
    if rows % 16:
        made = jnp.concatenate(
            [
                dot_rows(jnp.concatenate([own_grad, other_grad], 0), active),
                dot_rows(jnp.concatenate([own_hidden, other_hidden], 0), upper),
            ],
            1,
        )
        outs = []
        for third, group in enumerate(groups):
            columns = made[:, third * third_width : (third + 1) * third_width]
            for at, masks in enumerate(group):
                outs.append(placed_blocks(columns, owner, masks).astype(jnp.bfloat16 if at else jnp.float32))
        return outs
    step = 512
    outs = []
    for group in groups:
        for at, masks in enumerate(group):
            outs.append(
                shaped((len(masks) * far_count, rows, third_width), jnp.bfloat16 if at else jnp.float32)
            )
    kernel = functools.partial(wide_kernel, groups=groups, far_count=far_count, rows=rows, step=step)
    return local_call(
        kernel, outs, [own_grad, other_grad, active, own_hidden, other_hidden, upper], [owner],
        [pltpu.VMEM((own_grad.shape[1], step), jnp.float32)],
        flops=8 * own_grad.size * width, spare=12,
    )


def narrow_kernel(
    own_ref, other_ref, kv_grad_ref, query_grad_ref, own_grad_ref, other_grad_ref, low_ref, made_ref
):
    half, near = own_ref.shape[0], own_grad_ref.shape[0]
    width = query_grad_ref.shape[1]
    made_ref[:, :width] = dot_rows(own_ref[:near, :], query_grad_ref[:near, :]) + dot_rows(
        other_ref[:near, :], query_grad_ref[near:, :]
    )
    made_ref[:, width : 2 * width] = dot_rows(own_grad_ref[...], low_ref[:near, :]) + dot_rows(
        other_grad_ref[...], low_ref[near:, :]
    )
    made_ref[:, 2 * width :] = dot_rows(own_ref[...], kv_grad_ref[:half, :])
    made_ref[:, 2 * width :] += dot_rows(other_ref[...], kv_grad_ref[half:, :])


def narrow_gradients(own, other, kv_grad, query_grad, own_grad, other_grad, low):
    width = query_grad.shape[1]
    return local_call(
        narrow_kernel, [shaped((own.shape[1], 4 * width))],
        [own, other, kv_grad, query_grad, own_grad, other_grad, low],
        flops=4 * own.size * 2 * width + 8 * own_grad.size * width, spare=12,
    )[0]


def token_other_kernel(kv_grad_ref, query_grad_ref, kv_weight_ref, query_weight_ref, out_ref):
    near, half = query_grad_ref.shape[0] // 2, kv_grad_ref.shape[0] // 2
    for start in range(0, half, near):
        total = dot_cols(kv_grad_ref[half + start : half + start + near, :], kv_weight_ref[...])
        if start == 0:
            total += dot_cols(query_grad_ref[near:, :], query_weight_ref[...])
        out_ref[start : start + near, :] = total.astype(jnp.bfloat16)


def token_other(kv_grad, query_grad, kv_weight, query_weight):
    return local_call(
        token_other_kernel, [shaped((kv_grad.shape[0] // 2, kv_weight.shape[0]), jnp.bfloat16)],
        [kv_grad, query_grad, kv_weight, query_weight],
        flops=kv_grad.size * kv_weight.shape[0], spare=12,
    )[0]


def small_kernel(own_ref, came_ref, out_ref):
    lines = own_ref[...] + came_ref[...]
    out_ref[...] = jnp.concatenate([lines, jnp.zeros((PAIR - lines.shape[0], lines.shape[1]), jnp.float32)], 0).T


def token_own_kernel(
    owner_ref, kv_grad_ref, query_grad_ref, kv_weight_ref, query_weight_ref, came_ref, made_ref, small_ref, *outs,
    masks, rows, placed
):
    near = query_grad_ref.shape[0] // 2
    half, columns = outs[0].shape[0], outs[0].shape[2]
    slot_rows = made_ref.shape[1] if placed else made_ref.shape[0] // (2 * half)
    for mask in range(2 * half):
        lines = slice(mask * near, (mask + 1) * near)
        total = dot_cols(kv_grad_ref[lines, :], kv_weight_ref[...]) + came_ref[lines, :].astype(jnp.float32)
        if mask == 0:
            total += dot_cols(query_grad_ref[:near, :], query_weight_ref[...])
        for third, order in enumerate(masks):
            slot = order.index(mask)
            out_ref = outs[2 * third + slot // half]
            at = slot % half
            out_ref[at, :near, :] = total[:, third * columns : (third + 1) * columns].astype(out_ref.dtype)
            for side in range(2):
                base = near + side * slot_rows
                part = slice((2 * third + side) * columns, (2 * third + side + 1) * columns)
                if placed:
                    out_ref[at, base : base + slot_rows, :] = made_ref[mask, :, part].astype(out_ref.dtype)
                    continue
                for far in range(slot_rows // rows):
                    start = pl.multiple_of(owner_ref[mask * (slot_rows // rows) + far] * rows, rows)
                    out_ref[at, base + far * rows : base + (far + 1) * rows, :] = made_ref[
                        pl.ds(start, rows), part
                    ].astype(out_ref.dtype)
            if third == 0:
                if placed:
                    small = small_ref[mask]
                else:
                    far_count = slot_rows // rows
                    small = jnp.concatenate(
                        [
                            small_ref[pl.ds(pl.multiple_of(owner_ref[mask * far_count + far] * rows, rows), rows), :]
                            for far in range(far_count)
                        ],
                        0,
                    )
                small = jnp.concatenate([small[: slot_rows // 2], small[slot_rows // 2 :]], 1)
                if slot >= half:
                    small = in_pieces(small)
                out_ref[at, near + 2 * slot_rows :, :] = small.astype(out_ref.dtype)


def token_own(owner, kv_grad, query_grad, kv_weight, query_weight, came, made, small, masks):
    near = query_grad.shape[0] // 2
    half = came.shape[0] // near // 2
    blocks, features = owner.shape[0], made.shape[0]
    rows, slot_rows = features // blocks, features // (2 * half)
    columns = kv_weight.shape[0] // 3
    placed = rows % 16 != 0
    if placed:
        made, small = (
            placed_blocks(one, owner, tuple(range(2 * half))).reshape(2 * half, slot_rows, one.shape[1])
            for one in (made, small)
        )
    outs = []
    for third in range(len(masks)):
        shape = (half, near + 2 * slot_rows + (slot_rows // 2 if third == 0 else 0), columns)
        outs += [shaped(shape), shaped(shape, jnp.bfloat16)]
    outs = local_call(
        functools.partial(token_own_kernel, masks=masks, rows=rows, placed=placed), outs,
        [kv_grad, query_grad, kv_weight, query_weight, came, made, small], [owner],
        flops=2 * came.shape[0] * kv_weight.size, spare=12,
    )
    return list(outs[::2]), list(outs[1::2])


def last_kernel(grad_ref, *refs):
    token_ref, made_ref = refs[-1], refs[6]
    near, columns = grad_ref.shape[0], refs[0].shape[2]
    slot_rows = made_ref.shape[0]
    width = 6 * columns
    for third in range(3):
        plain = near + 2 * slot_rows
        total = refs[2 * third][0, :plain] + refs[2 * third + 1][0, :plain].astype(jnp.float32)
        if third == 0:
            small = refs[0][0, plain:] + from_pieces(refs[1][0, plain:].astype(jnp.float32))
            made_ref[: slot_rows // 2, width:] = small[:, :PAIR]
            made_ref[slot_rows // 2 :, width:] = small[:, PAIR:]
        part = slice(third * columns, (third + 1) * columns)
        token_ref[:, part] = grad_ref[:, part] + total[:near]
        for side in range(2):
            at = (2 * third + side) * columns
            made_ref[:, at : at + columns] = total[near + side * slot_rows : near + (side + 1) * slot_rows]
    if len(refs) > 8:
        send_ref = refs[7]
        half = slot_rows // 2
        send_ref[:, :width] = made_ref[half:, :width].astype(jnp.bfloat16)
        send_ref[:, width:] = in_pieces(made_ref[half:, width:]).astype(jnp.bfloat16)


def end_kernel(made_ref, came_ref, query_ref, key_ref, value_ref, output_ref, small_ref):
    rows, width = query_ref.shape
    total = made_ref[:rows, : 4 * width] + came_ref[:, : 4 * width].astype(jnp.float32)
    query_ref[...] = total[:, :width]
    output_ref[...] = total[:, width : 2 * width]
    for at in range(0, width, PAIR):
        first = 2 * width + 2 * at
        key_ref[:, at : at + PAIR] = total[:, first : first + PAIR]
        value_ref[:, at : at + PAIR] = total[:, first + PAIR : first + 2 * PAIR]
    small_ref[...] = made_ref[:rows, 4 * width :] + from_pieces(came_ref[:, 4 * width :].astype(jnp.float32))


def merge_kernel(*refs, riders):
    keeps, cames, sends, kept, messages = (refs[at : at + 3] for at in range(0, 15, 3))
    for third, rider in enumerate(riders):
        kept[third][...] = keeps[third][0] + cames[third][0].astype(jnp.float32)
        later = (keeps[third][1] + cames[third][1].astype(jnp.float32)).astype(jnp.bfloat16)
        slots, lines, columns = sends[rider].shape
        for slot in range(slots):
            messages[rider][slot * lines : (slot + 1) * lines, :] = sends[rider][slot]
        base, rows = slots * lines, later.shape[0]
        for chunk in range(later.shape[1] // columns):
            messages[rider][base + chunk * rows : base + (chunk + 1) * rows, :] = later[
                :, chunk * columns : (chunk + 1) * columns
            ]


def part_kernel(*refs, riders, plain):
    keeps, cames, kept = refs[:3], refs[3:6], refs[6:9]
    outs, wide_ref = refs[9:15], refs[15]
    for third in range(3):
        keep_ref, came_ref = keeps[third], cames[third]
        slots, lines, _ = keep_ref.shape
        most = min(plain, lines)
        for slot in range(slots):
            side, at = slot // (slots // 2), slot % (slots // 2)
            out_ref, base = outs[2 * third + side], slot * lines
            total = keep_ref[slot, :most] + came_ref[base : base + most, :].astype(jnp.float32)
            out_ref[at, :most] = total.astype(out_ref.dtype)
            if most < lines:
                total = keep_ref[slot, most:] + from_pieces(
                    came_ref[base + most : base + lines, :].astype(jnp.float32)
                )
                out_ref[at, most:] = (in_pieces(total) if side else total).astype(out_ref.dtype)
    for third, rider in enumerate(riders):
        slots, lines, columns = keeps[rider].shape
        rows, width = kept[third].shape
        for chunk in range(width // columns):
            part = slice(chunk * columns, (chunk + 1) * columns)
            base = slots * lines + chunk * rows
            wide_ref[:, third * width + chunk * columns : third * width + (chunk + 1) * columns] = kept[third][
                :, part
            ] + cames[rider][base : base + rows, :].astype(jnp.float32)
    if len(refs) > 16:
        refs[16][...] = wide_ref[wide_ref.shape[0] // 2 :, :].astype(jnp.bfloat16)


def wide_out_kernel(made_ref, came_ref, outer_ref, inner_ref):
    rows, width = outer_ref.shape
    outer_ref[...] = made_ref[:rows, :width] + came_ref[:, :width].astype(jnp.float32)
    inner_ref[...] = made_ref[:rows, width:] + came_ref[:, width:].astype(jnp.float32)


def tie(first, second):
    leaves, tree = jax.tree.flatten(second)
    tied = lax.optimization_barrier(tuple(leaves) + (first,))
    return jax.tree.unflatten(tree, tied[:-1])


def shards(
    tokens,
    query_weight,
    key_weight,
    value_weight,
    output_weight,
    inner_weight,
    outer_weight,
    attn_gain,
    attn_shift,
    ffn_gain,
    ffn_shift,
    teacher,
    segments,
    random_blocks,
    valid_tokens,
):
    devices = lax.axis_size("dp")
    dp_index = lax.axis_index("dp")
    core = lax.axis_index("tensor")
    rows, width = tokens.shape
    length = 2 * rows
    span = segments.shape[1] // length
    near_bits = span.bit_length() - 1
    far_bits = tuple(range(near_bits, devices.bit_length() - 1))
    place, far_place = dp_index % span, dp_index // span
    far_count = devices // span
    each = width // devices
    slot_rows = far_count * each
    head_width = query_weight.shape[1]
    wide = inner_weight.shape[1]
    masks = jnp.arange(span, dtype=jnp.int32)
    fars = jnp.arange(far_count, dtype=jnp.int32)
    owner = ((fars[None, :] ^ far_place) * span + (masks[:, None] ^ place)).reshape(-1)

    def far_gather(block):
        held = block[None]
        for bit in far_bits:
            held = jnp.concatenate([held, swap_mask(held, 1 << bit)], 0)
        return held.reshape(slot_rows, block.shape[1])

    def step(held, at):
        return [swap_mask(one, 1 << bits[at]) for one, bits in zip(held, ROUTES)]

    def both(held, came):
        return [one for pair in zip(held, came) for one in pair]

    def messages(lines):
        return [shaped((one, third), jnp.bfloat16) for one in lines]

    third = width // 3
    tail = packed_rows(slot_rows, 4 * head_width // 3)
    cuts = (0, 2 * wide // 3, 4 * wide // 3, 2 * wide + PAIR)
    sizes = [packed_rows(slot_rows, last - first) for first, last in zip(cuts, cuts[1:])]
    valid_row = valid_tokens.reshape(1, rows)
    first, second = fetching_call(
        weight_start_kernel,
        [shaped((each, 4 * head_width), jnp.bfloat16), shaped((each, cuts[3]), jnp.bfloat16)],
        [query_weight, key_weight, value_weight, output_weight, inner_weight, outer_weight, valid_row],
    )
    held = list(
        fetching_call(token_start_kernel, [shaped((rows, third), jnp.bfloat16)] * 3, [tie(first, tokens)])
    )
    came = step(held, 0)
    first_held, second_held = far_gather(first), far_gather(second)
    held = local_call(
        functools.partial(first_pack_kernel, slot_rows=slot_rows), messages([2 * rows + tail] * 3),
        held + came + [first_held],
    )
    came = step(held, 1)
    held = local_call(
        functools.partial(second_pack_kernel, rows=2 * rows, slot_rows=slot_rows, cuts=cuts),
        messages([4 * rows + 2 * tail + size for size in sizes]), both(held, came) + [second_held],
    )
    came = step(held, 2)
    segment_all = lax.dynamic_index_in_dim(segments, far_place, 0, keepdims=False)
    tables = attention_tables(random_blocks, segment_all, place, core, span, length // BLOCK)
    tables, owner, came = lax.optimization_barrier((tables, owner, came))
    sent_masks = [tuple(slot_masks(bits[:2])) for bits in ROUTES]
    came_masks = [tuple(mask ^ (1 << bits[2]) for mask in sent) for sent, bits in zip(sent_masks, ROUTES)]
    own, *held = local_call(
        functools.partial(third_pack_kernel, masks=tuple(both(sent_masks, came_masks)), rows=rows, tail=2 * tail),
        [shaped((span * rows, width), jnp.bfloat16)] + messages([4 * tail + 2 * size for size in sizes]),
        both(held, came),
    )
    came = step(held, 0)
    other = swap_core(own)
    late = local_call(
        functools.partial(fourth_pack_kernel, skip=4 * tail), messages([4 * size for size in sizes]),
        both(held, came),
    )
    late_came = step(late, 1)

    held, came = tie(late[0], (held, came))
    units = units_of(
        ((0, 0, head_width),)
        + tuple((1, 2 * at + shift, PAIR) for shift in (0, PAIR) for at in range(0, head_width, PAIR))
        + ((2, 0, head_width),)
    )
    plan = []
    for at, bits in enumerate(ROUTES):
        part = units[at * len(units) // 3 : (at + 1) * len(units) // 3]
        sent = tuple(slot_masks((bits[1], bits[2])))
        plan += [(sent, part), (tuple(mask ^ (1 << bits[0]) for mask in sent), part)]
    full_query, full_kv, full_output = place_packed(
        owner, both(held, came), tuple(plan), (head_width, 2 * head_width, head_width), each
    )
    own_query, own_kv = local_call(
        token_kernel, [shaped((rows, head_width), jnp.bfloat16), shaped((span * rows, 2 * head_width), jnp.bfloat16)],
        [own, full_query, full_kv], flops=4 * own.size * head_width, spare=12,
    )
    mixed, mass, queries, kv = attend(tables, own_query, own_kv, other, full_query, full_kv)

    half_shape, low_shape = shaped((rows, width)), shaped((rows, width), jnp.bfloat16)
    gain_one, shift_one, gain_two, shift_two = (
        one.reshape(1, width) for one in (attn_gain, attn_shift, ffn_gain, ffn_shift)
    )
    part_own, part_other, attended = local_call(
        project_kernel, [half_shape, low_shape, shaped(mixed.shape, jnp.bfloat16)], [mixed, full_output],
        flops=2 * mixed.size * width,
    )
    part_came, late, late_came = lax.optimization_barrier((swap_core(part_other), late, late_came))
    first_sum, hidden, hidden_own = local_call(
        first_norm_kernel, [half_shape, half_shape, low_shape],
        [tokens, part_own, part_came, gain_one, shift_one],
    )
    hidden_other = swap_core(hidden_own)
    late, late_came = tie(hidden_own, (late, late_came))
    units = units_of(((0, 0, wide), (1, 0, wide), (2, 0, PAIR)))
    plan = []
    for at, bits in enumerate(ROUTES):
        part = units[cuts[at] // PAIR : cuts[at + 1] // PAIR]
        sent = tuple(slot_masks((bits[2], bits[0])))
        plan += [(sent, part), (tuple(mask ^ (1 << bits[1]) for mask in sent), part)]
    full_inner, full_outer, counts = place_packed(
        owner, both(late, late_came), tuple(plan), (wide, wide, PAIR), each
    )
    part_own, part_other, active, slope, count_own = local_call(
        functools.partial(feed_kernel, each=each),
        [half_shape, low_shape, shaped((length, wide), jnp.bfloat16), shaped((length, wide)), shaped((8, PAIR))],
        [hidden_own, hidden_other, full_inner, full_outer, counts],
        scratch=[pltpu.VMEM((length, width), jnp.float32)],
        flops=4 * length * width * wide, transcendentals=2 * length * wide, spare=12,
    )
    count_came = swap_core(count_own)
    token_total = devices * lax.axis_size("tensor") * rows
    grad_second, grad_ffn_own, stats_two, result = local_call(
        functools.partial(second_norm_kernel, token_total=token_total),
        [half_shape, low_shape, shaped((8, width)), low_shape],
        [hidden, part_own, swap_core(part_other), gain_two, shift_two, teacher, valid_row, count_own, count_came],
        free=1,
    )
    grad_ffn_other = swap_core(grad_ffn_own)
    upper_grad, part_own, part_other = local_call(
        feed_back_kernel, [shaped((length, wide), jnp.bfloat16), half_shape, low_shape],
        [grad_ffn_own, grad_ffn_other, slope, full_inner, full_outer],
        scratch=[pltpu.VMEM((length, width), jnp.float32)],
        flops=4 * length * width * wide, spare=12,
    )
    part_came = swap_core(part_other)
    scatter_masks = tuple(tuple(slot_masks(bits[::-1])) for bits in ROUTES)
    groups = tuple((one[: span // 2], one[span // 2 :]) for one in scatter_masks)
    outs = wide_gradients(
        owner, grad_ffn_own, grad_ffn_other, active, hidden_own, hidden_other, upper_grad, groups
    )
    outs = [one.reshape(span // 2, slot_rows, one.shape[2]) for one in outs]
    wide_keep, wide_came = outs[::2], step(outs[1::2], 0)
    part_came = tie(outs[0], part_came)
    grad_first, grad_attn_own, stats_one = local_call(
        first_back_kernel, [half_shape, low_shape, shaped((8, width))],
        [grad_second, part_own, part_came, first_sum, gain_one, stats_two],
    )
    grad_attn_other = swap_core(grad_attn_own)
    stats_came = swap_core(stats_one)
    query_grad, kv_grad = attend_back(
        tables, queries, kv, mixed, mass, grad_attn_own, grad_attn_other, full_output
    )

    def folded(keep, came):
        return fold(keep, [[one] for one in came])

    small = local_call(small_kernel, [shaped((width, PAIR))], [stats_one, tie(query_grad, stats_came)])[0]
    wide_keep, wide_send = folded(wide_keep, tie(small, wide_came))
    wide_came = step(wide_send, 1)
    token_sent = token_other(tie(wide_keep[0], kv_grad), query_grad, full_kv, full_query)
    token_came = swap_core(token_sent)
    made = narrow_gradients(
        own, other, tie(token_sent, kv_grad), query_grad, grad_attn_own, grad_attn_other, attended
    )
    keep, send = token_own(
        owner, kv_grad, query_grad, full_kv, full_query, tie(made, token_came), made, small, scatter_masks
    )
    riders = tuple([bits[0] for bits in ROUTES].index(bits[2]) for bits in ROUTES)
    columns = width // 3
    ride = slot_rows * wide_keep[0].shape[2] // columns
    lengths = [one.shape[0] * one.shape[1] + ride for one in send]
    outs = local_call(
        functools.partial(merge_kernel, riders=riders),
        [shaped(one.shape[1:]) for one in wide_keep] + [shaped((one, columns), jnp.bfloat16) for one in lengths],
        wide_keep + tie(keep[0], wide_came) + send,
    )
    wide_keep, came = outs[:3], step(outs[3:], 0)
    plain = rows + 2 * slot_rows
    halves = []
    for one in keep:
        half = (one.shape[0] // 2,) + one.shape[1:]
        halves += [shaped(half), shaped(half, jnp.bfloat16)]
    far_send = [shaped((each, 2 * wide), jnp.bfloat16)] if far_count == 2 else []
    outs = local_call(
        functools.partial(part_kernel, riders=riders, plain=plain),
        halves + [shaped((slot_rows, 2 * wide))] + far_send, keep + came + list(wide_keep),
    )
    keep, send, wide_sum, wide_send = list(outs[:6:2]), list(outs[1:6:2]), outs[6], outs[7:]
    came = step(send, 1)

    def far_scatter(total, dtype=jnp.bfloat16):
        total = total.reshape(far_count, each, total.shape[1])
        for bit in far_bits[::-1]:
            half = total.shape[0] // 2
            total = total[:half] + swap_mask(total[half:].astype(dtype), 1 << bit).astype(jnp.float32)
        return total[0]

    keep, send = fold(keep, [[one] for one in came], plain)
    came = step(send, 2)
    if far_count == 2:
        part_outer, part_inner = local_call(
            wide_out_kernel, [shaped((each, wide))] * 2, [wide_sum, swap_mask(wide_send[0], 1 << far_bits[0])], free=2
        )
    else:
        wide_sum = far_scatter(wide_sum)
        part_outer, part_inner = wide_sum[:, :wide], wide_sum[:, wide:]
    came = tie(part_outer, came)
    made_shape = shaped((slot_rows, 4 * head_width + PAIR))
    send_shape = [shaped((each, 4 * head_width + PAIR), jnp.bfloat16)] if far_count == 2 else []
    *made, grad_tokens = local_call(
        last_kernel, [made_shape] + send_shape + [half_shape], [grad_first] + both(keep, came), free=1
    )
    made, send = made[0], made[1:]
    if far_count == 2:
        weight_shape = shaped((each, head_width))
        part_query, part_key, part_value, part_output, small = local_call(
            end_kernel, [weight_shape] * 4 + [shaped((each, PAIR))], [made, swap_mask(send[0], 1 << far_bits[0])],
            free=5,
        )
    else:
        narrow_sum = far_scatter(made[:, : 4 * head_width])
        small = far_scatter(made[:, 4 * head_width :], jnp.float32)
        part_query, part_output = narrow_sum[:, :head_width], narrow_sum[:, head_width : 2 * head_width]
        kv_sum = narrow_sum[:, 2 * head_width :].reshape(each, head_width // PAIR, 2, PAIR)
        part_key, part_value = (kv_sum[:, :, one].reshape(each, head_width) for one in range(2))
    loss_value = small[0, 4] / (2.0 * width * (count_own[0, 0] + count_came[0, 0]))
    half = each // 2
    mine = jnp.where(core == 0, small[:half], small[half:])
    return (
        result,
        loss_value,
        grad_tokens,
        part_query,
        part_key,
        part_value,
        part_output,
        part_inner,
        part_outer,
        mine[:, 0],
        mine[:, 1],
        mine[:, 2],
        mine[:, 3],
    )


def solution(mesh):
    both = P(("dp", "tensor"))
    rows_spec = P(("dp", "tensor"), None)
    weight_spec = P("dp", "tensor")
    in_specs = (rows_spec,) + (weight_spec,) * 6 + (P(),) * 4
    in_specs += (rows_spec, P(), P("tensor", None, None), both)
    out_specs = (rows_spec, P(), rows_spec) + (weight_spec,) * 6 + (both,) * 4
    return jax.shard_map(shards, mesh=mesh, in_specs=in_specs, out_specs=out_specs, check_vma=False)
```

```python
import functools

import jax
import jax.numpy as jnp
from jax import lax
from jax.experimental import pallas as pl
from jax.experimental.pallas import tpu as pltpu
from jax.sharding import PartitionSpec as P

BLOCK = 64
HEAD = 64
PAIR = 2 * HEAD
SLOTS = 6
ROUTES = ((0, 1, 2), (1, 2, 0), (2, 0, 1))

epsilon = 1e-05
masked_value = -1e30
score_scale = 0.125


def swap_mask(block, mask):
    count = lax.axis_size("dp")
    return lax.ppermute(block, "dp", [(one, one ^ mask) for one in range(count)])


def swap_core(block):
    return lax.ppermute(block, "tensor", [(0, 1), (1, 0)])


def dot_plain(left_side, right_side):
    return jnp.dot(left_side, right_side, preferred_element_type=jnp.float32)


def dot_cols(left_side, right_side):
    return lax.dot_general(
        left_side, right_side, (((1,), (1,)), ((), ())), preferred_element_type=jnp.float32
    )


def dot_rows(left_side, right_side):
    return lax.dot_general(
        left_side, right_side, (((0,), (0,)), ((), ())), preferred_element_type=jnp.float32
    )


def params(megabytes):
    return pltpu.CompilerParams(vmem_limit_bytes=int(megabytes) << 20)


def cost(flops=0, moved=0, transcendentals=0):
    return pl.CostEstimate(flops=int(flops), bytes_accessed=int(moved), transcendentals=int(transcendentals))


def in_vmem(count):
    return [pl.BlockSpec(memory_space=pltpu.VMEM)] * count


def in_smem(count):
    return [pl.BlockSpec(memory_space=pltpu.SMEM)] * count


def shaped(shape, dtype=jnp.float32):
    return jax.ShapeDtypeStruct(tuple(shape), dtype)


def local_call(kernel, outs, vmem_inputs, smem_inputs=(), scratch=(), flops=0, transcendentals=0, spare=8, free=0):
    moved = sum(one.size * one.dtype.itemsize for one in list(vmem_inputs) + list(outs))
    held = sum(one.size * one.dtype.itemsize for one in (shaped(s.shape, s.dtype) for s in scratch))
    held = held // (1 << 20) + 1 + spare
    return pl.pallas_call(
        kernel,
        out_shape=tuple(
            one if len(outs) - at <= free else pltpu.VMEM(one.shape, one.dtype) for at, one in enumerate(outs)
        ),
        in_specs=in_smem(len(smem_inputs)) + in_vmem(len(vmem_inputs)),
        out_specs=tuple(in_vmem(len(outs))),
        scratch_shapes=list(scratch),
        compiler_params=params(held),
        cost_estimate=pl.CostEstimate(flops=1000, bytes_accessed=1000, transcendentals=0),
    )(*smem_inputs, *[pltpu.with_memory_space_constraint(one, pltpu.VMEM) for one in vmem_inputs])


def slot_masks(bits):
    return [
        sum(((slot >> at) & 1) << bit for at, bit in enumerate(bits))
        for slot in range(1 << len(bits))
    ]


def in_pieces(values):
    high = values.astype(jnp.bfloat16).astype(jnp.float32)
    middle = (values - high).astype(jnp.bfloat16).astype(jnp.float32)
    return high + pltpu.roll(middle, 8, 1) + pltpu.roll(values - high - middle, 16, 1)


def from_pieces(pieces):
    lanes = pieces.shape[1]
    total = pieces + pltpu.roll(pieces, lanes - 8, 1) + pltpu.roll(pieces, lanes - 16, 1)
    return jnp.where(lax.broadcasted_iota(jnp.int32, pieces.shape, 1) % PAIR < 8, total, 0.0)


def fold_kernel(*refs, thirds, arrivals, plain):
    outs = refs[thirds * (1 + arrivals) :]
    for third in range(thirds):
        keep_ref = refs[third * (1 + arrivals)]
        came = refs[third * (1 + arrivals) + 1 : (third + 1) * (1 + arrivals)]
        half, lines = keep_ref.shape[0] // 2, keep_ref.shape[1]
        most = lines if plain is None else min(plain, lines)
        for side in range(2):
            part = slice(side * half, (side + 1) * half)
            total = sum([one[part, :most].astype(jnp.float32) for one in came], keep_ref[part, :most])
            out_ref = outs[2 * third + side]
            out_ref[:, :most] = total.astype(out_ref.dtype)
            if most == lines:
                continue
            for at in range(half):
                total = keep_ref[side * half + at, most:]
                for one in came:
                    total += from_pieces(one[side * half + at, most:].astype(jnp.float32))
                out_ref[at, most:] = (in_pieces(total) if side else total).astype(out_ref.dtype)


def fold(keeps, arrivals, plain=None):
    outs = []
    for keep in keeps:
        half = (keep.shape[0] // 2,) + keep.shape[1:]
        outs += [shaped(half), shaped(half, jnp.bfloat16)]
    operands = []
    for keep, came in zip(keeps, arrivals):
        operands += [keep] + list(came)
    kernel = functools.partial(fold_kernel, thirds=len(keeps), arrivals=len(arrivals[0]), plain=plain)
    outs = local_call(kernel, outs, operands)
    return list(outs[::2]), list(outs[1::2])


def pick(chosen, table):
    return lax.dot_general(
        chosen.astype(jnp.bfloat16), table.astype(jnp.bfloat16), (((chosen.ndim - 1,), (0,)), ((), ())),
        preferred_element_type=jnp.float32,
    )


def attention_tables(random_blocks, segment_all, place, core, span, row_blocks):
    heads, blocks, draws = random_blocks.shape
    half, pairs = row_blocks // 2, heads // 2
    local = jnp.arange(row_blocks, dtype=jnp.int32)
    owner = jnp.where(local < half, core, 1 - core)
    absolute = place * row_blocks + owner * half + local % half
    every = jnp.arange(blocks, dtype=jnp.int32)
    mine = absolute[:, None] == every
    edge = (every == 0) | (every == blocks - 1)
    fixed = (jnp.abs(absolute[:, None] - every) <= 1) | edge | edge[absolute][:, None]
    segment_table = segment_all.reshape(blocks, BLOCK).astype(jnp.float32)
    low, high = jnp.min(segment_table, 1), jnp.max(segment_table, 1)
    reach = (jnp.max(jnp.where(mine, low, -1.0), 1)[:, None] <= high) & (
        low <= jnp.max(jnp.where(mine, high, -1.0), 1)[:, None]
    )
    drawn = pick(mine, random_blocks.transpose(1, 0, 2).reshape(blocks, heads * draws))
    drawn = drawn.reshape(row_blocks, heads, draws, 1) == every.astype(jnp.float32)
    allowed = (jnp.any(drawn, 2) | fixed[:, None]) & reach[:, None]
    allowed = allowed.reshape(row_blocks, pairs, 2, blocks)
    listed = jnp.any(allowed, 2)
    rank = pick(listed, every[:, None] < every[None, :])
    count = jnp.max(jnp.sum(listed.astype(jnp.int32), -1), -1)
    chunks = -(-count // SLOTS)
    ends = jnp.sum(jnp.where(local[:, None] >= local[None, :], chunks[None, :], 0), 1)
    most = (row_blocks - 1) * -(-min(blocks, 5 + 2 * draws) // SLOTS) + -(-blocks // SLOTS)
    if span == 1:
        most += -(-blocks // SLOTS)
    items = jnp.arange(most, dtype=jnp.int32)
    item_query = jnp.minimum(jnp.sum((items[:, None] >= ends[None, :]).astype(jnp.int32), 1), row_blocks - 1)
    item_is = item_query[:, None] == local
    first = jnp.sum(jnp.where(item_is, (ends - chunks)[None, :], 0), 1)
    spots = ((items - first) * SLOTS)[:, None] + jnp.arange(SLOTS, dtype=jnp.int32)
    stored = (
        jnp.where((every % row_blocks) // half == core, 0, span * half)
        + ((every // row_blocks) ^ place) * half + every % half
    )
    rows = jnp.concatenate([jnp.where(listed, rank, -1.0)[:, :, None], allowed.astype(jnp.float32)], 2)
    rows = pick(item_is, rows.reshape(row_blocks, -1)).reshape(most, pairs, 3, blocks)
    here = rows[:, :, 0, None, :] == spots[:, None, :, None].astype(jnp.float32)
    code = rows[:, :, 1, None, :] * 256.0 + rows[:, :, 2, None, :] * 512.0 + stored.astype(jnp.float32)
    codes = jnp.sum(jnp.where(here, code, 0.0), -1).astype(jnp.int32)
    order = jnp.arange(2 * span * half, dtype=jnp.int32)
    order_block = (
        ((order % (span * half)) // half) ^ place
    ) * row_blocks + jnp.where(order < span * half, core, 1 - core) * half + order % half
    key_side = pick(order_block[:, None] == every, segment_table).reshape(-1, 1)
    query_side = pick(mine, segment_table)
    query_side = jnp.concatenate([query_side, query_side], 1)
    numbers = [ends[-1:], item_query, (items == first), codes.reshape(-1)]
    return (
        jnp.concatenate([one.astype(jnp.int32) for one in numbers]),
        query_side,
        jnp.broadcast_to(key_side, (key_side.shape[0], PAIR)),
    )


def two_heads(rows, low_lanes):
    rows = rows.astype(jnp.float32)
    zero = jnp.zeros_like(rows)
    return jnp.concatenate(
        [jnp.where(low_lanes, rows, zero), jnp.where(low_lanes, zero, rows)], 0
    )


def item_blocks(numbers_ref, first, side, key_side_ref):
    low_row = lax.broadcasted_iota(jnp.int32, (1, PAIR), 1) < HEAD
    spots, masks = [], []
    for slot in range(SLOTS):
        code = numbers_ref[first + slot]
        spot = pl.ds(pl.multiple_of((code & 255) * BLOCK, BLOCK), BLOCK)
        flags = jnp.where(low_row, code & 256, code & 512)
        spots.append(spot)
        masks.append(key_side_ref[spot, :] == jnp.where(flags != 0, side, -1.0))
    return spots, jnp.concatenate(masks, 0)


def attend_kernel(
    numbers_ref, query_side_ref, key_side_ref,
    own_query_ref, own_kv_ref, other_ref, query_weight_ref, kv_weight_ref,
    mixed_ref, mass_ref, q_ref, kv_ref, state_ref, mixture_ref, *, pairs
):
    half_rows, half_kv = own_query_ref.shape[0], own_kv_ref.shape[0]
    q_ref[:half_rows, :] = own_query_ref[...]
    q_ref[half_rows:, :] = dot_plain(other_ref[:half_rows, :], query_weight_ref[...]).astype(jnp.bfloat16)
    kv_ref[:half_kv, :] = own_kv_ref[...]
    step = 512

    def one_part(at, carry):
        lines = pl.ds(pl.multiple_of(at * step, step), step)
        kv_ref[pl.ds(pl.multiple_of(half_kv + at * step, step), step), :] = dot_plain(
            other_ref[lines, :], kv_weight_ref[...]
        ).astype(jnp.bfloat16)
        return carry

    lax.fori_loop(0, half_kv // step, one_part, 0)
    low_lanes = lax.broadcasted_iota(jnp.int32, (BLOCK, PAIR), 1) < HEAD
    most = (numbers_ref.shape[0] - 1) // (2 + pairs * SLOTS)

    def one_item(item, carry):
        query = numbers_ref[1 + item]
        fresh = numbers_ref[1 + most + item] == 1
        side = query_side_ref[pl.ds(query, 1), :]
        rows = pl.ds(pl.multiple_of(query * BLOCK, BLOCK), BLOCK)
        held = []
        for pair in range(pairs):
            both = two_heads(q_ref[rows, pair * PAIR : (pair + 1) * PAIR], low_lanes).astype(jnp.bfloat16)
            spots, mask = item_blocks(
                numbers_ref, 1 + 2 * most + (item * pairs + pair) * SLOTS, side, key_side_ref
            )
            start = pair * 2 * PAIR
            keys = jnp.concatenate([kv_ref[spot, start : start + PAIR] for spot in spots], 0)
            values = jnp.concatenate([kv_ref[spot, start + PAIR : start + 2 * PAIR] for spot in spots], 0)
            held.append((jnp.where(mask, dot_cols(keys, both) * score_scale, masked_value), values))
        done = []
        for pair in range(pairs):
            scores, values = held[pair]
            place = query * pairs + pair
            state = state_ref[place]
            old_top = jnp.where(fresh, masked_value, state[0:1, :])
            top = jnp.maximum(old_top, jnp.max(scores, axis=0, keepdims=True))
            raised = jnp.exp(scores - top)
            shrunk = jnp.exp(old_top - top)
            total = jnp.where(fresh, 0.0, state[1:2, :] * shrunk) + jnp.sum(raised, axis=0, keepdims=True)
            mixture = jnp.where(fresh, 0.0, mixture_ref[place] * shrunk) + dot_rows(
                values, raised.astype(jnp.bfloat16)
            )
            done.append((top, total, mixture))
        for pair in range(pairs):
            top, total, mixture = done[pair]
            place = query * pairs + pair
            state_ref[place, 0:1, :] = top
            state_ref[place, 1:2, :] = total
            mixture_ref[place] = mixture
            normed = (mixture / total).T
            mixed_ref[rows, pair * PAIR : (pair + 1) * PAIR] = jnp.where(
                low_lanes, normed[:BLOCK], normed[BLOCK:]
            )
            mass_ref[place] = jnp.broadcast_to(top + jnp.log(total), (8, PAIR))
        return carry

    lax.fori_loop(0, numbers_ref[0], one_item, 0)


def attend(tables, own_query, own_kv, other, query_weight, kv_weight):
    rows, width = 2 * own_query.shape[0], own_query.shape[1]
    pairs, row_blocks = width // PAIR, rows // BLOCK
    places = pairs * row_blocks
    return local_call(
        functools.partial(attend_kernel, pairs=pairs),
        [
            shaped((rows, width)),
            shaped((places, 8, PAIR)),
            shaped((rows, width), jnp.bfloat16),
            shaped((2 * own_kv.shape[0], own_kv.shape[1]), jnp.bfloat16),
        ],
        list(tables[1:]) + [own_query, own_kv, other, query_weight, kv_weight],
        tables[:1],
        [
            pltpu.VMEM((places, 8, PAIR), jnp.float32),
            pltpu.VMEM((places, PAIR, PAIR), jnp.float32),
        ],
        flops=8e9, transcendentals=4e6, spare=12,
    )


def attend_back_kernel(
    numbers_ref, query_side_ref, key_side_ref, q_ref, kv_ref,
    mixed_ref, mass_ref, own_grad_ref, other_grad_ref, weight_ref,
    query_grad_ref, kv_grad_ref, sum_ref, grad_ref, query_sum_ref, *, pairs
):
    half_rows = own_grad_ref.shape[0]
    grad_ref[:half_rows, :] = dot_plain(own_grad_ref[...], weight_ref[...]).astype(jnp.bfloat16)
    grad_ref[half_rows:, :] = dot_plain(other_grad_ref[...], weight_ref[...]).astype(jnp.bfloat16)
    low_lanes = lax.broadcasted_iota(jnp.int32, (BLOCK, PAIR), 1) < HEAD
    most = (numbers_ref.shape[0] - 1) // (2 + pairs * SLOTS)
    sum_ref[...] = jnp.zeros_like(sum_ref)

    def one_item(item, carry):
        query = numbers_ref[1 + item]
        fresh = numbers_ref[1 + most + item] == 1
        side = query_side_ref[pl.ds(query, 1), :]
        rows = pl.ds(pl.multiple_of(query * BLOCK, BLOCK), BLOCK)
        held = []
        for pair in range(pairs):
            lanes = slice(pair * PAIR, (pair + 1) * PAIR)
            both = two_heads(q_ref[rows, lanes], low_lanes).astype(jnp.bfloat16)
            grads = grad_ref[rows, lanes].astype(jnp.float32)
            turned = (grads * mixed_ref[rows, lanes]).T
            inner = jnp.concatenate(
                [jnp.sum(turned[:HEAD], axis=0, keepdims=True), jnp.sum(turned[HEAD:], axis=0, keepdims=True)], 1
            )
            grads = two_heads(grads, low_lanes).astype(jnp.bfloat16)
            spots, mask = item_blocks(
                numbers_ref, 1 + 2 * most + (item * pairs + pair) * SLOTS, side, key_side_ref
            )
            start = pair * 2 * PAIR
            kv = jnp.concatenate([kv_ref[spot, start : start + 2 * PAIR] for spot in spots], 0)
            blank = jnp.zeros_like(both)
            sides = jnp.concatenate(
                [jnp.concatenate([both, blank], 1), jnp.concatenate([blank, grads], 1)], 0
            )
            held.append((dot_cols(kv, sides), inner, sides, kv, spots, mask))
        done = []
        for pair in range(pairs):
            products, inner, sides, kv, spots, mask = held[pair]
            place = query * pairs + pair
            scores = jnp.where(mask, products[:, :PAIR] * score_scale, masked_value)
            chances = jnp.exp(scores - mass_ref[place, 0:1, :])
            score_grads = (chances * (products[:, PAIR:] - inner)).astype(jnp.bfloat16)
            query_grad = dot_rows(score_grads, kv[:, :PAIR])
            kv_grad = dot_plain(jnp.concatenate([score_grads, chances.astype(jnp.bfloat16)], 1), sides)
            done.append((query_grad, kv_grad))
        for pair in range(pairs):
            lanes = slice(pair * PAIR, (pair + 1) * PAIR)
            start = pair * 2 * PAIR
            query_grad, kv_grad = done[pair]
            spots = held[pair][4]
            query_grad = jnp.where(low_lanes, query_grad[:BLOCK], query_grad[BLOCK:])
            query_sum_ref[rows, lanes] = jnp.where(fresh, 0.0, query_sum_ref[rows, lanes]) + query_grad
            for slot, spot in enumerate(spots):
                sum_ref[spot, start : start + 2 * PAIR] += kv_grad[slot * BLOCK : (slot + 1) * BLOCK]
        return carry

    lax.fori_loop(0, numbers_ref[0], one_item, 0)
    query_grad_ref[...] = (query_sum_ref[...] * score_scale).astype(jnp.bfloat16)
    for pair in range(pairs):
        start = pair * 2 * PAIR
        kv_grad_ref[:, start : start + PAIR] = (sum_ref[:, start : start + PAIR] * score_scale).astype(jnp.bfloat16)
        kv_grad_ref[:, start + PAIR : start + 2 * PAIR] = sum_ref[:, start + PAIR : start + 2 * PAIR].astype(
            jnp.bfloat16
        )


def attend_back(tables, queries, kv, mixed, mass, own_grad, other_grad, weight):
    rows, width = queries.shape
    pairs = width // PAIR
    return local_call(
        functools.partial(attend_back_kernel, pairs=pairs),
        [shaped((rows, width), jnp.bfloat16), shaped(kv.shape, jnp.bfloat16)],
        list(tables[1:]) + [queries, kv, mixed, mass, own_grad, other_grad, weight],
        tables[:1],
        [
            pltpu.VMEM(kv.shape, jnp.float32),
            pltpu.VMEM((rows, width), jnp.bfloat16),
            pltpu.VMEM((rows, width), jnp.float32),
        ],
        flops=10e9, transcendentals=4e6, spare=12,
    )


LANES = 2 * PAIR


def packed_rows(slot_rows, columns):
    return columns // LANES * slot_rows + (slot_rows // 2 if columns % LANES else 0)


def put_packed(out_ref, base, source_ref, first, columns, slot_rows):
    for chunk in range(columns // LANES):
        at = first + chunk * LANES
        out_ref[base : base + slot_rows, :] = source_ref[:, at : at + LANES]
        base += slot_rows
    if columns % LANES:
        half, at = slot_rows // 2, first + columns - PAIR
        out_ref[base : base + half, :PAIR] = source_ref[:half, at : at + PAIR]
        out_ref[base : base + half, PAIR:] = source_ref[half:, at : at + PAIR]


def unpacked(packed, slot_rows):
    full = packed.shape[0] // slot_rows
    parts = [packed[at * slot_rows : (at + 1) * slot_rows] for at in range(full)]
    tail = packed[full * slot_rows :]
    if tail.shape[0]:
        parts.append(jnp.concatenate([tail[:, :PAIR], tail[:, PAIR:]], 0))
    return jnp.concatenate(parts, 1)


def fetched(far, near, arrived):
    copies = [
        pltpu.make_async_copy(far_ref, near_ref, arrived.at[at])
        for at, (far_ref, near_ref) in enumerate(zip(far, near))
    ]
    for copy in copies:
        copy.start()
    for copy in copies:
        copy.wait()


def weight_start_kernel(*refs):
    near = refs[9:-1]
    fetched(refs[:7], near, refs[-1])
    first_ref, second_ref = refs[7:9]
    for out_ref, sources in ((first_ref, near[:4]), (second_ref, near[4:6])):
        at = 0
        for one in sources:
            out_ref[:, at : at + one.shape[1]] = one[...]
            at += one.shape[1]
    count = jnp.sum(near[6][...].astype(jnp.float32), axis=1, keepdims=True)
    second_ref[:, at:] = jnp.broadcast_to(count, (second_ref.shape[0], PAIR)).astype(jnp.bfloat16)


def token_start_kernel(tokens_ref, *refs):
    near_ref, arrived = refs[3:]
    fetched([tokens_ref], [near_ref], arrived)
    columns = refs[0].shape[1]
    for at in range(3):
        refs[at][...] = near_ref[:, at * columns : (at + 1) * columns]


def fetching_call(kernel, outs, sources):
    return pl.pallas_call(
        kernel,
        out_shape=[pltpu.VMEM(one.shape, one.dtype) for one in outs],
        in_specs=[pl.BlockSpec(memory_space=pltpu.HBM)] * len(sources),
        out_specs=in_vmem(len(outs)),
        scratch_shapes=[pltpu.VMEM(one.shape, one.dtype) for one in sources]
        + [pltpu.SemaphoreType.DMA((len(sources),))],
        compiler_params=params(8),
    )(*[pltpu.with_memory_space_constraint(one, pltpu.HBM) for one in sources])


def first_pack_kernel(*refs, slot_rows):
    sent, came, weights_ref, outs = refs[:3], refs[3:6], refs[6], refs[7:]
    rows = sent[0].shape[0]
    third = weights_ref.shape[1] // 3
    for at in range(3):
        outs[at][:rows, :] = sent[at][...]
        outs[at][rows : 2 * rows, :] = came[at][...]
        put_packed(outs[at], 2 * rows, weights_ref, at * third, third, slot_rows)


def second_pack_kernel(*refs, rows, slot_rows, cuts):
    second_ref, outs = refs[6], refs[7:]
    for at in range(3):
        sent_ref, came_ref, out_ref = refs[2 * at], refs[2 * at + 1], outs[at]
        tail = sent_ref.shape[0] - rows
        out_ref[:rows, :] = sent_ref[:rows, :]
        out_ref[rows : 2 * rows, :] = came_ref[:rows, :]
        out_ref[2 * rows : 2 * rows + tail, :] = sent_ref[rows:, :]
        out_ref[2 * rows + tail : 2 * (rows + tail), :] = came_ref[rows:, :]
        put_packed(out_ref, 2 * (rows + tail), second_ref, cuts[at], cuts[at + 1] - cuts[at], slot_rows)


def third_pack_kernel(*refs, masks, rows, tail):
    out_ref = refs[6]
    columns = refs[0].shape[1]
    for at in range(3):
        tokens = len(masks[2 * at]) * rows
        for side in range(2):
            piece, target = refs[2 * at + side], refs[7 + at]
            for slot, mask in enumerate(masks[2 * at + side]):
                out_ref[mask * rows : (mask + 1) * rows, at * columns : (at + 1) * columns] = piece[
                    slot * rows : (slot + 1) * rows, :
                ]
            target[side * tail : (side + 1) * tail, :] = piece[tokens : tokens + tail, :]
            rest = piece.shape[0] - tokens - tail
            base = 2 * tail + side * rest
            target[base : base + rest, :] = piece[tokens + tail :, :]


def fourth_pack_kernel(*refs, skip):
    for at in range(3):
        rest = refs[2 * at].shape[0] - skip
        for side in range(2):
            refs[6 + at][side * rest : (side + 1) * rest, :] = refs[2 * at + side][skip:, :]


def place_packed_kernel(owner_ref, *refs, plan, slot_rows, rows):
    pieces, outs = refs[: len(plan)], refs[len(plan) :]
    for piece, (masks, units) in zip(pieces, plan):
        size = packed_rows(slot_rows, len(units) * PAIR)
        for slot, mask in enumerate(masks):
            for far in range(2):
                lines = pl.ds(pl.multiple_of(owner_ref[mask * 2 + far] * rows, rows), rows)
                unit = 0
                while unit < len(units):
                    out, column = units[unit]
                    base = slot * size + unit // 2 * slot_rows
                    if unit + 1 == len(units) and unit % 2 == 0:
                        outs[out][lines, column : column + PAIR] = piece[
                            base : base + rows, far * PAIR : (far + 1) * PAIR
                        ]
                        unit += 1
                        continue
                    base += far * rows
                    if unit % 2 == 0 and units[unit + 1] == (out, column + PAIR):
                        outs[out][lines, column : column + LANES] = piece[base : base + rows, :]
                        unit += 2
                        continue
                    side = unit % 2 * PAIR
                    outs[out][lines, column : column + PAIR] = piece[base : base + rows, side : side + PAIR]
                    unit += 1


def place_packed(owner, pieces, plan, widths, rows):
    blocks = owner.shape[0]
    far_count = blocks // 8
    slot_rows = far_count * rows
    outs = [shaped((blocks * rows, width), jnp.bfloat16) for width in widths]
    if rows % 16 == 0 and far_count == 2:
        kernel = functools.partial(place_packed_kernel, plan=plan, slot_rows=slot_rows, rows=rows)
        return local_call(kernel, outs, pieces, [owner], spare=12)
    made = [jnp.zeros(out.shape, out.dtype) for out in outs]
    for piece, (masks, units) in zip(pieces, plan):
        size = packed_rows(slot_rows, len(units) * PAIR)
        for slot, mask in enumerate(masks):
            block = unpacked(piece[slot * size : (slot + 1) * size], slot_rows)
            lines = owner.reshape(8, far_count)[mask][:, None] * rows + jnp.arange(rows, dtype=jnp.int32)
            for unit, (out, column) in enumerate(units):
                made[out] = made[out].at[lines.reshape(-1), column : column + PAIR].set(
                    block[:, unit * PAIR : (unit + 1) * PAIR]
                )
    return made


def units_of(targets):
    return tuple((out, column + at) for out, column, size in targets for at in range(0, size, PAIR))


def placed_blocks(grad, owner, masks):
    blocks = owner.shape[0]
    rows = grad.shape[0] // blocks
    spots = owner.reshape(8, -1)[jnp.array(masks)].reshape(-1)
    return jnp.take(grad.reshape(blocks, rows, grad.shape[1]), spots, axis=0)


def token_kernel(x_ref, query_weight_ref, kv_weight_ref, query_ref, kv_ref):
    rows = query_ref.shape[0]
    query_ref[...] = dot_plain(x_ref[:rows, :], query_weight_ref[...]).astype(jnp.bfloat16)
    step = 512

    def one_part(at, carry):
        lines = pl.ds(pl.multiple_of(at * step, step), step)
        kv_ref[lines, :] = dot_plain(x_ref[lines, :], kv_weight_ref[...]).astype(jnp.bfloat16)
        return carry

    lax.fori_loop(0, kv_ref.shape[0] // step, one_part, 0)


def project_kernel(mixed_ref, weight_ref, own_ref, other_ref, low_ref):
    low = mixed_ref[...].astype(jnp.bfloat16)
    low_ref[...] = low
    total = dot_cols(low, weight_ref[...])
    half = own_ref.shape[0]
    own_ref[...] = total[:half]
    other_ref[...] = total[half:].astype(jnp.bfloat16)


def normed_rows(values):
    centred = values - jnp.mean(values, axis=-1, keepdims=True)
    spread = jnp.mean(centred * centred, axis=-1, keepdims=True)
    scale = lax.rsqrt(spread + epsilon)
    return centred * scale, scale


def norm_back(grads, normed, scale, gain):
    inner = grads * gain
    middle = jnp.mean(inner, axis=-1, keepdims=True)
    slant = jnp.mean(inner * normed, axis=-1, keepdims=True)
    return scale * (inner - middle - normed * slant)


def first_norm_kernel(tokens_ref, own_ref, came_ref, gain_ref, shift_ref, sum_ref, hidden_ref, low_ref):
    total = tokens_ref[...].astype(jnp.float32) + (own_ref[...] + came_ref[...].astype(jnp.float32))
    sum_ref[...] = total
    normed, _ = normed_rows(total)
    hidden = normed * gain_ref[...] + shift_ref[...]
    hidden_ref[...] = hidden
    low_ref[...] = hidden.astype(jnp.bfloat16)


def feed_kernel(
    own_hidden_ref, other_hidden_ref, inner_ref, outer_ref, counts_ref,
    own_ref, other_ref, active_ref, slope_ref, count_ref, total_ref, *, each
):
    count = jnp.sum(counts_ref[...].astype(jnp.float32), axis=0, keepdims=True) / each
    count_ref[...] = jnp.broadcast_to(count, count_ref.shape)
    hidden = jnp.concatenate([own_hidden_ref[...], other_hidden_ref[...]], 0)
    step = 256
    for start in range(0, inner_ref.shape[1], step):
        columns = slice(start, start + step)
        upper = dot_plain(hidden, inner_ref[:, columns])
        chance = 0.5 * (1.0 + lax.erf(upper * (0.5**0.5)))
        active = (upper * chance).astype(jnp.bfloat16)
        active_ref[:, columns] = active
        slope_ref[:, columns] = chance + upper * (jnp.exp(-0.5 * upper * upper) * 0.3989422804014327)
        part = dot_cols(active, outer_ref[:, columns])
        if start:
            total_ref[...] += part
        else:
            total_ref[...] = part
    half = own_ref.shape[0]
    own_ref[...] = total_ref[:half, :]
    other_ref[...] = total_ref[half:, :].astype(jnp.bfloat16)


def second_norm_kernel(
    hidden_ref, own_ref, came_ref, gain_ref, shift_ref, teacher_ref, valid_ref, count_own_ref, count_came_ref,
    grad_ref, low_ref, stats_ref, result_ref, *, token_total
):
    valid = jnp.broadcast_to(valid_ref[...].astype(jnp.float32), (PAIR, valid_ref.shape[1])).T[:, :1]
    factor = token_total / (count_own_ref[0:1, 0:1] + count_came_ref[0:1, 0:1])
    total = hidden_ref[...] + (own_ref[...] + came_ref[...].astype(jnp.float32))
    normed, scale = normed_rows(total)
    gain = gain_ref[...]
    result = normed * gain + shift_ref[...]
    result_ref[...] = result.astype(jnp.bfloat16)
    errors = (result - teacher_ref[...].astype(jnp.float32)) * valid
    grads = errors * factor
    grad = norm_back(grads, normed, scale, gain)
    grad_ref[...] = grad
    low_ref[...] = grad.astype(jnp.bfloat16)
    stats_ref[...] = jnp.zeros_like(stats_ref)
    stats_ref[2:3, :] = jnp.sum(grads * normed, axis=0, keepdims=True)
    stats_ref[3:4, :] = jnp.sum(grads, axis=0, keepdims=True)
    squares = jnp.sum(jnp.sum(errors * errors, axis=0, keepdims=True), axis=1, keepdims=True)
    stats_ref[4:5, :] = jnp.broadcast_to(squares, (1, stats_ref.shape[1]))


def feed_back_kernel(own_grad_ref, other_grad_ref, slope_ref, inner_ref, outer_ref, upper_ref, own_ref, other_ref, total_ref):
    grads = jnp.concatenate([own_grad_ref[...], other_grad_ref[...]], 0)
    step = 256
    for start in range(0, inner_ref.shape[1], step):
        columns = slice(start, start + step)
        upper = (dot_plain(grads, outer_ref[:, columns]) * slope_ref[:, columns]).astype(jnp.bfloat16)
        upper_ref[:, columns] = upper
        part = dot_cols(upper, inner_ref[:, columns])
        if start:
            total_ref[...] += part
        else:
            total_ref[...] = part
    half = own_ref.shape[0]
    own_ref[...] = total_ref[:half, :]
    other_ref[...] = total_ref[half:, :].astype(jnp.bfloat16)


def first_back_kernel(
    grad_ref, own_ref, came_ref, sum_ref, gain_ref, other_stats_ref, out_ref, low_ref, stats_ref
):
    grads = grad_ref[...] + (own_ref[...] + came_ref[...].astype(jnp.float32))
    normed, scale = normed_rows(sum_ref[...])
    grad = norm_back(grads, normed, scale, gain_ref[...])
    out_ref[...] = grad
    low_ref[...] = grad.astype(jnp.bfloat16)
    stats_ref[...] = other_stats_ref[...]
    stats_ref[0:1, :] = jnp.sum(grads * normed, axis=0, keepdims=True)
    stats_ref[1:2, :] = jnp.sum(grads, axis=0, keepdims=True)


def write_blocks(owner_ref, made_ref, column, width, out_ref, out_column, masks, far_count, rows):
    for slot, mask in enumerate(masks):
        for far in range(far_count):
            start = pl.multiple_of(owner_ref[mask * far_count + far] * rows, rows)
            out_ref[slot * far_count + far, :, out_column : out_column + width] = made_ref[
                pl.ds(start, rows), column : column + width
            ].astype(out_ref.dtype)


def wide_kernel(
    owner_ref, own_grad_ref, other_grad_ref, active_ref, own_hidden_ref, other_hidden_ref, upper_ref, *refs,
    groups, far_count, rows, step
):
    outs, made_ref = refs[:-1], refs[-1]
    grads = jnp.concatenate([own_grad_ref[...], other_grad_ref[...]], 0)
    hidden = jnp.concatenate([own_hidden_ref[...], other_hidden_ref[...]], 0)
    width = active_ref.shape[1]
    third_width = 2 * width // 3
    for start in range(0, 2 * width, step):
        if start < width:
            made_ref[...] = dot_rows(grads, active_ref[:, start : start + step])
        else:
            made_ref[...] = dot_rows(hidden, upper_ref[:, start - width : start - width + step])
        third = start // third_width
        for at, masks in enumerate(groups[third]):
            write_blocks(
                owner_ref, made_ref, 0, step, outs[third * len(groups[third]) + at], start % third_width,
                masks, far_count, rows
            )


def wide_gradients(owner, own_grad, other_grad, active, own_hidden, other_hidden, upper, groups):
    blocks = owner.shape[0]
    far_count, rows = blocks // 8, own_grad.shape[1] // blocks
    width = active.shape[1]
    third_width = 2 * width // 3
    if rows % 16:
        made = jnp.concatenate(
            [
                dot_rows(jnp.concatenate([own_grad, other_grad], 0), active),
                dot_rows(jnp.concatenate([own_hidden, other_hidden], 0), upper),
            ],
            1,
        )
        outs = []
        for third, group in enumerate(groups):
            columns = made[:, third * third_width : (third + 1) * third_width]
            for at, masks in enumerate(group):
                outs.append(placed_blocks(columns, owner, masks).astype(jnp.bfloat16 if at else jnp.float32))
        return outs
    step = 512
    outs = []
    for group in groups:
        for at, masks in enumerate(group):
            outs.append(
                shaped((len(masks) * far_count, rows, third_width), jnp.bfloat16 if at else jnp.float32)
            )
    kernel = functools.partial(wide_kernel, groups=groups, far_count=far_count, rows=rows, step=step)
    return local_call(
        kernel, outs, [own_grad, other_grad, active, own_hidden, other_hidden, upper], [owner],
        [pltpu.VMEM((own_grad.shape[1], step), jnp.float32)],
        flops=8 * own_grad.size * width, spare=12,
    )


def narrow_kernel(
    own_ref, other_ref, kv_grad_ref, query_grad_ref, own_grad_ref, other_grad_ref, low_ref, made_ref
):
    half, near = own_ref.shape[0], own_grad_ref.shape[0]
    width = query_grad_ref.shape[1]
    made_ref[:, :width] = dot_rows(own_ref[:near, :], query_grad_ref[:near, :]) + dot_rows(
        other_ref[:near, :], query_grad_ref[near:, :]
    )
    made_ref[:, width : 2 * width] = dot_rows(own_grad_ref[...], low_ref[:near, :]) + dot_rows(
        other_grad_ref[...], low_ref[near:, :]
    )
    made_ref[:, 2 * width :] = dot_rows(own_ref[...], kv_grad_ref[:half, :])
    made_ref[:, 2 * width :] += dot_rows(other_ref[...], kv_grad_ref[half:, :])


def narrow_gradients(own, other, kv_grad, query_grad, own_grad, other_grad, low):
    width = query_grad.shape[1]
    return local_call(
        narrow_kernel, [shaped((own.shape[1], 4 * width))],
        [own, other, kv_grad, query_grad, own_grad, other_grad, low],
        flops=4 * own.size * 2 * width + 8 * own_grad.size * width, spare=12,
    )[0]


def token_other_kernel(kv_grad_ref, query_grad_ref, kv_weight_ref, query_weight_ref, out_ref):
    near, half = query_grad_ref.shape[0] // 2, kv_grad_ref.shape[0] // 2
    step = 512

    def one_part(at, carry):
        lines = pl.ds(pl.multiple_of(half + at * step, step), step)
        total = dot_cols(kv_grad_ref[lines, :], kv_weight_ref[...])
        out_ref[pl.ds(pl.multiple_of(at * step, step), step), :] = total.astype(jnp.bfloat16)
        return carry

    lax.fori_loop(1, half // step, one_part, 0)
    total = dot_cols(kv_grad_ref[half : half + step, :], kv_weight_ref[...])
    total = jnp.concatenate(
        [total[:near] + dot_cols(query_grad_ref[near:, :], query_weight_ref[...]), total[near:]], 0
    )
    out_ref[:step, :] = total.astype(jnp.bfloat16)


def token_other(kv_grad, query_grad, kv_weight, query_weight):
    return local_call(
        token_other_kernel, [shaped((kv_grad.shape[0] // 2, kv_weight.shape[0]), jnp.bfloat16)],
        [kv_grad, query_grad, kv_weight, query_weight],
        flops=kv_grad.size * kv_weight.shape[0], spare=12,
    )[0]


def small_kernel(own_ref, came_ref, out_ref):
    lines = own_ref[...] + came_ref[...]
    out_ref[...] = jnp.concatenate([lines, jnp.zeros((PAIR - lines.shape[0], lines.shape[1]), jnp.float32)], 0).T


def token_own_kernel(
    owner_ref, kv_grad_ref, query_grad_ref, kv_weight_ref, query_weight_ref, came_ref, made_ref, small_ref, *outs,
    masks, rows, placed
):
    near = query_grad_ref.shape[0] // 2
    half, columns = outs[0].shape[0], outs[0].shape[2]
    slot_rows = made_ref.shape[1] if placed else made_ref.shape[0] // (2 * half)
    for mask in range(2 * half):
        lines = slice(mask * near, (mask + 1) * near)
        total = dot_cols(kv_grad_ref[lines, :], kv_weight_ref[...]) + came_ref[lines, :].astype(jnp.float32)
        if mask == 0:
            total += dot_cols(query_grad_ref[:near, :], query_weight_ref[...])
        for third, order in enumerate(masks):
            slot = order.index(mask)
            out_ref = outs[2 * third + slot // half]
            at = slot % half
            out_ref[at, :near, :] = total[:, third * columns : (third + 1) * columns].astype(out_ref.dtype)
            for side in range(2):
                base = near + side * slot_rows
                part = slice((2 * third + side) * columns, (2 * third + side + 1) * columns)
                if placed:
                    out_ref[at, base : base + slot_rows, :] = made_ref[mask, :, part].astype(out_ref.dtype)
                    continue
                for far in range(slot_rows // rows):
                    start = pl.multiple_of(owner_ref[mask * (slot_rows // rows) + far] * rows, rows)
                    out_ref[at, base + far * rows : base + (far + 1) * rows, :] = made_ref[
                        pl.ds(start, rows), part
                    ].astype(out_ref.dtype)
            if third == 0:
                if placed:
                    small = small_ref[mask]
                else:
                    far_count = slot_rows // rows
                    small = jnp.concatenate(
                        [
                            small_ref[pl.ds(pl.multiple_of(owner_ref[mask * far_count + far] * rows, rows), rows), :]
                            for far in range(far_count)
                        ],
                        0,
                    )
                small = jnp.concatenate([small[: slot_rows // 2], small[slot_rows // 2 :]], 1)
                if slot >= half:
                    small = in_pieces(small)
                out_ref[at, near + 2 * slot_rows :, :] = small.astype(out_ref.dtype)


def token_own(owner, kv_grad, query_grad, kv_weight, query_weight, came, made, small, masks):
    near = query_grad.shape[0] // 2
    half = came.shape[0] // near // 2
    blocks, features = owner.shape[0], made.shape[0]
    rows, slot_rows = features // blocks, features // (2 * half)
    columns = kv_weight.shape[0] // 3
    placed = rows % 16 != 0
    if placed:
        made, small = (
            placed_blocks(one, owner, tuple(range(2 * half))).reshape(2 * half, slot_rows, one.shape[1])
            for one in (made, small)
        )
    outs = []
    for third in range(len(masks)):
        shape = (half, near + 2 * slot_rows + (slot_rows // 2 if third == 0 else 0), columns)
        outs += [shaped(shape), shaped(shape, jnp.bfloat16)]
    outs = local_call(
        functools.partial(token_own_kernel, masks=masks, rows=rows, placed=placed), outs,
        [kv_grad, query_grad, kv_weight, query_weight, came, made, small], [owner],
        flops=2 * came.shape[0] * kv_weight.size, spare=12,
    )
    return list(outs[::2]), list(outs[1::2])


def last_kernel(grad_ref, *refs):
    token_ref, made_ref = refs[-1], refs[6]
    near, columns = grad_ref.shape[0], refs[0].shape[2]
    slot_rows = made_ref.shape[0]
    width = 6 * columns
    for third in range(3):
        plain = near + 2 * slot_rows
        total = refs[2 * third][0, :plain] + refs[2 * third + 1][0, :plain].astype(jnp.float32)
        if third == 0:
            small = refs[0][0, plain:] + from_pieces(refs[1][0, plain:].astype(jnp.float32))
            made_ref[: slot_rows // 2, width:] = small[:, :PAIR]
            made_ref[slot_rows // 2 :, width:] = small[:, PAIR:]
        part = slice(third * columns, (third + 1) * columns)
        token_ref[:, part] = grad_ref[:, part] + total[:near]
        for side in range(2):
            at = (2 * third + side) * columns
            made_ref[:, at : at + columns] = total[near + side * slot_rows : near + (side + 1) * slot_rows]
    if len(refs) > 8:
        send_ref = refs[7]
        half = slot_rows // 2
        send_ref[:, :width] = made_ref[half:, :width].astype(jnp.bfloat16)
        send_ref[:, width:] = in_pieces(made_ref[half:, width:]).astype(jnp.bfloat16)


def end_kernel(
    core_ref, made_ref, came_ref, count_own_ref, count_came_ref,
    query_ref, key_ref, value_ref, output_ref, loss_ref, *norm_refs
):
    rows, width = query_ref.shape
    total = made_ref[:rows, : 4 * width] + came_ref[:, : 4 * width].astype(jnp.float32)
    query_ref[...] = total[:, :width]
    output_ref[...] = total[:, width : 2 * width]
    for at in range(0, width, PAIR):
        first = 2 * width + 2 * at
        key_ref[:, at : at + PAIR] = total[:, first : first + PAIR]
        value_ref[:, at : at + PAIR] = total[:, first + PAIR : first + 2 * PAIR]
    small = made_ref[:rows, 4 * width :] + from_pieces(came_ref[:, 4 * width :].astype(jnp.float32))
    features = 2.0 * rows * core_ref[1].astype(jnp.float32)
    loss_ref[...] = small[:1, 4:5] / (features * (count_own_ref[0:1, 0:1] + count_came_ref[0:1, 0:1]))
    lines = jnp.concatenate([small, jnp.zeros((PAIR - rows, PAIR), jnp.float32)], 0).T
    half = rows // 2
    mine = jnp.where(core_ref[0] == 0, lines[:, :half], lines[:, half:rows])
    for at, one_ref in enumerate(norm_refs):
        one_ref[...] = mine[at : at + 1, :]


def merge_kernel(*refs, riders):
    keeps, cames, sends, kept, messages = (refs[at : at + 3] for at in range(0, 15, 3))
    for third, rider in enumerate(riders):
        kept[third][...] = keeps[third][0] + cames[third][0].astype(jnp.float32)
        later = (keeps[third][1] + cames[third][1].astype(jnp.float32)).astype(jnp.bfloat16)
        slots, lines, columns = sends[rider].shape
        for slot in range(slots):
            messages[rider][slot * lines : (slot + 1) * lines, :] = sends[rider][slot]
        base, rows = slots * lines, later.shape[0]
        for chunk in range(later.shape[1] // columns):
            messages[rider][base + chunk * rows : base + (chunk + 1) * rows, :] = later[
                :, chunk * columns : (chunk + 1) * columns
            ]


def part_kernel(*refs, riders, plain):
    keeps, cames, kept = refs[:3], refs[3:6], refs[6:9]
    outs, wide_ref = refs[9:15], refs[15]
    for third in range(3):
        keep_ref, came_ref = keeps[third], cames[third]
        slots, lines, _ = keep_ref.shape
        most = min(plain, lines)
        for slot in range(slots):
            side, at = slot // (slots // 2), slot % (slots // 2)
            out_ref, base = outs[2 * third + side], slot * lines
            total = keep_ref[slot, :most] + came_ref[base : base + most, :].astype(jnp.float32)
            out_ref[at, :most] = total.astype(out_ref.dtype)
            if most < lines:
                total = keep_ref[slot, most:] + from_pieces(
                    came_ref[base + most : base + lines, :].astype(jnp.float32)
                )
                out_ref[at, most:] = (in_pieces(total) if side else total).astype(out_ref.dtype)
    for third, rider in enumerate(riders):
        slots, lines, columns = keeps[rider].shape
        rows, width = kept[third].shape
        for chunk in range(width // columns):
            part = slice(chunk * columns, (chunk + 1) * columns)
            base = slots * lines + chunk * rows
            wide_ref[:, third * width + chunk * columns : third * width + (chunk + 1) * columns] = kept[third][
                :, part
            ] + cames[rider][base : base + rows, :].astype(jnp.float32)
    if len(refs) > 16:
        refs[16][...] = wide_ref[wide_ref.shape[0] // 2 :, :].astype(jnp.bfloat16)


def wide_out_kernel(made_ref, came_ref, outer_ref, inner_ref):
    rows, width = outer_ref.shape
    outer_ref[...] = made_ref[:rows, :width] + came_ref[:, :width].astype(jnp.float32)
    inner_ref[...] = made_ref[:rows, width:] + came_ref[:, width:].astype(jnp.float32)


def tie(first, second):
    leaves, tree = jax.tree.flatten(second)
    tied = lax.optimization_barrier(tuple(leaves) + (first,))
    return jax.tree.unflatten(tree, tied[:-1])


def shards(
    tokens,
    query_weight,
    key_weight,
    value_weight,
    output_weight,
    inner_weight,
    outer_weight,
    attn_gain,
    attn_shift,
    ffn_gain,
    ffn_shift,
    teacher,
    segments,
    random_blocks,
    valid_tokens,
):
    devices = lax.axis_size("dp")
    dp_index = lax.axis_index("dp")
    core = lax.axis_index("tensor")
    rows, width = tokens.shape
    length = 2 * rows
    span = segments.shape[1] // length
    near_bits = span.bit_length() - 1
    far_bits = tuple(range(near_bits, devices.bit_length() - 1))
    place, far_place = dp_index % span, dp_index // span
    far_count = devices // span
    each = width // devices
    slot_rows = far_count * each
    head_width = query_weight.shape[1]
    wide = inner_weight.shape[1]
    masks = jnp.arange(span, dtype=jnp.int32)
    fars = jnp.arange(far_count, dtype=jnp.int32)
    owner = ((fars[None, :] ^ far_place) * span + (masks[:, None] ^ place)).reshape(-1)

    def far_gather(block):
        held = block[None]
        for bit in far_bits:
            held = jnp.concatenate([held, swap_mask(held, 1 << bit)], 0)
        return held.reshape(slot_rows, block.shape[1])

    def step(held, at):
        return [swap_mask(one, 1 << bits[at]) for one, bits in zip(held, ROUTES)]

    def both(held, came):
        return [one for pair in zip(held, came) for one in pair]

    def messages(lines):
        return [shaped((one, third), jnp.bfloat16) for one in lines]

    third = width // 3
    tail = packed_rows(slot_rows, 4 * head_width // 3)
    cuts = (0, 2 * wide // 3, 4 * wide // 3, 2 * wide + PAIR)
    sizes = [packed_rows(slot_rows, last - first) for first, last in zip(cuts, cuts[1:])]
    valid_row = valid_tokens.reshape(1, rows)
    first, second = fetching_call(
        weight_start_kernel,
        [shaped((each, 4 * head_width), jnp.bfloat16), shaped((each, cuts[3]), jnp.bfloat16)],
        [query_weight, key_weight, value_weight, output_weight, inner_weight, outer_weight, valid_row],
    )
    held = list(
        fetching_call(token_start_kernel, [shaped((rows, third), jnp.bfloat16)] * 3, [tie(first, tokens)])
    )
    came = step(held, 0)
    first_held, second_held = far_gather(first), far_gather(second)
    held = local_call(
        functools.partial(first_pack_kernel, slot_rows=slot_rows), messages([2 * rows + tail] * 3),
        held + came + [first_held],
    )
    came = step(held, 1)
    held = local_call(
        functools.partial(second_pack_kernel, rows=2 * rows, slot_rows=slot_rows, cuts=cuts),
        messages([4 * rows + 2 * tail + size for size in sizes]), both(held, came) + [second_held],
    )
    came = step(held, 2)
    segment_all = lax.dynamic_index_in_dim(segments, far_place, 0, keepdims=False)
    tables = attention_tables(random_blocks, segment_all, place, core, span, length // BLOCK)
    tables, owner, came = lax.optimization_barrier((tables, owner, came))
    sent_masks = [tuple(slot_masks(bits[:2])) for bits in ROUTES]
    came_masks = [tuple(mask ^ (1 << bits[2]) for mask in sent) for sent, bits in zip(sent_masks, ROUTES)]
    own, *held = local_call(
        functools.partial(third_pack_kernel, masks=tuple(both(sent_masks, came_masks)), rows=rows, tail=2 * tail),
        [shaped((span * rows, width), jnp.bfloat16)] + messages([4 * tail + 2 * size for size in sizes]),
        both(held, came),
    )
    came = step(held, 0)
    other = swap_core(own)
    late = local_call(
        functools.partial(fourth_pack_kernel, skip=4 * tail), messages([4 * size for size in sizes]),
        both(held, came),
    )
    late_came = step(late, 1)

    held, came = tie(late[0], (held, came))
    units = units_of(
        ((0, 0, head_width),)
        + tuple((1, 2 * at + shift, PAIR) for shift in (0, PAIR) for at in range(0, head_width, PAIR))
        + ((2, 0, head_width),)
    )
    plan = []
    for at, bits in enumerate(ROUTES):
        part = units[at * len(units) // 3 : (at + 1) * len(units) // 3]
        sent = tuple(slot_masks((bits[1], bits[2])))
        plan += [(sent, part), (tuple(mask ^ (1 << bits[0]) for mask in sent), part)]
    full_query, full_kv, full_output = place_packed(
        owner, both(held, came), tuple(plan), (head_width, 2 * head_width, head_width), each
    )
    own_query, own_kv = local_call(
        token_kernel, [shaped((rows, head_width), jnp.bfloat16), shaped((span * rows, 2 * head_width), jnp.bfloat16)],
        [own, full_query, full_kv], flops=4 * own.size * head_width, spare=12,
    )
    mixed, mass, queries, kv = attend(tables, own_query, own_kv, other, full_query, full_kv)

    half_shape, low_shape = shaped((rows, width)), shaped((rows, width), jnp.bfloat16)
    gain_one, shift_one, gain_two, shift_two = (
        one.reshape(1, width) for one in (attn_gain, attn_shift, ffn_gain, ffn_shift)
    )
    part_own, part_other, attended = local_call(
        project_kernel, [half_shape, low_shape, shaped(mixed.shape, jnp.bfloat16)], [mixed, full_output],
        flops=2 * mixed.size * width,
    )
    part_came, late, late_came = lax.optimization_barrier((swap_core(part_other), late, late_came))
    first_sum, hidden, hidden_own = local_call(
        first_norm_kernel, [half_shape, half_shape, low_shape],
        [tokens, part_own, part_came, gain_one, shift_one],
    )
    hidden_other = swap_core(hidden_own)
    late, late_came = tie(hidden_own, (late, late_came))
    units = units_of(((0, 0, wide), (1, 0, wide), (2, 0, PAIR)))
    plan = []
    for at, bits in enumerate(ROUTES):
        part = units[cuts[at] // PAIR : cuts[at + 1] // PAIR]
        sent = tuple(slot_masks((bits[2], bits[0])))
        plan += [(sent, part), (tuple(mask ^ (1 << bits[1]) for mask in sent), part)]
    full_inner, full_outer, counts = place_packed(
        owner, both(late, late_came), tuple(plan), (wide, wide, PAIR), each
    )
    part_own, part_other, active, slope, count_own = local_call(
        functools.partial(feed_kernel, each=each),
        [half_shape, low_shape, shaped((length, wide), jnp.bfloat16), shaped((length, wide)), shaped((8, PAIR))],
        [hidden_own, hidden_other, full_inner, full_outer, counts],
        scratch=[pltpu.VMEM((length, width), jnp.float32)],
        flops=4 * length * width * wide, transcendentals=2 * length * wide, spare=12,
    )
    count_came = swap_core(count_own)
    token_total = devices * lax.axis_size("tensor") * rows
    grad_second, grad_ffn_own, stats_two, result = local_call(
        functools.partial(second_norm_kernel, token_total=token_total),
        [half_shape, low_shape, shaped((8, width)), low_shape],
        [hidden, part_own, swap_core(part_other), gain_two, shift_two, teacher, valid_row, count_own, count_came],
        free=1,
    )
    grad_ffn_other = swap_core(grad_ffn_own)
    upper_grad, part_own, part_other = local_call(
        feed_back_kernel, [shaped((length, wide), jnp.bfloat16), half_shape, low_shape],
        [grad_ffn_own, grad_ffn_other, slope, full_inner, full_outer],
        scratch=[pltpu.VMEM((length, width), jnp.float32)],
        flops=4 * length * width * wide, spare=12,
    )
    part_came = swap_core(part_other)
    scatter_masks = tuple(tuple(slot_masks(bits[::-1])) for bits in ROUTES)
    groups = tuple((one[: span // 2], one[span // 2 :]) for one in scatter_masks)
    outs = wide_gradients(
        owner, grad_ffn_own, grad_ffn_other, active, hidden_own, hidden_other, upper_grad, groups
    )
    outs = [one.reshape(span // 2, slot_rows, one.shape[2]) for one in outs]
    wide_keep, wide_came = outs[::2], step(outs[1::2], 0)
    part_came = tie(outs[0], part_came)
    grad_first, grad_attn_own, stats_one = local_call(
        first_back_kernel, [half_shape, low_shape, shaped((8, width))],
        [grad_second, part_own, part_came, first_sum, gain_one, stats_two],
    )
    grad_attn_other = swap_core(grad_attn_own)
    stats_came = swap_core(stats_one)
    query_grad, kv_grad = attend_back(
        tables, queries, kv, mixed, mass, grad_attn_own, grad_attn_other, full_output
    )

    def folded(keep, came):
        return fold(keep, [[one] for one in came])

    small = local_call(small_kernel, [shaped((width, PAIR))], [stats_one, tie(query_grad, stats_came)])[0]
    token_sent = token_other(tie(small, kv_grad), query_grad, full_kv, full_query)
    wide_keep, wide_send = folded(wide_keep, tie(token_sent, wide_came))
    wide_came = step(wide_send, 1)
    token_came = swap_core(tie(wide_keep[0], token_sent))
    made = narrow_gradients(
        own, other, tie(wide_keep[0], kv_grad), query_grad, grad_attn_own, grad_attn_other, attended
    )
    keep, send = token_own(
        owner, kv_grad, query_grad, full_kv, full_query, tie(made, token_came), made, small, scatter_masks
    )
    riders = tuple([bits[0] for bits in ROUTES].index(bits[2]) for bits in ROUTES)
    columns = width // 3
    ride = slot_rows * wide_keep[0].shape[2] // columns
    lengths = [one.shape[0] * one.shape[1] + ride for one in send]
    outs = local_call(
        functools.partial(merge_kernel, riders=riders),
        [shaped(one.shape[1:]) for one in wide_keep] + [shaped((one, columns), jnp.bfloat16) for one in lengths],
        wide_keep + tie(keep[0], wide_came) + send,
    )
    wide_keep, came = outs[:3], step(outs[3:], 0)
    plain = rows + 2 * slot_rows
    halves = []
    for one in keep:
        half = (one.shape[0] // 2,) + one.shape[1:]
        halves += [shaped(half), shaped(half, jnp.bfloat16)]
    far_send = [shaped((each, 2 * wide), jnp.bfloat16)] if far_count == 2 else []
    outs = local_call(
        functools.partial(part_kernel, riders=riders, plain=plain),
        halves + [shaped((slot_rows, 2 * wide))] + far_send, keep + came + list(wide_keep),
    )
    keep, send, wide_sum, wide_send = list(outs[:6:2]), list(outs[1:6:2]), outs[6], outs[7:]
    came = step(send, 1)

    def far_scatter(total, dtype=jnp.bfloat16):
        total = total.reshape(far_count, each, total.shape[1])
        for bit in far_bits[::-1]:
            half = total.shape[0] // 2
            total = total[:half] + swap_mask(total[half:].astype(dtype), 1 << bit).astype(jnp.float32)
        return total[0]

    keep, send = fold(keep, [[one] for one in came], plain)
    came = step(send, 2)
    if far_count == 2:
        part_outer, part_inner = local_call(
            wide_out_kernel, [shaped((each, wide))] * 2, [wide_sum, swap_mask(wide_send[0], 1 << far_bits[0])], free=2
        )
    else:
        wide_sum = far_scatter(wide_sum)
        part_outer, part_inner = wide_sum[:, :wide], wide_sum[:, wide:]
    came = tie(part_outer, came)
    made_shape = shaped((slot_rows, 4 * head_width + PAIR))
    send_shape = [shaped((each, 4 * head_width + PAIR), jnp.bfloat16)] if far_count == 2 else []
    *made, grad_tokens = local_call(
        last_kernel, [made_shape] + send_shape + [half_shape], [grad_first] + both(keep, came), free=1
    )
    made, send = made[0], made[1:]
    half = each // 2
    if far_count == 2:
        weight_shape = shaped((each, head_width))
        outs = local_call(
            end_kernel, [weight_shape] * 4 + [shaped((1, 1))] + [shaped((1, half))] * 4,
            [made, swap_mask(send[0], 1 << far_bits[0]), count_own, count_came],
            [jnp.stack([core, jnp.int32(devices)])], free=9,
        )
        part_query, part_key, part_value, part_output = outs[:4]
        loss_value = outs[4].reshape(())
        norm_parts = [one.reshape(half) for one in outs[5:]]
    else:
        narrow_sum = far_scatter(made[:, : 4 * head_width])
        small = far_scatter(made[:, 4 * head_width :], jnp.float32)
        part_query, part_output = narrow_sum[:, :head_width], narrow_sum[:, head_width : 2 * head_width]
        kv_sum = narrow_sum[:, 2 * head_width :].reshape(each, head_width // PAIR, 2, PAIR)
        part_key, part_value = (kv_sum[:, :, one].reshape(each, head_width) for one in range(2))
        loss_value = small[0, 4] / (2.0 * width * (count_own[0, 0] + count_came[0, 0]))
        mine = jnp.where(core == 0, small[:half], small[half:])
        norm_parts = [mine[:, at] for at in range(4)]
    return (
        result,
        loss_value,
        grad_tokens,
        part_query,
        part_key,
        part_value,
        part_output,
        part_inner,
        part_outer,
        *norm_parts,
    )


def solution(mesh):
    both = P(("dp", "tensor"))
    rows_spec = P(("dp", "tensor"), None)
    weight_spec = P("dp", "tensor")
    in_specs = (rows_spec,) + (weight_spec,) * 6 + (P(),) * 4
    in_specs += (rows_spec, P(), P("tensor", None, None), both)
    out_specs = (rows_spec, P(), rows_spec) + (weight_spec,) * 6 + (both,) * 4
    return jax.shard_map(shards, mesh=mesh, in_specs=in_specs, out_specs=out_specs, check_vma=False)
```

```python
import functools

import jax
import jax.numpy as jnp
from jax import lax
from jax.experimental import pallas as pl
from jax.experimental.pallas import tpu as pltpu
from jax.sharding import PartitionSpec as P

BLOCK = 64
HEAD = 64
PAIR = 2 * HEAD
SLOTS = 6
ROUTES = ((0, 1, 2), (1, 2, 0), (2, 0, 1))

epsilon = 1e-05
masked_value = -1e30
score_scale = 0.125


def swap_mask(block, mask):
    count = lax.axis_size("dp")
    return lax.ppermute(block, "dp", [(one, one ^ mask) for one in range(count)])


def swap_core(block):
    return lax.ppermute(block, "tensor", [(0, 1), (1, 0)])


def dot_plain(left_side, right_side):
    return jnp.dot(left_side, right_side, preferred_element_type=jnp.float32)


def dot_cols(left_side, right_side):
    return lax.dot_general(
        left_side, right_side, (((1,), (1,)), ((), ())), preferred_element_type=jnp.float32
    )


def dot_rows(left_side, right_side):
    return lax.dot_general(
        left_side, right_side, (((0,), (0,)), ((), ())), preferred_element_type=jnp.float32
    )


def params(megabytes):
    return pltpu.CompilerParams(vmem_limit_bytes=int(megabytes) << 20)


def cost(flops=0, moved=0, transcendentals=0):
    return pl.CostEstimate(flops=int(flops), bytes_accessed=int(moved), transcendentals=int(transcendentals))


def in_vmem(count):
    return [pl.BlockSpec(memory_space=pltpu.VMEM)] * count


def in_smem(count):
    return [pl.BlockSpec(memory_space=pltpu.SMEM)] * count


def shaped(shape, dtype=jnp.float32):
    return jax.ShapeDtypeStruct(tuple(shape), dtype)


def local_call(kernel, outs, vmem_inputs, smem_inputs=(), scratch=(), flops=0, transcendentals=0, spare=8, free=0):
    moved = sum(one.size * one.dtype.itemsize for one in list(vmem_inputs) + list(outs))
    held = sum(one.size * one.dtype.itemsize for one in (shaped(s.shape, s.dtype) for s in scratch))
    held = held // (1 << 20) + 1 + spare
    return pl.pallas_call(
        kernel,
        out_shape=tuple(
            one if len(outs) - at <= free else pltpu.VMEM(one.shape, one.dtype) for at, one in enumerate(outs)
        ),
        in_specs=in_smem(len(smem_inputs)) + in_vmem(len(vmem_inputs)),
        out_specs=tuple(in_vmem(len(outs))),
        scratch_shapes=list(scratch),
        compiler_params=params(held),
        cost_estimate=pl.CostEstimate(flops=1000, bytes_accessed=1000, transcendentals=0),
    )(*smem_inputs, *[pltpu.with_memory_space_constraint(one, pltpu.VMEM) for one in vmem_inputs])


def slot_masks(bits):
    return [
        sum(((slot >> at) & 1) << bit for at, bit in enumerate(bits))
        for slot in range(1 << len(bits))
    ]


def in_pieces(values):
    high = values.astype(jnp.bfloat16).astype(jnp.float32)
    middle = (values - high).astype(jnp.bfloat16).astype(jnp.float32)
    return high + pltpu.roll(middle, 8, 1) + pltpu.roll(values - high - middle, 16, 1)


def from_pieces(pieces):
    lanes = pieces.shape[1]
    total = pieces + pltpu.roll(pieces, lanes - 8, 1) + pltpu.roll(pieces, lanes - 16, 1)
    return jnp.where(lax.broadcasted_iota(jnp.int32, pieces.shape, 1) % PAIR < 8, total, 0.0)


def fold_kernel(*refs, thirds, arrivals, plain):
    outs = refs[thirds * (1 + arrivals) :]
    for third in range(thirds):
        keep_ref = refs[third * (1 + arrivals)]
        came = refs[third * (1 + arrivals) + 1 : (third + 1) * (1 + arrivals)]
        half, lines = keep_ref.shape[0] // 2, keep_ref.shape[1]
        most = lines if plain is None else min(plain, lines)
        for side in range(2):
            part = slice(side * half, (side + 1) * half)
            total = sum([one[part, :most].astype(jnp.float32) for one in came], keep_ref[part, :most])
            out_ref = outs[2 * third + side]
            out_ref[:, :most] = total.astype(out_ref.dtype)
            if most == lines:
                continue
            for at in range(half):
                total = keep_ref[side * half + at, most:]
                for one in came:
                    total += from_pieces(one[side * half + at, most:].astype(jnp.float32))
                out_ref[at, most:] = (in_pieces(total) if side else total).astype(out_ref.dtype)


def fold(keeps, arrivals, plain=None):
    outs = []
    for keep in keeps:
        half = (keep.shape[0] // 2,) + keep.shape[1:]
        outs += [shaped(half), shaped(half, jnp.bfloat16)]
    operands = []
    for keep, came in zip(keeps, arrivals):
        operands += [keep] + list(came)
    kernel = functools.partial(fold_kernel, thirds=len(keeps), arrivals=len(arrivals[0]), plain=plain)
    outs = local_call(kernel, outs, operands)
    return list(outs[::2]), list(outs[1::2])


def pick(chosen, table):
    return lax.dot_general(
        chosen.astype(jnp.bfloat16), table.astype(jnp.bfloat16), (((chosen.ndim - 1,), (0,)), ((), ())),
        preferred_element_type=jnp.float32,
    )


def attention_tables(random_blocks, segment_all, place, core, span, row_blocks):
    heads, blocks, draws = random_blocks.shape
    half, pairs = row_blocks // 2, heads // 2
    local = jnp.arange(row_blocks, dtype=jnp.int32)
    owner = jnp.where(local < half, core, 1 - core)
    absolute = place * row_blocks + owner * half + local % half
    every = jnp.arange(blocks, dtype=jnp.int32)
    mine = absolute[:, None] == every
    edge = (every == 0) | (every == blocks - 1)
    fixed = (jnp.abs(absolute[:, None] - every) <= 1) | edge | edge[absolute][:, None]
    segment_table = segment_all.reshape(blocks, BLOCK).astype(jnp.float32)
    low, high = jnp.min(segment_table, 1), jnp.max(segment_table, 1)
    reach = (jnp.max(jnp.where(mine, low, -1.0), 1)[:, None] <= high) & (
        low <= jnp.max(jnp.where(mine, high, -1.0), 1)[:, None]
    )
    drawn = pick(mine, random_blocks.transpose(1, 0, 2).reshape(blocks, heads * draws))
    drawn = drawn.reshape(row_blocks, heads, draws, 1) == every.astype(jnp.float32)
    allowed = (jnp.any(drawn, 2) | fixed[:, None]) & reach[:, None]
    allowed = allowed.reshape(row_blocks, pairs, 2, blocks)
    listed = jnp.any(allowed, 2)
    rank = pick(listed, every[:, None] < every[None, :])
    count = jnp.max(jnp.sum(listed.astype(jnp.int32), -1), -1)
    chunks = -(-count // SLOTS)
    ends = jnp.sum(jnp.where(local[:, None] >= local[None, :], chunks[None, :], 0), 1)
    most = (row_blocks - 1) * -(-min(blocks, 5 + 2 * draws) // SLOTS) + -(-blocks // SLOTS)
    if span == 1:
        most += -(-blocks // SLOTS)
    items = jnp.arange(most, dtype=jnp.int32)
    item_query = jnp.minimum(jnp.sum((items[:, None] >= ends[None, :]).astype(jnp.int32), 1), row_blocks - 1)
    item_is = item_query[:, None] == local
    first = jnp.sum(jnp.where(item_is, (ends - chunks)[None, :], 0), 1)
    spots = ((items - first) * SLOTS)[:, None] + jnp.arange(SLOTS, dtype=jnp.int32)
    stored = (
        jnp.where((every % row_blocks) // half == core, 0, span * half)
        + ((every // row_blocks) ^ place) * half + every % half
    )
    rows = jnp.concatenate([jnp.where(listed, rank, -1.0)[:, :, None], allowed.astype(jnp.float32)], 2)
    rows = pick(item_is, rows.reshape(row_blocks, -1)).reshape(most, pairs, 3, blocks)
    here = rows[:, :, 0, None, :] == spots[:, None, :, None].astype(jnp.float32)
    code = rows[:, :, 1, None, :] * 256.0 + rows[:, :, 2, None, :] * 512.0 + stored.astype(jnp.float32)
    codes = jnp.sum(jnp.where(here, code, 0.0), -1).astype(jnp.int32)
    order = jnp.arange(2 * span * half, dtype=jnp.int32)
    order_block = (
        ((order % (span * half)) // half) ^ place
    ) * row_blocks + jnp.where(order < span * half, core, 1 - core) * half + order % half
    key_side = pick(order_block[:, None] == every, segment_table).reshape(-1, 1)
    query_side = pick(mine, segment_table)
    query_side = jnp.concatenate([query_side, query_side], 1)
    numbers = [ends[-1:], item_query, (items == first), codes.reshape(-1)]
    return (
        jnp.concatenate([one.astype(jnp.int32) for one in numbers]),
        query_side,
        jnp.broadcast_to(key_side, (key_side.shape[0], PAIR)),
    )


def two_heads(rows, low_lanes):
    rows = rows.astype(jnp.float32)
    zero = jnp.zeros_like(rows)
    return jnp.concatenate(
        [jnp.where(low_lanes, rows, zero), jnp.where(low_lanes, zero, rows)], 0
    )


def item_blocks(numbers_ref, first, side, key_side_ref):
    low_row = lax.broadcasted_iota(jnp.int32, (1, PAIR), 1) < HEAD
    spots, masks = [], []
    for slot in range(SLOTS):
        code = numbers_ref[first + slot]
        spot = pl.ds(pl.multiple_of((code & 255) * BLOCK, BLOCK), BLOCK)
        flags = jnp.where(low_row, code & 256, code & 512)
        spots.append(spot)
        masks.append(key_side_ref[spot, :] == jnp.where(flags != 0, side, -1.0))
    return spots, jnp.concatenate(masks, 0)


def attend_kernel(
    numbers_ref, query_side_ref, key_side_ref,
    own_query_ref, own_kv_ref, other_ref, query_weight_ref, kv_weight_ref,
    mixed_ref, mass_ref, q_ref, kv_ref, state_ref, mixture_ref, *, pairs
):
    half_rows, half_kv = own_query_ref.shape[0], own_kv_ref.shape[0]
    q_ref[:half_rows, :] = own_query_ref[...]
    q_ref[half_rows:, :] = dot_plain(other_ref[:half_rows, :], query_weight_ref[...]).astype(jnp.bfloat16)
    kv_ref[:half_kv, :] = own_kv_ref[...]
    step = 512

    def one_part(at, carry):
        lines = pl.ds(pl.multiple_of(at * step, step), step)
        kv_ref[pl.ds(pl.multiple_of(half_kv + at * step, step), step), :] = dot_plain(
            other_ref[lines, :], kv_weight_ref[...]
        ).astype(jnp.bfloat16)
        return carry

    lax.fori_loop(0, half_kv // step, one_part, 0)
    low_lanes = lax.broadcasted_iota(jnp.int32, (BLOCK, PAIR), 1) < HEAD
    most = (numbers_ref.shape[0] - 1) // (2 + pairs * SLOTS)

    def one_item(item, carry):
        query = numbers_ref[1 + item]
        fresh = numbers_ref[1 + most + item] == 1
        side = query_side_ref[pl.ds(query, 1), :]
        rows = pl.ds(pl.multiple_of(query * BLOCK, BLOCK), BLOCK)
        held = []
        for pair in range(pairs):
            both = two_heads(q_ref[rows, pair * PAIR : (pair + 1) * PAIR], low_lanes).astype(jnp.bfloat16)
            spots, mask = item_blocks(
                numbers_ref, 1 + 2 * most + (item * pairs + pair) * SLOTS, side, key_side_ref
            )
            start = pair * 2 * PAIR
            keys = jnp.concatenate([kv_ref[spot, start : start + PAIR] for spot in spots], 0)
            values = jnp.concatenate([kv_ref[spot, start + PAIR : start + 2 * PAIR] for spot in spots], 0)
            held.append((jnp.where(mask, dot_cols(keys, both) * score_scale, masked_value), values))
        done = []
        for pair in range(pairs):
            scores, values = held[pair]
            place = query * pairs + pair
            state = state_ref[place]
            old_top = jnp.where(fresh, masked_value, state[0:1, :])
            top = jnp.maximum(old_top, jnp.max(scores, axis=0, keepdims=True))
            raised = jnp.exp(scores - top)
            shrunk = jnp.exp(old_top - top)
            total = jnp.where(fresh, 0.0, state[1:2, :] * shrunk) + jnp.sum(raised, axis=0, keepdims=True)
            mixture = jnp.where(fresh, 0.0, mixture_ref[place] * shrunk) + dot_rows(
                values, raised.astype(jnp.bfloat16)
            )
            done.append((top, total, mixture))
        for pair in range(pairs):
            top, total, mixture = done[pair]
            place = query * pairs + pair
            state_ref[place, 0:1, :] = top
            state_ref[place, 1:2, :] = total
            mixture_ref[place] = mixture
            normed = (mixture / total).T
            mixed_ref[rows, pair * PAIR : (pair + 1) * PAIR] = jnp.where(
                low_lanes, normed[:BLOCK], normed[BLOCK:]
            )
            mass_ref[place] = jnp.broadcast_to(top + jnp.log(total), (8, PAIR))
        return carry

    lax.fori_loop(0, numbers_ref[0], one_item, 0)


def attend(tables, own_query, own_kv, other, query_weight, kv_weight):
    rows, width = 2 * own_query.shape[0], own_query.shape[1]
    pairs, row_blocks = width // PAIR, rows // BLOCK
    places = pairs * row_blocks
    return local_call(
        functools.partial(attend_kernel, pairs=pairs),
        [
            shaped((rows, width)),
            shaped((places, 8, PAIR)),
            shaped((rows, width), jnp.bfloat16),
            shaped((2 * own_kv.shape[0], own_kv.shape[1]), jnp.bfloat16),
        ],
        list(tables[1:]) + [own_query, own_kv, other, query_weight, kv_weight],
        tables[:1],
        [
            pltpu.VMEM((places, 8, PAIR), jnp.float32),
            pltpu.VMEM((places, PAIR, PAIR), jnp.float32),
        ],
        flops=8e9, transcendentals=4e6, spare=12,
    )


def attend_back_kernel(
    numbers_ref, query_side_ref, key_side_ref, q_ref, kv_ref,
    mixed_ref, mass_ref, own_grad_ref, other_grad_ref, weight_ref,
    query_grad_ref, kv_grad_ref, sum_ref, grad_ref, query_sum_ref, *, pairs
):
    half_rows = own_grad_ref.shape[0]
    grad_ref[:half_rows, :] = dot_plain(own_grad_ref[...], weight_ref[...]).astype(jnp.bfloat16)
    grad_ref[half_rows:, :] = dot_plain(other_grad_ref[...], weight_ref[...]).astype(jnp.bfloat16)
    low_lanes = lax.broadcasted_iota(jnp.int32, (BLOCK, PAIR), 1) < HEAD
    most = (numbers_ref.shape[0] - 1) // (2 + pairs * SLOTS)
    sum_ref[...] = jnp.zeros_like(sum_ref)

    def one_item(item, carry):
        query = numbers_ref[1 + item]
        fresh = numbers_ref[1 + most + item] == 1
        side = query_side_ref[pl.ds(query, 1), :]
        rows = pl.ds(pl.multiple_of(query * BLOCK, BLOCK), BLOCK)
        held = []
        for pair in range(pairs):
            lanes = slice(pair * PAIR, (pair + 1) * PAIR)
            both = two_heads(q_ref[rows, lanes], low_lanes).astype(jnp.bfloat16)
            grads = grad_ref[rows, lanes].astype(jnp.float32)
            turned = (grads * mixed_ref[rows, lanes]).T
            inner = jnp.concatenate(
                [jnp.sum(turned[:HEAD], axis=0, keepdims=True), jnp.sum(turned[HEAD:], axis=0, keepdims=True)], 1
            )
            grads = two_heads(grads, low_lanes).astype(jnp.bfloat16)
            spots, mask = item_blocks(
                numbers_ref, 1 + 2 * most + (item * pairs + pair) * SLOTS, side, key_side_ref
            )
            start = pair * 2 * PAIR
            kv = jnp.concatenate([kv_ref[spot, start : start + 2 * PAIR] for spot in spots], 0)
            blank = jnp.zeros_like(both)
            sides = jnp.concatenate(
                [jnp.concatenate([both, blank], 1), jnp.concatenate([blank, grads], 1)], 0
            )
            held.append((dot_cols(kv, sides), inner, sides, kv, spots, mask))
        done = []
        for pair in range(pairs):
            products, inner, sides, kv, spots, mask = held[pair]
            place = query * pairs + pair
            scores = jnp.where(mask, products[:, :PAIR] * score_scale, masked_value)
            chances = jnp.exp(scores - mass_ref[place, 0:1, :])
            score_grads = (chances * (products[:, PAIR:] - inner)).astype(jnp.bfloat16)
            query_grad = dot_rows(score_grads, kv[:, :PAIR])
            kv_grad = dot_plain(jnp.concatenate([score_grads, chances.astype(jnp.bfloat16)], 1), sides)
            done.append((query_grad, kv_grad))
        for pair in range(pairs):
            lanes = slice(pair * PAIR, (pair + 1) * PAIR)
            start = pair * 2 * PAIR
            query_grad, kv_grad = done[pair]
            spots = held[pair][4]
            query_grad = jnp.where(low_lanes, query_grad[:BLOCK], query_grad[BLOCK:])
            query_sum_ref[rows, lanes] = jnp.where(fresh, 0.0, query_sum_ref[rows, lanes]) + query_grad
            for slot, spot in enumerate(spots):
                sum_ref[spot, start : start + 2 * PAIR] += kv_grad[slot * BLOCK : (slot + 1) * BLOCK]
        return carry

    lax.fori_loop(0, numbers_ref[0], one_item, 0)
    query_grad_ref[...] = (query_sum_ref[...] * score_scale).astype(jnp.bfloat16)
    for pair in range(pairs):
        start = pair * 2 * PAIR
        kv_grad_ref[:, start : start + PAIR] = (sum_ref[:, start : start + PAIR] * score_scale).astype(jnp.bfloat16)
        kv_grad_ref[:, start + PAIR : start + 2 * PAIR] = sum_ref[:, start + PAIR : start + 2 * PAIR].astype(
            jnp.bfloat16
        )


def attend_back(tables, queries, kv, mixed, mass, own_grad, other_grad, weight):
    rows, width = queries.shape
    pairs = width // PAIR
    return local_call(
        functools.partial(attend_back_kernel, pairs=pairs),
        [shaped((rows, width), jnp.bfloat16), shaped(kv.shape, jnp.bfloat16)],
        list(tables[1:]) + [queries, kv, mixed, mass, own_grad, other_grad, weight],
        tables[:1],
        [
            pltpu.VMEM(kv.shape, jnp.float32),
            pltpu.VMEM((rows, width), jnp.bfloat16),
            pltpu.VMEM((rows, width), jnp.float32),
        ],
        flops=10e9, transcendentals=4e6, spare=12,
    )


LANES = 2 * PAIR


def packed_rows(slot_rows, columns):
    return columns // LANES * slot_rows + (slot_rows // 2 if columns % LANES else 0)


def put_packed(out_ref, base, source_ref, first, columns, slot_rows):
    for chunk in range(columns // LANES):
        at = first + chunk * LANES
        out_ref[base : base + slot_rows, :] = source_ref[:, at : at + LANES]
        base += slot_rows
    if columns % LANES:
        half, at = slot_rows // 2, first + columns - PAIR
        out_ref[base : base + half, :PAIR] = source_ref[:half, at : at + PAIR]
        out_ref[base : base + half, PAIR:] = source_ref[half:, at : at + PAIR]


def unpacked(packed, slot_rows):
    full = packed.shape[0] // slot_rows
    parts = [packed[at * slot_rows : (at + 1) * slot_rows] for at in range(full)]
    tail = packed[full * slot_rows :]
    if tail.shape[0]:
        parts.append(jnp.concatenate([tail[:, :PAIR], tail[:, PAIR:]], 0))
    return jnp.concatenate(parts, 1)


def fetched(far, near, arrived):
    copies = [
        pltpu.make_async_copy(far_ref, near_ref, arrived.at[at])
        for at, (far_ref, near_ref) in enumerate(zip(far, near))
    ]
    for copy in copies:
        copy.start()
    for copy in copies:
        copy.wait()


def start_kernel(*refs):
    near = refs[13:-1]
    fetched(refs[:8], near, refs[-1])
    first_ref, second_ref, thirds = refs[8], refs[9], refs[10:13]
    columns = thirds[0].shape[1]
    for at in range(3):
        thirds[at][...] = near[7][:, at * columns : (at + 1) * columns]
    for out_ref, sources in ((first_ref, near[:4]), (second_ref, near[4:6])):
        at = 0
        for one in sources:
            out_ref[:, at : at + one.shape[1]] = one[...]
            at += one.shape[1]
    count = jnp.sum(near[6][...].astype(jnp.float32), axis=1, keepdims=True)
    second_ref[:, at:] = jnp.broadcast_to(count, (second_ref.shape[0], PAIR)).astype(jnp.bfloat16)


def fetching_call(kernel, outs, sources):
    return pl.pallas_call(
        kernel,
        out_shape=[pltpu.VMEM(one.shape, one.dtype) for one in outs],
        in_specs=[pl.BlockSpec(memory_space=pltpu.HBM)] * len(sources),
        out_specs=in_vmem(len(outs)),
        scratch_shapes=[pltpu.VMEM(one.shape, one.dtype) for one in sources]
        + [pltpu.SemaphoreType.DMA((len(sources),))],
        compiler_params=params(8),
    )(*[pltpu.with_memory_space_constraint(one, pltpu.HBM) for one in sources])


def first_pack_kernel(*refs, slot_rows):
    sent, came, weights_ref, outs = refs[:3], refs[3:6], refs[6], refs[7:]
    rows = sent[0].shape[0]
    third = weights_ref.shape[1] // 3
    for at in range(3):
        outs[at][:rows, :] = sent[at][...]
        outs[at][rows : 2 * rows, :] = came[at][...]
        put_packed(outs[at], 2 * rows, weights_ref, at * third, third, slot_rows)


def second_pack_kernel(*refs, rows, slot_rows, cuts):
    second_ref, outs = refs[6], refs[7:]
    for at in range(3):
        sent_ref, came_ref, out_ref = refs[2 * at], refs[2 * at + 1], outs[at]
        tail = sent_ref.shape[0] - rows
        out_ref[:rows, :] = sent_ref[:rows, :]
        out_ref[rows : 2 * rows, :] = came_ref[:rows, :]
        out_ref[2 * rows : 2 * rows + tail, :] = sent_ref[rows:, :]
        out_ref[2 * rows + tail : 2 * (rows + tail), :] = came_ref[rows:, :]
        put_packed(out_ref, 2 * (rows + tail), second_ref, cuts[at], cuts[at + 1] - cuts[at], slot_rows)


def place_tokens_kernel(*refs, masks, rows):
    out_ref = refs[6]
    columns = refs[0].shape[1]
    for at, group in enumerate(masks):
        third = at // 2
        for slot, mask in enumerate(group):
            out_ref[mask * rows : (mask + 1) * rows, third * columns : (third + 1) * columns] = refs[at][
                slot * rows : (slot + 1) * rows, :
            ]


def third_pack_kernel(*refs, tokens, tail):
    for at in range(3):
        for side in range(2):
            piece, target = refs[2 * at + side], refs[6 + at]
            target[side * tail : (side + 1) * tail, :] = piece[tokens : tokens + tail, :]
            rest = piece.shape[0] - tokens - tail
            base = 2 * tail + side * rest
            target[base : base + rest, :] = piece[tokens + tail :, :]


def fourth_pack_kernel(*refs, skip):
    for at in range(3):
        rest = refs[2 * at].shape[0] - skip
        for side in range(2):
            refs[6 + at][side * rest : (side + 1) * rest, :] = refs[2 * at + side][skip:, :]


def place_packed_kernel(owner_ref, *refs, plan, slot_rows, rows):
    pieces, outs = refs[: len(plan)], refs[len(plan) :]
    for piece, (masks, units) in zip(pieces, plan):
        size = packed_rows(slot_rows, len(units) * PAIR)
        for slot, mask in enumerate(masks):
            for far in range(2):
                lines = pl.ds(pl.multiple_of(owner_ref[mask * 2 + far] * rows, rows), rows)
                unit = 0
                while unit < len(units):
                    out, column = units[unit]
                    base = slot * size + unit // 2 * slot_rows
                    if unit + 1 == len(units) and unit % 2 == 0:
                        outs[out][lines, column : column + PAIR] = piece[
                            base : base + rows, far * PAIR : (far + 1) * PAIR
                        ]
                        unit += 1
                        continue
                    base += far * rows
                    if unit % 2 == 0 and units[unit + 1] == (out, column + PAIR):
                        outs[out][lines, column : column + LANES] = piece[base : base + rows, :]
                        unit += 2
                        continue
                    side = unit % 2 * PAIR
                    outs[out][lines, column : column + PAIR] = piece[base : base + rows, side : side + PAIR]
                    unit += 1


def place_packed(owner, pieces, plan, widths, rows):
    blocks = owner.shape[0]
    far_count = blocks // 8
    slot_rows = far_count * rows
    outs = [shaped((blocks * rows, width), jnp.bfloat16) for width in widths]
    if rows % 16 == 0 and far_count == 2:
        kernel = functools.partial(place_packed_kernel, plan=plan, slot_rows=slot_rows, rows=rows)
        return local_call(kernel, outs, pieces, [owner], spare=12)
    made = [jnp.zeros(out.shape, out.dtype) for out in outs]
    for piece, (masks, units) in zip(pieces, plan):
        size = packed_rows(slot_rows, len(units) * PAIR)
        for slot, mask in enumerate(masks):
            block = unpacked(piece[slot * size : (slot + 1) * size], slot_rows)
            lines = owner.reshape(8, far_count)[mask][:, None] * rows + jnp.arange(rows, dtype=jnp.int32)
            for unit, (out, column) in enumerate(units):
                made[out] = made[out].at[lines.reshape(-1), column : column + PAIR].set(
                    block[:, unit * PAIR : (unit + 1) * PAIR]
                )
    return made


def units_of(targets):
    return tuple((out, column + at) for out, column, size in targets for at in range(0, size, PAIR))


def placed_blocks(grad, owner, masks):
    blocks = owner.shape[0]
    rows = grad.shape[0] // blocks
    spots = owner.reshape(8, -1)[jnp.array(masks)].reshape(-1)
    return jnp.take(grad.reshape(blocks, rows, grad.shape[1]), spots, axis=0)


def token_kernel(x_ref, query_weight_ref, kv_weight_ref, query_ref, kv_ref):
    rows = query_ref.shape[0]
    query_ref[...] = dot_plain(x_ref[:rows, :], query_weight_ref[...]).astype(jnp.bfloat16)
    step = 512

    def one_part(at, carry):
        lines = pl.ds(pl.multiple_of(at * step, step), step)
        kv_ref[lines, :] = dot_plain(x_ref[lines, :], kv_weight_ref[...]).astype(jnp.bfloat16)
        return carry

    lax.fori_loop(0, kv_ref.shape[0] // step, one_part, 0)


def project_kernel(mixed_ref, weight_ref, own_ref, other_ref, low_ref):
    low = mixed_ref[...].astype(jnp.bfloat16)
    low_ref[...] = low
    total = dot_cols(low, weight_ref[...])
    half = own_ref.shape[0]
    own_ref[...] = total[:half]
    other_ref[...] = total[half:].astype(jnp.bfloat16)


def normed_rows(values):
    centred = values - jnp.mean(values, axis=-1, keepdims=True)
    spread = jnp.mean(centred * centred, axis=-1, keepdims=True)
    scale = lax.rsqrt(spread + epsilon)
    return centred * scale, scale


def norm_back(grads, normed, scale, gain):
    inner = grads * gain
    middle = jnp.mean(inner, axis=-1, keepdims=True)
    slant = jnp.mean(inner * normed, axis=-1, keepdims=True)
    return scale * (inner - middle - normed * slant)


def first_norm_kernel(tokens_ref, own_ref, came_ref, gain_ref, shift_ref, sum_ref, hidden_ref, low_ref):
    total = tokens_ref[...].astype(jnp.float32) + (own_ref[...] + came_ref[...].astype(jnp.float32))
    sum_ref[...] = total
    normed, _ = normed_rows(total)
    hidden = normed * gain_ref[...] + shift_ref[...]
    hidden_ref[...] = hidden
    low_ref[...] = hidden.astype(jnp.bfloat16)


def feed_kernel(
    own_hidden_ref, other_hidden_ref, inner_ref, outer_ref, counts_ref,
    own_ref, other_ref, active_ref, slope_ref, count_ref, total_ref, *, each
):
    count = jnp.sum(counts_ref[...].astype(jnp.float32), axis=0, keepdims=True) / each
    count_ref[...] = jnp.broadcast_to(count, count_ref.shape)
    hidden = jnp.concatenate([own_hidden_ref[...], other_hidden_ref[...]], 0)
    step = 256
    for start in range(0, inner_ref.shape[1], step):
        columns = slice(start, start + step)
        upper = dot_plain(hidden, inner_ref[:, columns])
        chance = 0.5 * (1.0 + lax.erf(upper * (0.5**0.5)))
        active = (upper * chance).astype(jnp.bfloat16)
        active_ref[:, columns] = active
        slope_ref[:, columns] = chance + upper * (jnp.exp(-0.5 * upper * upper) * 0.3989422804014327)
        part = dot_cols(active, outer_ref[:, columns])
        if start:
            total_ref[...] += part
        else:
            total_ref[...] = part
    half = own_ref.shape[0]
    own_ref[...] = total_ref[:half, :]
    other_ref[...] = total_ref[half:, :].astype(jnp.bfloat16)


def second_norm_kernel(
    hidden_ref, own_ref, came_ref, gain_ref, shift_ref, teacher_ref, valid_ref, count_own_ref, count_came_ref,
    grad_ref, low_ref, stats_ref, result_ref, *, token_total
):
    valid = jnp.broadcast_to(valid_ref[...].astype(jnp.float32), (PAIR, valid_ref.shape[1])).T[:, :1]
    factor = token_total / (count_own_ref[0:1, 0:1] + count_came_ref[0:1, 0:1])
    total = hidden_ref[...] + (own_ref[...] + came_ref[...].astype(jnp.float32))
    normed, scale = normed_rows(total)
    gain = gain_ref[...]
    result = normed * gain + shift_ref[...]
    result_ref[...] = result.astype(jnp.bfloat16)
    errors = (result - teacher_ref[...].astype(jnp.float32)) * valid
    grads = errors * factor
    grad = norm_back(grads, normed, scale, gain)
    grad_ref[...] = grad
    low_ref[...] = grad.astype(jnp.bfloat16)
    stats_ref[...] = jnp.zeros_like(stats_ref)
    stats_ref[2:3, :] = jnp.sum(grads * normed, axis=0, keepdims=True)
    stats_ref[3:4, :] = jnp.sum(grads, axis=0, keepdims=True)
    squares = jnp.sum(jnp.sum(errors * errors, axis=0, keepdims=True), axis=1, keepdims=True)
    stats_ref[4:5, :] = jnp.broadcast_to(squares, (1, stats_ref.shape[1]))


def feed_back_kernel(own_grad_ref, other_grad_ref, slope_ref, inner_ref, outer_ref, upper_ref, own_ref, other_ref, total_ref):
    grads = jnp.concatenate([own_grad_ref[...], other_grad_ref[...]], 0)
    step = 256
    for start in range(0, inner_ref.shape[1], step):
        columns = slice(start, start + step)
        upper = (dot_plain(grads, outer_ref[:, columns]) * slope_ref[:, columns]).astype(jnp.bfloat16)
        upper_ref[:, columns] = upper
        part = dot_cols(upper, inner_ref[:, columns])
        if start:
            total_ref[...] += part
        else:
            total_ref[...] = part
    half = own_ref.shape[0]
    own_ref[...] = total_ref[:half, :]
    other_ref[...] = total_ref[half:, :].astype(jnp.bfloat16)


def first_back_kernel(
    grad_ref, own_ref, came_ref, sum_ref, gain_ref, other_stats_ref, out_ref, low_ref, stats_ref
):
    grads = grad_ref[...] + (own_ref[...] + came_ref[...].astype(jnp.float32))
    normed, scale = normed_rows(sum_ref[...])
    grad = norm_back(grads, normed, scale, gain_ref[...])
    out_ref[...] = grad
    low_ref[...] = grad.astype(jnp.bfloat16)
    stats_ref[...] = other_stats_ref[...]
    stats_ref[0:1, :] = jnp.sum(grads * normed, axis=0, keepdims=True)
    stats_ref[1:2, :] = jnp.sum(grads, axis=0, keepdims=True)


def write_blocks(owner_ref, made_ref, column, width, out_ref, out_column, masks, far_count, rows):
    for slot, mask in enumerate(masks):
        for far in range(far_count):
            start = pl.multiple_of(owner_ref[mask * far_count + far] * rows, rows)
            out_ref[slot * far_count + far, :, out_column : out_column + width] = made_ref[
                pl.ds(start, rows), column : column + width
            ].astype(out_ref.dtype)


def wide_kernel(
    owner_ref, own_grad_ref, other_grad_ref, active_ref, own_hidden_ref, other_hidden_ref, upper_ref, *refs,
    groups, far_count, rows, step
):
    outs, made_ref = refs[:-1], refs[-1]
    grads = jnp.concatenate([own_grad_ref[...], other_grad_ref[...]], 0)
    hidden = jnp.concatenate([own_hidden_ref[...], other_hidden_ref[...]], 0)
    width = active_ref.shape[1]
    third_width = 2 * width // 3
    for start in range(0, 2 * width, step):
        if start < width:
            made_ref[...] = dot_rows(grads, active_ref[:, start : start + step])
        else:
            made_ref[...] = dot_rows(hidden, upper_ref[:, start - width : start - width + step])
        third = start // third_width
        for at, masks in enumerate(groups[third]):
            write_blocks(
                owner_ref, made_ref, 0, step, outs[third * len(groups[third]) + at], start % third_width,
                masks, far_count, rows
            )


def wide_gradients(owner, own_grad, other_grad, active, own_hidden, other_hidden, upper, groups):
    blocks = owner.shape[0]
    far_count, rows = blocks // 8, own_grad.shape[1] // blocks
    width = active.shape[1]
    third_width = 2 * width // 3
    if rows % 16:
        made = jnp.concatenate(
            [
                dot_rows(jnp.concatenate([own_grad, other_grad], 0), active),
                dot_rows(jnp.concatenate([own_hidden, other_hidden], 0), upper),
            ],
            1,
        )
        outs = []
        for third, group in enumerate(groups):
            columns = made[:, third * third_width : (third + 1) * third_width]
            for at, masks in enumerate(group):
                outs.append(placed_blocks(columns, owner, masks).astype(jnp.bfloat16 if at else jnp.float32))
        return outs
    step = 512
    outs = []
    for group in groups:
        for at, masks in enumerate(group):
            outs.append(
                shaped((len(masks) * far_count, rows, third_width), jnp.bfloat16 if at else jnp.float32)
            )
    kernel = functools.partial(wide_kernel, groups=groups, far_count=far_count, rows=rows, step=step)
    return local_call(
        kernel, outs, [own_grad, other_grad, active, own_hidden, other_hidden, upper], [owner],
        [pltpu.VMEM((own_grad.shape[1], step), jnp.float32)],
        flops=8 * own_grad.size * width, spare=12,
    )


def narrow_kernel(
    own_ref, other_ref, kv_grad_ref, query_grad_ref, own_grad_ref, other_grad_ref, low_ref, made_ref
):
    half, near = own_ref.shape[0], own_grad_ref.shape[0]
    width = query_grad_ref.shape[1]
    made_ref[:, :width] = dot_rows(own_ref[:near, :], query_grad_ref[:near, :]) + dot_rows(
        other_ref[:near, :], query_grad_ref[near:, :]
    )
    made_ref[:, width : 2 * width] = dot_rows(own_grad_ref[...], low_ref[:near, :]) + dot_rows(
        other_grad_ref[...], low_ref[near:, :]
    )
    made_ref[:, 2 * width :] = dot_rows(own_ref[...], kv_grad_ref[:half, :])
    made_ref[:, 2 * width :] += dot_rows(other_ref[...], kv_grad_ref[half:, :])


def narrow_gradients(own, other, kv_grad, query_grad, own_grad, other_grad, low):
    width = query_grad.shape[1]
    return local_call(
        narrow_kernel, [shaped((own.shape[1], 4 * width))],
        [own, other, kv_grad, query_grad, own_grad, other_grad, low],
        flops=4 * own.size * 2 * width + 8 * own_grad.size * width, spare=12,
    )[0]


def turn_kernel(*refs):
    half = len(refs) // 2
    for source_ref, out_ref in zip(refs[:half], refs[half:]):
        out_ref[...] = source_ref[...].astype(jnp.float32).T.astype(jnp.bfloat16)


def token_other_kernel(kv_grad_ref, query_grad_ref, kv_weight_ref, query_weight_ref, out_ref):
    near, half = query_grad_ref.shape[0] // 2, kv_grad_ref.shape[0] // 2
    step = 512

    def one_part(at, carry):
        lines = pl.ds(pl.multiple_of(half + at * step, step), step)
        total = dot_plain(kv_grad_ref[lines, :], kv_weight_ref[...])
        out_ref[pl.ds(pl.multiple_of(at * step, step), step), :] = total.astype(jnp.bfloat16)
        return carry

    lax.fori_loop(1, half // step, one_part, 0)
    total = dot_plain(kv_grad_ref[half : half + step, :], kv_weight_ref[...])
    total = jnp.concatenate(
        [total[:near] + dot_plain(query_grad_ref[near:, :], query_weight_ref[...]), total[near:]], 0
    )
    out_ref[:step, :] = total.astype(jnp.bfloat16)


def token_other(kv_grad, query_grad, kv_weight, query_weight):
    return local_call(
        token_other_kernel, [shaped((kv_grad.shape[0] // 2, kv_weight.shape[1]), jnp.bfloat16)],
        [kv_grad, query_grad, kv_weight, query_weight],
        flops=kv_grad.size * kv_weight.shape[1], spare=12,
    )[0]


def small_kernel(own_ref, came_ref, out_ref):
    lines = own_ref[...] + came_ref[...]
    out_ref[...] = jnp.concatenate([lines, jnp.zeros((PAIR - lines.shape[0], lines.shape[1]), jnp.float32)], 0).T


def token_own_kernel(
    owner_ref, kv_grad_ref, query_grad_ref, kv_weight_ref, query_weight_ref, came_ref, made_ref, small_ref, *outs,
    masks, rows, placed
):
    near = query_grad_ref.shape[0] // 2
    half, columns = outs[0].shape[0], outs[0].shape[2]
    slot_rows = made_ref.shape[1] if placed else made_ref.shape[0] // (2 * half)
    for mask in range(2 * half):
        lines = slice(mask * near, (mask + 1) * near)
        total = dot_plain(kv_grad_ref[lines, :], kv_weight_ref[...]) + came_ref[lines, :].astype(jnp.float32)
        if mask == 0:
            total += dot_plain(query_grad_ref[:near, :], query_weight_ref[...])
        for third, order in enumerate(masks):
            slot = order.index(mask)
            out_ref = outs[2 * third + slot // half]
            at = slot % half
            out_ref[at, :near, :] = total[:, third * columns : (third + 1) * columns].astype(out_ref.dtype)
            for side in range(2):
                base = near + side * slot_rows
                part = slice((2 * third + side) * columns, (2 * third + side + 1) * columns)
                if placed:
                    out_ref[at, base : base + slot_rows, :] = made_ref[mask, :, part].astype(out_ref.dtype)
                    continue
                for far in range(slot_rows // rows):
                    start = pl.multiple_of(owner_ref[mask * (slot_rows // rows) + far] * rows, rows)
                    out_ref[at, base + far * rows : base + (far + 1) * rows, :] = made_ref[
                        pl.ds(start, rows), part
                    ].astype(out_ref.dtype)
            if third == 0:
                if placed:
                    small = small_ref[mask]
                else:
                    far_count = slot_rows // rows
                    small = jnp.concatenate(
                        [
                            small_ref[pl.ds(pl.multiple_of(owner_ref[mask * far_count + far] * rows, rows), rows), :]
                            for far in range(far_count)
                        ],
                        0,
                    )
                small = jnp.concatenate([small[: slot_rows // 2], small[slot_rows // 2 :]], 1)
                if slot >= half:
                    small = in_pieces(small)
                out_ref[at, near + 2 * slot_rows :, :] = small.astype(out_ref.dtype)


def token_own(owner, kv_grad, query_grad, kv_weight, query_weight, came, made, small, masks):
    near = query_grad.shape[0] // 2
    half = came.shape[0] // near // 2
    blocks, features = owner.shape[0], made.shape[0]
    rows, slot_rows = features // blocks, features // (2 * half)
    columns = kv_weight.shape[1] // 3
    placed = rows % 16 != 0
    if placed:
        made, small = (
            placed_blocks(one, owner, tuple(range(2 * half))).reshape(2 * half, slot_rows, one.shape[1])
            for one in (made, small)
        )
    outs = []
    for third in range(len(masks)):
        shape = (half, near + 2 * slot_rows + (slot_rows // 2 if third == 0 else 0), columns)
        outs += [shaped(shape), shaped(shape, jnp.bfloat16)]
    outs = local_call(
        functools.partial(token_own_kernel, masks=masks, rows=rows, placed=placed), outs,
        [kv_grad, query_grad, kv_weight, query_weight, came, made, small], [owner],
        flops=2 * came.shape[0] * kv_weight.size, spare=12,
    )
    return list(outs[::2]), list(outs[1::2])


def narrow_last_kernel(*refs, near):
    made_ref = refs[6]
    columns = refs[0].shape[2]
    slot_rows = made_ref.shape[0]
    width, plain = 6 * columns, near + 2 * slot_rows
    for third in range(3):
        total = refs[2 * third][0, near:plain] + refs[2 * third + 1][0, near:plain].astype(jnp.float32)
        for side in range(2):
            at = (2 * third + side) * columns
            made_ref[:, at : at + columns] = total[side * slot_rows : (side + 1) * slot_rows]
    small = refs[0][0, plain:] + from_pieces(refs[1][0, plain:].astype(jnp.float32))
    made_ref[: slot_rows // 2, width:] = small[:, :PAIR]
    made_ref[slot_rows // 2 :, width:] = small[:, PAIR:]
    if len(refs) > 7:
        half = slot_rows // 2
        refs[7][:, :width] = made_ref[half:, :width].astype(jnp.bfloat16)
        refs[7][:, width:] = in_pieces(made_ref[half:, width:]).astype(jnp.bfloat16)


def token_end_kernel(grad_ref, *refs):
    out_ref = refs[-1]
    near, columns = grad_ref.shape[0], refs[0].shape[2]
    for third in range(3):
        part = slice(third * columns, (third + 1) * columns)
        out_ref[:, part] = grad_ref[:, part] + (
            refs[2 * third][0, :near] + refs[2 * third + 1][0, :near].astype(jnp.float32)
        )


def end_kernel(
    core_ref, made_ref, came_ref, count_own_ref, count_came_ref,
    query_ref, key_ref, value_ref, output_ref, loss_ref, *norm_refs
):
    rows, width = query_ref.shape
    total = made_ref[:rows, : 4 * width] + came_ref[:, : 4 * width].astype(jnp.float32)
    query_ref[...] = total[:, :width]
    output_ref[...] = total[:, width : 2 * width]
    for at in range(0, width, PAIR):
        first = 2 * width + 2 * at
        key_ref[:, at : at + PAIR] = total[:, first : first + PAIR]
        value_ref[:, at : at + PAIR] = total[:, first + PAIR : first + 2 * PAIR]
    small = made_ref[:rows, 4 * width :] + from_pieces(came_ref[:, 4 * width :].astype(jnp.float32))
    features = 2.0 * rows * core_ref[1].astype(jnp.float32)
    loss_ref[...] = small[:1, 4:5] / (features * (count_own_ref[0:1, 0:1] + count_came_ref[0:1, 0:1]))
    lines = jnp.concatenate([small, jnp.zeros((PAIR - rows, PAIR), jnp.float32)], 0).T
    half = rows // 2
    mine = jnp.where(core_ref[0] == 0, lines[:, :half], lines[:, half:rows])
    for at, one_ref in enumerate(norm_refs):
        one_ref[...] = mine[at : at + 1, :]


def merge_kernel(*refs, riders):
    keeps, cames, sends, kept, messages = (refs[at : at + 3] for at in range(0, 15, 3))
    for third, rider in enumerate(riders):
        kept[third][...] = keeps[third][0] + cames[third][0].astype(jnp.float32)
        later = (keeps[third][1] + cames[third][1].astype(jnp.float32)).astype(jnp.bfloat16)
        slots, lines, columns = sends[rider].shape
        for slot in range(slots):
            messages[rider][slot * lines : (slot + 1) * lines, :] = sends[rider][slot]
        base, rows = slots * lines, later.shape[0]
        for chunk in range(later.shape[1] // columns):
            messages[rider][base + chunk * rows : base + (chunk + 1) * rows, :] = later[
                :, chunk * columns : (chunk + 1) * columns
            ]


def part_kernel(*refs, plain):
    keeps, cames, outs = refs[:3], refs[3:6], refs[6:12]
    for third in range(3):
        keep_ref, came_ref = keeps[third], cames[third]
        slots, lines, _ = keep_ref.shape
        most = min(plain, lines)
        for slot in range(slots):
            side, at = slot // (slots // 2), slot % (slots // 2)
            out_ref, base = outs[2 * third + side], slot * lines
            total = keep_ref[slot, :most] + came_ref[base : base + most, :].astype(jnp.float32)
            out_ref[at, :most] = total.astype(out_ref.dtype)
            if most < lines:
                total = keep_ref[slot, most:] + from_pieces(
                    came_ref[base + most : base + lines, :].astype(jnp.float32)
                )
                out_ref[at, most:] = (in_pieces(total) if side else total).astype(out_ref.dtype)


def wide_end_kernel(*refs, riders, lengths):
    cames, kept, wide_ref = refs[:3], refs[3:6], refs[6]
    for third, rider in enumerate(riders):
        rows, width = kept[third].shape
        columns = cames[rider].shape[1]
        for chunk in range(width // columns):
            part = slice(chunk * columns, (chunk + 1) * columns)
            base = lengths[rider] + chunk * rows
            wide_ref[:, third * width + chunk * columns : third * width + (chunk + 1) * columns] = kept[third][
                :, part
            ] + cames[rider][base : base + rows, :].astype(jnp.float32)
    if len(refs) > 7:
        refs[7][...] = wide_ref[wide_ref.shape[0] // 2 :, :].astype(jnp.bfloat16)


def wide_out_kernel(made_ref, came_ref, outer_ref, inner_ref):
    rows, width = outer_ref.shape
    outer_ref[...] = made_ref[:rows, :width] + came_ref[:, :width].astype(jnp.float32)
    inner_ref[...] = made_ref[:rows, width:] + came_ref[:, width:].astype(jnp.float32)


def tie(first, second):
    leaves, tree = jax.tree.flatten(second)
    tied = lax.optimization_barrier(tuple(leaves) + (first,))
    return jax.tree.unflatten(tree, tied[:-1])


def shards(
    tokens,
    query_weight,
    key_weight,
    value_weight,
    output_weight,
    inner_weight,
    outer_weight,
    attn_gain,
    attn_shift,
    ffn_gain,
    ffn_shift,
    teacher,
    segments,
    random_blocks,
    valid_tokens,
):
    devices = lax.axis_size("dp")
    dp_index = lax.axis_index("dp")
    core = lax.axis_index("tensor")
    rows, width = tokens.shape
    length = 2 * rows
    span = segments.shape[1] // length
    near_bits = span.bit_length() - 1
    far_bits = tuple(range(near_bits, devices.bit_length() - 1))
    place, far_place = dp_index % span, dp_index // span
    far_count = devices // span
    each = width // devices
    slot_rows = far_count * each
    head_width = query_weight.shape[1]
    wide = inner_weight.shape[1]
    masks = jnp.arange(span, dtype=jnp.int32)
    fars = jnp.arange(far_count, dtype=jnp.int32)
    owner = ((fars[None, :] ^ far_place) * span + (masks[:, None] ^ place)).reshape(-1)

    def far_gather(block):
        held = block[None]
        for bit in far_bits:
            held = jnp.concatenate([held, swap_mask(held, 1 << bit)], 0)
        return held.reshape(slot_rows, block.shape[1])

    def step(held, at):
        return [swap_mask(one, 1 << bits[at]) for one, bits in zip(held, ROUTES)]

    def both(held, came):
        return [one for pair in zip(held, came) for one in pair]

    def messages(lines):
        return [shaped((one, third), jnp.bfloat16) for one in lines]

    third = width // 3
    tail = packed_rows(slot_rows, 4 * head_width // 3)
    cuts = (0, 2 * wide // 3, 4 * wide // 3, 2 * wide + PAIR)
    sizes = [packed_rows(slot_rows, last - first) for first, last in zip(cuts, cuts[1:])]
    valid_row = valid_tokens.reshape(1, rows)
    first, second, *held = fetching_call(
        start_kernel,
        [shaped((each, 4 * head_width), jnp.bfloat16), shaped((each, cuts[3]), jnp.bfloat16)]
        + [shaped((rows, third), jnp.bfloat16)] * 3,
        [query_weight, key_weight, value_weight, output_weight, inner_weight, outer_weight, valid_row, tokens],
    )
    came = step(held, 0)
    first_held, second_held = far_gather(first), far_gather(second)
    held = local_call(
        functools.partial(first_pack_kernel, slot_rows=slot_rows), messages([2 * rows + tail] * 3),
        held + came + [first_held],
    )
    came = step(held, 1)
    held = local_call(
        functools.partial(second_pack_kernel, rows=2 * rows, slot_rows=slot_rows, cuts=cuts),
        messages([4 * rows + 2 * tail + size for size in sizes]), both(held, came) + [second_held],
    )
    came = step(held, 2)
    segment_all = lax.dynamic_index_in_dim(segments, far_place, 0, keepdims=False)
    tables = attention_tables(random_blocks, segment_all, place, core, span, length // BLOCK)
    tables, owner, came = lax.optimization_barrier((tables, owner, came))
    sent_masks = [tuple(slot_masks(bits[:2])) for bits in ROUTES]
    came_masks = [tuple(mask ^ (1 << bits[2]) for mask in sent) for sent, bits in zip(sent_masks, ROUTES)]
    arrived = both(held, came)
    held = local_call(
        functools.partial(third_pack_kernel, tokens=4 * rows, tail=2 * tail),
        messages([4 * tail + 2 * size for size in sizes]), arrived,
    )
    came = step(held, 0)
    own = local_call(
        functools.partial(place_tokens_kernel, masks=tuple(both(sent_masks, came_masks)), rows=rows),
        [shaped((span * rows, width), jnp.bfloat16)], [tie(held[0], arrived[0])] + arrived[1:],
    )[0]
    other = swap_core(own)
    late = local_call(
        functools.partial(fourth_pack_kernel, skip=4 * tail), messages([4 * size for size in sizes]),
        both(held, came),
    )
    late_came = step(late, 1)

    held, came = tie(late[0], (held, came))
    units = units_of(
        ((0, 0, head_width),)
        + tuple((1, 2 * at + shift, PAIR) for shift in (0, PAIR) for at in range(0, head_width, PAIR))
        + ((2, 0, head_width),)
    )
    plan = []
    for at, bits in enumerate(ROUTES):
        part = units[at * len(units) // 3 : (at + 1) * len(units) // 3]
        sent = tuple(slot_masks((bits[1], bits[2])))
        plan += [(sent, part), (tuple(mask ^ (1 << bits[0]) for mask in sent), part)]
    full_query, full_kv, full_output = place_packed(
        owner, both(held, came), tuple(plan), (head_width, 2 * head_width, head_width), each
    )
    own_query, own_kv = local_call(
        token_kernel, [shaped((rows, head_width), jnp.bfloat16), shaped((span * rows, 2 * head_width), jnp.bfloat16)],
        [own, full_query, full_kv], flops=4 * own.size * head_width, spare=12,
    )
    mixed, mass, queries, kv = attend(tables, own_query, own_kv, other, full_query, full_kv)

    half_shape, low_shape = shaped((rows, width)), shaped((rows, width), jnp.bfloat16)
    gain_one, shift_one, gain_two, shift_two = (
        one.reshape(1, width) for one in (attn_gain, attn_shift, ffn_gain, ffn_shift)
    )
    part_own, part_other, attended = local_call(
        project_kernel, [half_shape, low_shape, shaped(mixed.shape, jnp.bfloat16)], [mixed, full_output],
        flops=2 * mixed.size * width,
    )
    turned = local_call(
        turn_kernel, [shaped(one.shape[::-1], jnp.bfloat16) for one in (full_query, full_kv)],
        [tie(part_own, full_query), full_kv],
    )
    part_came, late, late_came, turned = lax.optimization_barrier((swap_core(part_other), late, late_came, turned))
    turned_query, turned_kv = turned
    first_sum, hidden, hidden_own = local_call(
        first_norm_kernel, [half_shape, half_shape, low_shape],
        [tokens, part_own, part_came, gain_one, shift_one],
    )
    hidden_other = swap_core(hidden_own)
    late, late_came = tie(hidden_own, (late, late_came))
    units = units_of(((0, 0, wide), (1, 0, wide), (2, 0, PAIR)))
    plan = []
    for at, bits in enumerate(ROUTES):
        part = units[cuts[at] // PAIR : cuts[at + 1] // PAIR]
        sent = tuple(slot_masks((bits[2], bits[0])))
        plan += [(sent, part), (tuple(mask ^ (1 << bits[1]) for mask in sent), part)]
    full_inner, full_outer, counts = place_packed(
        owner, both(late, late_came), tuple(plan), (wide, wide, PAIR), each
    )
    part_own, part_other, active, slope, count_own = local_call(
        functools.partial(feed_kernel, each=each),
        [half_shape, low_shape, shaped((length, wide), jnp.bfloat16), shaped((length, wide)), shaped((8, PAIR))],
        [hidden_own, hidden_other, full_inner, full_outer, counts],
        scratch=[pltpu.VMEM((length, width), jnp.float32)],
        flops=4 * length * width * wide, transcendentals=2 * length * wide, spare=12,
    )
    count_came = swap_core(count_own)
    token_total = devices * lax.axis_size("tensor") * rows
    grad_second, grad_ffn_own, stats_two, result = local_call(
        functools.partial(second_norm_kernel, token_total=token_total),
        [half_shape, low_shape, shaped((8, width)), low_shape],
        [hidden, part_own, swap_core(part_other), gain_two, shift_two, teacher, valid_row, count_own, count_came],
        free=1,
    )
    grad_ffn_other = swap_core(grad_ffn_own)
    upper_grad, part_own, part_other = local_call(
        feed_back_kernel, [shaped((length, wide), jnp.bfloat16), half_shape, low_shape],
        [grad_ffn_own, grad_ffn_other, slope, full_inner, full_outer],
        scratch=[pltpu.VMEM((length, width), jnp.float32)],
        flops=4 * length * width * wide, spare=12,
    )
    part_came = swap_core(part_other)
    scatter_masks = tuple(tuple(slot_masks(bits[::-1])) for bits in ROUTES)
    groups = tuple((one[: span // 2], one[span // 2 :]) for one in scatter_masks)
    outs = wide_gradients(
        owner, grad_ffn_own, grad_ffn_other, active, hidden_own, hidden_other, upper_grad, groups
    )
    outs = [one.reshape(span // 2, slot_rows, one.shape[2]) for one in outs]
    wide_keep, wide_came = outs[::2], step(outs[1::2], 0)
    part_came = tie(outs[0], part_came)
    grad_first, grad_attn_own, stats_one = local_call(
        first_back_kernel, [half_shape, low_shape, shaped((8, width))],
        [grad_second, part_own, part_came, first_sum, gain_one, stats_two],
    )
    grad_attn_other = swap_core(grad_attn_own)
    stats_came = swap_core(stats_one)
    query_grad, kv_grad = attend_back(
        tables, queries, kv, mixed, mass, grad_attn_own, grad_attn_other, full_output
    )

    def folded(keep, came):
        return fold(keep, [[one] for one in came])

    small = local_call(small_kernel, [shaped((width, PAIR))], [stats_one, tie(query_grad, stats_came)])[0]
    token_sent = token_other(tie(small, kv_grad), query_grad, turned_kv, turned_query)
    wide_keep, wide_send = folded(wide_keep, tie(token_sent, wide_came))
    wide_came = step(wide_send, 1)
    token_came = swap_core(tie(wide_keep[0], token_sent))
    made = narrow_gradients(
        own, other, tie(wide_keep[0], kv_grad), query_grad, grad_attn_own, grad_attn_other, attended
    )
    keep, send = token_own(
        owner, kv_grad, query_grad, turned_kv, turned_query, tie(made, token_came), made, small, scatter_masks
    )
    riders = tuple([bits[0] for bits in ROUTES].index(bits[2]) for bits in ROUTES)
    columns = width // 3
    ride = slot_rows * wide_keep[0].shape[2] // columns
    lengths = [one.shape[0] * one.shape[1] + ride for one in send]
    outs = local_call(
        functools.partial(merge_kernel, riders=riders),
        [shaped(one.shape[1:]) for one in wide_keep] + [shaped((one, columns), jnp.bfloat16) for one in lengths],
        wide_keep + tie(keep[0], wide_came) + send,
    )
    wide_keep, came = outs[:3], step(outs[3:], 0)
    plain = rows + 2 * slot_rows
    halves = []
    for one in keep:
        half = (one.shape[0] // 2,) + one.shape[1:]
        halves += [shaped(half), shaped(half, jnp.bfloat16)]
    far_send = [shaped((each, 2 * wide), jnp.bfloat16)] if far_count == 2 else []
    cames = came
    outs = local_call(functools.partial(part_kernel, plain=plain), halves, keep + cames)
    keep, send = list(outs[::2]), list(outs[1::2])
    came = step(send, 1)
    wide_sum, *wide_send = local_call(
        functools.partial(wide_end_kernel, riders=riders, lengths=tuple(one - ride for one in lengths)),
        [shaped((slot_rows, 2 * wide))] + far_send, [tie(keep[0], cames[0])] + list(cames[1:]) + list(wide_keep),
    )

    def far_scatter(total, dtype=jnp.bfloat16):
        total = total.reshape(far_count, each, total.shape[1])
        for bit in far_bits[::-1]:
            half = total.shape[0] // 2
            total = total[:half] + swap_mask(total[half:].astype(dtype), 1 << bit).astype(jnp.float32)
        return total[0]

    keep, send = fold(keep, [[one] for one in came], plain)
    came = step(send, 2)
    if far_count == 2:
        part_outer, part_inner = local_call(
            wide_out_kernel, [shaped((each, wide))] * 2, [wide_sum, swap_mask(wide_send[0], 1 << far_bits[0])], free=2
        )
    else:
        wide_sum = far_scatter(wide_sum)
        part_outer, part_inner = wide_sum[:, :wide], wide_sum[:, wide:]
    came = tie(part_outer, came)
    made_shape = shaped((slot_rows, 4 * head_width + PAIR))
    send_shape = [shaped((each, 4 * head_width + PAIR), jnp.bfloat16)] if far_count == 2 else []
    arrived = both(keep, came)
    made, *send = local_call(
        functools.partial(narrow_last_kernel, near=rows), [made_shape] + send_shape, arrived
    )
    grad_tokens = local_call(
        token_end_kernel, [half_shape], [grad_first, tie(made, arrived[0])] + arrived[1:], free=1
    )[0]
    half = each // 2
    if far_count == 2:
        weight_shape = shaped((each, head_width))
        outs = local_call(
            end_kernel, [weight_shape] * 4 + [shaped((1, 1))] + [shaped((1, half))] * 4,
            [made, tie(grad_tokens, swap_mask(send[0], 1 << far_bits[0])), count_own, count_came],
            [jnp.stack([core, jnp.int32(devices)])], free=9,
        )
        part_query, part_key, part_value, part_output = outs[:4]
        loss_value = outs[4].reshape(())
        norm_parts = [one.reshape(half) for one in outs[5:]]
    else:
        narrow_sum = far_scatter(made[:, : 4 * head_width])
        small = far_scatter(made[:, 4 * head_width :], jnp.float32)
        part_query, part_output = narrow_sum[:, :head_width], narrow_sum[:, head_width : 2 * head_width]
        kv_sum = narrow_sum[:, 2 * head_width :].reshape(each, head_width // PAIR, 2, PAIR)
        part_key, part_value = (kv_sum[:, :, one].reshape(each, head_width) for one in range(2))
        loss_value = small[0, 4] / (2.0 * width * (count_own[0, 0] + count_came[0, 0]))
        mine = jnp.where(core == 0, small[:half], small[half:])
        norm_parts = [mine[:, at] for at in range(4)]
    return (
        result,
        loss_value,
        grad_tokens,
        part_query,
        part_key,
        part_value,
        part_output,
        part_inner,
        part_outer,
        *norm_parts,
    )


def solution(mesh):
    both = P(("dp", "tensor"))
    rows_spec = P(("dp", "tensor"), None)
    weight_spec = P("dp", "tensor")
    in_specs = (rows_spec,) + (weight_spec,) * 6 + (P(),) * 4
    in_specs += (rows_spec, P(), P("tensor", None, None), both)
    out_specs = (rows_spec, P(), rows_spec) + (weight_spec,) * 6 + (both,) * 4
    return jax.shard_map(shards, mesh=mesh, in_specs=in_specs, out_specs=out_specs, check_vma=False)
```

```python
import functools

import jax
import jax.numpy as jnp
from jax import lax
from jax.experimental import pallas as pl
from jax.experimental.pallas import tpu as pltpu
from jax.sharding import PartitionSpec as P

BLOCK = 64
HEAD = 64
PAIR = 2 * HEAD
SLOTS = 6
ROUTES = ((0, 1, 2), (1, 2, 0), (2, 0, 1))

epsilon = 1e-05
masked_value = -1e30
score_scale = 0.125


def swap_mask(block, mask):
    count = lax.axis_size("dp")
    return lax.ppermute(block, "dp", [(one, one ^ mask) for one in range(count)])


def swap_core(block):
    return lax.ppermute(block, "tensor", [(0, 1), (1, 0)])


def dot_plain(left_side, right_side):
    return jnp.dot(left_side, right_side, preferred_element_type=jnp.float32)


def dot_cols(left_side, right_side):
    return lax.dot_general(
        left_side, right_side, (((1,), (1,)), ((), ())), preferred_element_type=jnp.float32
    )


def dot_rows(left_side, right_side):
    return lax.dot_general(
        left_side, right_side, (((0,), (0,)), ((), ())), preferred_element_type=jnp.float32
    )


def params(megabytes):
    return pltpu.CompilerParams(vmem_limit_bytes=int(megabytes) << 20)


def cost(flops=0, moved=0, transcendentals=0):
    return pl.CostEstimate(flops=int(flops), bytes_accessed=int(moved), transcendentals=int(transcendentals))


def in_vmem(count):
    return [pl.BlockSpec(memory_space=pltpu.VMEM)] * count


def in_smem(count):
    return [pl.BlockSpec(memory_space=pltpu.SMEM)] * count


def shaped(shape, dtype=jnp.float32):
    return jax.ShapeDtypeStruct(tuple(shape), dtype)


def local_call(kernel, outs, vmem_inputs, smem_inputs=(), scratch=(), flops=0, transcendentals=0, spare=8, free=0):
    moved = sum(one.size * one.dtype.itemsize for one in list(vmem_inputs) + list(outs))
    held = sum(one.size * one.dtype.itemsize for one in (shaped(s.shape, s.dtype) for s in scratch))
    held = held // (1 << 20) + 1 + spare
    return pl.pallas_call(
        kernel,
        out_shape=tuple(
            one if len(outs) - at <= free else pltpu.VMEM(one.shape, one.dtype) for at, one in enumerate(outs)
        ),
        in_specs=in_smem(len(smem_inputs)) + in_vmem(len(vmem_inputs)),
        out_specs=tuple(in_vmem(len(outs))),
        scratch_shapes=list(scratch),
        compiler_params=params(held),
        cost_estimate=pl.CostEstimate(flops=1000, bytes_accessed=1000, transcendentals=0),
    )(*smem_inputs, *[pltpu.with_memory_space_constraint(one, pltpu.VMEM) for one in vmem_inputs])


def slot_masks(bits):
    return [
        sum(((slot >> at) & 1) << bit for at, bit in enumerate(bits))
        for slot in range(1 << len(bits))
    ]


def in_pieces(values):
    high = values.astype(jnp.bfloat16).astype(jnp.float32)
    middle = (values - high).astype(jnp.bfloat16).astype(jnp.float32)
    return high + pltpu.roll(middle, 8, 1) + pltpu.roll(values - high - middle, 16, 1)


def from_pieces(pieces):
    lanes = pieces.shape[1]
    total = pieces + pltpu.roll(pieces, lanes - 8, 1) + pltpu.roll(pieces, lanes - 16, 1)
    return jnp.where(lax.broadcasted_iota(jnp.int32, pieces.shape, 1) % PAIR < 8, total, 0.0)


def fold_kernel(*refs, thirds, arrivals, plain):
    outs = refs[thirds * (1 + arrivals) :]
    for third in range(thirds):
        keep_ref = refs[third * (1 + arrivals)]
        came = refs[third * (1 + arrivals) + 1 : (third + 1) * (1 + arrivals)]
        half, lines = keep_ref.shape[0] // 2, keep_ref.shape[1]
        most = lines if plain is None else min(plain, lines)
        for side in range(2):
            part = slice(side * half, (side + 1) * half)
            total = sum([one[part, :most].astype(jnp.float32) for one in came], keep_ref[part, :most])
            out_ref = outs[2 * third + side]
            out_ref[:, :most] = total.astype(out_ref.dtype)
            if most == lines:
                continue
            for at in range(half):
                total = keep_ref[side * half + at, most:]
                for one in came:
                    total += from_pieces(one[side * half + at, most:].astype(jnp.float32))
                out_ref[at, most:] = (in_pieces(total) if side else total).astype(out_ref.dtype)


def fold(keeps, arrivals, plain=None):
    outs = []
    for keep in keeps:
        half = (keep.shape[0] // 2,) + keep.shape[1:]
        outs += [shaped(half), shaped(half, jnp.bfloat16)]
    operands = []
    for keep, came in zip(keeps, arrivals):
        operands += [keep] + list(came)
    kernel = functools.partial(fold_kernel, thirds=len(keeps), arrivals=len(arrivals[0]), plain=plain)
    outs = local_call(kernel, outs, operands)
    return list(outs[::2]), list(outs[1::2])


def pick(chosen, table):
    return lax.dot_general(
        chosen.astype(jnp.bfloat16), table.astype(jnp.bfloat16), (((chosen.ndim - 1,), (0,)), ((), ())),
        preferred_element_type=jnp.float32,
    )


def attention_tables(random_blocks, segment_all, place, core, span, row_blocks):
    heads, blocks, draws = random_blocks.shape
    half, pairs = row_blocks // 2, heads // 2
    local = jnp.arange(row_blocks, dtype=jnp.int32)
    owner = jnp.where(local < half, core, 1 - core)
    absolute = place * row_blocks + owner * half + local % half
    every = jnp.arange(blocks, dtype=jnp.int32)
    mine = absolute[:, None] == every
    edge = (every == 0) | (every == blocks - 1)
    fixed = (jnp.abs(absolute[:, None] - every) <= 1) | edge | edge[absolute][:, None]
    segment_table = segment_all.reshape(blocks, BLOCK).astype(jnp.float32)
    low, high = jnp.min(segment_table, 1), jnp.max(segment_table, 1)
    reach = (jnp.max(jnp.where(mine, low, -1.0), 1)[:, None] <= high) & (
        low <= jnp.max(jnp.where(mine, high, -1.0), 1)[:, None]
    )
    drawn = pick(mine, random_blocks.transpose(1, 0, 2).reshape(blocks, heads * draws))
    drawn = drawn.reshape(row_blocks, heads, draws, 1) == every.astype(jnp.float32)
    allowed = (jnp.any(drawn, 2) | fixed[:, None]) & reach[:, None]
    allowed = allowed.reshape(row_blocks, pairs, 2, blocks)
    listed = jnp.any(allowed, 2)
    rank = pick(listed, every[:, None] < every[None, :])
    count = jnp.max(jnp.sum(listed.astype(jnp.int32), -1), -1)
    chunks = -(-count // SLOTS)
    ends = jnp.sum(jnp.where(local[:, None] >= local[None, :], chunks[None, :], 0), 1)
    most = (row_blocks - 1) * -(-min(blocks, 5 + 2 * draws) // SLOTS) + -(-blocks // SLOTS)
    if span == 1:
        most += -(-blocks // SLOTS)
    items = jnp.arange(most, dtype=jnp.int32)
    item_query = jnp.minimum(jnp.sum((items[:, None] >= ends[None, :]).astype(jnp.int32), 1), row_blocks - 1)
    item_is = item_query[:, None] == local
    first = jnp.sum(jnp.where(item_is, (ends - chunks)[None, :], 0), 1)
    spots = ((items - first) * SLOTS)[:, None] + jnp.arange(SLOTS, dtype=jnp.int32)
    stored = (
        jnp.where((every % row_blocks) // half == core, 0, span * half)
        + ((every // row_blocks) ^ place) * half + every % half
    )
    rows = jnp.concatenate([jnp.where(listed, rank, -1.0)[:, :, None], allowed.astype(jnp.float32)], 2)
    rows = pick(item_is, rows.reshape(row_blocks, -1)).reshape(most, pairs, 3, blocks)
    here = rows[:, :, 0, None, :] == spots[:, None, :, None].astype(jnp.float32)
    code = rows[:, :, 1, None, :] * 256.0 + rows[:, :, 2, None, :] * 512.0 + stored.astype(jnp.float32)
    codes = jnp.sum(jnp.where(here, code, 0.0), -1).astype(jnp.int32)
    order = jnp.arange(2 * span * half, dtype=jnp.int32)
    order_block = (
        ((order % (span * half)) // half) ^ place
    ) * row_blocks + jnp.where(order < span * half, core, 1 - core) * half + order % half
    key_side = pick(order_block[:, None] == every, segment_table).reshape(-1, 1)
    query_side = pick(mine, segment_table)
    query_side = jnp.concatenate([query_side, query_side], 1)
    numbers = [ends[-1:], item_query, (items == first), codes.reshape(-1)]
    return (
        jnp.concatenate([one.astype(jnp.int32) for one in numbers]),
        query_side,
        jnp.broadcast_to(key_side, (key_side.shape[0], PAIR)),
    )


def two_heads(rows, low_lanes):
    rows = rows.astype(jnp.float32)
    zero = jnp.zeros_like(rows)
    return jnp.concatenate(
        [jnp.where(low_lanes, rows, zero), jnp.where(low_lanes, zero, rows)], 0
    )


def item_blocks(numbers_ref, first, side, key_side_ref):
    low_row = lax.broadcasted_iota(jnp.int32, (1, PAIR), 1) < HEAD
    spots, masks = [], []
    for slot in range(SLOTS):
        code = numbers_ref[first + slot]
        spot = pl.ds(pl.multiple_of((code & 255) * BLOCK, BLOCK), BLOCK)
        flags = jnp.where(low_row, code & 256, code & 512)
        spots.append(spot)
        masks.append(key_side_ref[spot, :] == jnp.where(flags != 0, side, -1.0))
    return spots, jnp.concatenate(masks, 0)


def attend_kernel(
    numbers_ref, query_side_ref, key_side_ref,
    own_query_ref, own_kv_ref, other_ref, query_weight_ref, kv_weight_ref,
    mixed_ref, mass_ref, q_ref, kv_ref, state_ref, mixture_ref, *, pairs
):
    half_rows, half_kv = own_query_ref.shape[0], own_kv_ref.shape[0]
    q_ref[:half_rows, :] = own_query_ref[...]
    q_ref[half_rows:, :] = dot_plain(other_ref[:half_rows, :], query_weight_ref[...]).astype(jnp.bfloat16)
    kv_ref[:half_kv, :] = own_kv_ref[...]
    step = 512

    def one_part(at, carry):
        lines = pl.ds(pl.multiple_of(at * step, step), step)
        kv_ref[pl.ds(pl.multiple_of(half_kv + at * step, step), step), :] = dot_plain(
            other_ref[lines, :], kv_weight_ref[...]
        ).astype(jnp.bfloat16)
        return carry

    lax.fori_loop(0, half_kv // step, one_part, 0)
    low_lanes = lax.broadcasted_iota(jnp.int32, (BLOCK, PAIR), 1) < HEAD
    most = (numbers_ref.shape[0] - 1) // (2 + pairs * SLOTS)

    def one_item(item, carry):
        query = numbers_ref[1 + item]
        fresh = numbers_ref[1 + most + item] == 1
        side = query_side_ref[pl.ds(query, 1), :]
        rows = pl.ds(pl.multiple_of(query * BLOCK, BLOCK), BLOCK)
        held = []
        for pair in range(pairs):
            both = two_heads(q_ref[rows, pair * PAIR : (pair + 1) * PAIR], low_lanes).astype(jnp.bfloat16)
            spots, mask = item_blocks(
                numbers_ref, 1 + 2 * most + (item * pairs + pair) * SLOTS, side, key_side_ref
            )
            start = pair * 2 * PAIR
            keys = jnp.concatenate([kv_ref[spot, start : start + PAIR] for spot in spots], 0)
            values = jnp.concatenate([kv_ref[spot, start + PAIR : start + 2 * PAIR] for spot in spots], 0)
            held.append((jnp.where(mask, dot_cols(keys, both) * score_scale, masked_value), values))
        done = []
        for pair in range(pairs):
            scores, values = held[pair]
            place = query * pairs + pair
            state = state_ref[place]
            old_top = jnp.where(fresh, masked_value, state[0:1, :])
            top = jnp.maximum(old_top, jnp.max(scores, axis=0, keepdims=True))
            raised = jnp.exp(scores - top)
            shrunk = jnp.exp(old_top - top)
            total = jnp.where(fresh, 0.0, state[1:2, :] * shrunk) + jnp.sum(raised, axis=0, keepdims=True)
            mixture = jnp.where(fresh, 0.0, mixture_ref[place] * shrunk) + dot_rows(
                values, raised.astype(jnp.bfloat16)
            )
            done.append((top, total, mixture))
        for pair in range(pairs):
            top, total, mixture = done[pair]
            place = query * pairs + pair
            state_ref[place, 0:1, :] = top
            state_ref[place, 1:2, :] = total
            mixture_ref[place] = mixture
            normed = (mixture / total).T
            mixed_ref[rows, pair * PAIR : (pair + 1) * PAIR] = jnp.where(
                low_lanes, normed[:BLOCK], normed[BLOCK:]
            )
            mass_ref[place] = jnp.broadcast_to(top + jnp.log(total), (8, PAIR))
        return carry

    lax.fori_loop(0, numbers_ref[0], one_item, 0)


def attend(tables, own_query, own_kv, other, query_weight, kv_weight):
    rows, width = 2 * own_query.shape[0], own_query.shape[1]
    pairs, row_blocks = width // PAIR, rows // BLOCK
    places = pairs * row_blocks
    return local_call(
        functools.partial(attend_kernel, pairs=pairs),
        [
            shaped((rows, width)),
            shaped((places, 8, PAIR)),
            shaped((rows, width), jnp.bfloat16),
            shaped((2 * own_kv.shape[0], own_kv.shape[1]), jnp.bfloat16),
        ],
        list(tables[1:]) + [own_query, own_kv, other, query_weight, kv_weight],
        tables[:1],
        [
            pltpu.VMEM((places, 8, PAIR), jnp.float32),
            pltpu.VMEM((places, PAIR, PAIR), jnp.float32),
        ],
        flops=8e9, transcendentals=4e6, spare=12,
    )


def attend_back_kernel(
    numbers_ref, query_side_ref, key_side_ref, q_ref, kv_ref,
    mixed_ref, mass_ref, own_grad_ref, other_grad_ref, weight_ref,
    query_grad_ref, kv_grad_ref, sum_ref, grad_ref, query_sum_ref, *, pairs
):
    half_rows = own_grad_ref.shape[0]
    grad_ref[:half_rows, :] = dot_plain(own_grad_ref[...], weight_ref[...]).astype(jnp.bfloat16)
    grad_ref[half_rows:, :] = dot_plain(other_grad_ref[...], weight_ref[...]).astype(jnp.bfloat16)
    low_lanes = lax.broadcasted_iota(jnp.int32, (BLOCK, PAIR), 1) < HEAD
    most = (numbers_ref.shape[0] - 1) // (2 + pairs * SLOTS)
    sum_ref[...] = jnp.zeros_like(sum_ref)

    def one_item(item, carry):
        query = numbers_ref[1 + item]
        fresh = numbers_ref[1 + most + item] == 1
        side = query_side_ref[pl.ds(query, 1), :]
        rows = pl.ds(pl.multiple_of(query * BLOCK, BLOCK), BLOCK)
        held = []
        for pair in range(pairs):
            lanes = slice(pair * PAIR, (pair + 1) * PAIR)
            both = two_heads(q_ref[rows, lanes], low_lanes).astype(jnp.bfloat16)
            grads = grad_ref[rows, lanes].astype(jnp.float32)
            turned = (grads * mixed_ref[rows, lanes]).T
            inner = jnp.concatenate(
                [jnp.sum(turned[:HEAD], axis=0, keepdims=True), jnp.sum(turned[HEAD:], axis=0, keepdims=True)], 1
            )
            grads = two_heads(grads, low_lanes).astype(jnp.bfloat16)
            spots, mask = item_blocks(
                numbers_ref, 1 + 2 * most + (item * pairs + pair) * SLOTS, side, key_side_ref
            )
            start = pair * 2 * PAIR
            kv = jnp.concatenate([kv_ref[spot, start : start + 2 * PAIR] for spot in spots], 0)
            blank = jnp.zeros_like(both)
            sides = jnp.concatenate(
                [jnp.concatenate([both, blank], 1), jnp.concatenate([blank, grads], 1)], 0
            )
            held.append((dot_cols(kv, sides), inner, sides, kv, spots, mask))
        done = []
        for pair in range(pairs):
            products, inner, sides, kv, spots, mask = held[pair]
            place = query * pairs + pair
            scores = jnp.where(mask, products[:, :PAIR] * score_scale, masked_value)
            chances = jnp.exp(scores - mass_ref[place, 0:1, :])
            score_grads = (chances * (products[:, PAIR:] - inner)).astype(jnp.bfloat16)
            query_grad = dot_rows(score_grads, kv[:, :PAIR])
            kv_grad = dot_plain(jnp.concatenate([score_grads, chances.astype(jnp.bfloat16)], 1), sides)
            done.append((query_grad, kv_grad))
        for pair in range(pairs):
            lanes = slice(pair * PAIR, (pair + 1) * PAIR)
            start = pair * 2 * PAIR
            query_grad, kv_grad = done[pair]
            spots = held[pair][4]
            query_grad = jnp.where(low_lanes, query_grad[:BLOCK], query_grad[BLOCK:])
            query_sum_ref[rows, lanes] = jnp.where(fresh, 0.0, query_sum_ref[rows, lanes]) + query_grad
            for slot, spot in enumerate(spots):
                sum_ref[spot, start : start + 2 * PAIR] += kv_grad[slot * BLOCK : (slot + 1) * BLOCK]
        return carry

    lax.fori_loop(0, numbers_ref[0], one_item, 0)
    query_grad_ref[...] = (query_sum_ref[...] * score_scale).astype(jnp.bfloat16)
    for pair in range(pairs):
        start = pair * 2 * PAIR
        kv_grad_ref[:, start : start + PAIR] = (sum_ref[:, start : start + PAIR] * score_scale).astype(jnp.bfloat16)
        kv_grad_ref[:, start + PAIR : start + 2 * PAIR] = sum_ref[:, start + PAIR : start + 2 * PAIR].astype(
            jnp.bfloat16
        )


def attend_back(tables, queries, kv, mixed, mass, own_grad, other_grad, weight):
    rows, width = queries.shape
    pairs = width // PAIR
    return local_call(
        functools.partial(attend_back_kernel, pairs=pairs),
        [shaped((rows, width), jnp.bfloat16), shaped(kv.shape, jnp.bfloat16)],
        list(tables[1:]) + [queries, kv, mixed, mass, own_grad, other_grad, weight],
        tables[:1],
        [
            pltpu.VMEM(kv.shape, jnp.float32),
            pltpu.VMEM((rows, width), jnp.bfloat16),
            pltpu.VMEM((rows, width), jnp.float32),
        ],
        flops=10e9, transcendentals=4e6, spare=12,
    )


LANES = 2 * PAIR


def packed_rows(slot_rows, columns):
    return columns // LANES * slot_rows + (slot_rows // 2 if columns % LANES else 0)


def put_packed(out_ref, base, source_ref, first, columns, slot_rows):
    for chunk in range(columns // LANES):
        at = first + chunk * LANES
        out_ref[base : base + slot_rows, :] = source_ref[:, at : at + LANES]
        base += slot_rows
    if columns % LANES:
        half, at = slot_rows // 2, first + columns - PAIR
        out_ref[base : base + half, :PAIR] = source_ref[:half, at : at + PAIR]
        out_ref[base : base + half, PAIR:] = source_ref[half:, at : at + PAIR]


def unpacked(packed, slot_rows):
    full = packed.shape[0] // slot_rows
    parts = [packed[at * slot_rows : (at + 1) * slot_rows] for at in range(full)]
    tail = packed[full * slot_rows :]
    if tail.shape[0]:
        parts.append(jnp.concatenate([tail[:, :PAIR], tail[:, PAIR:]], 0))
    return jnp.concatenate(parts, 1)


def fetched(far, near, arrived):
    copies = [
        pltpu.make_async_copy(far_ref, near_ref, arrived.at[at])
        for at, (far_ref, near_ref) in enumerate(zip(far, near))
    ]
    for copy in copies:
        copy.start()
    for copy in copies:
        copy.wait()


def start_kernel(*refs):
    near = refs[13:-1]
    fetched(refs[:8], near, refs[-1])
    first_ref, second_ref, thirds = refs[8], refs[9], refs[10:13]
    columns = thirds[0].shape[1]
    for at in range(3):
        thirds[at][...] = near[7][:, at * columns : (at + 1) * columns]
    for out_ref, sources in ((first_ref, near[:4]), (second_ref, near[4:6])):
        at = 0
        for one in sources:
            out_ref[:, at : at + one.shape[1]] = one[...]
            at += one.shape[1]
    count = jnp.sum(near[6][...].astype(jnp.float32), axis=1, keepdims=True)
    second_ref[:, at:] = jnp.broadcast_to(count, (second_ref.shape[0], PAIR)).astype(jnp.bfloat16)


def fetching_call(kernel, outs, sources):
    return pl.pallas_call(
        kernel,
        out_shape=[pltpu.VMEM(one.shape, one.dtype) for one in outs],
        in_specs=[pl.BlockSpec(memory_space=pltpu.HBM)] * len(sources),
        out_specs=in_vmem(len(outs)),
        scratch_shapes=[pltpu.VMEM(one.shape, one.dtype) for one in sources]
        + [pltpu.SemaphoreType.DMA((len(sources),))],
        compiler_params=params(8),
    )(*[pltpu.with_memory_space_constraint(one, pltpu.HBM) for one in sources])


def first_pack_kernel(*refs, slot_rows):
    sent, came, weights_ref, outs = refs[:3], refs[3:6], refs[6], refs[7:]
    rows = sent[0].shape[0]
    third = weights_ref.shape[1] // 3
    for at in range(3):
        outs[at][:rows, :] = sent[at][...]
        outs[at][rows : 2 * rows, :] = came[at][...]
        put_packed(outs[at], 2 * rows, weights_ref, at * third, third, slot_rows)


def second_pack_kernel(*refs, rows, slot_rows, cuts):
    second_ref, outs = refs[6], refs[7:]
    for at in range(3):
        sent_ref, came_ref, out_ref = refs[2 * at], refs[2 * at + 1], outs[at]
        tail = sent_ref.shape[0] - rows
        out_ref[:rows, :] = sent_ref[:rows, :]
        out_ref[rows : 2 * rows, :] = came_ref[:rows, :]
        out_ref[2 * rows : 2 * rows + tail, :] = sent_ref[rows:, :]
        out_ref[2 * rows + tail : 2 * (rows + tail), :] = came_ref[rows:, :]
        put_packed(out_ref, 2 * (rows + tail), second_ref, cuts[at], cuts[at + 1] - cuts[at], slot_rows)


def place_tokens_kernel(*refs, masks, rows):
    out_ref = refs[6]
    columns = refs[0].shape[1]
    for at, group in enumerate(masks):
        third = at // 2
        for slot, mask in enumerate(group):
            out_ref[mask * rows : (mask + 1) * rows, third * columns : (third + 1) * columns] = refs[at][
                slot * rows : (slot + 1) * rows, :
            ]


def third_pack_kernel(*refs, tokens, tail):
    for at in range(3):
        for side in range(2):
            piece, target = refs[2 * at + side], refs[6 + at]
            target[side * tail : (side + 1) * tail, :] = piece[tokens : tokens + tail, :]
            rest = piece.shape[0] - tokens - tail
            base = 2 * tail + side * rest
            target[base : base + rest, :] = piece[tokens + tail :, :]


def fourth_pack_kernel(*refs, skip):
    for at in range(3):
        rest = refs[2 * at].shape[0] - skip
        for side in range(2):
            refs[6 + at][side * rest : (side + 1) * rest, :] = refs[2 * at + side][skip:, :]


def place_packed_kernel(owner_ref, *refs, plan, slot_rows, rows):
    pieces, outs = refs[: len(plan)], refs[len(plan) :]
    for piece, (masks, units) in zip(pieces, plan):
        size = packed_rows(slot_rows, len(units) * PAIR)
        for slot, mask in enumerate(masks):
            for far in range(2):
                lines = pl.ds(pl.multiple_of(owner_ref[mask * 2 + far] * rows, rows), rows)
                unit = 0
                while unit < len(units):
                    out, column = units[unit]
                    base = slot * size + unit // 2 * slot_rows
                    if unit + 1 == len(units) and unit % 2 == 0:
                        outs[out][lines, column : column + PAIR] = piece[
                            base : base + rows, far * PAIR : (far + 1) * PAIR
                        ]
                        unit += 1
                        continue
                    base += far * rows
                    if unit % 2 == 0 and units[unit + 1] == (out, column + PAIR):
                        outs[out][lines, column : column + LANES] = piece[base : base + rows, :]
                        unit += 2
                        continue
                    side = unit % 2 * PAIR
                    outs[out][lines, column : column + PAIR] = piece[base : base + rows, side : side + PAIR]
                    unit += 1


def place_packed(owner, pieces, plan, widths, rows):
    blocks = owner.shape[0]
    far_count = blocks // 8
    slot_rows = far_count * rows
    outs = [shaped((blocks * rows, width), jnp.bfloat16) for width in widths]
    if rows % 16 == 0 and far_count == 2:
        kernel = functools.partial(place_packed_kernel, plan=plan, slot_rows=slot_rows, rows=rows)
        return local_call(kernel, outs, pieces, [owner], spare=12)
    made = [jnp.zeros(out.shape, out.dtype) for out in outs]
    for piece, (masks, units) in zip(pieces, plan):
        size = packed_rows(slot_rows, len(units) * PAIR)
        for slot, mask in enumerate(masks):
            block = unpacked(piece[slot * size : (slot + 1) * size], slot_rows)
            lines = owner.reshape(8, far_count)[mask][:, None] * rows + jnp.arange(rows, dtype=jnp.int32)
            for unit, (out, column) in enumerate(units):
                made[out] = made[out].at[lines.reshape(-1), column : column + PAIR].set(
                    block[:, unit * PAIR : (unit + 1) * PAIR]
                )
    return made


def units_of(targets):
    return tuple((out, column + at) for out, column, size in targets for at in range(0, size, PAIR))


def placed_blocks(grad, owner, masks):
    blocks = owner.shape[0]
    rows = grad.shape[0] // blocks
    spots = owner.reshape(8, -1)[jnp.array(masks)].reshape(-1)
    return jnp.take(grad.reshape(blocks, rows, grad.shape[1]), spots, axis=0)


def token_kernel(x_ref, query_weight_ref, kv_weight_ref, query_ref, kv_ref):
    rows = query_ref.shape[0]
    query_ref[...] = dot_plain(x_ref[:rows, :], query_weight_ref[...]).astype(jnp.bfloat16)
    step = 512

    def one_part(at, carry):
        lines = pl.ds(pl.multiple_of(at * step, step), step)
        kv_ref[lines, :] = dot_plain(x_ref[lines, :], kv_weight_ref[...]).astype(jnp.bfloat16)
        return carry

    lax.fori_loop(0, kv_ref.shape[0] // step, one_part, 0)


def project_kernel(mixed_ref, weight_ref, own_ref, other_ref, low_ref):
    low = mixed_ref[...].astype(jnp.bfloat16)
    low_ref[...] = low
    total = dot_cols(low, weight_ref[...])
    half = own_ref.shape[0]
    own_ref[...] = total[:half]
    other_ref[...] = total[half:].astype(jnp.bfloat16)


def normed_rows(values):
    centred = values - jnp.mean(values, axis=-1, keepdims=True)
    spread = jnp.mean(centred * centred, axis=-1, keepdims=True)
    scale = lax.rsqrt(spread + epsilon)
    return centred * scale, scale


def norm_back(grads, normed, scale, gain):
    inner = grads * gain
    middle = jnp.mean(inner, axis=-1, keepdims=True)
    slant = jnp.mean(inner * normed, axis=-1, keepdims=True)
    return scale * (inner - middle - normed * slant)


def first_norm_kernel(tokens_ref, own_ref, came_ref, gain_ref, shift_ref, sum_ref, hidden_ref, low_ref):
    total = tokens_ref[...].astype(jnp.float32) + (own_ref[...] + came_ref[...].astype(jnp.float32))
    sum_ref[...] = total
    normed, _ = normed_rows(total)
    hidden = normed * gain_ref[...] + shift_ref[...]
    hidden_ref[...] = hidden
    low_ref[...] = hidden.astype(jnp.bfloat16)


def feed_kernel(hidden_ref, inner_ref, outer_ref, total_ref, active_ref, slope_ref, sum_ref):
    hidden = hidden_ref[...]
    step = 256
    for start in range(0, inner_ref.shape[1], step):
        columns = slice(start, start + step)
        upper = dot_plain(hidden, inner_ref[:, columns])
        chance = 0.5 * (1.0 + lax.erf(upper * (0.5**0.5)))
        active = (upper * chance).astype(jnp.bfloat16)
        active_ref[:, columns] = active
        slope_ref[:, columns] = chance + upper * (jnp.exp(-0.5 * upper * upper) * 0.3989422804014327)
        part = dot_cols(active, outer_ref[:, columns])
        if start:
            sum_ref[...] += part
        else:
            sum_ref[...] = part
    total_ref[...] = sum_ref[...].astype(total_ref.dtype)


def count_kernel(counts_ref, count_ref, *, each):
    count = jnp.sum(counts_ref[...].astype(jnp.float32), axis=0, keepdims=True) / each
    count_ref[...] = jnp.broadcast_to(count, count_ref.shape)


def second_norm_kernel(
    hidden_ref, own_ref, came_ref, gain_ref, shift_ref, teacher_ref, valid_ref, count_own_ref, count_came_ref,
    grad_ref, low_ref, stats_ref, result_ref, *, token_total
):
    valid = jnp.broadcast_to(valid_ref[...].astype(jnp.float32), (PAIR, valid_ref.shape[1])).T[:, :1]
    factor = token_total / (count_own_ref[0:1, 0:1] + count_came_ref[0:1, 0:1])
    total = hidden_ref[...] + (own_ref[...] + came_ref[...].astype(jnp.float32))
    normed, scale = normed_rows(total)
    gain = gain_ref[...]
    result = normed * gain + shift_ref[...]
    result_ref[...] = result.astype(jnp.bfloat16)
    errors = (result - teacher_ref[...].astype(jnp.float32)) * valid
    grads = errors * factor
    grad = norm_back(grads, normed, scale, gain)
    grad_ref[...] = grad
    low_ref[...] = grad.astype(jnp.bfloat16)
    stats_ref[...] = jnp.zeros_like(stats_ref)
    stats_ref[2:3, :] = jnp.sum(grads * normed, axis=0, keepdims=True)
    stats_ref[3:4, :] = jnp.sum(grads, axis=0, keepdims=True)
    squares = jnp.sum(jnp.sum(errors * errors, axis=0, keepdims=True), axis=1, keepdims=True)
    stats_ref[4:5, :] = jnp.broadcast_to(squares, (1, stats_ref.shape[1]))


def feed_back_kernel(grads_ref, slope_ref, inner_ref, outer_ref, upper_ref, total_ref, sum_ref):
    grads = grads_ref[...]
    step = 256
    for start in range(0, inner_ref.shape[1], step):
        columns = slice(start, start + step)
        upper = (dot_plain(grads, outer_ref[:, columns]) * slope_ref[:, columns]).astype(jnp.bfloat16)
        upper_ref[:, columns] = upper
        part = dot_cols(upper, inner_ref[:, columns])
        if start:
            sum_ref[...] += part
        else:
            sum_ref[...] = part
    total_ref[...] = sum_ref[...].astype(total_ref.dtype)


def first_back_kernel(
    grad_ref, own_ref, came_ref, sum_ref, gain_ref, other_stats_ref, out_ref, low_ref, stats_ref
):
    grads = grad_ref[...] + (own_ref[...] + came_ref[...].astype(jnp.float32))
    normed, scale = normed_rows(sum_ref[...])
    grad = norm_back(grads, normed, scale, gain_ref[...])
    out_ref[...] = grad
    low_ref[...] = grad.astype(jnp.bfloat16)
    stats_ref[...] = other_stats_ref[...]
    stats_ref[0:1, :] = jnp.sum(grads * normed, axis=0, keepdims=True)
    stats_ref[1:2, :] = jnp.sum(grads, axis=0, keepdims=True)


def write_blocks(owner_ref, made_ref, column, width, out_ref, out_column, masks, far_count, rows):
    for slot, mask in enumerate(masks):
        for far in range(far_count):
            start = pl.multiple_of(owner_ref[mask * far_count + far] * rows, rows)
            out_ref[slot * far_count + far, :, out_column : out_column + width] = made_ref[
                pl.ds(start, rows), column : column + width
            ].astype(out_ref.dtype)


def wide_kernel(
    owner_ref, own_grad_ref, other_grad_ref, own_active_ref, other_active_ref, own_hidden_ref, other_hidden_ref,
    own_upper_ref, other_upper_ref, *refs, groups, far_count, rows, step
):
    outs, made_ref = refs[:-1], refs[-1]
    grads = jnp.concatenate([own_grad_ref[...], other_grad_ref[...]], 0)
    hidden = jnp.concatenate([own_hidden_ref[...], other_hidden_ref[...]], 0)
    width = own_active_ref.shape[1]
    third_width = 2 * width // 3
    for start in range(0, 2 * width, step):
        part = slice(start % width, start % width + step)
        if start < width:
            made_ref[...] = dot_rows(grads, jnp.concatenate([own_active_ref[:, part], other_active_ref[:, part]], 0))
        else:
            made_ref[...] = dot_rows(hidden, jnp.concatenate([own_upper_ref[:, part], other_upper_ref[:, part]], 0))
        third = start // third_width
        for at, masks in enumerate(groups[third]):
            write_blocks(
                owner_ref, made_ref, 0, step, outs[third * len(groups[third]) + at], start % third_width,
                masks, far_count, rows
            )


def wide_gradients(owner, grads, active, hidden, upper, groups):
    blocks = owner.shape[0]
    far_count, rows = blocks // 8, grads[0].shape[1] // blocks
    width = active[0].shape[1]
    third_width = 2 * width // 3
    if rows % 16:
        whole = [jnp.concatenate(one, 0) for one in (grads, active, hidden, upper)]
        made = jnp.concatenate([dot_rows(whole[0], whole[1]), dot_rows(whole[2], whole[3])], 1)
        outs = []
        for third, group in enumerate(groups):
            columns = made[:, third * third_width : (third + 1) * third_width]
            for at, masks in enumerate(group):
                outs.append(placed_blocks(columns, owner, masks).astype(jnp.bfloat16 if at else jnp.float32))
        return outs
    step = 512
    outs = []
    for group in groups:
        for at, masks in enumerate(group):
            outs.append(
                shaped((len(masks) * far_count, rows, third_width), jnp.bfloat16 if at else jnp.float32)
            )
    kernel = functools.partial(wide_kernel, groups=groups, far_count=far_count, rows=rows, step=step)
    return local_call(
        kernel, outs, [*grads, *active, *hidden, *upper], [owner],
        [pltpu.VMEM((grads[0].shape[1], step), jnp.float32)], spare=12,
    )


def narrow_kernel(
    own_ref, other_ref, kv_grad_ref, query_grad_ref, own_grad_ref, other_grad_ref, low_ref, made_ref
):
    half, near = own_ref.shape[0], own_grad_ref.shape[0]
    width = query_grad_ref.shape[1]
    made_ref[:, :width] = dot_rows(own_ref[:near, :], query_grad_ref[:near, :]) + dot_rows(
        other_ref[:near, :], query_grad_ref[near:, :]
    )
    made_ref[:, width : 2 * width] = dot_rows(own_grad_ref[...], low_ref[:near, :]) + dot_rows(
        other_grad_ref[...], low_ref[near:, :]
    )
    made_ref[:, 2 * width :] = dot_rows(own_ref[...], kv_grad_ref[:half, :])
    made_ref[:, 2 * width :] += dot_rows(other_ref[...], kv_grad_ref[half:, :])


def narrow_gradients(own, other, kv_grad, query_grad, own_grad, other_grad, low):
    width = query_grad.shape[1]
    return local_call(
        narrow_kernel, [shaped((own.shape[1], 4 * width))],
        [own, other, kv_grad, query_grad, own_grad, other_grad, low],
        flops=4 * own.size * 2 * width + 8 * own_grad.size * width, spare=12,
    )[0]


def turn_kernel(*refs):
    half = len(refs) // 2
    for source_ref, out_ref in zip(refs[:half], refs[half:]):
        out_ref[...] = source_ref[...].astype(jnp.float32).T.astype(jnp.bfloat16)


def token_other_kernel(kv_grad_ref, query_grad_ref, kv_weight_ref, query_weight_ref, out_ref):
    near, half = query_grad_ref.shape[0] // 2, kv_grad_ref.shape[0] // 2
    step = 1024

    def one_part(at, carry):
        lines = pl.ds(pl.multiple_of(half + at * step, step), step)
        total = dot_plain(kv_grad_ref[lines, :], kv_weight_ref[...])
        out_ref[pl.ds(pl.multiple_of(at * step, step), step), :] = total.astype(jnp.bfloat16)
        return carry

    lax.fori_loop(1, half // step, one_part, 0)
    total = dot_plain(kv_grad_ref[half : half + step, :], kv_weight_ref[...])
    total = jnp.concatenate(
        [total[:near] + dot_plain(query_grad_ref[near:, :], query_weight_ref[...]), total[near:]], 0
    )
    out_ref[:step, :] = total.astype(jnp.bfloat16)


def token_other(kv_grad, query_grad, kv_weight, query_weight):
    return local_call(
        token_other_kernel, [shaped((kv_grad.shape[0] // 2, kv_weight.shape[1]), jnp.bfloat16)],
        [kv_grad, query_grad, kv_weight, query_weight],
        flops=kv_grad.size * kv_weight.shape[1], spare=12,
    )[0]


def small_kernel(own_ref, came_ref, out_ref):
    lines = own_ref[...] + came_ref[...]
    out_ref[...] = jnp.concatenate([lines, jnp.zeros((PAIR - lines.shape[0], lines.shape[1]), jnp.float32)], 0).T


def token_own_kernel(
    owner_ref, kv_grad_ref, query_grad_ref, kv_weight_ref, query_weight_ref, came_ref, made_ref, small_ref, *outs,
    masks, rows, placed
):
    near = query_grad_ref.shape[0] // 2
    half, columns = outs[0].shape[0], outs[0].shape[2]
    slot_rows = made_ref.shape[1] if placed else made_ref.shape[0] // (2 * half)
    for mask in range(2 * half):
        lines = slice(mask * near, (mask + 1) * near)
        total = dot_plain(kv_grad_ref[lines, :], kv_weight_ref[...]) + came_ref[lines, :].astype(jnp.float32)
        if mask == 0:
            total += dot_plain(query_grad_ref[:near, :], query_weight_ref[...])
        for third, order in enumerate(masks):
            slot = order.index(mask)
            out_ref = outs[2 * third + slot // half]
            at = slot % half
            out_ref[at, :near, :] = total[:, third * columns : (third + 1) * columns].astype(out_ref.dtype)
            for side in range(2):
                base = near + side * slot_rows
                part = slice((2 * third + side) * columns, (2 * third + side + 1) * columns)
                if placed:
                    out_ref[at, base : base + slot_rows, :] = made_ref[mask, :, part].astype(out_ref.dtype)
                    continue
                for far in range(slot_rows // rows):
                    start = pl.multiple_of(owner_ref[mask * (slot_rows // rows) + far] * rows, rows)
                    out_ref[at, base + far * rows : base + (far + 1) * rows, :] = made_ref[
                        pl.ds(start, rows), part
                    ].astype(out_ref.dtype)
            if third == 0:
                if placed:
                    small = small_ref[mask]
                else:
                    far_count = slot_rows // rows
                    small = jnp.concatenate(
                        [
                            small_ref[pl.ds(pl.multiple_of(owner_ref[mask * far_count + far] * rows, rows), rows), :]
                            for far in range(far_count)
                        ],
                        0,
                    )
                small = jnp.concatenate([small[: slot_rows // 2], small[slot_rows // 2 :]], 1)
                if slot >= half:
                    small = in_pieces(small)
                out_ref[at, near + 2 * slot_rows :, :] = small.astype(out_ref.dtype)


def token_own(owner, kv_grad, query_grad, kv_weight, query_weight, came, made, small, masks):
    near = query_grad.shape[0] // 2
    half = came.shape[0] // near // 2
    blocks, features = owner.shape[0], made.shape[0]
    rows, slot_rows = features // blocks, features // (2 * half)
    columns = kv_weight.shape[1] // 3
    placed = rows % 16 != 0
    if placed:
        made, small = (
            placed_blocks(one, owner, tuple(range(2 * half))).reshape(2 * half, slot_rows, one.shape[1])
            for one in (made, small)
        )
    outs = []
    for third in range(len(masks)):
        shape = (half, near + 2 * slot_rows + (slot_rows // 2 if third == 0 else 0), columns)
        outs += [shaped(shape), shaped(shape, jnp.bfloat16)]
    outs = local_call(
        functools.partial(token_own_kernel, masks=masks, rows=rows, placed=placed), outs,
        [kv_grad, query_grad, kv_weight, query_weight, came, made, small], [owner],
        flops=2 * came.shape[0] * kv_weight.size, spare=12,
    )
    return list(outs[::2]), list(outs[1::2])


def narrow_last_kernel(*refs, near):
    made_ref = refs[6]
    columns = refs[0].shape[2]
    slot_rows = made_ref.shape[0]
    width, plain = 6 * columns, near + 2 * slot_rows
    for third in range(3):
        total = refs[2 * third][0, near:plain] + refs[2 * third + 1][0, near:plain].astype(jnp.float32)
        for side in range(2):
            at = (2 * third + side) * columns
            made_ref[:, at : at + columns] = total[side * slot_rows : (side + 1) * slot_rows]
    small = refs[0][0, plain:] + from_pieces(refs[1][0, plain:].astype(jnp.float32))
    made_ref[: slot_rows // 2, width:] = small[:, :PAIR]
    made_ref[slot_rows // 2 :, width:] = small[:, PAIR:]
    if len(refs) > 7:
        half = slot_rows // 2
        refs[7][:, :width] = made_ref[half:, :width].astype(jnp.bfloat16)
        refs[7][:, width:] = in_pieces(made_ref[half:, width:]).astype(jnp.bfloat16)


def token_end_kernel(grad_ref, *refs):
    out_ref = refs[-1]
    near, columns = grad_ref.shape[0], refs[0].shape[2]
    for third in range(3):
        part = slice(third * columns, (third + 1) * columns)
        out_ref[:, part] = grad_ref[:, part] + (
            refs[2 * third][0, :near] + refs[2 * third + 1][0, :near].astype(jnp.float32)
        )


def end_kernel(
    core_ref, made_ref, came_ref, count_own_ref, count_came_ref,
    query_ref, key_ref, value_ref, output_ref, loss_ref, *norm_refs
):
    rows, width = query_ref.shape
    total = made_ref[:rows, : 4 * width] + came_ref[:, : 4 * width].astype(jnp.float32)
    query_ref[...] = total[:, :width]
    output_ref[...] = total[:, width : 2 * width]
    for at in range(0, width, PAIR):
        first = 2 * width + 2 * at
        key_ref[:, at : at + PAIR] = total[:, first : first + PAIR]
        value_ref[:, at : at + PAIR] = total[:, first + PAIR : first + 2 * PAIR]
    small = made_ref[:rows, 4 * width :] + from_pieces(came_ref[:, 4 * width :].astype(jnp.float32))
    features = 2.0 * rows * core_ref[1].astype(jnp.float32)
    loss_ref[...] = small[:1, 4:5] / (features * (count_own_ref[0:1, 0:1] + count_came_ref[0:1, 0:1]))
    lines = jnp.concatenate([small, jnp.zeros((PAIR - rows, PAIR), jnp.float32)], 0).T
    half = rows // 2
    mine = jnp.where(core_ref[0] == 0, lines[:, :half], lines[:, half:rows])
    for at, one_ref in enumerate(norm_refs):
        one_ref[...] = mine[at : at + 1, :]


def merge_kernel(*refs, riders):
    keeps, cames, sends, kept, messages = (refs[at : at + 3] for at in range(0, 15, 3))
    for third, rider in enumerate(riders):
        kept[third][...] = keeps[third][0] + cames[third][0].astype(jnp.float32)
        later = (keeps[third][1] + cames[third][1].astype(jnp.float32)).astype(jnp.bfloat16)
        slots, lines, columns = sends[rider].shape
        for slot in range(slots):
            messages[rider][slot * lines : (slot + 1) * lines, :] = sends[rider][slot]
        base, rows = slots * lines, later.shape[0]
        for chunk in range(later.shape[1] // columns):
            messages[rider][base + chunk * rows : base + (chunk + 1) * rows, :] = later[
                :, chunk * columns : (chunk + 1) * columns
            ]


def part_kernel(*refs, plain):
    keeps, cames, outs = refs[:3], refs[3:6], refs[6:12]
    for third in range(3):
        keep_ref, came_ref = keeps[third], cames[third]
        slots, lines, _ = keep_ref.shape
        most = min(plain, lines)
        for slot in range(slots):
            side, at = slot // (slots // 2), slot % (slots // 2)
            out_ref, base = outs[2 * third + side], slot * lines
            total = keep_ref[slot, :most] + came_ref[base : base + most, :].astype(jnp.float32)
            out_ref[at, :most] = total.astype(out_ref.dtype)
            if most < lines:
                total = keep_ref[slot, most:] + from_pieces(
                    came_ref[base + most : base + lines, :].astype(jnp.float32)
                )
                out_ref[at, most:] = (in_pieces(total) if side else total).astype(out_ref.dtype)


def wide_end_kernel(*refs, riders, lengths):
    cames, kept, wide_ref = refs[:3], refs[3:6], refs[6]
    for third, rider in enumerate(riders):
        rows, width = kept[third].shape
        columns = cames[rider].shape[1]
        for chunk in range(width // columns):
            part = slice(chunk * columns, (chunk + 1) * columns)
            base = lengths[rider] + chunk * rows
            wide_ref[:, third * width + chunk * columns : third * width + (chunk + 1) * columns] = kept[third][
                :, part
            ] + cames[rider][base : base + rows, :].astype(jnp.float32)
    if len(refs) > 7:
        refs[7][...] = wide_ref[wide_ref.shape[0] // 2 :, :].astype(jnp.bfloat16)


def wide_out_kernel(made_ref, came_ref, outer_ref, inner_ref):
    rows, width = outer_ref.shape
    outer_ref[...] = made_ref[:rows, :width] + came_ref[:, :width].astype(jnp.float32)
    inner_ref[...] = made_ref[:rows, width:] + came_ref[:, width:].astype(jnp.float32)


def tie(first, second):
    leaves, tree = jax.tree.flatten(second)
    tied = lax.optimization_barrier(tuple(leaves) + (first,))
    return jax.tree.unflatten(tree, tied[:-1])


def shards(
    tokens,
    query_weight,
    key_weight,
    value_weight,
    output_weight,
    inner_weight,
    outer_weight,
    attn_gain,
    attn_shift,
    ffn_gain,
    ffn_shift,
    teacher,
    segments,
    random_blocks,
    valid_tokens,
):
    devices = lax.axis_size("dp")
    dp_index = lax.axis_index("dp")
    core = lax.axis_index("tensor")
    rows, width = tokens.shape
    length = 2 * rows
    span = segments.shape[1] // length
    near_bits = span.bit_length() - 1
    far_bits = tuple(range(near_bits, devices.bit_length() - 1))
    place, far_place = dp_index % span, dp_index // span
    far_count = devices // span
    each = width // devices
    slot_rows = far_count * each
    head_width = query_weight.shape[1]
    wide = inner_weight.shape[1]
    masks = jnp.arange(span, dtype=jnp.int32)
    fars = jnp.arange(far_count, dtype=jnp.int32)
    owner = ((fars[None, :] ^ far_place) * span + (masks[:, None] ^ place)).reshape(-1)

    def far_gather(block):
        held = block[None]
        for bit in far_bits:
            held = jnp.concatenate([held, swap_mask(held, 1 << bit)], 0)
        return held.reshape(slot_rows, block.shape[1])

    def step(held, at):
        return [swap_mask(one, 1 << bits[at]) for one, bits in zip(held, ROUTES)]

    def both(held, came):
        return [one for pair in zip(held, came) for one in pair]

    def messages(lines):
        return [shaped((one, third), jnp.bfloat16) for one in lines]

    third = width // 3
    tail = packed_rows(slot_rows, 4 * head_width // 3)
    cuts = (0, 2 * wide // 3, 4 * wide // 3, 2 * wide + PAIR)
    sizes = [packed_rows(slot_rows, last - first) for first, last in zip(cuts, cuts[1:])]
    valid_row = valid_tokens.reshape(1, rows)
    first, second, *held = fetching_call(
        start_kernel,
        [shaped((each, 4 * head_width), jnp.bfloat16), shaped((each, cuts[3]), jnp.bfloat16)]
        + [shaped((rows, third), jnp.bfloat16)] * 3,
        [query_weight, key_weight, value_weight, output_weight, inner_weight, outer_weight, valid_row, tokens],
    )
    came = step(held, 0)
    first_held, second_held = far_gather(first), far_gather(second)
    held = local_call(
        functools.partial(first_pack_kernel, slot_rows=slot_rows), messages([2 * rows + tail] * 3),
        held + came + [first_held],
    )
    came = step(held, 1)
    held = local_call(
        functools.partial(second_pack_kernel, rows=2 * rows, slot_rows=slot_rows, cuts=cuts),
        messages([4 * rows + 2 * tail + size for size in sizes]), both(held, came) + [second_held],
    )
    came = step(held, 2)
    segment_all = lax.dynamic_index_in_dim(segments, far_place, 0, keepdims=False)
    tables = attention_tables(random_blocks, segment_all, place, core, span, length // BLOCK)
    tables, owner, came = lax.optimization_barrier((tables, owner, came))
    sent_masks = [tuple(slot_masks(bits[:2])) for bits in ROUTES]
    came_masks = [tuple(mask ^ (1 << bits[2]) for mask in sent) for sent, bits in zip(sent_masks, ROUTES)]
    arrived = both(held, came)
    held = local_call(
        functools.partial(third_pack_kernel, tokens=4 * rows, tail=2 * tail),
        messages([4 * tail + 2 * size for size in sizes]), arrived,
    )
    came = step(held, 0)
    own = local_call(
        functools.partial(place_tokens_kernel, masks=tuple(both(sent_masks, came_masks)), rows=rows),
        [shaped((span * rows, width), jnp.bfloat16)], [tie(held[0], arrived[0])] + arrived[1:],
    )[0]
    other = swap_core(own)
    late = local_call(
        functools.partial(fourth_pack_kernel, skip=4 * tail), messages([4 * size for size in sizes]),
        both(held, came),
    )
    late_came = step(late, 1)

    held, came = tie(late[0], (held, came))
    units = units_of(
        ((0, 0, head_width),)
        + tuple((1, 2 * at + shift, PAIR) for shift in (0, PAIR) for at in range(0, head_width, PAIR))
        + ((2, 0, head_width),)
    )
    plan = []
    for at, bits in enumerate(ROUTES):
        part = units[at * len(units) // 3 : (at + 1) * len(units) // 3]
        sent = tuple(slot_masks((bits[1], bits[2])))
        plan += [(sent, part), (tuple(mask ^ (1 << bits[0]) for mask in sent), part)]
    full_query, full_kv, full_output = place_packed(
        owner, both(held, came), tuple(plan), (head_width, 2 * head_width, head_width), each
    )
    own_query, own_kv = local_call(
        token_kernel, [shaped((rows, head_width), jnp.bfloat16), shaped((span * rows, 2 * head_width), jnp.bfloat16)],
        [own, full_query, full_kv], flops=4 * own.size * head_width, spare=12,
    )
    mixed, mass, queries, kv = attend(tables, own_query, own_kv, other, full_query, full_kv)

    half_shape, low_shape = shaped((rows, width)), shaped((rows, width), jnp.bfloat16)
    gain_one, shift_one, gain_two, shift_two = (
        one.reshape(1, width) for one in (attn_gain, attn_shift, ffn_gain, ffn_shift)
    )
    part_own, part_other, attended = local_call(
        project_kernel, [half_shape, low_shape, shaped(mixed.shape, jnp.bfloat16)], [mixed, full_output],
        flops=2 * mixed.size * width,
    )
    turned = local_call(
        turn_kernel, [shaped(one.shape[::-1], jnp.bfloat16) for one in (full_query, full_kv)],
        [tie(part_own, full_query), full_kv],
    )
    part_came, late, late_came, turned = lax.optimization_barrier((swap_core(part_other), late, late_came, turned))
    turned_query, turned_kv = turned
    first_sum, hidden, hidden_own = local_call(
        first_norm_kernel, [half_shape, half_shape, low_shape],
        [tokens, part_own, part_came, gain_one, shift_one],
    )
    hidden_other = swap_core(hidden_own)
    late, late_came = tie(hidden_own, (late, late_came))
    units = units_of(((0, 0, wide), (1, 0, wide), (2, 0, PAIR)))
    plan = []
    for at, bits in enumerate(ROUTES):
        part = units[cuts[at] // PAIR : cuts[at + 1] // PAIR]
        sent = tuple(slot_masks((bits[2], bits[0])))
        plan += [(sent, part), (tuple(mask ^ (1 << bits[1]) for mask in sent), part)]
    full_inner, full_outer, counts = place_packed(
        owner, both(late, late_came), tuple(plan), (wide, wide, PAIR), each
    )
    active_shape, slope_shape = shaped((rows, wide), jnp.bfloat16), shaped((rows, wide))
    sums = [pltpu.VMEM((rows, width), jnp.float32)]
    count_own = local_call(functools.partial(count_kernel, each=each), [shaped((8, PAIR))], [counts])[0]
    count_came = swap_core(count_own)
    part_other, active_other, slope_other = local_call(
        feed_kernel, [low_shape, active_shape, slope_shape], [hidden_other, full_inner, full_outer],
        scratch=sums, spare=12,
    )
    part_came = swap_core(part_other)
    part_own, active_own, slope_own = local_call(
        feed_kernel, [half_shape, active_shape, slope_shape], [tie(part_other, hidden_own), full_inner, full_outer],
        scratch=sums, spare=12,
    )
    token_total = devices * lax.axis_size("tensor") * rows
    grad_second, grad_ffn_own, stats_two, result = local_call(
        functools.partial(second_norm_kernel, token_total=token_total),
        [half_shape, low_shape, shaped((8, width)), low_shape],
        [hidden, part_own, part_came, gain_two, shift_two, teacher, valid_row, count_own, count_came],
        free=1,
    )
    grad_ffn_other = swap_core(grad_ffn_own)
    upper_own, part_own = local_call(
        feed_back_kernel, [active_shape, half_shape], [grad_ffn_own, slope_own, full_inner, full_outer],
        scratch=sums, spare=12,
    )
    upper_other, part_other = local_call(
        feed_back_kernel, [active_shape, low_shape],
        [tie(part_own, grad_ffn_other), slope_other, full_inner, full_outer], scratch=sums, spare=12,
    )
    part_came = swap_core(part_other)
    scatter_masks = tuple(tuple(slot_masks(bits[::-1])) for bits in ROUTES)
    groups = tuple((one[: span // 2], one[span // 2 :]) for one in scatter_masks)
    outs = wide_gradients(
        owner, (grad_ffn_own, grad_ffn_other), (active_own, active_other), (hidden_own, hidden_other),
        (upper_own, upper_other), groups
    )
    outs = [one.reshape(span // 2, slot_rows, one.shape[2]) for one in outs]
    wide_keep, wide_came = outs[::2], step(outs[1::2], 0)
    part_came = tie(outs[0], part_came)
    grad_first, grad_attn_own, stats_one = local_call(
        first_back_kernel, [half_shape, low_shape, shaped((8, width))],
        [grad_second, part_own, part_came, first_sum, gain_one, stats_two],
    )
    grad_attn_other = swap_core(grad_attn_own)
    stats_came = swap_core(stats_one)
    query_grad, kv_grad = attend_back(
        tables, queries, kv, mixed, mass, grad_attn_own, grad_attn_other, full_output
    )

    def folded(keep, came):
        return fold(keep, [[one] for one in came])

    small = local_call(small_kernel, [shaped((width, PAIR))], [stats_one, tie(query_grad, stats_came)])[0]
    token_sent = token_other(tie(small, kv_grad), query_grad, turned_kv, turned_query)
    wide_keep, wide_send = folded(wide_keep, tie(token_sent, wide_came))
    wide_came = step(wide_send, 1)
    token_came = swap_core(tie(wide_keep[0], token_sent))
    made = narrow_gradients(
        own, other, tie(wide_keep[0], kv_grad), query_grad, grad_attn_own, grad_attn_other, attended
    )
    keep, send = token_own(
        owner, kv_grad, query_grad, turned_kv, turned_query, tie(made, token_came), made, small, scatter_masks
    )
    riders = tuple([bits[0] for bits in ROUTES].index(bits[2]) for bits in ROUTES)
    columns = width // 3
    ride = slot_rows * wide_keep[0].shape[2] // columns
    lengths = [one.shape[0] * one.shape[1] + ride for one in send]
    outs = local_call(
        functools.partial(merge_kernel, riders=riders),
        [shaped(one.shape[1:]) for one in wide_keep] + [shaped((one, columns), jnp.bfloat16) for one in lengths],
        wide_keep + tie(keep[0], wide_came) + send,
    )
    wide_keep, came = outs[:3], step(outs[3:], 0)
    plain = rows + 2 * slot_rows
    halves = []
    for one in keep:
        half = (one.shape[0] // 2,) + one.shape[1:]
        halves += [shaped(half), shaped(half, jnp.bfloat16)]
    far_send = [shaped((each, 2 * wide), jnp.bfloat16)] if far_count == 2 else []
    cames = came
    outs = local_call(functools.partial(part_kernel, plain=plain), halves, keep + cames)
    keep, send = list(outs[::2]), list(outs[1::2])
    came = step(send, 1)
    wide_sum, *wide_send = local_call(
        functools.partial(wide_end_kernel, riders=riders, lengths=tuple(one - ride for one in lengths)),
        [shaped((slot_rows, 2 * wide))] + far_send, [tie(keep[0], cames[0])] + list(cames[1:]) + list(wide_keep),
    )

    def far_scatter(total, dtype=jnp.bfloat16):
        total = total.reshape(far_count, each, total.shape[1])
        for bit in far_bits[::-1]:
            half = total.shape[0] // 2
            total = total[:half] + swap_mask(total[half:].astype(dtype), 1 << bit).astype(jnp.float32)
        return total[0]

    keep, send = fold(keep, [[one] for one in came], plain)
    came = step(send, 2)
    if far_count == 2:
        part_outer, part_inner = local_call(
            wide_out_kernel, [shaped((each, wide))] * 2, [wide_sum, swap_mask(wide_send[0], 1 << far_bits[0])], free=2
        )
    else:
        wide_sum = far_scatter(wide_sum)
        part_outer, part_inner = wide_sum[:, :wide], wide_sum[:, wide:]
    came = tie(part_outer, came)
    made_shape = shaped((slot_rows, 4 * head_width + PAIR))
    send_shape = [shaped((each, 4 * head_width + PAIR), jnp.bfloat16)] if far_count == 2 else []
    arrived = both(keep, came)
    made, *send = local_call(
        functools.partial(narrow_last_kernel, near=rows), [made_shape] + send_shape, arrived
    )
    grad_tokens = local_call(
        token_end_kernel, [half_shape], [grad_first, tie(made, arrived[0])] + arrived[1:], free=1
    )[0]
    half = each // 2
    if far_count == 2:
        weight_shape = shaped((each, head_width))
        outs = local_call(
            end_kernel, [weight_shape] * 4 + [shaped((1, 1))] + [shaped((1, half))] * 4,
            [made, tie(grad_tokens, swap_mask(send[0], 1 << far_bits[0])), count_own, count_came],
            [jnp.stack([core, jnp.int32(devices)])], free=9,
        )
        part_query, part_key, part_value, part_output = outs[:4]
        loss_value = outs[4].reshape(())
        norm_parts = [one.reshape(half) for one in outs[5:]]
    else:
        narrow_sum = far_scatter(made[:, : 4 * head_width])
        small = far_scatter(made[:, 4 * head_width :], jnp.float32)
        part_query, part_output = narrow_sum[:, :head_width], narrow_sum[:, head_width : 2 * head_width]
        kv_sum = narrow_sum[:, 2 * head_width :].reshape(each, head_width // PAIR, 2, PAIR)
        part_key, part_value = (kv_sum[:, :, one].reshape(each, head_width) for one in range(2))
        loss_value = small[0, 4] / (2.0 * width * (count_own[0, 0] + count_came[0, 0]))
        mine = jnp.where(core == 0, small[:half], small[half:])
        norm_parts = [mine[:, at] for at in range(4)]
    return (
        result,
        loss_value,
        grad_tokens,
        part_query,
        part_key,
        part_value,
        part_output,
        part_inner,
        part_outer,
        *norm_parts,
    )


def solution(mesh):
    both = P(("dp", "tensor"))
    rows_spec = P(("dp", "tensor"), None)
    weight_spec = P("dp", "tensor")
    in_specs = (rows_spec,) + (weight_spec,) * 6 + (P(),) * 4
    in_specs += (rows_spec, P(), P("tensor", None, None), both)
    out_specs = (rows_spec, P(), rows_spec) + (weight_spec,) * 6 + (both,) * 4
    return jax.shard_map(shards, mesh=mesh, in_specs=in_specs, out_specs=out_specs, check_vma=False)
```

```python
import functools

import jax
import jax.numpy as jnp
from jax import lax
from jax.experimental import pallas as pl
from jax.experimental.pallas import tpu as pltpu
from jax.sharding import PartitionSpec as P

BLOCK = 64
HEAD = 64
PAIR = 2 * HEAD
SLOTS = 6
ROUTES = ((0, 1, 2), (1, 2, 0), (2, 0, 1))

epsilon = 1e-05
masked_value = -1e30
score_scale = 0.125


def swap_mask(block, mask):
    count = lax.axis_size("dp")
    return lax.ppermute(block, "dp", [(one, one ^ mask) for one in range(count)])


def swap_core(block):
    return lax.ppermute(block, "tensor", [(0, 1), (1, 0)])


def dot_plain(left_side, right_side):
    return jnp.dot(left_side, right_side, preferred_element_type=jnp.float32)


def dot_cols(left_side, right_side):
    return lax.dot_general(
        left_side, right_side, (((1,), (1,)), ((), ())), preferred_element_type=jnp.float32
    )


def dot_rows(left_side, right_side):
    return lax.dot_general(
        left_side, right_side, (((0,), (0,)), ((), ())), preferred_element_type=jnp.float32
    )


def params(megabytes):
    return pltpu.CompilerParams(vmem_limit_bytes=int(megabytes) << 20)


def cost(flops=0, moved=0, transcendentals=0):
    return pl.CostEstimate(flops=int(flops), bytes_accessed=int(moved), transcendentals=int(transcendentals))


def in_vmem(count):
    return [pl.BlockSpec(memory_space=pltpu.VMEM)] * count


def in_smem(count):
    return [pl.BlockSpec(memory_space=pltpu.SMEM)] * count


def shaped(shape, dtype=jnp.float32):
    return jax.ShapeDtypeStruct(tuple(shape), dtype)


def local_call(kernel, outs, vmem_inputs, smem_inputs=(), scratch=(), flops=0, transcendentals=0, spare=8, free=0):
    moved = sum(one.size * one.dtype.itemsize for one in list(vmem_inputs) + list(outs))
    held = sum(one.size * one.dtype.itemsize for one in (shaped(s.shape, s.dtype) for s in scratch))
    held = held // (1 << 20) + 1 + spare
    return pl.pallas_call(
        kernel,
        out_shape=tuple(
            one if len(outs) - at <= free else pltpu.VMEM(one.shape, one.dtype) for at, one in enumerate(outs)
        ),
        in_specs=in_smem(len(smem_inputs)) + in_vmem(len(vmem_inputs)),
        out_specs=tuple(in_vmem(len(outs))),
        scratch_shapes=list(scratch),
        compiler_params=params(held),
        cost_estimate=pl.CostEstimate(flops=1000, bytes_accessed=1000, transcendentals=0),
    )(*smem_inputs, *[pltpu.with_memory_space_constraint(one, pltpu.VMEM) for one in vmem_inputs])


def slot_masks(bits):
    return [
        sum(((slot >> at) & 1) << bit for at, bit in enumerate(bits))
        for slot in range(1 << len(bits))
    ]


def in_pieces(values):
    high = values.astype(jnp.bfloat16).astype(jnp.float32)
    middle = (values - high).astype(jnp.bfloat16).astype(jnp.float32)
    return high + pltpu.roll(middle, 8, 1) + pltpu.roll(values - high - middle, 16, 1)


def from_pieces(pieces):
    lanes = pieces.shape[1]
    total = pieces + pltpu.roll(pieces, lanes - 8, 1) + pltpu.roll(pieces, lanes - 16, 1)
    return jnp.where(lax.broadcasted_iota(jnp.int32, pieces.shape, 1) % PAIR < 8, total, 0.0)


def fold_kernel(*refs, thirds, arrivals, plain):
    outs = refs[thirds * (1 + arrivals) :]
    for third in range(thirds):
        keep_ref = refs[third * (1 + arrivals)]
        came = refs[third * (1 + arrivals) + 1 : (third + 1) * (1 + arrivals)]
        half, lines = keep_ref.shape[0] // 2, keep_ref.shape[1]
        most = lines if plain is None else min(plain, lines)
        for side in range(2):
            part = slice(side * half, (side + 1) * half)
            total = sum([one[part, :most].astype(jnp.float32) for one in came], keep_ref[part, :most])
            out_ref = outs[2 * third + side]
            out_ref[:, :most] = total.astype(out_ref.dtype)
            if most == lines:
                continue
            for at in range(half):
                total = keep_ref[side * half + at, most:]
                for one in came:
                    total += from_pieces(one[side * half + at, most:].astype(jnp.float32))
                out_ref[at, most:] = (in_pieces(total) if side else total).astype(out_ref.dtype)


def fold(keeps, arrivals, plain=None):
    outs = []
    for keep in keeps:
        half = (keep.shape[0] // 2,) + keep.shape[1:]
        outs += [shaped(half), shaped(half, jnp.bfloat16)]
    operands = []
    for keep, came in zip(keeps, arrivals):
        operands += [keep] + list(came)
    kernel = functools.partial(fold_kernel, thirds=len(keeps), arrivals=len(arrivals[0]), plain=plain)
    outs = local_call(kernel, outs, operands)
    return list(outs[::2]), list(outs[1::2])


def pick(chosen, table):
    return lax.dot_general(
        chosen.astype(jnp.bfloat16), table.astype(jnp.bfloat16), (((chosen.ndim - 1,), (0,)), ((), ())),
        preferred_element_type=jnp.float32,
    )


def attention_tables(random_blocks, segment_all, place, core, span, row_blocks):
    heads, blocks, draws = random_blocks.shape
    half, pairs = row_blocks // 2, heads // 2
    local = jnp.arange(row_blocks, dtype=jnp.int32)
    owner = jnp.where(local < half, core, 1 - core)
    absolute = place * row_blocks + owner * half + local % half
    every = jnp.arange(blocks, dtype=jnp.int32)
    mine = absolute[:, None] == every
    edge = (every == 0) | (every == blocks - 1)
    fixed = (jnp.abs(absolute[:, None] - every) <= 1) | edge | edge[absolute][:, None]
    segment_table = segment_all.reshape(blocks, BLOCK).astype(jnp.float32)
    low, high = jnp.min(segment_table, 1), jnp.max(segment_table, 1)
    reach = (jnp.max(jnp.where(mine, low, -1.0), 1)[:, None] <= high) & (
        low <= jnp.max(jnp.where(mine, high, -1.0), 1)[:, None]
    )
    drawn = pick(mine, random_blocks.transpose(1, 0, 2).reshape(blocks, heads * draws))
    drawn = drawn.reshape(row_blocks, heads, draws, 1) == every.astype(jnp.float32)
    allowed = (jnp.any(drawn, 2) | fixed[:, None]) & reach[:, None]
    allowed = allowed.reshape(row_blocks, pairs, 2, blocks)
    listed = jnp.any(allowed, 2)
    rank = pick(listed, every[:, None] < every[None, :])
    count = jnp.max(jnp.sum(listed.astype(jnp.int32), -1), -1)
    chunks = -(-count // SLOTS)
    ends = jnp.sum(jnp.where(local[:, None] >= local[None, :], chunks[None, :], 0), 1)
    most = (row_blocks - 1) * -(-min(blocks, 5 + 2 * draws) // SLOTS) + -(-blocks // SLOTS)
    if span == 1:
        most += -(-blocks // SLOTS)
    items = jnp.arange(most, dtype=jnp.int32)
    item_query = jnp.minimum(jnp.sum((items[:, None] >= ends[None, :]).astype(jnp.int32), 1), row_blocks - 1)
    item_is = item_query[:, None] == local
    first = jnp.sum(jnp.where(item_is, (ends - chunks)[None, :], 0), 1)
    spots = ((items - first) * SLOTS)[:, None] + jnp.arange(SLOTS, dtype=jnp.int32)
    stored = (
        jnp.where((every % row_blocks) // half == core, 0, span * half)
        + ((every // row_blocks) ^ place) * half + every % half
    )
    rows = jnp.concatenate([jnp.where(listed, rank, -1.0)[:, :, None], allowed.astype(jnp.float32)], 2)
    rows = pick(item_is, rows.reshape(row_blocks, -1)).reshape(most, pairs, 3, blocks)
    here = rows[:, :, 0, None, :] == spots[:, None, :, None].astype(jnp.float32)
    code = rows[:, :, 1, None, :] * 256.0 + rows[:, :, 2, None, :] * 512.0 + stored.astype(jnp.float32)
    codes = jnp.sum(jnp.where(here, code, 0.0), -1).astype(jnp.int32)
    order = jnp.arange(2 * span * half, dtype=jnp.int32)
    order_block = (
        ((order % (span * half)) // half) ^ place
    ) * row_blocks + jnp.where(order < span * half, core, 1 - core) * half + order % half
    key_side = pick(order_block[:, None] == every, segment_table).reshape(-1, 1)
    query_side = pick(mine, segment_table)
    query_side = jnp.concatenate([query_side, query_side], 1)
    numbers = [ends[-1:], item_query, (items == first), codes.reshape(-1)]
    return (
        jnp.concatenate([one.astype(jnp.int32) for one in numbers]),
        query_side,
        jnp.broadcast_to(key_side, (key_side.shape[0], PAIR)),
    )


def two_heads(rows, low_lanes):
    rows = rows.astype(jnp.float32)
    zero = jnp.zeros_like(rows)
    return jnp.concatenate(
        [jnp.where(low_lanes, rows, zero), jnp.where(low_lanes, zero, rows)], 0
    )


def item_blocks(numbers_ref, first, side, key_side_ref):
    low_row = lax.broadcasted_iota(jnp.int32, (1, PAIR), 1) < HEAD
    spots, masks = [], []
    for slot in range(SLOTS):
        code = numbers_ref[first + slot]
        spot = pl.ds(pl.multiple_of((code & 255) * BLOCK, BLOCK), BLOCK)
        flags = jnp.where(low_row, code & 256, code & 512)
        spots.append(spot)
        masks.append(key_side_ref[spot, :] == jnp.where(flags != 0, side, -1.0))
    return spots, jnp.concatenate(masks, 0)


def attend_kernel(
    numbers_ref, query_side_ref, key_side_ref,
    own_query_ref, own_kv_ref, other_ref, query_weight_ref, kv_weight_ref,
    mixed_ref, mass_ref, q_ref, kv_ref, state_ref, mixture_ref, *, pairs
):
    half_rows, half_kv = own_query_ref.shape[0], own_kv_ref.shape[0]
    q_ref[:half_rows, :] = own_query_ref[...]
    q_ref[half_rows:, :] = dot_plain(other_ref[:half_rows, :], query_weight_ref[...]).astype(jnp.bfloat16)
    kv_ref[:half_kv, :] = own_kv_ref[...]
    step = 512

    def one_part(at, carry):
        lines = pl.ds(pl.multiple_of(at * step, step), step)
        kv_ref[pl.ds(pl.multiple_of(half_kv + at * step, step), step), :] = dot_plain(
            other_ref[lines, :], kv_weight_ref[...]
        ).astype(jnp.bfloat16)
        return carry

    lax.fori_loop(0, half_kv // step, one_part, 0)
    low_lanes = lax.broadcasted_iota(jnp.int32, (BLOCK, PAIR), 1) < HEAD
    most = (numbers_ref.shape[0] - 1) // (2 + pairs * SLOTS)

    def one_item(item, carry):
        query = numbers_ref[1 + item]
        fresh = numbers_ref[1 + most + item] == 1
        side = query_side_ref[pl.ds(query, 1), :]
        rows = pl.ds(pl.multiple_of(query * BLOCK, BLOCK), BLOCK)
        held = []
        for pair in range(pairs):
            both = two_heads(q_ref[rows, pair * PAIR : (pair + 1) * PAIR], low_lanes).astype(jnp.bfloat16)
            spots, mask = item_blocks(
                numbers_ref, 1 + 2 * most + (item * pairs + pair) * SLOTS, side, key_side_ref
            )
            start = pair * 2 * PAIR
            keys = jnp.concatenate([kv_ref[spot, start : start + PAIR] for spot in spots], 0)
            values = jnp.concatenate([kv_ref[spot, start + PAIR : start + 2 * PAIR] for spot in spots], 0)
            held.append((jnp.where(mask, dot_cols(keys, both) * score_scale, masked_value), values))
        done = []
        for pair in range(pairs):
            scores, values = held[pair]
            place = query * pairs + pair
            state = state_ref[place]
            old_top = jnp.where(fresh, masked_value, state[0:1, :])
            top = jnp.maximum(old_top, jnp.max(scores, axis=0, keepdims=True))
            raised = jnp.exp(scores - top)
            shrunk = jnp.exp(old_top - top)
            total = jnp.where(fresh, 0.0, state[1:2, :] * shrunk) + jnp.sum(raised, axis=0, keepdims=True)
            mixture = jnp.where(fresh, 0.0, mixture_ref[place] * shrunk) + dot_rows(
                values, raised.astype(jnp.bfloat16)
            )
            done.append((top, total, mixture))
        for pair in range(pairs):
            top, total, mixture = done[pair]
            place = query * pairs + pair
            state_ref[place, 0:1, :] = top
            state_ref[place, 1:2, :] = total
            mixture_ref[place] = mixture
            normed = (mixture / total).T
            mixed_ref[rows, pair * PAIR : (pair + 1) * PAIR] = jnp.where(
                low_lanes, normed[:BLOCK], normed[BLOCK:]
            )
            mass_ref[place] = jnp.broadcast_to(top + jnp.log(total), (8, PAIR))
        return carry

    lax.fori_loop(0, numbers_ref[0], one_item, 0)


def attend(tables, own_query, own_kv, other, query_weight, kv_weight):
    rows, width = 2 * own_query.shape[0], own_query.shape[1]
    pairs, row_blocks = width // PAIR, rows // BLOCK
    places = pairs * row_blocks
    return local_call(
        functools.partial(attend_kernel, pairs=pairs),
        [
            shaped((rows, width)),
            shaped((places, 8, PAIR)),
            shaped((rows, width), jnp.bfloat16),
            shaped((2 * own_kv.shape[0], own_kv.shape[1]), jnp.bfloat16),
        ],
        list(tables[1:]) + [own_query, own_kv, other, query_weight, kv_weight],
        tables[:1],
        [
            pltpu.VMEM((places, 8, PAIR), jnp.float32),
            pltpu.VMEM((places, PAIR, PAIR), jnp.float32),
        ],
        flops=8e9, transcendentals=4e6, spare=12,
    )


def attend_back_kernel(
    numbers_ref, query_side_ref, key_side_ref, q_ref, kv_ref,
    mixed_ref, mass_ref, own_grad_ref, other_grad_ref, weight_ref,
    query_grad_ref, kv_grad_ref, sum_ref, grad_ref, query_sum_ref, *, pairs
):
    half_rows = own_grad_ref.shape[0]
    grad_ref[:half_rows, :] = dot_plain(own_grad_ref[...], weight_ref[...]).astype(jnp.bfloat16)
    grad_ref[half_rows:, :] = dot_plain(other_grad_ref[...], weight_ref[...]).astype(jnp.bfloat16)
    low_lanes = lax.broadcasted_iota(jnp.int32, (BLOCK, PAIR), 1) < HEAD
    most = (numbers_ref.shape[0] - 1) // (2 + pairs * SLOTS)
    sum_ref[...] = jnp.zeros_like(sum_ref)

    def one_item(item, carry):
        query = numbers_ref[1 + item]
        fresh = numbers_ref[1 + most + item] == 1
        side = query_side_ref[pl.ds(query, 1), :]
        rows = pl.ds(pl.multiple_of(query * BLOCK, BLOCK), BLOCK)
        held = []
        for pair in range(pairs):
            lanes = slice(pair * PAIR, (pair + 1) * PAIR)
            both = two_heads(q_ref[rows, lanes], low_lanes).astype(jnp.bfloat16)
            grads = grad_ref[rows, lanes].astype(jnp.float32)
            turned = (grads * mixed_ref[rows, lanes]).T
            inner = jnp.concatenate(
                [jnp.sum(turned[:HEAD], axis=0, keepdims=True), jnp.sum(turned[HEAD:], axis=0, keepdims=True)], 1
            )
            grads = two_heads(grads, low_lanes).astype(jnp.bfloat16)
            spots, mask = item_blocks(
                numbers_ref, 1 + 2 * most + (item * pairs + pair) * SLOTS, side, key_side_ref
            )
            start = pair * 2 * PAIR
            kv = jnp.concatenate([kv_ref[spot, start : start + 2 * PAIR] for spot in spots], 0)
            blank = jnp.zeros_like(both)
            sides = jnp.concatenate(
                [jnp.concatenate([both, blank], 1), jnp.concatenate([blank, grads], 1)], 0
            )
            held.append((dot_cols(kv, sides), inner, sides, kv, spots, mask))
        done = []
        for pair in range(pairs):
            products, inner, sides, kv, spots, mask = held[pair]
            place = query * pairs + pair
            scores = jnp.where(mask, products[:, :PAIR] * score_scale, masked_value)
            chances = jnp.exp(scores - mass_ref[place, 0:1, :])
            score_grads = (chances * (products[:, PAIR:] - inner)).astype(jnp.bfloat16)
            query_grad = dot_rows(score_grads, kv[:, :PAIR])
            kv_grad = dot_plain(jnp.concatenate([score_grads, chances.astype(jnp.bfloat16)], 1), sides)
            done.append((query_grad, kv_grad))
        for pair in range(pairs):
            lanes = slice(pair * PAIR, (pair + 1) * PAIR)
            start = pair * 2 * PAIR
            query_grad, kv_grad = done[pair]
            spots = held[pair][4]
            query_grad = jnp.where(low_lanes, query_grad[:BLOCK], query_grad[BLOCK:])
            query_sum_ref[rows, lanes] = jnp.where(fresh, 0.0, query_sum_ref[rows, lanes]) + query_grad
            for slot, spot in enumerate(spots):
                sum_ref[spot, start : start + 2 * PAIR] += kv_grad[slot * BLOCK : (slot + 1) * BLOCK]
        return carry

    lax.fori_loop(0, numbers_ref[0], one_item, 0)
    query_grad_ref[...] = (query_sum_ref[...] * score_scale).astype(jnp.bfloat16)
    for pair in range(pairs):
        start = pair * 2 * PAIR
        kv_grad_ref[:, start : start + PAIR] = (sum_ref[:, start : start + PAIR] * score_scale).astype(jnp.bfloat16)
        kv_grad_ref[:, start + PAIR : start + 2 * PAIR] = sum_ref[:, start + PAIR : start + 2 * PAIR].astype(
            jnp.bfloat16
        )


def attend_back(tables, queries, kv, mixed, mass, own_grad, other_grad, weight):
    rows, width = queries.shape
    pairs = width // PAIR
    return local_call(
        functools.partial(attend_back_kernel, pairs=pairs),
        [shaped((rows, width), jnp.bfloat16), shaped(kv.shape, jnp.bfloat16)],
        list(tables[1:]) + [queries, kv, mixed, mass, own_grad, other_grad, weight],
        tables[:1],
        [
            pltpu.VMEM(kv.shape, jnp.float32),
            pltpu.VMEM((rows, width), jnp.bfloat16),
            pltpu.VMEM((rows, width), jnp.float32),
        ],
        flops=10e9, transcendentals=4e6, spare=12,
    )


LANES = 2 * PAIR


def packed_rows(slot_rows, columns):
    return columns // LANES * slot_rows + (slot_rows // 2 if columns % LANES else 0)


def put_packed(out_ref, base, source_ref, first, columns, slot_rows):
    for chunk in range(columns // LANES):
        at = first + chunk * LANES
        out_ref[base : base + slot_rows, :] = source_ref[:, at : at + LANES]
        base += slot_rows
    if columns % LANES:
        half, at = slot_rows // 2, first + columns - PAIR
        out_ref[base : base + half, :PAIR] = source_ref[:half, at : at + PAIR]
        out_ref[base : base + half, PAIR:] = source_ref[half:, at : at + PAIR]


def unpacked(packed, slot_rows):
    full = packed.shape[0] // slot_rows
    parts = [packed[at * slot_rows : (at + 1) * slot_rows] for at in range(full)]
    tail = packed[full * slot_rows :]
    if tail.shape[0]:
        parts.append(jnp.concatenate([tail[:, :PAIR], tail[:, PAIR:]], 0))
    return jnp.concatenate(parts, 1)


def fetched(far, near, arrived):
    copies = [
        pltpu.make_async_copy(far_ref, near_ref, arrived.at[at])
        for at, (far_ref, near_ref) in enumerate(zip(far, near))
    ]
    for copy in copies:
        copy.start()
    for copy in copies:
        copy.wait()


def start_kernel(*refs):
    near = refs[13:-1]
    fetched(refs[:8], near, refs[-1])
    first_ref, second_ref, thirds = refs[8], refs[9], refs[10:13]
    columns = thirds[0].shape[1]
    for at in range(3):
        thirds[at][...] = near[7][:, at * columns : (at + 1) * columns]
    for out_ref, sources in ((first_ref, near[:4]), (second_ref, near[4:6])):
        at = 0
        for one in sources:
            out_ref[:, at : at + one.shape[1]] = one[...]
            at += one.shape[1]
    count = jnp.sum(near[6][...].astype(jnp.float32), axis=1, keepdims=True)
    second_ref[:, at:] = jnp.broadcast_to(count, (second_ref.shape[0], PAIR)).astype(jnp.bfloat16)


def fetching_call(kernel, outs, sources):
    return pl.pallas_call(
        kernel,
        out_shape=[pltpu.VMEM(one.shape, one.dtype) for one in outs],
        in_specs=[pl.BlockSpec(memory_space=pltpu.HBM)] * len(sources),
        out_specs=in_vmem(len(outs)),
        scratch_shapes=[pltpu.VMEM(one.shape, one.dtype) for one in sources]
        + [pltpu.SemaphoreType.DMA((len(sources),))],
        compiler_params=params(8),
    )(*[pltpu.with_memory_space_constraint(one, pltpu.HBM) for one in sources])


def first_pack_kernel(*refs, slot_rows):
    sent, came, weights_ref, outs = refs[:3], refs[3:6], refs[6], refs[7:]
    rows = sent[0].shape[0]
    third = weights_ref.shape[1] // 3
    for at in range(3):
        outs[at][:rows, :] = sent[at][...]
        outs[at][rows : 2 * rows, :] = came[at][...]
        put_packed(outs[at], 2 * rows, weights_ref, at * third, third, slot_rows)


def second_pack_kernel(*refs, rows, slot_rows, cuts):
    second_ref, outs = refs[6], refs[7:]
    for at in range(3):
        sent_ref, came_ref, out_ref = refs[2 * at], refs[2 * at + 1], outs[at]
        tail = sent_ref.shape[0] - rows
        out_ref[:rows, :] = sent_ref[:rows, :]
        out_ref[rows : 2 * rows, :] = came_ref[:rows, :]
        out_ref[2 * rows : 2 * rows + tail, :] = sent_ref[rows:, :]
        out_ref[2 * rows + tail : 2 * (rows + tail), :] = came_ref[rows:, :]
        put_packed(out_ref, 2 * (rows + tail), second_ref, cuts[at], cuts[at + 1] - cuts[at], slot_rows)


def third_pack_kernel(*refs, masks, rows, tail):
    out_ref = refs[6]
    columns = refs[0].shape[1]
    for at in range(3):
        tokens = len(masks[2 * at]) * rows
        for side in range(2):
            piece, target = refs[2 * at + side], refs[7 + at]
            for slot, mask in enumerate(masks[2 * at + side]):
                out_ref[mask * rows : (mask + 1) * rows, at * columns : (at + 1) * columns] = piece[
                    slot * rows : (slot + 1) * rows, :
                ]
            target[side * tail : (side + 1) * tail, :] = piece[tokens : tokens + tail, :]
            rest = piece.shape[0] - tokens - tail
            base = 2 * tail + side * rest
            target[base : base + rest, :] = piece[tokens + tail :, :]


def fourth_pack_kernel(*refs, skip):
    for at in range(3):
        rest = refs[2 * at].shape[0] - skip
        for side in range(2):
            refs[6 + at][side * rest : (side + 1) * rest, :] = refs[2 * at + side][skip:, :]


def place_packed_kernel(owner_ref, *refs, plan, slot_rows, rows):
    pieces, outs = refs[: len(plan)], refs[len(plan) :]
    for piece, (masks, units) in zip(pieces, plan):
        size = packed_rows(slot_rows, len(units) * PAIR)
        for slot, mask in enumerate(masks):
            for far in range(2):
                lines = pl.ds(pl.multiple_of(owner_ref[mask * 2 + far] * rows, rows), rows)
                unit = 0
                while unit < len(units):
                    out, column = units[unit]
                    base = slot * size + unit // 2 * slot_rows
                    if unit + 1 == len(units) and unit % 2 == 0:
                        outs[out][lines, column : column + PAIR] = piece[
                            base : base + rows, far * PAIR : (far + 1) * PAIR
                        ]
                        unit += 1
                        continue
                    base += far * rows
                    if unit % 2 == 0 and units[unit + 1] == (out, column + PAIR):
                        outs[out][lines, column : column + LANES] = piece[base : base + rows, :]
                        unit += 2
                        continue
                    side = unit % 2 * PAIR
                    outs[out][lines, column : column + PAIR] = piece[base : base + rows, side : side + PAIR]
                    unit += 1


def place_packed(owner, pieces, plan, widths, rows):
    blocks = owner.shape[0]
    far_count = blocks // 8
    slot_rows = far_count * rows
    outs = [shaped((blocks * rows, width), jnp.bfloat16) for width in widths]
    if rows % 16 == 0 and far_count == 2:
        kernel = functools.partial(place_packed_kernel, plan=plan, slot_rows=slot_rows, rows=rows)
        return local_call(kernel, outs, pieces, [owner], spare=12)
    made = [jnp.zeros(out.shape, out.dtype) for out in outs]
    for piece, (masks, units) in zip(pieces, plan):
        size = packed_rows(slot_rows, len(units) * PAIR)
        for slot, mask in enumerate(masks):
            block = unpacked(piece[slot * size : (slot + 1) * size], slot_rows)
            lines = owner.reshape(8, far_count)[mask][:, None] * rows + jnp.arange(rows, dtype=jnp.int32)
            for unit, (out, column) in enumerate(units):
                made[out] = made[out].at[lines.reshape(-1), column : column + PAIR].set(
                    block[:, unit * PAIR : (unit + 1) * PAIR]
                )
    return made


def units_of(targets):
    return tuple((out, column + at) for out, column, size in targets for at in range(0, size, PAIR))


def placed_blocks(grad, owner, masks):
    blocks = owner.shape[0]
    rows = grad.shape[0] // blocks
    spots = owner.reshape(8, -1)[jnp.array(masks)].reshape(-1)
    return jnp.take(grad.reshape(blocks, rows, grad.shape[1]), spots, axis=0)


def token_kernel(x_ref, query_weight_ref, kv_weight_ref, query_ref, kv_ref):
    rows = query_ref.shape[0]
    query_ref[...] = dot_plain(x_ref[:rows, :], query_weight_ref[...]).astype(jnp.bfloat16)
    step = 512

    def one_part(at, carry):
        lines = pl.ds(pl.multiple_of(at * step, step), step)
        kv_ref[lines, :] = dot_plain(x_ref[lines, :], kv_weight_ref[...]).astype(jnp.bfloat16)
        return carry

    lax.fori_loop(0, kv_ref.shape[0] // step, one_part, 0)


def project_kernel(mixed_ref, weight_ref, own_ref, other_ref, low_ref):
    low = mixed_ref[...].astype(jnp.bfloat16)
    low_ref[...] = low
    total = dot_cols(low, weight_ref[...])
    half = own_ref.shape[0]
    own_ref[...] = total[:half]
    other_ref[...] = total[half:].astype(jnp.bfloat16)


def normed_rows(values):
    centred = values - jnp.mean(values, axis=-1, keepdims=True)
    spread = jnp.mean(centred * centred, axis=-1, keepdims=True)
    scale = lax.rsqrt(spread + epsilon)
    return centred * scale, scale


def norm_back(grads, normed, scale, gain):
    inner = grads * gain
    middle = jnp.mean(inner, axis=-1, keepdims=True)
    slant = jnp.mean(inner * normed, axis=-1, keepdims=True)
    return scale * (inner - middle - normed * slant)


def first_norm_kernel(tokens_ref, own_ref, came_ref, gain_ref, shift_ref, sum_ref, hidden_ref, low_ref):
    total = tokens_ref[...].astype(jnp.float32) + (own_ref[...] + came_ref[...].astype(jnp.float32))
    sum_ref[...] = total
    normed, _ = normed_rows(total)
    hidden = normed * gain_ref[...] + shift_ref[...]
    hidden_ref[...] = hidden
    low_ref[...] = hidden.astype(jnp.bfloat16)


def feed_kernel(hidden_ref, inner_ref, outer_ref, total_ref, active_ref, slope_ref, sum_ref):
    hidden = hidden_ref[...]
    step = 256
    for start in range(0, inner_ref.shape[1], step):
        columns = slice(start, start + step)
        upper = dot_plain(hidden, inner_ref[:, columns])
        chance = 0.5 * (1.0 + lax.erf(upper * (0.5**0.5)))
        active = (upper * chance).astype(jnp.bfloat16)
        active_ref[:, columns] = active
        slope_ref[:, columns] = chance + upper * (jnp.exp(-0.5 * upper * upper) * 0.3989422804014327)
        part = dot_cols(active, outer_ref[:, columns])
        if start:
            sum_ref[...] += part
        else:
            sum_ref[...] = part
    total_ref[...] = sum_ref[...].astype(total_ref.dtype)


def count_kernel(counts_ref, count_ref, *, each):
    count = jnp.sum(counts_ref[...].astype(jnp.float32), axis=0, keepdims=True) / each
    count_ref[...] = jnp.broadcast_to(count, count_ref.shape)


def second_norm_kernel(
    hidden_ref, own_ref, came_ref, gain_ref, shift_ref, teacher_ref, valid_ref, count_own_ref, count_came_ref,
    grad_ref, low_ref, stats_ref, result_ref, *, token_total
):
    valid = jnp.broadcast_to(valid_ref[...].astype(jnp.float32), (PAIR, valid_ref.shape[1])).T[:, :1]
    factor = token_total / (count_own_ref[0:1, 0:1] + count_came_ref[0:1, 0:1])
    total = hidden_ref[...] + (own_ref[...] + came_ref[...].astype(jnp.float32))
    normed, scale = normed_rows(total)
    gain = gain_ref[...]
    result = normed * gain + shift_ref[...]
    result_ref[...] = result.astype(jnp.bfloat16)
    errors = (result - teacher_ref[...].astype(jnp.float32)) * valid
    grads = errors * factor
    grad = norm_back(grads, normed, scale, gain)
    grad_ref[...] = grad
    low_ref[...] = grad.astype(jnp.bfloat16)
    stats_ref[...] = jnp.zeros_like(stats_ref)
    stats_ref[2:3, :] = jnp.sum(grads * normed, axis=0, keepdims=True)
    stats_ref[3:4, :] = jnp.sum(grads, axis=0, keepdims=True)
    squares = jnp.sum(jnp.sum(errors * errors, axis=0, keepdims=True), axis=1, keepdims=True)
    stats_ref[4:5, :] = jnp.broadcast_to(squares, (1, stats_ref.shape[1]))


def feed_back_kernel(grads_ref, slope_ref, inner_ref, outer_ref, upper_ref, total_ref, sum_ref):
    grads = grads_ref[...]
    step = 256
    for start in range(0, inner_ref.shape[1], step):
        columns = slice(start, start + step)
        upper = (dot_plain(grads, outer_ref[:, columns]) * slope_ref[:, columns]).astype(jnp.bfloat16)
        upper_ref[:, columns] = upper
        part = dot_cols(upper, inner_ref[:, columns])
        if start:
            sum_ref[...] += part
        else:
            sum_ref[...] = part
    total_ref[...] = sum_ref[...].astype(total_ref.dtype)


def first_back_kernel(
    grad_ref, own_ref, came_ref, sum_ref, gain_ref, other_stats_ref, out_ref, low_ref, stats_ref
):
    grads = grad_ref[...] + (own_ref[...] + came_ref[...].astype(jnp.float32))
    normed, scale = normed_rows(sum_ref[...])
    grad = norm_back(grads, normed, scale, gain_ref[...])
    out_ref[...] = grad
    low_ref[...] = grad.astype(jnp.bfloat16)
    stats_ref[...] = other_stats_ref[...]
    stats_ref[0:1, :] = jnp.sum(grads * normed, axis=0, keepdims=True)
    stats_ref[1:2, :] = jnp.sum(grads, axis=0, keepdims=True)


def write_blocks(owner_ref, made_ref, column, width, out_ref, out_column, masks, far_count, rows):
    for slot, mask in enumerate(masks):
        for far in range(far_count):
            start = pl.multiple_of(owner_ref[mask * far_count + far] * rows, rows)
            out_ref[slot * far_count + far, :, out_column : out_column + width] = made_ref[
                pl.ds(start, rows), column : column + width
            ].astype(out_ref.dtype)


def wide_kernel(
    owner_ref, own_grad_ref, other_grad_ref, own_active_ref, other_active_ref, own_hidden_ref, other_hidden_ref,
    own_upper_ref, other_upper_ref, *refs, groups, far_count, rows, step
):
    outs, made_ref = refs[:-1], refs[-1]
    grads = jnp.concatenate([own_grad_ref[...], other_grad_ref[...]], 0)
    hidden = jnp.concatenate([own_hidden_ref[...], other_hidden_ref[...]], 0)
    width = own_active_ref.shape[1]
    third_width = 2 * width // 3
    for start in range(0, 2 * width, step):
        part = slice(start % width, start % width + step)
        if start < width:
            made_ref[...] = dot_rows(grads, jnp.concatenate([own_active_ref[:, part], other_active_ref[:, part]], 0))
        else:
            made_ref[...] = dot_rows(hidden, jnp.concatenate([own_upper_ref[:, part], other_upper_ref[:, part]], 0))
        third = start // third_width
        for at, masks in enumerate(groups[third]):
            write_blocks(
                owner_ref, made_ref, 0, step, outs[third * len(groups[third]) + at], start % third_width,
                masks, far_count, rows
            )


def wide_gradients(owner, grads, active, hidden, upper, groups):
    blocks = owner.shape[0]
    far_count, rows = blocks // 8, grads[0].shape[1] // blocks
    width = active[0].shape[1]
    third_width = 2 * width // 3
    if rows % 16:
        whole = [jnp.concatenate(one, 0) for one in (grads, active, hidden, upper)]
        made = jnp.concatenate([dot_rows(whole[0], whole[1]), dot_rows(whole[2], whole[3])], 1)
        outs = []
        for third, group in enumerate(groups):
            columns = made[:, third * third_width : (third + 1) * third_width]
            for at, masks in enumerate(group):
                outs.append(placed_blocks(columns, owner, masks).astype(jnp.bfloat16 if at else jnp.float32))
        return outs
    step = 512
    outs = []
    for group in groups:
        for at, masks in enumerate(group):
            outs.append(
                shaped((len(masks) * far_count, rows, third_width), jnp.bfloat16 if at else jnp.float32)
            )
    kernel = functools.partial(wide_kernel, groups=groups, far_count=far_count, rows=rows, step=step)
    return local_call(
        kernel, outs, [*grads, *active, *hidden, *upper], [owner],
        [pltpu.VMEM((grads[0].shape[1], step), jnp.float32)], spare=12,
    )


def narrow_kernel(
    own_ref, other_ref, kv_grad_ref, query_grad_ref, own_grad_ref, other_grad_ref, low_ref, made_ref
):
    half, near = own_ref.shape[0], own_grad_ref.shape[0]
    width = query_grad_ref.shape[1]
    made_ref[:, :width] = dot_rows(own_ref[:near, :], query_grad_ref[:near, :]) + dot_rows(
        other_ref[:near, :], query_grad_ref[near:, :]
    )
    made_ref[:, width : 2 * width] = dot_rows(own_grad_ref[...], low_ref[:near, :]) + dot_rows(
        other_grad_ref[...], low_ref[near:, :]
    )
    made_ref[:, 2 * width :] = dot_rows(own_ref[...], kv_grad_ref[:half, :])
    made_ref[:, 2 * width :] += dot_rows(other_ref[...], kv_grad_ref[half:, :])


def narrow_gradients(own, other, kv_grad, query_grad, own_grad, other_grad, low):
    width = query_grad.shape[1]
    return local_call(
        narrow_kernel, [shaped((own.shape[1], 4 * width))],
        [own, other, kv_grad, query_grad, own_grad, other_grad, low],
        flops=4 * own.size * 2 * width + 8 * own_grad.size * width, spare=12,
    )[0]


def turn_kernel(*refs):
    half = len(refs) // 2
    for source_ref, out_ref in zip(refs[:half], refs[half:]):
        out_ref[...] = source_ref[...].astype(jnp.float32).T.astype(jnp.bfloat16)


def token_other_kernel(kv_grad_ref, query_grad_ref, kv_weight_ref, query_weight_ref, out_ref):
    near, half = query_grad_ref.shape[0] // 2, kv_grad_ref.shape[0] // 2
    step = 1024

    def one_part(at, carry):
        lines = pl.ds(pl.multiple_of(half + at * step, step), step)
        total = dot_plain(kv_grad_ref[lines, :], kv_weight_ref[...])
        out_ref[pl.ds(pl.multiple_of(at * step, step), step), :] = total.astype(jnp.bfloat16)
        return carry

    lax.fori_loop(1, half // step, one_part, 0)
    total = dot_plain(kv_grad_ref[half : half + step, :], kv_weight_ref[...])
    total = jnp.concatenate(
        [total[:near] + dot_plain(query_grad_ref[near:, :], query_weight_ref[...]), total[near:]], 0
    )
    out_ref[:step, :] = total.astype(jnp.bfloat16)


def token_other(kv_grad, query_grad, kv_weight, query_weight):
    return local_call(
        token_other_kernel, [shaped((kv_grad.shape[0] // 2, kv_weight.shape[1]), jnp.bfloat16)],
        [kv_grad, query_grad, kv_weight, query_weight],
        flops=kv_grad.size * kv_weight.shape[1], spare=12,
    )[0]


def small_kernel(own_ref, came_ref, out_ref):
    lines = own_ref[...] + came_ref[...]
    out_ref[...] = jnp.concatenate([lines, jnp.zeros((PAIR - lines.shape[0], lines.shape[1]), jnp.float32)], 0).T


def token_own_kernel(
    owner_ref, kv_grad_ref, query_grad_ref, kv_weight_ref, query_weight_ref, came_ref, made_ref, small_ref, *outs,
    masks, rows, placed
):
    near = query_grad_ref.shape[0] // 2
    half, columns = outs[0].shape[0], outs[0].shape[2]
    slot_rows = made_ref.shape[1] if placed else made_ref.shape[0] // (2 * half)
    for mask in range(2 * half):
        lines = slice(mask * near, (mask + 1) * near)
        total = dot_plain(kv_grad_ref[lines, :], kv_weight_ref[...]) + came_ref[lines, :].astype(jnp.float32)
        if mask == 0:
            total += dot_plain(query_grad_ref[:near, :], query_weight_ref[...])
        for third, order in enumerate(masks):
            slot = order.index(mask)
            out_ref = outs[2 * third + slot // half]
            at = slot % half
            out_ref[at, :near, :] = total[:, third * columns : (third + 1) * columns].astype(out_ref.dtype)
            for side in range(2):
                base = near + side * slot_rows
                part = slice((2 * third + side) * columns, (2 * third + side + 1) * columns)
                if placed:
                    out_ref[at, base : base + slot_rows, :] = made_ref[mask, :, part].astype(out_ref.dtype)
                    continue
                for far in range(slot_rows // rows):
                    start = pl.multiple_of(owner_ref[mask * (slot_rows // rows) + far] * rows, rows)
                    out_ref[at, base + far * rows : base + (far + 1) * rows, :] = made_ref[
                        pl.ds(start, rows), part
                    ].astype(out_ref.dtype)
            if third == 0:
                if placed:
                    small = small_ref[mask]
                else:
                    far_count = slot_rows // rows
                    small = jnp.concatenate(
                        [
                            small_ref[pl.ds(pl.multiple_of(owner_ref[mask * far_count + far] * rows, rows), rows), :]
                            for far in range(far_count)
                        ],
                        0,
                    )
                small = jnp.concatenate([small[: slot_rows // 2], small[slot_rows // 2 :]], 1)
                if slot >= half:
                    small = in_pieces(small)
                out_ref[at, near + 2 * slot_rows :, :] = small.astype(out_ref.dtype)


def token_own(owner, kv_grad, query_grad, kv_weight, query_weight, came, made, small, masks):
    near = query_grad.shape[0] // 2
    half = came.shape[0] // near // 2
    blocks, features = owner.shape[0], made.shape[0]
    rows, slot_rows = features // blocks, features // (2 * half)
    columns = kv_weight.shape[1] // 3
    placed = rows % 16 != 0
    if placed:
        made, small = (
            placed_blocks(one, owner, tuple(range(2 * half))).reshape(2 * half, slot_rows, one.shape[1])
            for one in (made, small)
        )
    outs = []
    for third in range(len(masks)):
        shape = (half, near + 2 * slot_rows + (slot_rows // 2 if third == 0 else 0), columns)
        outs += [shaped(shape), shaped(shape, jnp.bfloat16)]
    outs = local_call(
        functools.partial(token_own_kernel, masks=masks, rows=rows, placed=placed), outs,
        [kv_grad, query_grad, kv_weight, query_weight, came, made, small], [owner],
        flops=2 * came.shape[0] * kv_weight.size, spare=12,
    )
    return list(outs[::2]), list(outs[1::2])


def narrow_last_kernel(*refs, near):
    made_ref = refs[6]
    columns = refs[0].shape[2]
    slot_rows = made_ref.shape[0]
    width, plain = 6 * columns, near + 2 * slot_rows
    for third in range(3):
        total = refs[2 * third][0, near:plain] + refs[2 * third + 1][0, near:plain].astype(jnp.float32)
        for side in range(2):
            at = (2 * third + side) * columns
            made_ref[:, at : at + columns] = total[side * slot_rows : (side + 1) * slot_rows]
    small = refs[0][0, plain:] + from_pieces(refs[1][0, plain:].astype(jnp.float32))
    made_ref[: slot_rows // 2, width:] = small[:, :PAIR]
    made_ref[slot_rows // 2 :, width:] = small[:, PAIR:]
    if len(refs) > 7:
        half = slot_rows // 2
        refs[7][:, :width] = made_ref[half:, :width].astype(jnp.bfloat16)
        refs[7][:, width:] = in_pieces(made_ref[half:, width:]).astype(jnp.bfloat16)


def token_end_kernel(grad_ref, *refs):
    out_ref = refs[-1]
    near, columns = grad_ref.shape[0], refs[0].shape[2]
    for third in range(3):
        part = slice(third * columns, (third + 1) * columns)
        out_ref[:, part] = grad_ref[:, part] + (
            refs[2 * third][0, :near] + refs[2 * third + 1][0, :near].astype(jnp.float32)
        )


def end_kernel(
    core_ref, made_ref, came_ref, count_own_ref, count_came_ref,
    query_ref, key_ref, value_ref, output_ref, loss_ref, *norm_refs
):
    rows, width = query_ref.shape
    total = made_ref[:rows, : 4 * width] + came_ref[:, : 4 * width].astype(jnp.float32)
    query_ref[...] = total[:, :width]
    output_ref[...] = total[:, width : 2 * width]
    for at in range(0, width, PAIR):
        first = 2 * width + 2 * at
        key_ref[:, at : at + PAIR] = total[:, first : first + PAIR]
        value_ref[:, at : at + PAIR] = total[:, first + PAIR : first + 2 * PAIR]
    small = made_ref[:rows, 4 * width :] + from_pieces(came_ref[:, 4 * width :].astype(jnp.float32))
    features = 2.0 * rows * core_ref[1].astype(jnp.float32)
    loss_ref[...] = small[:1, 4:5] / (features * (count_own_ref[0:1, 0:1] + count_came_ref[0:1, 0:1]))
    lines = jnp.concatenate([small, jnp.zeros((PAIR - rows, PAIR), jnp.float32)], 0).T
    half = rows // 2
    mine = jnp.where(core_ref[0] == 0, lines[:, :half], lines[:, half:rows])
    for at, one_ref in enumerate(norm_refs):
        one_ref[...] = mine[at : at + 1, :]


def merge_kernel(*refs, riders):
    keeps, cames, sends, kept, messages = (refs[at : at + 3] for at in range(0, 15, 3))
    for third, rider in enumerate(riders):
        kept[third][...] = keeps[third][0] + cames[third][0].astype(jnp.float32)
        later = (keeps[third][1] + cames[third][1].astype(jnp.float32)).astype(jnp.bfloat16)
        slots, lines, columns = sends[rider].shape
        for slot in range(slots):
            messages[rider][slot * lines : (slot + 1) * lines, :] = sends[rider][slot]
        base, rows = slots * lines, later.shape[0]
        for chunk in range(later.shape[1] // columns):
            messages[rider][base + chunk * rows : base + (chunk + 1) * rows, :] = later[
                :, chunk * columns : (chunk + 1) * columns
            ]


def part_kernel(*refs, plain):
    keeps, cames, outs = refs[:3], refs[3:6], refs[6:12]
    for third in range(3):
        keep_ref, came_ref = keeps[third], cames[third]
        slots, lines, _ = keep_ref.shape
        most = min(plain, lines)
        for slot in range(slots):
            side, at = slot // (slots // 2), slot % (slots // 2)
            out_ref, base = outs[2 * third + side], slot * lines
            total = keep_ref[slot, :most] + came_ref[base : base + most, :].astype(jnp.float32)
            out_ref[at, :most] = total.astype(out_ref.dtype)
            if most < lines:
                total = keep_ref[slot, most:] + from_pieces(
                    came_ref[base + most : base + lines, :].astype(jnp.float32)
                )
                out_ref[at, most:] = (in_pieces(total) if side else total).astype(out_ref.dtype)


def wide_end_kernel(*refs, riders, lengths):
    cames, kept, wide_ref = refs[:3], refs[3:6], refs[6]
    for third, rider in enumerate(riders):
        rows, width = kept[third].shape
        columns = cames[rider].shape[1]
        for chunk in range(width // columns):
            part = slice(chunk * columns, (chunk + 1) * columns)
            base = lengths[rider] + chunk * rows
            wide_ref[:, third * width + chunk * columns : third * width + (chunk + 1) * columns] = kept[third][
                :, part
            ] + cames[rider][base : base + rows, :].astype(jnp.float32)
    if len(refs) > 7:
        refs[7][...] = wide_ref[wide_ref.shape[0] // 2 :, :].astype(jnp.bfloat16)


def wide_out_kernel(made_ref, came_ref, outer_ref, inner_ref):
    rows, width = outer_ref.shape
    outer_ref[...] = made_ref[:rows, :width] + came_ref[:, :width].astype(jnp.float32)
    inner_ref[...] = made_ref[:rows, width:] + came_ref[:, width:].astype(jnp.float32)


def tie(first, second):
    leaves, tree = jax.tree.flatten(second)
    tied = lax.optimization_barrier(tuple(leaves) + (first,))
    return jax.tree.unflatten(tree, tied[:-1])


def shards(
    tokens,
    query_weight,
    key_weight,
    value_weight,
    output_weight,
    inner_weight,
    outer_weight,
    attn_gain,
    attn_shift,
    ffn_gain,
    ffn_shift,
    teacher,
    segments,
    random_blocks,
    valid_tokens,
):
    devices = lax.axis_size("dp")
    dp_index = lax.axis_index("dp")
    core = lax.axis_index("tensor")
    rows, width = tokens.shape
    length = 2 * rows
    span = segments.shape[1] // length
    near_bits = span.bit_length() - 1
    far_bits = tuple(range(near_bits, devices.bit_length() - 1))
    place, far_place = dp_index % span, dp_index // span
    far_count = devices // span
    each = width // devices
    slot_rows = far_count * each
    head_width = query_weight.shape[1]
    wide = inner_weight.shape[1]
    masks = jnp.arange(span, dtype=jnp.int32)
    fars = jnp.arange(far_count, dtype=jnp.int32)
    owner = ((fars[None, :] ^ far_place) * span + (masks[:, None] ^ place)).reshape(-1)

    def far_gather(block):
        held = block[None]
        for bit in far_bits:
            held = jnp.concatenate([held, swap_mask(held, 1 << bit)], 0)
        return held.reshape(slot_rows, block.shape[1])

    def step(held, at):
        return [swap_mask(one, 1 << bits[at]) for one, bits in zip(held, ROUTES)]

    def both(held, came):
        return [one for pair in zip(held, came) for one in pair]

    def messages(lines):
        return [shaped((one, third), jnp.bfloat16) for one in lines]

    third = width // 3
    tail = packed_rows(slot_rows, 4 * head_width // 3)
    cuts = (0, 2 * wide // 3, 4 * wide // 3, 2 * wide + PAIR)
    sizes = [packed_rows(slot_rows, last - first) for first, last in zip(cuts, cuts[1:])]
    valid_row = valid_tokens.reshape(1, rows)
    first, second, *held = fetching_call(
        start_kernel,
        [shaped((each, 4 * head_width), jnp.bfloat16), shaped((each, cuts[3]), jnp.bfloat16)]
        + [shaped((rows, third), jnp.bfloat16)] * 3,
        [query_weight, key_weight, value_weight, output_weight, inner_weight, outer_weight, valid_row, tokens],
    )
    came = step(held, 0)
    first_held, second_held = far_gather(first), far_gather(second)
    held = local_call(
        functools.partial(first_pack_kernel, slot_rows=slot_rows), messages([2 * rows + tail] * 3),
        held + came + [first_held],
    )
    came = step(held, 1)
    held = local_call(
        functools.partial(second_pack_kernel, rows=2 * rows, slot_rows=slot_rows, cuts=cuts),
        messages([4 * rows + 2 * tail + size for size in sizes]), both(held, came) + [second_held],
    )
    came = step(held, 2)
    segment_all = lax.dynamic_index_in_dim(segments, far_place, 0, keepdims=False)
    tables = attention_tables(random_blocks, segment_all, place, core, span, length // BLOCK)
    tables, owner, came = lax.optimization_barrier((tables, owner, came))
    sent_masks = [tuple(slot_masks(bits[:2])) for bits in ROUTES]
    came_masks = [tuple(mask ^ (1 << bits[2]) for mask in sent) for sent, bits in zip(sent_masks, ROUTES)]
    own, *held = local_call(
        functools.partial(third_pack_kernel, masks=tuple(both(sent_masks, came_masks)), rows=rows, tail=2 * tail),
        [shaped((span * rows, width), jnp.bfloat16)] + messages([4 * tail + 2 * size for size in sizes]),
        both(held, came),
    )
    came = step(held, 0)
    other = swap_core(own)
    late = local_call(
        functools.partial(fourth_pack_kernel, skip=4 * tail), messages([4 * size for size in sizes]),
        both(held, came),
    )
    late_came = step(late, 1)

    held, came = tie(late[0], (held, came))
    units = units_of(
        ((0, 0, head_width),)
        + tuple((1, 2 * at + shift, PAIR) for shift in (0, PAIR) for at in range(0, head_width, PAIR))
        + ((2, 0, head_width),)
    )
    plan = []
    for at, bits in enumerate(ROUTES):
        part = units[at * len(units) // 3 : (at + 1) * len(units) // 3]
        sent = tuple(slot_masks((bits[1], bits[2])))
        plan += [(sent, part), (tuple(mask ^ (1 << bits[0]) for mask in sent), part)]
    full_query, full_kv, full_output = place_packed(
        owner, both(held, came), tuple(plan), (head_width, 2 * head_width, head_width), each
    )
    own_query, own_kv = local_call(
        token_kernel, [shaped((rows, head_width), jnp.bfloat16), shaped((span * rows, 2 * head_width), jnp.bfloat16)],
        [own, full_query, full_kv], flops=4 * own.size * head_width, spare=12,
    )
    mixed, mass, queries, kv = attend(tables, own_query, own_kv, other, full_query, full_kv)

    half_shape, low_shape = shaped((rows, width)), shaped((rows, width), jnp.bfloat16)
    gain_one, shift_one, gain_two, shift_two = (
        one.reshape(1, width) for one in (attn_gain, attn_shift, ffn_gain, ffn_shift)
    )
    part_own, part_other, attended = local_call(
        project_kernel, [half_shape, low_shape, shaped(mixed.shape, jnp.bfloat16)], [mixed, full_output],
        flops=2 * mixed.size * width,
    )
    turned = local_call(
        turn_kernel, [shaped(one.shape[::-1], jnp.bfloat16) for one in (full_query, full_kv)],
        [tie(part_own, full_query), full_kv],
    )
    part_came, late, late_came, turned = lax.optimization_barrier((swap_core(part_other), late, late_came, turned))
    turned_query, turned_kv = turned
    first_sum, hidden, hidden_own = local_call(
        first_norm_kernel, [half_shape, half_shape, low_shape],
        [tokens, part_own, part_came, gain_one, shift_one],
    )
    hidden_other = swap_core(hidden_own)
    late, late_came = tie(hidden_own, (late, late_came))
    units = units_of(((0, 0, wide), (1, 0, wide), (2, 0, PAIR)))
    plan = []
    for at, bits in enumerate(ROUTES):
        part = units[cuts[at] // PAIR : cuts[at + 1] // PAIR]
        sent = tuple(slot_masks((bits[2], bits[0])))
        plan += [(sent, part), (tuple(mask ^ (1 << bits[1]) for mask in sent), part)]
    full_inner, full_outer, counts = place_packed(
        owner, both(late, late_came), tuple(plan), (wide, wide, PAIR), each
    )
    active_shape, slope_shape = shaped((rows, wide), jnp.bfloat16), shaped((rows, wide))
    sums = [pltpu.VMEM((rows, width), jnp.float32)]
    count_own = local_call(functools.partial(count_kernel, each=each), [shaped((8, PAIR))], [counts])[0]
    count_came = swap_core(count_own)
    part_other, active_other, slope_other = local_call(
        feed_kernel, [low_shape, active_shape, slope_shape], [hidden_other, full_inner, full_outer],
        scratch=sums, spare=12,
    )
    part_came = swap_core(part_other)
    part_own, active_own, slope_own = local_call(
        feed_kernel, [half_shape, active_shape, slope_shape], [tie(part_other, hidden_own), full_inner, full_outer],
        scratch=sums, spare=12,
    )
    token_total = devices * lax.axis_size("tensor") * rows
    grad_second, grad_ffn_own, stats_two, result = local_call(
        functools.partial(second_norm_kernel, token_total=token_total),
        [half_shape, low_shape, shaped((8, width)), low_shape],
        [hidden, part_own, part_came, gain_two, shift_two, teacher, valid_row, count_own, count_came],
        free=1,
    )
    grad_ffn_other = swap_core(grad_ffn_own)
    upper_own, part_own = local_call(
        feed_back_kernel, [active_shape, half_shape], [grad_ffn_own, slope_own, full_inner, full_outer],
        scratch=sums, spare=12,
    )
    upper_other, part_other = local_call(
        feed_back_kernel, [active_shape, low_shape],
        [tie(part_own, grad_ffn_other), slope_other, full_inner, full_outer], scratch=sums, spare=12,
    )
    part_came = swap_core(part_other)
    scatter_masks = tuple(tuple(slot_masks(bits[::-1])) for bits in ROUTES)
    groups = tuple((one[: span // 2], one[span // 2 :]) for one in scatter_masks)
    outs = wide_gradients(
        owner, (grad_ffn_own, grad_ffn_other), (active_own, active_other), (hidden_own, hidden_other),
        (upper_own, upper_other), groups
    )
    outs = [one.reshape(span // 2, slot_rows, one.shape[2]) for one in outs]
    wide_keep, wide_came = outs[::2], step(outs[1::2], 0)
    part_came = tie(outs[0], part_came)
    grad_first, grad_attn_own, stats_one = local_call(
        first_back_kernel, [half_shape, low_shape, shaped((8, width))],
        [grad_second, part_own, part_came, first_sum, gain_one, stats_two],
    )
    grad_attn_other = swap_core(grad_attn_own)
    stats_came = swap_core(stats_one)
    query_grad, kv_grad = attend_back(
        tables, queries, kv, mixed, mass, grad_attn_own, grad_attn_other, full_output
    )

    def folded(keep, came):
        return fold(keep, [[one] for one in came])

    small = local_call(small_kernel, [shaped((width, PAIR))], [stats_one, tie(query_grad, stats_came)])[0]
    token_sent = token_other(tie(small, kv_grad), query_grad, turned_kv, turned_query)
    wide_keep, wide_send = folded(wide_keep, tie(token_sent, wide_came))
    wide_came = step(wide_send, 1)
    token_came = swap_core(tie(wide_keep[0], token_sent))
    made = narrow_gradients(
        own, other, tie(wide_keep[0], kv_grad), query_grad, grad_attn_own, grad_attn_other, attended
    )
    keep, send = token_own(
        owner, kv_grad, query_grad, turned_kv, turned_query, tie(made, token_came), made, small, scatter_masks
    )
    riders = tuple([bits[0] for bits in ROUTES].index(bits[2]) for bits in ROUTES)
    columns = width // 3
    ride = slot_rows * wide_keep[0].shape[2] // columns
    lengths = [one.shape[0] * one.shape[1] + ride for one in send]
    outs = local_call(
        functools.partial(merge_kernel, riders=riders),
        [shaped(one.shape[1:]) for one in wide_keep] + [shaped((one, columns), jnp.bfloat16) for one in lengths],
        wide_keep + tie(keep[0], wide_came) + send,
    )
    wide_keep, came = outs[:3], step(outs[3:], 0)
    plain = rows + 2 * slot_rows
    halves = []
    for one in keep:
        half = (one.shape[0] // 2,) + one.shape[1:]
        halves += [shaped(half), shaped(half, jnp.bfloat16)]
    far_send = [shaped((each, 2 * wide), jnp.bfloat16)] if far_count == 2 else []
    cames = came
    outs = local_call(functools.partial(part_kernel, plain=plain), halves, keep + cames)
    keep, send = list(outs[::2]), list(outs[1::2])
    came = step(send, 1)
    wide_sum, *wide_send = local_call(
        functools.partial(wide_end_kernel, riders=riders, lengths=tuple(one - ride for one in lengths)),
        [shaped((slot_rows, 2 * wide))] + far_send, [tie(keep[0], cames[0])] + list(cames[1:]) + list(wide_keep),
    )

    def far_scatter(total, dtype=jnp.bfloat16):
        total = total.reshape(far_count, each, total.shape[1])
        for bit in far_bits[::-1]:
            half = total.shape[0] // 2
            total = total[:half] + swap_mask(total[half:].astype(dtype), 1 << bit).astype(jnp.float32)
        return total[0]

    keep, send = fold(keep, [[one] for one in came], plain)
    came = step(send, 2)
    if far_count == 2:
        part_outer, part_inner = local_call(
            wide_out_kernel, [shaped((each, wide))] * 2, [wide_sum, swap_mask(wide_send[0], 1 << far_bits[0])], free=2
        )
    else:
        wide_sum = far_scatter(wide_sum)
        part_outer, part_inner = wide_sum[:, :wide], wide_sum[:, wide:]
    came = tie(part_outer, came)
    made_shape = shaped((slot_rows, 4 * head_width + PAIR))
    send_shape = [shaped((each, 4 * head_width + PAIR), jnp.bfloat16)] if far_count == 2 else []
    arrived = both(keep, came)
    made, *send = local_call(
        functools.partial(narrow_last_kernel, near=rows), [made_shape] + send_shape, arrived
    )
    grad_tokens = local_call(
        token_end_kernel, [half_shape], [grad_first, tie(made, arrived[0])] + arrived[1:], free=1
    )[0]
    half = each // 2
    if far_count == 2:
        weight_shape = shaped((each, head_width))
        outs = local_call(
            end_kernel, [weight_shape] * 4 + [shaped((1, 1))] + [shaped((1, half))] * 4,
            [made, tie(grad_tokens, swap_mask(send[0], 1 << far_bits[0])), count_own, count_came],
            [jnp.stack([core, jnp.int32(devices)])], free=9,
        )
        part_query, part_key, part_value, part_output = outs[:4]
        loss_value = outs[4].reshape(())
        norm_parts = [one.reshape(half) for one in outs[5:]]
    else:
        narrow_sum = far_scatter(made[:, : 4 * head_width])
        small = far_scatter(made[:, 4 * head_width :], jnp.float32)
        part_query, part_output = narrow_sum[:, :head_width], narrow_sum[:, head_width : 2 * head_width]
        kv_sum = narrow_sum[:, 2 * head_width :].reshape(each, head_width // PAIR, 2, PAIR)
        part_key, part_value = (kv_sum[:, :, one].reshape(each, head_width) for one in range(2))
        loss_value = small[0, 4] / (2.0 * width * (count_own[0, 0] + count_came[0, 0]))
        mine = jnp.where(core == 0, small[:half], small[half:])
        norm_parts = [mine[:, at] for at in range(4)]
    return (
        result,
        loss_value,
        grad_tokens,
        part_query,
        part_key,
        part_value,
        part_output,
        part_inner,
        part_outer,
        *norm_parts,
    )


def solution(mesh):
    both = P(("dp", "tensor"))
    rows_spec = P(("dp", "tensor"), None)
    weight_spec = P("dp", "tensor")
    in_specs = (rows_spec,) + (weight_spec,) * 6 + (P(),) * 4
    in_specs += (rows_spec, P(), P("tensor", None, None), both)
    out_specs = (rows_spec, P(), rows_spec) + (weight_spec,) * 6 + (both,) * 4
    return jax.shard_map(shards, mesh=mesh, in_specs=in_specs, out_specs=out_specs, check_vma=False)
```
